32 devices in a mesh: groups: 2 (over y), rows: 4 (over z), feat: 2 (over x), ent: 2 (over core).
Axes of the slice: x: 2, y: 2, z: 4, core: 2. Of those that a mesh axis runs over, the one named last changes fastest.
Arguments:
- features: bfloat16 [16384, 4096], P(('groups', 'rows', 'ent'), 'feat'), parts along dimension 0, may hold values from -6 to 6
- global_weight: bfloat16 [8192], P(('groups', 'feat')), parts along dimension 0, may hold values from -0.09375 to 0.09375
- entity_feats: bfloat16 [16384, 512], P(('groups', 'rows', 'ent'), 'feat'), parts along dimension 0, may hold values from -6 to 6
- coefs: float32 [8192, 512], P(('groups', 'rows', 'ent'), 'feat'), parts along dimension 0, may hold values from -0.4 to 0.4
- member_owner: int32 [16384, 1], P(('groups', 'rows', 'ent')), parts along dimension 0, may hold values from 0 to 7; in each aligned block of 1024 rows (0 to 1023, 1024 to 2047, ...) at most 256 rows name the same one
- member_local: int32 [16384], P(('groups', 'rows', 'ent')), parts along dimension 0, may hold values from 0 to 511
- item_owner: int32 [16384, 1], P(('groups', 'rows', 'ent')), parts along dimension 0, may hold values from 0 to 7; in each aligned block of 1024 rows (0 to 1023, 1024 to 2047, ...) at most 256 rows name the same one
- item_local: int32 [16384], P(('groups', 'rows', 'ent')), parts along dimension 0, may hold values from 0 to 511
- clicks: int32 [16384], P(('groups', 'rows', 'ent')), parts along dimension 0, may hold values from 0 to 1
- valid: int32 [16384], P(('groups', 'rows', 'ent')), parts along dimension 0, may hold values 0 or 1
Outputs:
- grad_global: float32 [8192], P(('groups', 'feat')), parts along dimension 0
- grad_coefs: float32 [8192, 512], P(('groups', 'rows', 'ent'), 'feat'), parts along dimension 0
The draws below stay inside these ranges and needn't reach their ends.
There are 2 independent parts, one for each index of `groups`. The reference program is written for one: setup_inputs(seed, part) draws one part's arguments, and reference() takes and returns one part's arrays. A program takes and returns all parts, laid end to end along the dimension named above; each array names one. Nothing has to cross between parts.
Inputs may be any that keep to these rules, and one draw needn't show every extreme that they name: `member_owner`: in the rows of one device no owner is named by more than 256 rows. `item_owner`: in the rows of one device no owner is named by more than 256 rows.
All inputs are finite; a program needn't handle non-finite values. No bound on the sum of `valid` on one device may be relied on, other than what follows from the above.
Results may differ from the reference program's by a relative error of at most 0.0023.
Values may be sent and summed in bfloat16 or wider, within the bound.
No kernel may reach another device: no remote copies, remote signals or barrier semaphores. Data moves between devices by JAX's collectives and lax.ppermute only.
A program may use at most 64 MiB of HBM per device.

```python
import math
import jax
import jax.numpy as jnp
import numpy as np
from jax import lax

G = 4096
EF = 256
ROW_DEV = 1024
ENT_DEV = 512
CAP = 256
ROWS = 8192
ENT = 4096
N_ROWS = 4
N_ENT = 2


def set_ends(entries, key, low, high):
    extent = entries.shape
    index_at = [jax.random.randint(jax.random.fold_in(key, axis), (), 0, extent[axis]) for axis in range(len(extent))]
    entries = entries.at[tuple(index_at)].set(low)
    longest = extent.index(max(extent))
    index_at[longest] = (index_at[longest] + 1) % extent[longest]
    return entries.at[tuple(index_at)].set(high)


def block_scale(own_key, extent, pieces, least, high):
    level, own = 1.0, jax.random.fold_in(own_key, 6)
    for position, parts in pieces:
        draws = jnp.exp(jax.random.uniform(jax.random.fold_in(own, position), (parts,), jnp.float32, least / len(pieces), high / len(pieces)))
        level = level * jnp.repeat(draws, extent[position] // parts).reshape([-1 if axis == position else 1 for axis in range(len(extent))])
    return level


def assign_block(rng, own, number, rows, number_of, top, most, lean):
    order = jax.random.permutation(rng, number_of)
    heavy_load, ordinary = shares(number_of, rows * top, most, lean, True), shares(number_of, rows * top, most, lean, False)
    places = jnp.arange(number_of)

    def named(sizes, rotation):
        used = int((sizes > 0).sum())
        fixed = max(1, used // 4)
        passed = fixed + (places - fixed + rotation * (used - fixed)) % max(1, number_of - fixed)
        return jnp.zeros((number_of,), jnp.int32).at[order[jnp.where(places < fixed, places, passed)]].set(jnp.asarray(sizes, jnp.int32))

    sizes = jnp.where(number % 4 == 0, named(heavy_load, number // 4), named(ordinary, number - number // 4 - 1))
    mixed = jax.random.permutation(jax.random.fold_in(own, 3), number_of)
    donor, receiver = mixed[0:number_of // 2 * 2:2], mixed[1:number_of // 2 * 2:2]
    slack = jnp.minimum(sizes[donor] - 1, most - sizes[receiver]) // 2
    slack = jnp.where((donor == order[0]) | (receiver == order[0]) | (sizes[receiver] == 0), 0, jnp.maximum(slack, 0))
    passed = jax.random.randint(jax.random.fold_in(own, 4), (number_of // 2,), 0, 1 << 20) % (slack + 1)
    sizes = sizes.at[donor].add(-passed).at[receiver].add(passed)
    members = jnp.searchsorted(jnp.cumsum(sizes), jnp.arange(rows * top), side="right").astype(jnp.int32)
    table = members.reshape(top, rows).T
    table = table[jax.random.permutation(jax.random.fold_in(own, 1), rows)]
    rotation = jax.random.randint(jax.random.fold_in(own, 2), (rows, 1), 0, top)
    return jnp.take_along_axis(table, (jnp.arange(top)[None, :] + rotation) % top, axis=1)


def shares(count, total, limit, lean, full):
    portions = [(1 << 20) // math.isqrt(grade ** lean) + 1 for grade in range(1, count + 1)]
    largest = limit if full else min(limit, max(-(-total // count), total * portions[0] // sum(portions)))
    least = 1 if total - largest >= count - 1 else 0
    given, rest = [largest] + [least] * (count - 1), total - largest - least * (count - 1)
    while rest > 0:
        free = [i for i in range(1, count) if given[i] < largest] or [i for i in range(1, count) if given[i] < limit]
        pool, left = sum([portions[i] for i in free]), rest
        for i in free:
            extra = min(limit - given[i], max(1, left * portions[i] // pool), rest)
            given[i] = given[i] + extra
            rest = rest - extra
    return np.array(given)


def centred(rng, extent, spread, bound, pieces=(), dtype=jnp.bfloat16):
    level = block_scale(rng, extent, pieces, -0.22, 0.18) if pieces else 1.0
    values = jax.random.normal(rng, extent, jnp.float32) * spread * level
    return jnp.minimum(jnp.maximum(values, -bound), bound).astype(dtype)


def setup_inputs(seed: int = 0, part: int = 0) -> dict:
    streams_of = jax.random.split(jax.random.key(seed), 11)
    part_keys = jax.random.split(jax.random.fold_in(streams_of[10], part), 11)
    features = centred(part_keys[0], (ROWS, G), 1.0, 6.0, ((0, 8), (1, 2)))
    global_weight = centred(part_keys[1], (G,), G ** -0.5, 0.09375, ((0, 2),))
    entity_feats = centred(part_keys[2], (ROWS, 2 * EF), 1.0, 6.0, ((0, 8), (1, 2)))
    coefs = centred(part_keys[3], (ENT, 2 * EF), 0.0625, 0.4, ((0, 8), (1, 2)), jnp.float32)
    member_owner_keys = jax.random.split(jax.random.fold_in(part_keys[4], 1), ROWS // ROW_DEV)
    member_owner_turns = jax.random.permutation(jax.random.fold_in(part_keys[4], 3), ROWS // ROW_DEV)
    member_owner = jax.vmap(lambda own, number: assign_block(jax.random.fold_in(part_keys[4], 2), own, number, ROW_DEV, N_ROWS * N_ENT, 1, CAP, 2))(member_owner_keys, member_owner_turns).reshape((ROWS, 1))
    member_local = set_ends(jax.random.randint(part_keys[5], (ROWS,), 0, ENT_DEV), jax.random.fold_in(part_keys[5], 1), 0, ENT_DEV - 1).astype(jnp.int32)
    item_owner_keys = jax.random.split(jax.random.fold_in(part_keys[6], 1), ROWS // ROW_DEV)
    item_owner_turns = jax.random.permutation(jax.random.fold_in(part_keys[6], 3), ROWS // ROW_DEV)
    item_owner = jax.vmap(lambda own, number: assign_block(jax.random.fold_in(part_keys[6], 2), own, number, ROW_DEV, N_ROWS * N_ENT, 1, CAP, 3))(item_owner_keys, item_owner_turns).reshape((ROWS, 1))
    item_local = set_ends(jax.random.randint(part_keys[7], (ROWS,), 0, ENT_DEV), jax.random.fold_in(part_keys[7], 1), 0, ENT_DEV - 1).astype(jnp.int32)
    clicks = set_ends(jax.random.randint(part_keys[8], (ROWS,), 0, 2), jax.random.fold_in(part_keys[8], 1), 0, 1).astype(jnp.int32)
    valid = set_ends((jax.random.randint(part_keys[9], (ROWS,), 0, 8) < 7).astype(jnp.int32), jax.random.fold_in(part_keys[9], 1), 0, 1)
    return dict(features=features, global_weight=global_weight, entity_feats=entity_feats, coefs=coefs, member_owner=member_owner, member_local=member_local, item_owner=item_owner, item_local=item_local, clicks=clicks, valid=valid)


def reference(features, global_weight, entity_feats, coefs, member_owner, member_local, item_owner, item_local, clicks, valid):
    member = (member_owner[:, 0] * ENT_DEV + member_local).astype(jnp.int32)
    item = (item_owner[:, 0] * ENT_DEV + item_local).astype(jnp.int32)
    member_feats = entity_feats[:, :EF].astype(jnp.float32)
    item_feats = entity_feats[:, EF:].astype(jnp.float32)
    global_part = jnp.dot(features, global_weight, preferred_element_type=jnp.float32)
    member_part = lax.optimization_barrier(jnp.sum(member_feats * coefs[member, :EF], axis=1))
    item_part = lax.optimization_barrier(jnp.sum(item_feats * coefs[item, EF:], axis=1))
    margin = global_part + member_part + item_part
    resid = valid.astype(jnp.float32) * (jax.nn.sigmoid(margin) - clicks.astype(jnp.float32))
    resid_low = resid.astype(jnp.bfloat16)
    summed = jnp.dot(resid_low, features, preferred_element_type=jnp.float32)
    grad_global = summed / math.sqrt(ROWS) + 4.0 * global_weight.astype(jnp.float32)
    member_grad = jnp.zeros((ENT, EF), jnp.float32).at[member].add(resid[:, None] * member_feats)
    item_grad = jnp.zeros((ENT, EF), jnp.float32).at[item].add(resid[:, None] * item_feats)
    grad_coefs = jnp.concatenate([member_grad, item_grad], axis=1) + coefs
    return (grad_global, grad_coefs)
```

```python
import math

import jax
import jax.numpy as jnp
from jax import lax
from jax.experimental import pallas as pl
from jax.experimental.pallas import tpu as pltpu
from jax.sharding import PartitionSpec as P

F32 = jnp.float32
BF16 = jnp.bfloat16
HOME = ("rows", "ent")
EVERY = ("rows", "feat", "ent")
IDS = 16
PARAMS = pltpu.CompilerParams(vmem_limit_bytes=24 * 2**20)


def lanes_dot(a, b):
    return lax.dot_general(a, b, (((1,), (1,)), ((), ())), preferred_element_type=F32)


def plain_dot(a, b):
    return lax.dot_general(a, b, (((1,), (0,)), ((), ())), preferred_element_type=F32)


def halves(x):
    high = x.astype(BF16)
    return high, (x - high.astype(F32)).astype(BF16)


def one_hot(row, count):
    return row == lax.broadcasted_iota(jnp.int32, (count, row.shape[1]), 0)


def dispatch_kernel(owners, capacity, where, member, item, member_local, item_local, feats, ranks, *chunks):
    rows = feats.shape[0]
    step = min(256, rows)
    blocks = rows // step
    mine, on_item = where[0], where[1] > 0
    hits = jnp.concatenate(
        [one_hot(member[...], owners).astype(F32), one_hot(item[...], owners).astype(F32)], axis=0
    )
    stacked = jnp.concatenate([hits[:, b * step : (b + 1) * step] for b in range(blocks)], axis=0)
    upper = lax.broadcasted_iota(jnp.int32, (step, step), 0) <= lax.broadcasted_iota(
        jnp.int32, (step, step), 1
    )
    counts = plain_dot(stacked.astype(BF16), upper.astype(F32).astype(BF16))
    before = jnp.zeros((2 * owners, 1), F32)
    pieces = []
    for b in range(blocks):
        here = counts[2 * owners * b : 2 * owners * (b + 1)]
        taken = (here + before) * hits[:, b * step : (b + 1) * step]
        pieces.append(
            jnp.concatenate(
                [
                    jnp.sum(taken[:owners], axis=0, keepdims=True),
                    jnp.sum(taken[owners:], axis=0, keepdims=True),
                ],
                axis=0,
            )
        )
        before = before + here[:, step - 1 : step]
    rank = jnp.concatenate(pieces, axis=1).astype(jnp.int32) - 1
    ranks[...] = rank
    own = jnp.where(on_item, item[...], member[...])
    own_rank = jnp.where(on_item, rank[1:2], rank[0:1])
    local = jnp.where(on_item, item_local[...], member_local[...])
    place = (own ^ mine) * capacity + own_rank
    high = local >> 8
    ids = jnp.concatenate([high, local - (high << 8), jnp.zeros((IDS - 2, rows), jnp.int32)], axis=0)
    ids = ids.astype(F32).astype(BF16)
    for k in range(owners):
        pick = one_hot(place - k * capacity, capacity).astype(F32).astype(BF16)
        chunks[k][:capacity] = plain_dot(pick, feats[...]).astype(BF16)
        chunks[k][capacity:, :capacity] = lanes_dot(ids, pick).astype(BF16)


def chunk_ids(chunk, capacity):
    pair = chunk[capacity:, :capacity].astype(F32)
    return (pair[0:1] * 256.0 + pair[1:2]).astype(jnp.int32)


def scores_kernel(owners, capacity, coefs, *refs):
    entities = coefs.shape[0]
    high, low = halves(coefs[...])
    for k in range(owners):
        chunk, out = refs[k], refs[owners + k]
        feats = chunk[:capacity]
        every = lanes_dot(high, feats) + lanes_dot(low, feats)
        out[...] = jnp.sum(
            jnp.where(one_hot(chunk_ids(chunk, capacity), entities), every, 0.0), axis=0, keepdims=True
        )


def home_kernel(owners, capacity, sides, where, member, item, ranks, clicks, valid, margin, *refs):
    mine, on_item = where[0], where[1] > 0
    scores = refs[: sides * owners]
    resid_out = refs[sides * owners]
    outs = refs[sides * owners + 1 :]
    total = margin[...]
    hits_of, spot_of = [], []
    for side, owner in ((0, member), (1, item)):
        hits = one_hot(owner[...] ^ mine, owners)
        spot = one_hot(ranks[side : side + 1], capacity).astype(F32).astype(BF16)
        hits_of.append(hits)
        spot_of.append(spot)
    for q in range(sides):
        table = jnp.concatenate([scores[q * owners + k][...] for k in range(owners)], axis=0)
        high, low = halves(table)
        is_item = where[2 + q] > 0
        spot = jnp.where(is_item, spot_of[1], spot_of[0])
        hits = jnp.where(is_item, hits_of[1].astype(F32), hits_of[0].astype(F32))
        found = plain_dot(jnp.concatenate([high, low], axis=0), spot)
        total = total + jnp.sum((found[:owners] + found[owners:]) * hits, axis=0, keepdims=True)
    resid = valid[...].astype(F32) * (jax.nn.sigmoid(total) - clicks[...].astype(F32))
    resid_out[...] = resid
    hits = jnp.where(on_item, hits_of[1].astype(F32), hits_of[0].astype(F32))
    spot = jnp.where(on_item, spot_of[1], spot_of[0])
    high, low = halves(hits * resid)
    sent = lanes_dot(jnp.concatenate([high, low], axis=0), spot)
    sent = sent[:owners] + sent[owners:]
    for k in range(owners):
        outs[k][...] = sent[k : k + 1]


def coefs_kernel(owners, capacity, coefs, *refs):
    entities = coefs.shape[0]
    total = coefs[...]
    for k in range(owners):
        chunk, resid = refs[k], refs[owners + k]
        hits = one_hot(chunk_ids(chunk, capacity), entities)
        high, low = halves(jnp.where(hits, resid[...], 0.0))
        feats = chunk[:capacity]
        total = total + plain_dot(high, feats) + plain_dot(low, feats)
    refs[2 * owners][...] = total


def xor_send(x, axes, size, k):
    return x if k == 0 else lax.ppermute(x, axes, [(i, i ^ k) for i in range(size)])


def call(kernel, out_shape, operands, scalars=0, flops=0):
    smem = pl.BlockSpec(memory_space=pltpu.SMEM)
    vmem = pl.BlockSpec(memory_space=pltpu.VMEM)
    moved = sum(x.size * x.dtype.itemsize for x in (*operands, *out_shape))
    return pl.pallas_call(
        kernel,
        out_shape=out_shape,
        in_specs=[smem] * scalars + [vmem] * (len(operands) - scalars),
        out_specs=[vmem] * len(out_shape),
        compiler_params=PARAMS,
        cost_estimate=pl.CostEstimate(flops=flops, bytes_accessed=moved, transcendentals=0),
    )(*operands)


def body(
    features,
    global_weight,
    entity_feats,
    coefs,
    member_owner,
    member_local,
    item_owner,
    item_local,
    clicks,
    valid,
):
    rows_here, width = entity_feats.shape
    n_feat = lax.axis_size("feat")
    n_ent = lax.axis_size("ent")
    owners = lax.axis_size("rows") * n_ent
    capacity = 2 * rows_here // owners
    mine = lax.axis_index(HOME)
    feat = lax.axis_index("feat")
    sides_item = [((feat ^ q) >= n_feat // 2).astype(jnp.int32) for q in range(n_feat)]
    where = jnp.stack([mine.astype(jnp.int32), sides_item[0], *sides_item])
    member, item = member_owner.reshape(1, rows_here), item_owner.reshape(1, rows_here)

    def shape(*dims, dtype=F32):
        return jax.ShapeDtypeStruct(dims, dtype)

    def partial(kernel, *args):
        return lambda *refs: kernel(*args, *refs)

    order = sorted(range(1, owners), reverse=True)
    ranks, *chunks = call(
        partial(dispatch_kernel, owners, capacity),
        [shape(2, rows_here, dtype=jnp.int32)] + [shape(capacity + IDS, width, dtype=BF16)] * owners,
        (where, member, item, member_local.reshape(1, rows_here), item_local.reshape(1, rows_here), entity_feats),
        scalars=1,
        flops=2 * owners * capacity * rows_here * width,
    )
    arrived = [None] * owners
    for k in order + [0]:
        arrived[k] = xor_send(chunks[k], HOME, owners, k)

    global_part = jnp.dot(features, global_weight, preferred_element_type=F32)
    global_total = global_part
    for q in range(1, n_feat):
        global_total = global_total + xor_send(global_part, "feat", n_feat, q)

    scores = call(
        partial(scores_kernel, owners, capacity),
        [shape(1, capacity)] * owners,
        (coefs, *arrived),
        flops=4 * coefs.size * owners * capacity,
    )
    returned = []
    for q in range(n_feat):
        for k in range(owners):
            apart = (k // n_ent * n_feat + q) * n_ent + k % n_ent
            returned.append(xor_send(scores[k], EVERY, n_feat * owners, apart))
    resid, *resid_out = call(
        partial(home_kernel, owners, capacity, n_feat),
        [shape(1, rows_here)] + [shape(1, capacity)] * owners,
        (
            where,
            member,
            item,
            ranks,
            clicks.reshape(1, rows_here),
            valid.reshape(1, rows_here),
            global_total.reshape(1, rows_here),
            *returned,
        ),
        scalars=1,
    )
    resid_in = [xor_send(resid_out[k], HOME, owners, k) for k in range(owners)]
    partial_grad = jnp.dot(resid.reshape(rows_here).astype(BF16), features, preferred_element_type=F32)
    terms = [xor_send(partial_grad, HOME, owners, k) for k in range(owners)]
    while len(terms) > 1:
        terms = [a + b for a, b in zip(terms[::2], terms[1::2])]
    (summed,) = terms
    (grad_coefs,) = call(
        partial(coefs_kernel, owners, capacity),
        [shape(*coefs.shape)],
        (coefs, *arrived, *resid_in),
        flops=4 * coefs.size * owners * capacity,
    )
    scale = 1.0 / math.sqrt(rows_here * owners)
    grad_global = summed * scale + 4.0 * global_weight.astype(F32)
    return (grad_global, grad_coefs)


def solution(mesh):
    by_row = P(("groups", "rows", "ent"))
    by_both = P(("groups", "rows", "ent"), "feat")
    column = P(("groups", "rows", "ent"), None)
    by_feat = P(("groups", "feat"))
    return jax.shard_map(
        body,
        mesh=mesh,
        in_specs=(by_both, by_feat, by_both, by_both, column, by_row, column, by_row, by_row, by_row),
        out_specs=(by_feat, by_both),
        check_vma=False,
    )
```

```python
import math

import jax
import jax.numpy as jnp
from jax import lax
from jax.experimental import pallas as pl
from jax.experimental.pallas import tpu as pltpu
from jax.sharding import PartitionSpec as P

F32 = jnp.float32
BF16 = jnp.bfloat16
HOME = ("rows", "ent")
EVERY = ("rows", "feat", "ent")
IDS = 16
PARAMS = pltpu.CompilerParams(vmem_limit_bytes=24 * 2**20)
SMEM = pl.BlockSpec(memory_space=pltpu.SMEM)
VMEM = pl.BlockSpec(memory_space=pltpu.VMEM)
HBM = pl.BlockSpec(memory_space=pltpu.HBM)


def lanes_dot(a, b):
    return lax.dot_general(a, b, (((1,), (1,)), ((), ())), preferred_element_type=F32)


def plain_dot(a, b):
    return lax.dot_general(a, b, (((1,), (0,)), ((), ())), preferred_element_type=F32)


def halves(x):
    high = x.astype(BF16)
    return high, (x - high.astype(F32)).astype(BF16)


def one_hot(row, count):
    return row == lax.broadcasted_iota(jnp.int32, (count, row.shape[1]), 0)


def dispatch_kernel(owners, capacity, where, *refs):
    sources, ranks, chunks = refs[:5], refs[5], refs[6 : 6 + owners]
    copies, sems = refs[6 + owners : 11 + owners], refs[11 + owners]
    moves = [pltpu.make_async_copy(sources[i], copies[i], sems.at[i]) for i in range(5)]
    for move in moves:
        move.start()
    member, item, member_local, item_local, feats = copies
    rows = feats.shape[0]
    step = min(256, rows)
    blocks = rows // step
    mine, on_item = where[0], where[1] > 0
    moves[0].wait()
    moves[1].wait()
    hits = jnp.concatenate(
        [one_hot(member[...], owners).astype(F32), one_hot(item[...], owners).astype(F32)], axis=0
    )
    stacked = jnp.concatenate([hits[:, b * step : (b + 1) * step] for b in range(blocks)], axis=0)
    upper = lax.broadcasted_iota(jnp.int32, (step, step), 0) <= lax.broadcasted_iota(
        jnp.int32, (step, step), 1
    )
    counts = plain_dot(stacked.astype(BF16), upper.astype(F32).astype(BF16))
    before = jnp.zeros((2 * owners, 1), F32)
    pieces = []
    for b in range(blocks):
        here = counts[2 * owners * b : 2 * owners * (b + 1)]
        taken = (here + before) * hits[:, b * step : (b + 1) * step]
        pieces.append(
            jnp.concatenate(
                [
                    jnp.sum(taken[:owners], axis=0, keepdims=True),
                    jnp.sum(taken[owners:], axis=0, keepdims=True),
                ],
                axis=0,
            )
        )
        before = before + here[:, step - 1 : step]
    rank = jnp.concatenate(pieces, axis=1).astype(jnp.int32) - 1
    ranks[...] = rank
    own = jnp.where(on_item, item[...], member[...])
    own_rank = jnp.where(on_item, rank[1:2], rank[0:1])
    moves[2].wait()
    moves[3].wait()
    local = jnp.where(on_item, item_local[...], member_local[...])
    place = (own ^ mine) * capacity + own_rank
    high = local >> 8
    ids = jnp.concatenate([high, local - (high << 8), jnp.zeros((IDS - 2, rows), jnp.int32)], axis=0)
    ids = ids.astype(F32).astype(BF16)
    moves[4].wait()
    for k in reversed(range(owners)):
        pick = one_hot(place - k * capacity, capacity).astype(F32).astype(BF16)
        chunks[k][:capacity] = plain_dot(pick, feats[...]).astype(BF16)
        chunks[k][capacity:, :capacity] = lanes_dot(ids, pick).astype(BF16)


def chunk_ids(chunk, capacity):
    pair = chunk[capacity:, :capacity].astype(F32)
    return (pair[0:1] * 256.0 + pair[1:2]).astype(jnp.int32)


def scores_kernel(owners, capacity, n_feat, n_ent, where, coefs, *refs):
    chunks, out = refs[:owners], refs[owners]
    entities = coefs.shape[0]
    mine = where[0]
    high, low = halves(coefs[...])
    for k in range(owners):
        feats = chunks[k][:capacity]
        every = lanes_dot(high, feats) + lanes_dot(low, feats)
        hits = one_hot(chunk_ids(chunks[k], capacity), entities)
        score = jnp.sum(jnp.where(hits, every, 0.0), axis=0, keepdims=True)
        home = mine ^ k
        for f in range(n_feat):
            out[(home // n_ent * n_feat + f) * n_ent + home % n_ent] = score


def home_kernel(
    owners, capacity, n_feat, n_ent, where, member, item, ranks, clicks, valid, margin, scores, features, out
):
    on_item = where[1] > 0
    total = margin[...]
    hits_of = [one_hot(owner[...], owners).astype(F32) for owner in (member, item)]
    spot_of = [one_hot(ranks[side : side + 1], capacity).astype(F32).astype(BF16) for side in (0, 1)]
    for side in (0, 1):
        table = None
        for f in range(side * n_feat // 2, (side + 1) * n_feat // 2):
            part = jnp.concatenate(
                [scores[(h // n_ent * n_feat + f) * n_ent + h % n_ent] for h in range(owners)], axis=0
            )
            table = part if table is None else table + part
        found = plain_dot(jnp.concatenate(halves(table), axis=0), spot_of[side])
        total = total + jnp.sum((found[:owners] + found[owners:]) * hits_of[side], axis=0, keepdims=True)
    resid = valid[...].astype(F32) * (jax.nn.sigmoid(total) - clicks[...].astype(F32))
    hits = jnp.where(on_item, hits_of[1], hits_of[0])
    spot = jnp.where(on_item, spot_of[1], spot_of[0])
    sent = lanes_dot(jnp.concatenate(halves(hits * resid), axis=0), spot)
    sent = sent[:owners] + sent[owners:]
    low = jnp.broadcast_to(resid, (16, resid.shape[1])).astype(BF16)
    grad = plain_dot(low, features[...])[0:1]
    for h in range(owners):
        out[h, :, :capacity] = sent[h : h + 1]
        out[h, :, capacity:] = grad


def grads_kernel(owners, capacity, scale, where, coefs, weight, came, *refs):
    chunks, grad_global, grad_coefs = refs[:owners], refs[owners], refs[owners + 1]
    entities = coefs.shape[0]
    mine = where[0]
    summed = came[0][:, capacity:]
    for h in range(1, owners):
        summed = summed + came[h][:, capacity:]
    grad_global[...] = summed * scale + 4.0 * weight[...]
    total = coefs[...]
    for k in range(owners):
        resid = came[mine ^ k][:, :capacity]
        hits = one_hot(chunk_ids(chunks[k], capacity), entities)
        high, low = halves(jnp.where(hits, resid, 0.0))
        feats = chunks[k][:capacity]
        total = total + plain_dot(high, feats) + plain_dot(low, feats)
    grad_coefs[...] = total


def xor_send(x, axes, size, k):
    return x if k == 0 else lax.ppermute(x, axes, [(i, i ^ k) for i in range(size)])


def call(kernel, out_shape, operands, in_specs, flops=0, scratch=()):
    moved = sum(x.size * x.dtype.itemsize for x in (*operands, *out_shape))
    return pl.pallas_call(
        kernel,
        out_shape=out_shape,
        in_specs=in_specs,
        out_specs=[VMEM] * len(out_shape),
        scratch_shapes=scratch,
        compiler_params=PARAMS,
        cost_estimate=pl.CostEstimate(flops=flops, bytes_accessed=moved, transcendentals=0),
    )(*operands)


def body(
    features,
    global_weight,
    entity_feats,
    coefs,
    member_owner,
    member_local,
    item_owner,
    item_local,
    clicks,
    valid,
):
    rows_here, width = entity_feats.shape
    columns = features.shape[1]
    n_feat, n_ent = lax.axis_size("feat"), lax.axis_size("ent")
    owners = lax.axis_size("rows") * n_ent
    capacity = 2 * rows_here // owners
    mine = lax.axis_index(HOME).astype(jnp.int32)
    on_item = (lax.axis_index("feat") >= n_feat // 2).astype(jnp.int32)
    where = jnp.stack([mine, on_item])
    member, item = member_owner.reshape(1, rows_here), item_owner.reshape(1, rows_here)

    def shape(*dims, dtype=F32):
        return jax.ShapeDtypeStruct(dims, dtype)

    def partial(kernel, *args):
        return lambda *refs: kernel(*args, *refs)

    row = pltpu.VMEM((1, rows_here), jnp.int32)
    ranks, *chunks = call(
        partial(dispatch_kernel, owners, capacity),
        [shape(2, rows_here, dtype=jnp.int32)] + [shape(capacity + IDS, width, dtype=BF16)] * owners,
        (where, member, item, member_local.reshape(1, rows_here), item_local.reshape(1, rows_here), entity_feats),
        [SMEM] + [HBM] * 5,
        flops=2 * owners * capacity * rows_here * width,
        scratch=[row, row, row, row, pltpu.VMEM((rows_here, width), BF16), pltpu.SemaphoreType.DMA((5,))],
    )
    arrived = [None] * owners
    for k in reversed(range(owners)):
        arrived[k] = xor_send(chunks[k], HOME, owners, k)

    global_part = jnp.dot(features, global_weight, preferred_element_type=F32)
    global_total = global_part
    for q in range(1, n_feat):
        global_total = global_total + xor_send(global_part, "feat", n_feat, q)

    (scores,) = call(
        partial(scores_kernel, owners, capacity, n_feat, n_ent),
        [shape(n_feat * owners, 1, capacity)],
        (where, coefs, *arrived),
        [SMEM] + [VMEM] * (1 + owners),
        flops=4 * coefs.size * owners * capacity,
    )
    returned = lax.all_to_all(scores, EVERY, split_axis=0, concat_axis=0, tiled=True)
    (sent,) = call(
        partial(home_kernel, owners, capacity, n_feat, n_ent),
        [shape(owners, 1, capacity + columns)],
        (
            where,
            member,
            item,
            ranks,
            clicks.reshape(1, rows_here),
            valid.reshape(1, rows_here),
            global_total.reshape(1, rows_here),
            returned,
            features,
        ),
        [SMEM] + [VMEM] * 8,
        flops=32 * features.size,
    )
    came = lax.all_to_all(sent, HOME, split_axis=0, concat_axis=0, tiled=True)
    grad_global, grad_coefs = call(
        partial(grads_kernel, owners, capacity, 1.0 / math.sqrt(rows_here * owners)),
        [shape(1, columns), shape(*coefs.shape)],
        (where, coefs, global_weight.astype(F32).reshape(1, columns), came, *arrived),
        [SMEM] + [VMEM] * (3 + owners),
        flops=4 * coefs.size * owners * capacity,
    )
    return (grad_global.reshape(columns), grad_coefs)


def solution(mesh):
    by_row = P(("groups", "rows", "ent"))
    by_both = P(("groups", "rows", "ent"), "feat")
    column = P(("groups", "rows", "ent"), None)
    by_feat = P(("groups", "feat"))
    return jax.shard_map(
        body,
        mesh=mesh,
        in_specs=(by_both, by_feat, by_both, by_both, column, by_row, column, by_row, by_row, by_row),
        out_specs=(by_feat, by_both),
        check_vma=False,
    )
```

```python
import math

import jax
import jax.numpy as jnp
from jax import lax
from jax.experimental import pallas as pl
from jax.experimental.pallas import tpu as pltpu
from jax.sharding import PartitionSpec as P

F32 = jnp.float32
BF16 = jnp.bfloat16
HOME = ("rows", "ent")
EVERY = ("rows", "feat", "ent")
IDS = 16
PARAMS = pltpu.CompilerParams(vmem_limit_bytes=24 * 2**20)
SMEM = pl.BlockSpec(memory_space=pltpu.SMEM)
VMEM = pl.BlockSpec(memory_space=pltpu.VMEM)
HBM = pl.BlockSpec(memory_space=pltpu.HBM)


def lanes_dot(a, b):
    return lax.dot_general(a, b, (((1,), (1,)), ((), ())), preferred_element_type=F32)


def plain_dot(a, b):
    return lax.dot_general(a, b, (((1,), (0,)), ((), ())), preferred_element_type=F32)


def halves(x):
    high = x.astype(BF16)
    return high, (x - high.astype(F32)).astype(BF16)


def one_hot(row, count):
    return row == lax.broadcasted_iota(jnp.int32, (count, row.shape[1]), 0)


def ranks_of(owners, member, item):
    rows = member.shape[1]
    step = min(256, rows)
    blocks = rows // step
    hits = jnp.concatenate([one_hot(member, owners).astype(F32), one_hot(item, owners).astype(F32)], axis=0)
    stacked = jnp.concatenate([hits[:, b * step : (b + 1) * step] for b in range(blocks)], axis=0)
    upper = lax.broadcasted_iota(jnp.int32, (step, step), 0) <= lax.broadcasted_iota(
        jnp.int32, (step, step), 1
    )
    counts = plain_dot(stacked.astype(BF16), upper.astype(F32).astype(BF16))
    before = jnp.zeros((2 * owners, 1), F32)
    pieces = []
    for b in range(blocks):
        here = counts[2 * owners * b : 2 * owners * (b + 1)]
        taken = (here + before) * hits[:, b * step : (b + 1) * step]
        sides = [jnp.sum(x, axis=0, keepdims=True) for x in (taken[:owners], taken[owners:])]
        pieces.append(jnp.concatenate(sides, axis=0))
        before = before + here[:, step - 1 : step]
    return jnp.concatenate(pieces, axis=1).astype(jnp.int32) - 1


def pack_chunk(k, capacity, place, ids, feats, chunk):
    pick = one_hot(place - k * capacity, capacity).astype(F32).astype(BF16)
    chunk[:capacity] = plain_dot(pick, feats).astype(BF16)
    chunk[capacity:, :capacity] = lanes_dot(ids, pick).astype(BF16)


def far_kernel(owners, capacity, far, where, *refs):
    sources, ranks, place_out, ids_out = refs[:5], refs[5], refs[6], refs[7]
    chunks, copies, sems = refs[8 : 8 + len(far)], refs[8 + len(far) : 13 + len(far)], refs[13 + len(far)]
    moves = [pltpu.make_async_copy(sources[i], copies[i], sems.at[i]) for i in range(5)]
    for move in moves:
        move.start()
    for move in moves[:4]:
        move.wait()
    member, item, member_local, item_local = [copy[...] for copy in copies[:4]]
    rows = member.shape[1]
    mine, on_item = where[0], where[1] > 0
    rank = ranks_of(owners, member, item)
    ranks[...] = rank
    own = jnp.where(on_item, item, member)
    place = (own ^ mine) * capacity + jnp.where(on_item, rank[1:2], rank[0:1])
    place_out[...] = place
    local = jnp.where(on_item, item_local, member_local)
    high = local >> 8
    ids = jnp.concatenate([high, local - (high << 8), jnp.zeros((IDS - 2, rows), jnp.int32)], axis=0)
    ids = ids.astype(F32).astype(BF16)
    ids_out[...] = ids
    moves[4].wait()
    for chunk, k in zip(chunks, far):
        pack_chunk(k, capacity, place, ids, copies[4][...], chunk)


def near_kernel(capacity, near, place, ids, feats, *chunks):
    for chunk, k in zip(chunks, near):
        pack_chunk(k, capacity, place[...], ids[...], feats[...], chunk)


def chunk_ids(chunk, capacity):
    pair = chunk[capacity:, :capacity].astype(F32)
    return (pair[0:1] * 256.0 + pair[1:2]).astype(jnp.int32)


def scores_kernel(owners, capacity, where, margin, coefs, *refs):
    chunks, out = refs[:owners], refs[owners]
    entities = coefs.shape[0]
    mine = where[0]
    high, low = halves(coefs[...])
    scores = []
    for k in range(owners):
        feats = chunks[k][:capacity]
        every = lanes_dot(high, feats) + lanes_dot(low, feats)
        hits = one_hot(chunk_ids(chunks[k], capacity), entities)
        scores.append(jnp.sum(jnp.where(hits, every, 0.0), axis=0, keepdims=True))
    for k in range(owners):
        out[0, pl.ds(mine ^ k, 1), :] = scores[k]


def home_kernel(
    owners, capacity, n_feat, n_ent, where, member, item, ranks, clicks, valid, margin, scores, features, out
):
    mine, on_item = where[0], where[1] > 0
    total = margin[...]
    hits_of = [one_hot(owner[...], owners).astype(F32) for owner in (member, item)]
    spot_of = [one_hot(ranks[side : side + 1], capacity).astype(F32).astype(BF16) for side in (0, 1)]
    for side in (0, 1):
        table = None
        for f in range(side * n_feat // 2, (side + 1) * n_feat // 2):
            part = jnp.concatenate(
                [scores[(h // n_ent * n_feat + f) * n_ent + h % n_ent, pl.ds(mine, 1), :] for h in range(owners)],
                axis=0,
            )
            table = part if table is None else table + part
        found = plain_dot(jnp.concatenate(halves(table), axis=0), spot_of[side])
        total = total + jnp.sum((found[:owners] + found[owners:]) * hits_of[side], axis=0, keepdims=True)
    resid = valid[...].astype(F32) * (jax.nn.sigmoid(total) - clicks[...].astype(F32))
    hits = jnp.where(on_item, hits_of[1], hits_of[0])
    spot = jnp.where(on_item, spot_of[1], spot_of[0])
    sent = lanes_dot(jnp.concatenate(halves(hits * resid), axis=0), spot)
    out[0, :owners] = sent[:owners] + sent[owners:]
    low = jnp.broadcast_to(resid, (16, resid.shape[1])).astype(BF16)
    grad = plain_dot(low, features[...])[0:1]
    for j in range(grad.shape[1] // capacity):
        out[0, owners + j : owners + j + 1] = grad[:, j * capacity : (j + 1) * capacity]


def grads_kernel(owners, capacity, scale, where, coefs, weight, came, *refs):
    chunks, grad_global, grad_coefs = refs[:owners], refs[owners], refs[owners + 1]
    entities = coefs.shape[0]
    mine = where[0]
    resids = [came[mine ^ k, pl.ds(mine, 1), :] for k in range(owners)]
    summed = came[0, owners:]
    for h in range(1, owners):
        summed = summed + came[h, owners:]
    summed = summed * scale
    for j in range(summed.shape[0]):
        here = slice(j * capacity, (j + 1) * capacity)
        grad_global[:, here] = summed[j : j + 1] + 4.0 * weight[:, here]
    total = coefs[...]
    for k in range(owners):
        hits = one_hot(chunk_ids(chunks[k], capacity), entities)
        feats = chunks[k][:capacity]
        for part in halves(resids[k]):
            total = total + plain_dot(jnp.where(hits, part.astype(F32), 0.0).astype(BF16), feats)
    grad_coefs[...] = total


def xor_send(x, axes, size, k):
    return x if k == 0 else lax.ppermute(x, axes, [(i, i ^ k) for i in range(size)])


def call(kernel, out_shape, operands, in_specs, flops=0, scratch=()):
    moved = sum(x.size * x.dtype.itemsize for x in (*operands, *out_shape))
    return pl.pallas_call(
        kernel,
        out_shape=out_shape,
        in_specs=in_specs,
        out_specs=[VMEM] * len(out_shape),
        scratch_shapes=scratch,
        compiler_params=PARAMS,
        cost_estimate=pl.CostEstimate(flops=flops, bytes_accessed=moved, transcendentals=0),
    )(*operands)


def body(
    features,
    global_weight,
    entity_feats,
    coefs,
    member_owner,
    member_local,
    item_owner,
    item_local,
    clicks,
    valid,
):
    rows_here, width = entity_feats.shape
    columns = features.shape[1]
    n_feat, n_ent = lax.axis_size("feat"), lax.axis_size("ent")
    owners = lax.axis_size("rows") * n_ent
    capacity = 2 * rows_here // owners
    mine = lax.axis_index(HOME).astype(jnp.int32)
    on_item = (lax.axis_index("feat") >= n_feat // 2).astype(jnp.int32)
    where = jnp.stack([mine, on_item])
    member, item = member_owner.reshape(1, rows_here), item_owner.reshape(1, rows_here)

    def shape(*dims, dtype=F32):
        return jax.ShapeDtypeStruct(dims, dtype)

    def partial(kernel, *args):
        return lambda *refs: kernel(*args, *refs)

    row = pltpu.VMEM((1, rows_here), jnp.int32)
    far, near = list(reversed(range(owners // 2, owners))), list(reversed(range(owners // 2)))
    chunk = shape(capacity + IDS, width, dtype=BF16)
    flops = owners * capacity * rows_here * width
    chunks = [None] * owners
    ranks, place, ids, *packed = call(
        partial(far_kernel, owners, capacity, far),
        [shape(2, rows_here, dtype=jnp.int32), shape(1, rows_here, dtype=jnp.int32), shape(IDS, rows_here, dtype=BF16)]
        + [chunk] * len(far),
        (
            where,
            *(
                pltpu.with_memory_space_constraint(x, pltpu.HBM)
                for x in (
                    member,
                    item,
                    member_local.reshape(1, rows_here),
                    item_local.reshape(1, rows_here),
                    entity_feats,
                )
            ),
        ),
        [SMEM] + [HBM] * 5,
        flops=flops,
        scratch=[row, row, row, row, pltpu.VMEM((rows_here, width), BF16), pltpu.SemaphoreType.DMA((5,))],
    )
    for k, x in zip(far, packed):
        chunks[k] = xor_send(x, HOME, owners, k)
    packed = call(
        partial(near_kernel, capacity, near), [chunk] * len(near), (place, ids, entity_feats), [VMEM] * 3, flops=flops
    )
    for k, x in zip(near, packed):
        chunks[k] = xor_send(x, HOME, owners, k)

    global_part = jnp.dot(features, global_weight, preferred_element_type=F32)
    global_total = global_part
    for q in range(1, n_feat):
        global_total = global_total + xor_send(global_part, "feat", n_feat, q)
    global_total = global_total.reshape(1, rows_here)

    (scores,) = call(
        partial(scores_kernel, owners, capacity),
        [shape(1, owners, capacity)],
        (where, global_total, coefs, *chunks),
        [SMEM] + [VMEM] * (2 + owners),
        flops=4 * coefs.size * owners * capacity,
    )
    returned = lax.all_gather(scores, EVERY, axis=0, tiled=True)
    (sent,) = call(
        partial(home_kernel, owners, capacity, n_feat, n_ent),
        [shape(1, owners + columns // capacity, capacity)],
        (
            where,
            member,
            item,
            ranks,
            clicks.reshape(1, rows_here),
            valid.reshape(1, rows_here),
            global_total,
            returned,
            features,
        ),
        [SMEM] + [VMEM] * 8,
        flops=32 * features.size,
    )
    came = lax.all_gather(sent, HOME, axis=0, tiled=True)
    grad_global, grad_coefs = call(
        partial(grads_kernel, owners, capacity, 1.0 / math.sqrt(rows_here * owners)),
        [shape(1, columns), shape(*coefs.shape)],
        (where, coefs, global_weight.astype(F32).reshape(1, columns), came, *chunks),
        [SMEM] + [VMEM] * (3 + owners),
        flops=4 * coefs.size * owners * capacity,
    )
    return (grad_global.reshape(columns), grad_coefs)


def solution(mesh):
    by_row = P(("groups", "rows", "ent"))
    by_both = P(("groups", "rows", "ent"), "feat")
    column = P(("groups", "rows", "ent"), None)
    by_feat = P(("groups", "feat"))
    return jax.shard_map(
        body,
        mesh=mesh,
        in_specs=(by_both, by_feat, by_both, by_both, column, by_row, column, by_row, by_row, by_row),
        out_specs=(by_feat, by_both),
        check_vma=False,
    )
```

```python
import math

import jax
import jax.numpy as jnp
from jax import lax
from jax.experimental import pallas as pl
from jax.experimental.pallas import tpu as pltpu
from jax.sharding import PartitionSpec as P

F32 = jnp.float32
BF16 = jnp.bfloat16
HOME = ("rows", "ent")
EVERY = ("rows", "feat", "ent")
IDS = 16
PARAMS = pltpu.CompilerParams(vmem_limit_bytes=24 * 2**20)
SMEM = pl.BlockSpec(memory_space=pltpu.SMEM)
VMEM = pl.BlockSpec(memory_space=pltpu.VMEM)
HBM = pl.BlockSpec(memory_space=pltpu.HBM)


def lanes_dot(a, b):
    return lax.dot_general(a, b, (((1,), (1,)), ((), ())), preferred_element_type=F32)


def plain_dot(a, b):
    return lax.dot_general(a, b, (((1,), (0,)), ((), ())), preferred_element_type=F32)


def halves(x):
    high = x.astype(BF16)
    return high, (x - high.astype(F32)).astype(BF16)


def one_hot(row, count):
    return row == lax.broadcasted_iota(jnp.int32, (count, row.shape[1]), 0)


def ranks_of(owners, member, item):
    rows = member.shape[1]
    step = min(256, rows)
    blocks = rows // step
    hits = jnp.concatenate([one_hot(member, owners).astype(F32), one_hot(item, owners).astype(F32)], axis=0)
    stacked = jnp.concatenate([hits[:, b * step : (b + 1) * step] for b in range(blocks)], axis=0)
    upper = lax.broadcasted_iota(jnp.int32, (step, step), 0) <= lax.broadcasted_iota(
        jnp.int32, (step, step), 1
    )
    counts = plain_dot(stacked.astype(BF16), upper.astype(F32).astype(BF16))
    before = jnp.zeros((2 * owners, 1), F32)
    pieces = []
    for b in range(blocks):
        here = counts[2 * owners * b : 2 * owners * (b + 1)]
        taken = (here + before) * hits[:, b * step : (b + 1) * step]
        sides = [jnp.sum(x, axis=0, keepdims=True) for x in (taken[:owners], taken[owners:])]
        pieces.append(jnp.concatenate(sides, axis=0))
        before = before + here[:, step - 1 : step]
    return jnp.concatenate(pieces, axis=1).astype(jnp.int32) - 1


def pack_chunk(k, capacity, place, ids, feats, chunk):
    pick = one_hot(place - k * capacity, capacity).astype(F32).astype(BF16)
    chunk[:capacity] = plain_dot(pick, feats).astype(BF16)
    chunk[capacity:, :capacity] = lanes_dot(ids, pick).astype(BF16)


def dispatch_kernel(owners, capacity, order, where, *refs):
    sources, ranks = refs[:5], refs[5]
    chunks, copies, sems = refs[6 : 6 + owners], refs[6 + owners : 11 + owners], refs[11 + owners]
    moves = [pltpu.make_async_copy(sources[i], copies[i], sems.at[i]) for i in range(5)]
    for move in moves:
        move.start()
    for move in moves[:4]:
        move.wait()
    member, item, member_local, item_local = [copy[...] for copy in copies[:4]]
    rows = member.shape[1]
    mine, on_item = where[0], where[1] > 0
    rank = ranks_of(owners, member, item)
    ranks[...] = rank
    own = jnp.where(on_item, item, member)
    place = (own ^ mine) * capacity + jnp.where(on_item, rank[1:2], rank[0:1])
    local = jnp.where(on_item, item_local, member_local)
    high = local >> 8
    ids = jnp.concatenate([high, local - (high << 8), jnp.zeros((IDS - 2, rows), jnp.int32)], axis=0)
    ids = ids.astype(F32).astype(BF16)
    moves[4].wait()
    for chunk, k in zip(chunks, order):
        pack_chunk(k, capacity, place, ids, copies[4][...], chunk)


def margin_kernel(first, weight, features, margin):
    wide = jnp.broadcast_to(weight[...], (16, weight.shape[1])).astype(BF16)
    margin[...] = lanes_dot(wide, features[...])[0:1]


def chunk_ids(chunk, capacity):
    pair = chunk[capacity:, :capacity].astype(F32)
    return (pair[0:1] * 256.0 + pair[1:2]).astype(jnp.int32)


def scores_kernel(order, capacity, n_feat, n_ent, where, margin, coefs, *refs):
    chunks, out = refs[:-1], refs[-1]
    entities = coefs.shape[0]
    mine = where[0]
    high, low = halves(coefs[...])
    scores = []
    for chunk in chunks:
        feats = chunk[:capacity]
        every = lanes_dot(high, feats) + lanes_dot(low, feats)
        hits = one_hot(chunk_ids(chunk, capacity), entities)
        scores.append(jnp.sum(jnp.where(hits, every, 0.0), axis=0, keepdims=True))
    for k, score in zip(order, scores):
        home = mine ^ k
        for f in range(n_feat):
            out[(home // n_ent * n_feat + f) * n_ent + home % n_ent] = score


def home_kernel(
    owners, capacity, n_feat, n_ent, where, member, item, ranks, clicks, valid, margin, scores, features, out
):
    on_item = where[1] > 0
    total = margin[...]
    hits_of = [one_hot(owner[...], owners).astype(F32) for owner in (member, item)]
    spot_of = [one_hot(ranks[side : side + 1], capacity).astype(F32).astype(BF16) for side in (0, 1)]
    for side in (0, 1):
        table = None
        for f in range(side * n_feat // 2, (side + 1) * n_feat // 2):
            part = jnp.concatenate(
                [scores[(h // n_ent * n_feat + f) * n_ent + h % n_ent] for h in range(owners)], axis=0
            )
            table = part if table is None else table + part
        found = plain_dot(jnp.concatenate(halves(table), axis=0), spot_of[side])
        total = total + jnp.sum((found[:owners] + found[owners:]) * hits_of[side], axis=0, keepdims=True)
    resid = valid[...].astype(F32) * (jax.nn.sigmoid(total) - clicks[...].astype(F32))
    hits = jnp.where(on_item, hits_of[1], hits_of[0])
    spot = jnp.where(on_item, spot_of[1], spot_of[0])
    sent = lanes_dot(jnp.concatenate(halves(hits * resid), axis=0), spot)
    sent = sent[:owners] + sent[owners:]
    low = jnp.broadcast_to(resid, (16, resid.shape[1])).astype(BF16)
    grad = plain_dot(low, features[...])[0:1]
    for h in range(owners):
        out[h, :, :capacity] = sent[h : h + 1]
        out[h, :, capacity:] = grad


def grads_kernel(order, capacity, scale, where, coefs, weight, came, *refs):
    chunks, grad_global, grad_coefs = refs[:-2], refs[-2], refs[-1]
    entities = coefs.shape[0]
    mine = where[0]
    resids = [came[mine ^ k][:, :capacity] for k in order]
    summed = came[0][:, capacity:]
    for h in range(1, len(order)):
        summed = summed + came[h][:, capacity:]
    grad_global[...] = summed * scale + 4.0 * weight[...]
    total = coefs[...]
    for chunk, resid in zip(chunks, resids):
        hits = one_hot(chunk_ids(chunk, capacity), entities)
        feats = chunk[:capacity]
        for part in halves(resid):
            total = total + plain_dot(jnp.where(hits, part.astype(F32), 0.0).astype(BF16), feats)
    grad_coefs[...] = total


def xor_send(x, axes, size, k):
    return x if k == 0 else lax.ppermute(x, axes, [(i, i ^ k) for i in range(size)])


def call(kernel, out_shape, operands, in_specs, flops=0, scratch=(), hidden=False):
    moved = 0 if hidden else sum(x.size * x.dtype.itemsize for x in (*operands, *out_shape))
    return pl.pallas_call(
        kernel,
        out_shape=out_shape,
        in_specs=in_specs,
        out_specs=[VMEM] * len(out_shape),
        scratch_shapes=scratch,
        compiler_params=PARAMS,
        cost_estimate=pl.CostEstimate(flops=flops, bytes_accessed=moved, transcendentals=0),
    )(*operands)


def body(
    features,
    global_weight,
    entity_feats,
    coefs,
    member_owner,
    member_local,
    item_owner,
    item_local,
    clicks,
    valid,
):
    rows_here, width = entity_feats.shape
    columns = features.shape[1]
    n_feat, n_ent = lax.axis_size("feat"), lax.axis_size("ent")
    owners = lax.axis_size("rows") * n_ent
    capacity = 2 * rows_here // owners
    mine = lax.axis_index(HOME).astype(jnp.int32)
    on_item = (lax.axis_index("feat") >= n_feat // 2).astype(jnp.int32)
    where = jnp.stack([mine, on_item])
    member, item = member_owner.reshape(1, rows_here), item_owner.reshape(1, rows_here)

    def shape(*dims, dtype=F32):
        return jax.ShapeDtypeStruct(dims, dtype)

    def partial(kernel, *args):
        return lambda *refs: kernel(*args, *refs)

    row = pltpu.VMEM((1, rows_here), jnp.int32)
    half = owners // 2
    order = [*range(half, owners), *reversed(range(half))]
    chunk = shape(capacity + IDS, width, dtype=BF16)
    ranks, *chunks = call(
        partial(dispatch_kernel, owners, capacity, order),
        [shape(2, rows_here, dtype=jnp.int32)] + [chunk] * owners,
        (
            where,
            *(
                pltpu.with_memory_space_constraint(x, pltpu.HBM)
                for x in (
                    member,
                    item,
                    member_local.reshape(1, rows_here),
                    item_local.reshape(1, rows_here),
                    entity_feats,
                )
            ),
        ),
        [SMEM] + [HBM] * 5,
        flops=2 * owners * capacity * rows_here * width,
        scratch=[row, row, row, row, pltpu.VMEM((rows_here, width), BF16), pltpu.SemaphoreType.DMA((5,))],
    )
    chunks = [xor_send(x, HOME, owners, k) for k, x in zip(order, chunks)]
    weight = global_weight.astype(F32).reshape(1, columns)
    (global_part,) = call(
        margin_kernel, [shape(1, rows_here)], (chunks[0], weight, features), [VMEM] * 3, hidden=True
    )
    global_total = lax.psum(global_part, "feat")

    (scores,) = call(
        partial(scores_kernel, order, capacity, n_feat, n_ent),
        [shape(n_feat * owners, 1, capacity)],
        (where, global_total, coefs, *chunks),
        [SMEM] + [VMEM] * (2 + owners),
        flops=4 * coefs.size * owners * capacity,
    )
    returned = lax.all_to_all(scores, EVERY, split_axis=0, concat_axis=0, tiled=True)
    (sent,) = call(
        partial(home_kernel, owners, capacity, n_feat, n_ent),
        [shape(owners, 1, capacity + columns)],
        (
            where,
            member,
            item,
            ranks,
            clicks.reshape(1, rows_here),
            valid.reshape(1, rows_here),
            global_total,
            returned,
            features,
        ),
        [SMEM] + [VMEM] * 8,
        flops=32 * features.size,
    )
    came = lax.all_to_all(sent, HOME, split_axis=0, concat_axis=0, tiled=True)
    grad_global, grad_coefs = call(
        partial(grads_kernel, order, capacity, 1.0 / math.sqrt(rows_here * owners)),
        [shape(1, columns), shape(*coefs.shape)],
        (where, coefs, weight, came, *chunks),
        [SMEM] + [VMEM] * (3 + owners),
        flops=4 * coefs.size * owners * capacity,
    )
    return (grad_global.reshape(columns), grad_coefs)


def solution(mesh):
    by_row = P(("groups", "rows", "ent"))
    by_both = P(("groups", "rows", "ent"), "feat")
    column = P(("groups", "rows", "ent"), None)
    by_feat = P(("groups", "feat"))
    return jax.shard_map(
        body,
        mesh=mesh,
        in_specs=(by_both, by_feat, by_both, by_both, column, by_row, column, by_row, by_row, by_row),
        out_specs=(by_feat, by_both),
        check_vma=False,
    )
```

```python
import math

import jax
import jax.numpy as jnp
from jax import lax
from jax.experimental import pallas as pl
from jax.experimental.pallas import tpu as pltpu
from jax.sharding import PartitionSpec as P

F32 = jnp.float32
BF16 = jnp.bfloat16
HOME = ("rows", "ent")
EVERY = ("rows", "feat", "ent")
IDS = 16
PARAMS = pltpu.CompilerParams(vmem_limit_bytes=24 * 2**20)
SMEM = pl.BlockSpec(memory_space=pltpu.SMEM)
VMEM = pl.BlockSpec(memory_space=pltpu.VMEM)
HBM = pl.BlockSpec(memory_space=pltpu.HBM)


def lanes_dot(a, b):
    return lax.dot_general(a, b, (((1,), (1,)), ((), ())), preferred_element_type=F32)


def plain_dot(a, b):
    return lax.dot_general(a, b, (((1,), (0,)), ((), ())), preferred_element_type=F32)


def halves(x):
    high = x.astype(BF16)
    return high, (x - high.astype(F32)).astype(BF16)


def one_hot(row, count):
    return row == lax.broadcasted_iota(jnp.int32, (count, row.shape[1]), 0)


def ranks_of(owners, member, item):
    rows = member.shape[1]
    step = min(256, rows)
    blocks = rows // step
    hits = jnp.concatenate([one_hot(member, owners).astype(F32), one_hot(item, owners).astype(F32)], axis=0)
    stacked = jnp.concatenate([hits[:, b * step : (b + 1) * step] for b in range(blocks)], axis=0)
    upper = lax.broadcasted_iota(jnp.int32, (step, step), 0) <= lax.broadcasted_iota(
        jnp.int32, (step, step), 1
    )
    counts = plain_dot(stacked.astype(BF16), upper.astype(F32).astype(BF16))
    before = jnp.zeros((2 * owners, 1), F32)
    pieces = []
    for b in range(blocks):
        here = counts[2 * owners * b : 2 * owners * (b + 1)]
        taken = (here + before) * hits[:, b * step : (b + 1) * step]
        sides = [jnp.sum(x, axis=0, keepdims=True) for x in (taken[:owners], taken[owners:])]
        pieces.append(jnp.concatenate(sides, axis=0))
        before = before + here[:, step - 1 : step]
    return jnp.concatenate(pieces, axis=1).astype(jnp.int32) - 1


def pack_chunk(k, capacity, place, ids, feats, chunk):
    pick = one_hot(place - k * capacity, capacity).astype(F32).astype(BF16)
    chunk[:capacity] = plain_dot(pick, feats).astype(BF16)
    chunk[capacity:, :capacity] = lanes_dot(ids, pick).astype(BF16)


def far_kernel(owners, capacity, far, where, *refs):
    sources, ranks, place_out, ids_out = refs[:5], refs[5], refs[6], refs[7]
    chunks, copies, sems = refs[8 : 8 + len(far)], refs[8 + len(far) : 13 + len(far)], refs[13 + len(far)]
    moves = [pltpu.make_async_copy(sources[i], copies[i], sems.at[i]) for i in range(5)]
    for move in moves:
        move.start()
    for move in moves[:4]:
        move.wait()
    member, item, member_local, item_local = [copy[...] for copy in copies[:4]]
    rows = member.shape[1]
    mine, on_item = where[0], where[1] > 0
    rank = ranks_of(owners, member, item)
    ranks[...] = rank
    own = jnp.where(on_item, item, member)
    place = (own ^ mine) * capacity + jnp.where(on_item, rank[1:2], rank[0:1])
    place_out[...] = place
    local = jnp.where(on_item, item_local, member_local)
    high = local >> 8
    ids = jnp.concatenate([high, local - (high << 8), jnp.zeros((IDS - 2, rows), jnp.int32)], axis=0)
    ids = ids.astype(F32).astype(BF16)
    ids_out[...] = ids
    moves[4].wait()
    for chunk, k in zip(chunks, far):
        pack_chunk(k, capacity, place, ids, copies[4][...], chunk)


def near_kernel(capacity, near, margin, place, ids, feats, *chunks):
    for chunk, k in zip(chunks, near):
        pack_chunk(k, capacity, place[...], ids[...], feats[...], chunk)


def margin_kernel(rank, weight, features, margin, copies, sems):
    parts = copies.shape[0]
    step = copies.shape[1]
    moves = [
        pltpu.make_async_copy(features.at[pl.ds(i * step, step)], copies.at[i], sems.at[i]) for i in range(parts)
    ]
    for move in moves:
        move.start()
    wide = jnp.broadcast_to(weight[...], (16, weight.shape[1])).astype(BF16)
    for i in range(parts):
        moves[i].wait()
        margin[:, i * step : (i + 1) * step] = lanes_dot(wide, copies[i])[0:1]


def chunk_ids(chunk, capacity):
    pair = chunk[capacity:, :capacity].astype(F32)
    return (pair[0:1] * 256.0 + pair[1:2]).astype(jnp.int32)


def scores_kernel(order, capacity, n_feat, n_ent, where, margin, coefs, *refs):
    chunks, out = refs[:-1], refs[-1]
    entities = coefs.shape[0]
    mine = where[0]
    high, low = halves(coefs[...])
    scores = []
    for chunk in chunks:
        feats = chunk[:capacity]
        every = lanes_dot(high, feats) + lanes_dot(low, feats)
        hits = one_hot(chunk_ids(chunk, capacity), entities)
        scores.append(jnp.sum(jnp.where(hits, every, 0.0), axis=0, keepdims=True))
    for k, score in zip(order, scores):
        home = mine ^ k
        for f in range(n_feat):
            out[(home // n_ent * n_feat + f) * n_ent + home % n_ent] = score


def home_kernel(
    owners, capacity, n_feat, n_ent, where, member, item, ranks, clicks, valid, margin, scores, features, out
):
    on_item = where[1] > 0
    total = margin[...]
    hits_of = [one_hot(owner[...], owners).astype(F32) for owner in (member, item)]
    spot_of = [one_hot(ranks[side : side + 1], capacity).astype(F32).astype(BF16) for side in (0, 1)]
    for side in (0, 1):
        table = None
        for f in range(side * n_feat // 2, (side + 1) * n_feat // 2):
            part = jnp.concatenate(
                [scores[(h // n_ent * n_feat + f) * n_ent + h % n_ent] for h in range(owners)], axis=0
            )
            table = part if table is None else table + part
        found = plain_dot(jnp.concatenate(halves(table), axis=0), spot_of[side])
        total = total + jnp.sum((found[:owners] + found[owners:]) * hits_of[side], axis=0, keepdims=True)
    resid = valid[...].astype(F32) * (jax.nn.sigmoid(total) - clicks[...].astype(F32))
    hits = jnp.where(on_item, hits_of[1], hits_of[0])
    spot = jnp.where(on_item, spot_of[1], spot_of[0])
    sent = lanes_dot(jnp.concatenate(halves(hits * resid), axis=0), spot)
    sent = sent[:owners] + sent[owners:]
    low = jnp.broadcast_to(resid, (16, resid.shape[1])).astype(BF16)
    grad = plain_dot(low, features[...])[0:1]
    for h in range(owners):
        out[h, :, :capacity] = sent[h : h + 1]
        out[h, :, capacity:] = grad


def grads_kernel(order, capacity, scale, where, coefs, weight, came, *refs):
    chunks, grad_global, grad_coefs = refs[:-2], refs[-2], refs[-1]
    entities = coefs.shape[0]
    mine = where[0]
    resids = [came[mine ^ k][:, :capacity] for k in order]
    summed = came[0][:, capacity:]
    for h in range(1, len(order)):
        summed = summed + came[h][:, capacity:]
    grad_global[...] = summed * scale + 4.0 * weight[...]
    total = coefs[...]
    for chunk, resid in zip(chunks, resids):
        hits = one_hot(chunk_ids(chunk, capacity), entities)
        feats = chunk[:capacity]
        for part in halves(resid):
            total = total + plain_dot(jnp.where(hits, part.astype(F32), 0.0).astype(BF16), feats)
    grad_coefs[...] = total


def xor_send(x, axes, size, k):
    return x if k == 0 else lax.ppermute(x, axes, [(i, i ^ k) for i in range(size)])


def call(kernel, out_shape, operands, in_specs, flops=0, scratch=(), hidden=False):
    moved = 0 if hidden else sum(x.size * x.dtype.itemsize for x in (*operands, *out_shape))
    return pl.pallas_call(
        kernel,
        out_shape=out_shape,
        in_specs=in_specs,
        out_specs=[VMEM] * len(out_shape),
        scratch_shapes=scratch,
        compiler_params=PARAMS,
        cost_estimate=pl.CostEstimate(flops=flops, bytes_accessed=moved, transcendentals=0),
    )(*operands)


def body(
    features,
    global_weight,
    entity_feats,
    coefs,
    member_owner,
    member_local,
    item_owner,
    item_local,
    clicks,
    valid,
):
    rows_here, width = entity_feats.shape
    columns = features.shape[1]
    n_feat, n_ent = lax.axis_size("feat"), lax.axis_size("ent")
    owners = lax.axis_size("rows") * n_ent
    capacity = 2 * rows_here // owners
    mine = lax.axis_index(HOME).astype(jnp.int32)
    on_item = (lax.axis_index("feat") >= n_feat // 2).astype(jnp.int32)
    where = jnp.stack([mine, on_item])
    member, item = member_owner.reshape(1, rows_here), item_owner.reshape(1, rows_here)

    def shape(*dims, dtype=F32):
        return jax.ShapeDtypeStruct(dims, dtype)

    def partial(kernel, *args):
        return lambda *refs: kernel(*args, *refs)

    row = pltpu.VMEM((1, rows_here), jnp.int32)
    half = owners // 2
    far, near = list(range(half, owners)), list(reversed(range(half)))
    chunk = shape(capacity + IDS, width, dtype=BF16)
    flops = owners * capacity * rows_here * width

    def in_hbm(x):
        return pltpu.with_memory_space_constraint(x, pltpu.HBM)

    ranks, place, ids, *far_chunks = call(
        partial(far_kernel, owners, capacity, far),
        [shape(2, rows_here, dtype=jnp.int32), shape(1, rows_here, dtype=jnp.int32), shape(IDS, rows_here, dtype=BF16)]
        + [chunk] * len(far),
        (
            where,
            in_hbm(member),
            in_hbm(item),
            in_hbm(member_local.reshape(1, rows_here)),
            in_hbm(item_local.reshape(1, rows_here)),
            in_hbm(entity_feats),
        ),
        [SMEM] + [HBM] * 5,
        flops=flops,
        scratch=[row, row, row, row, pltpu.VMEM((rows_here, width), BF16), pltpu.SemaphoreType.DMA((5,))],
    )
    order = far + near
    chunks = [xor_send(x, HOME, owners, k) for k, x in zip(far, far_chunks)]
    weight = global_weight.astype(F32).reshape(1, columns)
    parts = 4
    (global_part,) = call(
        margin_kernel,
        [shape(1, rows_here)],
        (place, weight, in_hbm(features)),
        [VMEM, VMEM, HBM],
        hidden=True,
        scratch=[pltpu.VMEM((parts, rows_here // parts, columns), BF16), pltpu.SemaphoreType.DMA((parts,))],
    )
    global_total = lax.psum(global_part, "feat")
    near_chunks = call(
        partial(near_kernel, capacity, near),
        [chunk] * len(near),
        (global_total, place, ids, entity_feats),
        [VMEM] * 4,
        hidden=True,
    )
    chunks += [xor_send(x, HOME, owners, k) for k, x in zip(near, near_chunks)]

    (scores,) = call(
        partial(scores_kernel, order, capacity, n_feat, n_ent),
        [shape(n_feat * owners, 1, capacity)],
        (where, global_total, coefs, *chunks),
        [SMEM] + [VMEM] * (2 + owners),
        flops=4 * coefs.size * owners * capacity,
    )
    returned = lax.all_to_all(scores, EVERY, split_axis=0, concat_axis=0, tiled=True)
    (sent,) = call(
        partial(home_kernel, owners, capacity, n_feat, n_ent),
        [shape(owners, 1, capacity + columns)],
        (
            where,
            member,
            item,
            ranks,
            clicks.reshape(1, rows_here),
            valid.reshape(1, rows_here),
            global_total,
            returned,
            features,
        ),
        [SMEM] + [VMEM] * 8,
        flops=32 * features.size,
    )
    came = lax.all_to_all(sent, HOME, split_axis=0, concat_axis=0, tiled=True)
    grad_global, grad_coefs = call(
        partial(grads_kernel, order, capacity, 1.0 / math.sqrt(rows_here * owners)),
        [shape(1, columns), shape(*coefs.shape)],
        (where, coefs, weight, came, *chunks),
        [SMEM] + [VMEM] * (3 + owners),
        flops=4 * coefs.size * owners * capacity,
    )
    return (grad_global.reshape(columns), grad_coefs)


def solution(mesh):
    by_row = P(("groups", "rows", "ent"))
    by_both = P(("groups", "rows", "ent"), "feat")
    column = P(("groups", "rows", "ent"), None)
    by_feat = P(("groups", "feat"))
    return jax.shard_map(
        body,
        mesh=mesh,
        in_specs=(by_both, by_feat, by_both, by_both, column, by_row, column, by_row, by_row, by_row),
        out_specs=(by_feat, by_both),
        check_vma=False,
    )
```

```python
import math

import jax
import jax.numpy as jnp
from jax import lax
from jax.experimental import pallas as pl
from jax.experimental.pallas import tpu as pltpu
from jax.sharding import PartitionSpec as P

F32 = jnp.float32
BF16 = jnp.bfloat16
HOME = ("rows", "ent")
IDS = 16
PARAMS = pltpu.CompilerParams(vmem_limit_bytes=24 * 2**20)
SMEM = pl.BlockSpec(memory_space=pltpu.SMEM)
VMEM = pl.BlockSpec(memory_space=pltpu.VMEM)
HBM = pl.BlockSpec(memory_space=pltpu.HBM)


def lanes_dot(a, b):
    return lax.dot_general(a, b, (((1,), (1,)), ((), ())), preferred_element_type=F32)


def plain_dot(a, b):
    return lax.dot_general(a, b, (((1,), (0,)), ((), ())), preferred_element_type=F32)


def halves(x):
    high = x.astype(BF16)
    return high, (x - high.astype(F32)).astype(BF16)


def one_hot(row, count):
    return row == lax.broadcasted_iota(jnp.int32, (count, row.shape[1]), 0)


def ranks_of(owners, member, item):
    rows = member.shape[1]
    step = min(256, rows)
    blocks = rows // step
    hits = jnp.concatenate([one_hot(member, owners).astype(F32), one_hot(item, owners).astype(F32)], axis=0)
    stacked = jnp.concatenate([hits[:, b * step : (b + 1) * step] for b in range(blocks)], axis=0)
    upper = lax.broadcasted_iota(jnp.int32, (step, step), 0) <= lax.broadcasted_iota(
        jnp.int32, (step, step), 1
    )
    counts = plain_dot(stacked.astype(BF16), upper.astype(F32).astype(BF16))
    before = jnp.zeros((2 * owners, 1), F32)
    pieces = []
    for b in range(blocks):
        here = counts[2 * owners * b : 2 * owners * (b + 1)]
        taken = (here + before) * hits[:, b * step : (b + 1) * step]
        sides = [jnp.sum(x, axis=0, keepdims=True) for x in (taken[:owners], taken[owners:])]
        pieces.append(jnp.concatenate(sides, axis=0))
        before = before + here[:, step - 1 : step]
    return jnp.concatenate(pieces, axis=1).astype(jnp.int32) - 1


def pack_chunk(k, capacity, place, ids, feats, chunk):
    pick = one_hot(place - k * capacity, capacity).astype(F32).astype(BF16)
    chunk[:capacity] = plain_dot(pick, feats).astype(BF16)
    chunk[capacity:, :capacity] = lanes_dot(ids, pick).astype(BF16)


def far_kernel(owners, capacity, far, where, *refs):
    sources, ranks, place_out, ids_out = refs[:5], refs[5], refs[6], refs[7]
    chunks, copies, sems = refs[8 : 8 + len(far)], refs[8 + len(far) : 13 + len(far)], refs[13 + len(far)]
    moves = [pltpu.make_async_copy(sources[i], copies[i], sems.at[i]) for i in range(5)]
    for move in moves:
        move.start()
    for move in moves[:4]:
        move.wait()
    member, item, member_local, item_local = [copy[...] for copy in copies[:4]]
    rows = member.shape[1]
    mine, on_item = where[0], where[1] > 0
    rank = ranks_of(owners, member, item)
    ranks[...] = rank
    own = jnp.where(on_item, item, member)
    place = (own ^ mine) * capacity + jnp.where(on_item, rank[1:2], rank[0:1])
    place_out[...] = place
    local = jnp.where(on_item, item_local, member_local)
    high = local >> 8
    ids = jnp.concatenate([high, local - (high << 8), jnp.zeros((IDS - 2, rows), jnp.int32)], axis=0)
    ids = ids.astype(F32).astype(BF16)
    ids_out[...] = ids
    moves[4].wait()
    for chunk, k in zip(chunks, far):
        pack_chunk(k, capacity, place, ids, copies[4][...], chunk)


def rest_kernel(capacity, rest, place, ids, feats, *chunks):
    for chunk, k in zip(chunks, rest):
        pack_chunk(k, capacity, place[...], ids[...], feats[...], chunk)


def margin_kernel(rank, weight, features, margin, copies, sems):
    parts = copies.shape[0]
    step = copies.shape[1]
    moves = [
        pltpu.make_async_copy(features.at[pl.ds(i * step, step)], copies.at[i], sems.at[i]) for i in range(parts)
    ]
    for move in moves:
        move.start()
    wide = jnp.broadcast_to(weight[...], (16, weight.shape[1])).astype(BF16)
    for i in range(parts):
        moves[i].wait()
        margin[:, i * step : (i + 1) * step] = lanes_dot(wide, copies[i])[0:1]


def chunk_ids(chunk, capacity):
    pair = chunk[capacity:, :capacity].astype(F32)
    return (pair[0:1] * 256.0 + pair[1:2]).astype(jnp.int32)


def scores_kernel(capacity, count, coefs, *refs):
    chunks, outs = refs[:count], refs[-count:]
    entities = coefs.shape[0]
    high, low = halves(coefs[...])
    for chunk, out in zip(chunks, outs):
        feats = chunk[:capacity]
        every = lanes_dot(high, feats) + lanes_dot(low, feats)
        hits = one_hot(chunk_ids(chunk, capacity), entities)
        out[...] = jnp.sum(jnp.where(hits, every, 0.0), axis=0, keepdims=True)


def margin_rows(owners, capacity, where, member, item, ranks):
    mine, on_item = where[0], where[1] > 0
    own = jnp.where(on_item, item[...], member[...])
    rank = jnp.where(on_item, ranks[1:2], ranks[0:1])
    return one_hot(own ^ mine, owners).astype(F32), one_hot(rank, capacity).astype(F32).astype(BF16)


def gather_kernel(owners, capacity, where, member, item, ranks, margin, *refs):
    scores, out = refs[:-1], refs[-1]
    hits, spot = margin_rows(owners, capacity, where, member, item, ranks)
    table = jnp.concatenate([score[...] for score in scores], axis=0)
    found = plain_dot(jnp.concatenate(halves(table), axis=0), spot)
    out[...] = margin[...] + jnp.sum((found[:owners] + found[owners:]) * hits, axis=0, keepdims=True)


def home_kernel(owners, capacity, where, member, item, ranks, clicks, valid, features, *refs):
    margins, out = refs[:-1], refs[-1]
    mine = where[0]
    total = margins[0][...]
    for margin in margins[1:]:
        total = total + margin[...]
    resid = valid[...].astype(F32) * (jax.nn.sigmoid(total) - clicks[...].astype(F32))
    hits, spot = margin_rows(owners, capacity, where, member, item, ranks)
    sent = lanes_dot(jnp.concatenate(halves(hits * resid), axis=0), spot)
    sent = sent[:owners] + sent[owners:]
    low = jnp.broadcast_to(resid, (16, resid.shape[1])).astype(BF16)
    grad = plain_dot(low, features[...])[0:1]
    for k in range(owners):
        out[mine ^ k, :, :capacity] = sent[k : k + 1]
        out[mine ^ k, :, capacity:] = grad


def grads_kernel(order, capacity, scale, where, coefs, weight, came, *refs):
    chunks, grad_global, grad_coefs = refs[:-2], refs[-2], refs[-1]
    entities = coefs.shape[0]
    mine = where[0]
    resids = [came[mine ^ k][:, :capacity] for k in order]
    summed = came[0][:, capacity:]
    for h in range(1, len(order)):
        summed = summed + came[h][:, capacity:]
    grad_global[...] = summed * scale + 4.0 * weight[...]
    total = coefs[...]
    for chunk, resid in zip(chunks, resids):
        hits = one_hot(chunk_ids(chunk, capacity), entities)
        feats = chunk[:capacity]
        for part in halves(resid):
            total = total + plain_dot(jnp.where(hits, part.astype(F32), 0.0).astype(BF16), feats)
    grad_coefs[...] = total


def xor_send(x, axes, size, k):
    return x if k == 0 else lax.ppermute(x, axes, [(i, i ^ k) for i in range(size)])


def call(kernel, out_shape, operands, in_specs, flops=0, scratch=(), hidden=False):
    moved = 0 if hidden else sum(x.size * x.dtype.itemsize for x in (*operands, *out_shape))
    return pl.pallas_call(
        kernel,
        out_shape=out_shape,
        in_specs=in_specs,
        out_specs=[VMEM] * len(out_shape),
        scratch_shapes=scratch,
        compiler_params=PARAMS,
        cost_estimate=pl.CostEstimate(flops=flops, bytes_accessed=moved, transcendentals=0),
    )(*operands)


def body(
    features,
    global_weight,
    entity_feats,
    coefs,
    member_owner,
    member_local,
    item_owner,
    item_local,
    clicks,
    valid,
):
    rows_here, width = entity_feats.shape
    columns = features.shape[1]
    n_feat, n_ent = lax.axis_size("feat"), lax.axis_size("ent")
    owners = lax.axis_size("rows") * n_ent
    capacity = 2 * rows_here // owners
    mine = lax.axis_index(HOME).astype(jnp.int32)
    feat = lax.axis_index("feat")
    where = jnp.stack([mine, (feat >= n_feat // 2).astype(jnp.int32)])
    member, item = member_owner.reshape(1, rows_here), item_owner.reshape(1, rows_here)

    def shape(*dims, dtype=F32):
        return jax.ShapeDtypeStruct(dims, dtype)

    def partial(kernel, *args):
        return lambda *refs: kernel(*args, *refs)

    row = pltpu.VMEM((1, rows_here), jnp.int32)
    half, early = owners // 2, 3 * owners // 4
    near, far = [*range(1, half), 0], list(range(half, owners))
    if half > 3:
        near = [*range(2, half), 1, 0]
    first = [*near[:-2], *range(half, early)]
    rest = [*near[-2:], *range(early, owners)]
    chunk = shape(capacity + IDS, width, dtype=BF16)

    def in_hbm(x):
        return pltpu.with_memory_space_constraint(x, pltpu.HBM)

    ranks, place, ids, *chunks = call(
        partial(far_kernel, owners, capacity, first),
        [shape(2, rows_here, dtype=jnp.int32), shape(1, rows_here, dtype=jnp.int32), shape(IDS, rows_here, dtype=BF16)]
        + [chunk] * len(first),
        (
            where,
            in_hbm(member),
            in_hbm(item),
            in_hbm(member_local.reshape(1, rows_here)),
            in_hbm(item_local.reshape(1, rows_here)),
            in_hbm(entity_feats),
        ),
        [SMEM] + [HBM] * 5,
        hidden=True,
        scratch=[row, row, row, row, pltpu.VMEM((rows_here, width), BF16), pltpu.SemaphoreType.DMA((5,))],
    )
    chunks += call(
        partial(rest_kernel, capacity, rest),
        [chunk] * len(rest),
        (place, ids, entity_feats),
        [VMEM] * 3,
        flops=owners * capacity * rows_here * width,
    )
    order = first + rest
    chunks = {k: xor_send(x, HOME, owners, k) for k, x in zip(order, chunks)}
    weight = global_weight.astype(F32).reshape(1, columns)
    parts = 16
    (global_part,) = call(
        margin_kernel,
        [shape(1, rows_here)],
        (place, weight, in_hbm(features)),
        [VMEM, VMEM, HBM],
        hidden=True,
        scratch=[pltpu.VMEM((parts, rows_here // parts, columns), BF16), pltpu.SemaphoreType.DMA((parts,))],
    )
    returned = [None] * owners
    before = [global_part]
    for group in [near, list(range(half, early)), *([k] for k in range(early, owners))]:
        scores = call(
            partial(scores_kernel, capacity, len(group)),
            [shape(1, capacity)] * len(group),
            (coefs, *(chunks[k] for k in group), *before),
            [VMEM] * (1 + len(group) + len(before)),
            hidden=True,
        )
        for k, score in zip(group, scores):
            returned[k] = xor_send(score, HOME, owners, k)
        if len(group) > 1:
            before = [returned[k] for k in group]
    (margin,) = call(
        partial(gather_kernel, owners, capacity),
        [shape(1, rows_here)],
        (where, member, item, ranks, global_part, *returned),
        [SMEM] + [VMEM] * (4 + owners),
        hidden=True,
    )
    margins = [xor_send(margin, "feat", n_feat, q) for q in range(n_feat)]
    (sent,) = call(
        partial(home_kernel, owners, capacity),
        [shape(owners, 1, capacity + columns)],
        (
            where,
            member,
            item,
            ranks,
            clicks.reshape(1, rows_here),
            valid.reshape(1, rows_here),
            features,
            *margins,
        ),
        [SMEM] + [VMEM] * (6 + n_feat),
        flops=32 * features.size,
    )
    came = lax.all_to_all(sent, HOME, split_axis=0, concat_axis=0, tiled=True)
    grad_global, grad_coefs = call(
        partial(grads_kernel, order, capacity, 1.0 / math.sqrt(rows_here * owners)),
        [shape(1, columns), shape(*coefs.shape)],
        (where, coefs, weight, came, *(chunks[k] for k in order)),
        [SMEM] + [VMEM] * (3 + owners),
        flops=4 * coefs.size * owners * capacity,
    )
    return (grad_global.reshape(columns), grad_coefs)


def solution(mesh):
    by_row = P(("groups", "rows", "ent"))
    by_both = P(("groups", "rows", "ent"), "feat")
    column = P(("groups", "rows", "ent"), None)
    by_feat = P(("groups", "feat"))
    return jax.shard_map(
        body,
        mesh=mesh,
        in_specs=(by_both, by_feat, by_both, by_both, column, by_row, column, by_row, by_row, by_row),
        out_specs=(by_feat, by_both),
        check_vma=False,
    )
```

```python
import math

import jax
import jax.numpy as jnp
from jax import lax
from jax.experimental import pallas as pl
from jax.experimental.pallas import tpu as pltpu
from jax.sharding import PartitionSpec as P

F32 = jnp.float32
BF16 = jnp.bfloat16
HOME = ("rows", "ent")
EVERY = ("rows", "feat", "ent")
IDS = 16
PARAMS = pltpu.CompilerParams(vmem_limit_bytes=24 * 2**20)
SMEM = pl.BlockSpec(memory_space=pltpu.SMEM)
VMEM = pl.BlockSpec(memory_space=pltpu.VMEM)
HBM = pl.BlockSpec(memory_space=pltpu.HBM)


def lanes_dot(a, b):
    return lax.dot_general(a, b, (((1,), (1,)), ((), ())), preferred_element_type=F32)


def plain_dot(a, b):
    return lax.dot_general(a, b, (((1,), (0,)), ((), ())), preferred_element_type=F32)


def halves(x):
    high = x.astype(BF16)
    return high, (x - high.astype(F32)).astype(BF16)


def one_hot(row, count):
    return row == lax.broadcasted_iota(jnp.int32, (count, row.shape[1]), 0)


def ranks_of(owners, member, item):
    rows = member.shape[1]
    step = min(256, rows)
    blocks = rows // step
    hits = jnp.concatenate([one_hot(member, owners).astype(F32), one_hot(item, owners).astype(F32)], axis=0)
    stacked = jnp.concatenate([hits[:, b * step : (b + 1) * step] for b in range(blocks)], axis=0)
    upper = lax.broadcasted_iota(jnp.int32, (step, step), 0) <= lax.broadcasted_iota(
        jnp.int32, (step, step), 1
    )
    counts = plain_dot(stacked.astype(BF16), upper.astype(F32).astype(BF16))
    before = jnp.zeros((2 * owners, 1), F32)
    pieces = []
    for b in range(blocks):
        here = counts[2 * owners * b : 2 * owners * (b + 1)]
        taken = (here + before) * hits[:, b * step : (b + 1) * step]
        sides = [jnp.sum(x, axis=0, keepdims=True) for x in (taken[:owners], taken[owners:])]
        pieces.append(jnp.concatenate(sides, axis=0))
        before = before + here[:, step - 1 : step]
    return jnp.concatenate(pieces, axis=1).astype(jnp.int32) - 1


def pack_chunk(k, capacity, place, ids, feats, chunk):
    pick = one_hot(place - k * capacity, capacity).astype(F32).astype(BF16)
    chunk[:capacity] = plain_dot(pick, feats).astype(BF16)
    chunk[capacity:, :capacity] = lanes_dot(ids, pick).astype(BF16)


def far_kernel(owners, capacity, far, where, *refs):
    sources, ranks, place_out, ids_out, feats = refs[:5], refs[5], refs[6], refs[7], refs[8]
    chunks, copies, sems = refs[9 : 9 + len(far)], refs[9 + len(far) : 13 + len(far)], refs[13 + len(far)]
    copies = (*copies, feats)
    moves = [pltpu.make_async_copy(sources[i], copies[i], sems.at[i]) for i in range(5)]
    for move in moves:
        move.start()
    for move in moves[:4]:
        move.wait()
    member, item, member_local, item_local = [copy[...] for copy in copies[:4]]
    rows = member.shape[1]
    mine, on_item = where[0], where[1] > 0
    rank = ranks_of(owners, member, item)
    ranks[...] = rank
    own = jnp.where(on_item, item, member)
    place = (own ^ mine) * capacity + jnp.where(on_item, rank[1:2], rank[0:1])
    place_out[...] = place
    local = jnp.where(on_item, item_local, member_local)
    high = local >> 8
    ids = jnp.concatenate([high, local - (high << 8), jnp.zeros((IDS - 2, rows), jnp.int32)], axis=0)
    ids = ids.astype(F32).astype(BF16)
    ids_out[...] = ids
    moves[4].wait()
    for chunk, k in zip(chunks, far):
        pack_chunk(k, capacity, place, ids, feats[...], chunk)


def rest_kernel(capacity, rest, place, ids, feats, *refs):
    chunks = refs[-len(rest) :]
    for chunk, k in zip(chunks, rest):
        pack_chunk(k, capacity, place[...], ids[...], feats[...], chunk)


def margin_kernel(place, weight, features, margin, copies, sems):
    parts = copies.shape[0]
    step = copies.shape[1]
    moves = [
        pltpu.make_async_copy(features.at[pl.ds(i * step, step)], copies.at[i], sems.at[i]) for i in range(parts)
    ]
    for move in moves:
        move.start()
    wide = jnp.broadcast_to(weight[...], (16, weight.shape[1])).astype(BF16)
    for i in range(parts):
        moves[i].wait()
        margin[:, i * step : (i + 1) * step] = lanes_dot(wide, copies[i])[0:1]


def chunk_ids(chunk, capacity):
    pair = chunk[capacity:, :capacity].astype(F32)
    return (pair[0:1] * 256.0 + pair[1:2]).astype(jnp.int32)


def chunk_scores(chunk, table, capacity):
    feats = chunk[:capacity]
    every = lanes_dot(table, jnp.concatenate([feats, feats], axis=1))
    hits = one_hot(chunk_ids(chunk, capacity), table.shape[0])
    return jnp.sum(jnp.where(hits, every, 0.0), axis=0, keepdims=True)


def early_kernel(capacity, coefs, *refs):
    half = len(refs) // 2
    table = jnp.concatenate(halves(coefs[...]), axis=1)
    for chunk, out in zip(refs[:half], refs[half:]):
        out[...] = chunk_scores(chunk, table, capacity)


def scores_kernel(order, capacity, n_feat, n_ent, where, coefs, *refs):
    out, mine = refs[-1], where[0]
    table = jnp.concatenate(halves(coefs[...]), axis=1)
    scores = [
        x[...] if x.shape[0] == 1 else chunk_scores(x, table, capacity) for x in refs[:-1]
    ]
    for k, score in zip(order, scores):
        home = mine ^ k
        for f in range(n_feat):
            out[(home // n_ent * n_feat + f) * n_ent + home % n_ent] = score


def home_kernel(
    owners, capacity, n_feat, n_ent, where, member, item, ranks, clicks, valid, margin, scores, features, out
):
    on_item = where[1] > 0
    total = margin[...]
    hits_of = [one_hot(owner[...], owners).astype(F32) for owner in (member, item)]
    spot_of = [one_hot(ranks[side : side + 1], capacity).astype(F32).astype(BF16) for side in (0, 1)]
    for side in (0, 1):
        table = None
        for f in range(side * n_feat // 2, (side + 1) * n_feat // 2):
            part = jnp.concatenate(
                [scores[(h // n_ent * n_feat + f) * n_ent + h % n_ent] for h in range(owners)], axis=0
            )
            table = part if table is None else table + part
        found = plain_dot(jnp.concatenate(halves(table), axis=0), spot_of[side])
        total = total + jnp.sum((found[:owners] + found[owners:]) * hits_of[side], axis=0, keepdims=True)
    resid = valid[...].astype(F32) * (jax.nn.sigmoid(total) - clicks[...].astype(F32))
    hits = jnp.where(on_item, hits_of[1], hits_of[0])
    spot = jnp.where(on_item, spot_of[1], spot_of[0])
    sent = lanes_dot(jnp.concatenate(halves(hits * resid), axis=0), spot)
    sent = sent[:owners] + sent[owners:]
    low = jnp.broadcast_to(resid, (16, resid.shape[1])).astype(BF16)
    grad = plain_dot(low, features[...])[0:1]
    for h in range(owners):
        out[h, :, :capacity] = sent[h : h + 1]
        out[h, :, capacity:] = grad


def grads_kernel(order, capacity, scale, where, coefs, weight, came, *refs):
    chunks, grad_global, grad_coefs = refs[:-2], refs[-2], refs[-1]
    entities = coefs.shape[0]
    mine = where[0]
    resids = [came[mine ^ k][:, :capacity] for k in order]
    summed = came[0][:, capacity:]
    for h in range(1, len(order)):
        summed = summed + came[h][:, capacity:]
    grad_global[...] = summed * scale + 4.0 * weight[...]
    highs, lows, feats = [], [], []
    for chunk, resid in zip(chunks, resids):
        hits = one_hot(chunk_ids(chunk, capacity), entities)
        high, low = halves(resid)
        highs.append(jnp.where(hits, high.astype(F32), 0.0).astype(BF16))
        lows.append(jnp.where(hits, low.astype(F32), 0.0).astype(BF16))
        feats.append(chunk[:capacity])
    spread = jnp.concatenate(highs + lows, axis=1)
    grad_coefs[...] = coefs[...] + plain_dot(spread, jnp.concatenate(feats + feats, axis=0))


def xor_send(x, axes, size, k):
    return x if k == 0 else lax.ppermute(x, axes, [(i, i ^ k) for i in range(size)])


def call(kernel, out_shape, operands, in_specs, flops=0, scratch=(), hidden=False):
    moved = 0 if hidden else sum(x.size * x.dtype.itemsize for x in (*operands, *out_shape))
    return pl.pallas_call(
        kernel,
        out_shape=out_shape,
        in_specs=in_specs,
        out_specs=[VMEM] * len(out_shape),
        scratch_shapes=scratch,
        compiler_params=PARAMS,
        cost_estimate=pl.CostEstimate(flops=flops, bytes_accessed=moved, transcendentals=0),
    )(*operands)


def body(
    features,
    global_weight,
    entity_feats,
    coefs,
    member_owner,
    member_local,
    item_owner,
    item_local,
    clicks,
    valid,
):
    rows_here, width = entity_feats.shape
    columns = features.shape[1]
    n_feat, n_ent = lax.axis_size("feat"), lax.axis_size("ent")
    owners = lax.axis_size("rows") * n_ent
    capacity = 2 * rows_here // owners
    mine = lax.axis_index(HOME).astype(jnp.int32)
    on_item = (lax.axis_index("feat") >= n_feat // 2).astype(jnp.int32)
    where = jnp.stack([mine, on_item])
    member, item = member_owner.reshape(1, rows_here), item_owner.reshape(1, rows_here)

    def shape(*dims, dtype=F32):
        return jax.ShapeDtypeStruct(dims, dtype)

    def partial(kernel, *args):
        return lambda *refs: kernel(*args, *refs)

    row = pltpu.VMEM((1, rows_here), jnp.int32)
    half, early = owners // 2, 3 * owners // 4
    first, second, near = list(range(half, early)), list(range(early, owners)), list(reversed(range(half)))
    chunk = shape(capacity + IDS, width, dtype=BF16)
    flops = len(first) * 2 * capacity * rows_here * width

    def in_hbm(x):
        return pltpu.with_memory_space_constraint(x, pltpu.HBM)

    ranks, place, ids, feats, *chunks = call(
        partial(far_kernel, owners, capacity, first),
        [
            shape(2, rows_here, dtype=jnp.int32),
            shape(1, rows_here, dtype=jnp.int32),
            shape(IDS, rows_here, dtype=BF16),
            shape(rows_here, width, dtype=BF16),
        ]
        + [chunk] * len(first),
        (
            where,
            in_hbm(member),
            in_hbm(item),
            in_hbm(member_local.reshape(1, rows_here)),
            in_hbm(item_local.reshape(1, rows_here)),
            in_hbm(entity_feats),
        ),
        [SMEM] + [HBM] * 5,
        flops=flops,
        scratch=[row, row, row, row, pltpu.SemaphoreType.DMA((5,))],
    )
    chunks += call(
        partial(rest_kernel, capacity, second),
        [chunk] * len(second),
        (place, ids, feats),
        [VMEM] * 3,
        flops=flops,
    )
    chunks = [xor_send(x, HOME, owners, k) for k, x in zip(first + second, chunks)]
    weight = global_weight.astype(F32).reshape(1, columns)
    parts = 8
    (global_part,) = call(
        margin_kernel,
        [shape(1, rows_here)],
        (place, weight, in_hbm(features)),
        [VMEM, VMEM, HBM],
        hidden=True,
        scratch=[pltpu.VMEM((parts, rows_here // parts, columns), BF16), pltpu.SemaphoreType.DMA((parts,))],
    )
    global_total = lax.psum(global_part, "feat")
    near_chunks = call(
        partial(rest_kernel, capacity, near),
        [chunk] * len(near),
        (place, ids, feats, global_total),
        [VMEM] * 4,
        hidden=True,
    )
    near_chunks = [xor_send(x, HOME, owners, k) for k, x in zip(near, near_chunks)]
    order = first + near[-1:] + second + near[:-1]
    chunks = chunks[: len(first)] + near_chunks[-1:] + chunks[len(first) :] + near_chunks[:-1]
    came_early = len(first) + 1
    scores = call(
        partial(early_kernel, capacity),
        [shape(1, capacity)] * came_early,
        (coefs, *chunks[:came_early]),
        [VMEM] * (1 + came_early),
        hidden=True,
    )
    (scores,) = call(
        partial(scores_kernel, order, capacity, n_feat, n_ent),
        [shape(n_feat * owners, 1, capacity)],
        (where, coefs, *scores, *chunks[came_early:]),
        [SMEM] + [VMEM] * (1 + owners),
        flops=2 * coefs.size * owners * capacity,
    )
    returned = lax.all_to_all(scores, EVERY, split_axis=0, concat_axis=0, tiled=True)
    (sent,) = call(
        partial(home_kernel, owners, capacity, n_feat, n_ent),
        [shape(owners, 1, capacity + columns)],
        (
            where,
            member,
            item,
            ranks,
            clicks.reshape(1, rows_here),
            valid.reshape(1, rows_here),
            global_total,
            returned,
            features,
        ),
        [SMEM] + [VMEM] * 8,
        flops=32 * features.size,
    )
    came = lax.all_to_all(sent, HOME, split_axis=0, concat_axis=0, tiled=True)
    grad_global, grad_coefs = call(
        partial(grads_kernel, order, capacity, 1.0 / math.sqrt(rows_here * owners)),
        [shape(1, columns), shape(*coefs.shape)],
        (where, coefs, weight, came, *chunks),
        [SMEM] + [VMEM] * (3 + owners),
        flops=4 * coefs.size * owners * capacity,
    )
    return (grad_global.reshape(columns), grad_coefs)


def solution(mesh):
    by_row = P(("groups", "rows", "ent"))
    by_both = P(("groups", "rows", "ent"), "feat")
    column = P(("groups", "rows", "ent"), None)
    by_feat = P(("groups", "feat"))
    return jax.shard_map(
        body,
        mesh=mesh,
        in_specs=(by_both, by_feat, by_both, by_both, column, by_row, column, by_row, by_row, by_row),
        out_specs=(by_feat, by_both),
        check_vma=False,
    )
```

```python
import math

import jax
import jax.numpy as jnp
from jax import lax
from jax.experimental import pallas as pl
from jax.experimental.pallas import tpu as pltpu
from jax.sharding import PartitionSpec as P

F32 = jnp.float32
BF16 = jnp.bfloat16
HOME = ("rows", "ent")
EVERY = ("rows", "feat", "ent")
IDS = 16
PARAMS = pltpu.CompilerParams(vmem_limit_bytes=24 * 2**20)
SMEM = pl.BlockSpec(memory_space=pltpu.SMEM)
VMEM = pl.BlockSpec(memory_space=pltpu.VMEM)
HBM = pl.BlockSpec(memory_space=pltpu.HBM)


def lanes_dot(a, b):
    return lax.dot_general(a, b, (((1,), (1,)), ((), ())), preferred_element_type=F32)


def plain_dot(a, b):
    return lax.dot_general(a, b, (((1,), (0,)), ((), ())), preferred_element_type=F32)


def halves(x):
    high = x.astype(BF16)
    return high, (x - high.astype(F32)).astype(BF16)


def one_hot(row, count):
    return row == lax.broadcasted_iota(jnp.int32, (count, row.shape[1]), 0)


def ranks_of(owners, member, item):
    rows = member.shape[1]
    step = min(256, rows)
    blocks = rows // step
    hits = jnp.concatenate([one_hot(member, owners).astype(F32), one_hot(item, owners).astype(F32)], axis=0)
    stacked = jnp.concatenate([hits[:, b * step : (b + 1) * step] for b in range(blocks)], axis=0)
    upper = lax.broadcasted_iota(jnp.int32, (step, step), 0) <= lax.broadcasted_iota(
        jnp.int32, (step, step), 1
    )
    counts = plain_dot(stacked.astype(BF16), upper.astype(F32).astype(BF16))
    before = jnp.zeros((2 * owners, 1), F32)
    pieces = []
    for b in range(blocks):
        here = counts[2 * owners * b : 2 * owners * (b + 1)]
        taken = (here + before) * hits[:, b * step : (b + 1) * step]
        sides = [jnp.sum(x, axis=0, keepdims=True) for x in (taken[:owners], taken[owners:])]
        pieces.append(jnp.concatenate(sides, axis=0))
        before = before + here[:, step - 1 : step]
    return jnp.concatenate(pieces, axis=1).astype(jnp.int32) - 1


def pack_chunk(k, capacity, place, ids, feats, chunk):
    pick = one_hot(place - k * capacity, capacity).astype(F32).astype(BF16)
    chunk[:capacity] = plain_dot(pick, feats).astype(BF16)
    chunk[capacity:, :capacity] = lanes_dot(ids, pick).astype(BF16)


def far_kernel(owners, capacity, far, where, *refs):
    sources, ranks, place_out, ids_out, feats = refs[:5], refs[5], refs[6], refs[7], refs[8]
    chunks, copies, sems = refs[9 : 9 + len(far)], refs[9 + len(far) : 13 + len(far)], refs[13 + len(far)]
    copies = (*copies, feats)
    moves = [pltpu.make_async_copy(sources[i], copies[i], sems.at[i]) for i in range(5)]
    for move in moves:
        move.start()
    for move in moves[:4]:
        move.wait()
    member, item, member_local, item_local = [copy[...] for copy in copies[:4]]
    rows = member.shape[1]
    mine, on_item = where[0], where[1] > 0
    rank = ranks_of(owners, member, item)
    ranks[...] = rank
    own = jnp.where(on_item, item, member)
    place = (own ^ mine) * capacity + jnp.where(on_item, rank[1:2], rank[0:1])
    place_out[...] = place
    local = jnp.where(on_item, item_local, member_local)
    high = local >> 8
    ids = jnp.concatenate([high, local - (high << 8), jnp.zeros((IDS - 2, rows), jnp.int32)], axis=0)
    ids = ids.astype(F32).astype(BF16)
    ids_out[...] = ids
    moves[4].wait()
    for chunk, k in zip(chunks, far):
        pack_chunk(k, capacity, place, ids, feats[...], chunk)


def rest_kernel(capacity, rest, place, ids, feats, *refs):
    chunks = refs[-len(rest) :]
    for chunk, k in zip(chunks, rest):
        pack_chunk(k, capacity, place[...], ids[...], feats[...], chunk)


def margin_kernel(parts, place, weight, features, margin, kept, sems):
    step = kept.shape[0] // parts
    moves = [
        pltpu.make_async_copy(features.at[pl.ds(i * step, step)], kept.at[pl.ds(i * step, step)], sems.at[i])
        for i in range(parts)
    ]
    for move in moves:
        move.start()
    wide = jnp.broadcast_to(weight[...], (16, weight.shape[1])).astype(BF16)
    for i in range(parts):
        moves[i].wait()
        here = slice(i * step, (i + 1) * step)
        margin[:, here] = lanes_dot(wide, kept[here])[0:1]


def chunk_ids(chunk, capacity):
    pair = chunk[capacity:, :capacity].astype(F32)
    return (pair[0:1] * 256.0 + pair[1:2]).astype(jnp.int32)


def chunk_scores(chunk, table, capacity):
    entities = table.shape[0] // 2
    every = lanes_dot(table, chunk[:capacity])
    hits = one_hot(chunk_ids(chunk, capacity), entities)
    return jnp.sum(jnp.where(hits, every[:entities] + every[entities:], 0.0), axis=0, keepdims=True)


def early_kernel(capacity, coefs, *refs):
    half = len(refs) // 2
    table = jnp.concatenate(halves(coefs[...]), axis=0)
    for chunk, out in zip(refs[:half], refs[half:]):
        out[...] = chunk_scores(chunk, table, capacity)


def scores_kernel(order, capacity, n_feat, n_ent, where, coefs, *refs):
    out, mine = refs[-1], where[0]
    table = jnp.concatenate(halves(coefs[...]), axis=0)
    scores = [
        x[...] if x.shape[0] == 1 else chunk_scores(x, table, capacity) for x in refs[:-1]
    ]
    for k, score in zip(order, scores):
        home = mine ^ k
        for f in range(n_feat):
            out[(home // n_ent * n_feat + f) * n_ent + home % n_ent] = score


def home_kernel(
    owners, capacity, n_feat, n_ent, where, member, item, ranks, clicks, valid, margin, scores, features, out
):
    on_item = where[1] > 0
    total = margin[...]
    hits_of = [one_hot(owner[...], owners).astype(F32) for owner in (member, item)]
    spot_of = [one_hot(ranks[side : side + 1], capacity).astype(F32).astype(BF16) for side in (0, 1)]
    for side in (0, 1):
        table = None
        for f in range(side * n_feat // 2, (side + 1) * n_feat // 2):
            part = jnp.concatenate(
                [scores[(h // n_ent * n_feat + f) * n_ent + h % n_ent] for h in range(owners)], axis=0
            )
            table = part if table is None else table + part
        found = plain_dot(jnp.concatenate(halves(table), axis=0), spot_of[side])
        total = total + jnp.sum((found[:owners] + found[owners:]) * hits_of[side], axis=0, keepdims=True)
    resid = valid[...].astype(F32) * (jax.nn.sigmoid(total) - clicks[...].astype(F32))
    hits = jnp.where(on_item, hits_of[1], hits_of[0])
    spot = jnp.where(on_item, spot_of[1], spot_of[0])
    sent = lanes_dot(jnp.concatenate(halves(hits * resid), axis=0), spot)
    sent = sent[:owners] + sent[owners:]
    low = jnp.broadcast_to(resid, (16, resid.shape[1])).astype(BF16)
    grad = plain_dot(low, features[...])[0:1]
    for h in range(owners):
        out[h, :, :capacity] = sent[h : h + 1]
        out[h, :, capacity:] = grad


def grads_kernel(order, capacity, scale, where, coefs, weight, came, *refs):
    chunks, grad_global, grad_coefs = refs[:-2], refs[-2], refs[-1]
    entities = coefs.shape[0]
    mine = where[0]
    resids = [came[mine ^ k][:, :capacity] for k in order]
    summed = came[0][:, capacity:]
    for h in range(1, len(order)):
        summed = summed + came[h][:, capacity:]
    grad_global[...] = summed * scale + 4.0 * weight[...]
    highs, lows, feats = [], [], []
    for chunk, resid in zip(chunks, resids):
        hits = one_hot(chunk_ids(chunk, capacity), entities)
        high, low = halves(resid)
        highs.append(jnp.where(hits, high.astype(F32), 0.0).astype(BF16))
        lows.append(jnp.where(hits, low.astype(F32), 0.0).astype(BF16))
        feats.append(chunk[:capacity])
    spread = jnp.concatenate([jnp.concatenate(highs, axis=1), jnp.concatenate(lows, axis=1)], axis=0)
    both = plain_dot(spread, jnp.concatenate(feats, axis=0))
    grad_coefs[...] = coefs[...] + both[:entities] + both[entities:]


def xor_send(x, axes, size, k):
    return x if k == 0 else lax.ppermute(x, axes, [(i, i ^ k) for i in range(size)])


def call(kernel, out_shape, operands, in_specs, flops=0, scratch=(), hidden=False):
    moved = 0 if hidden else sum(x.size * x.dtype.itemsize for x in (*operands, *out_shape))
    return pl.pallas_call(
        kernel,
        out_shape=out_shape,
        in_specs=in_specs,
        out_specs=[VMEM] * len(out_shape),
        scratch_shapes=scratch,
        compiler_params=PARAMS,
        cost_estimate=pl.CostEstimate(flops=flops, bytes_accessed=moved, transcendentals=0),
    )(*operands)


def body(
    features,
    global_weight,
    entity_feats,
    coefs,
    member_owner,
    member_local,
    item_owner,
    item_local,
    clicks,
    valid,
):
    rows_here, width = entity_feats.shape
    columns = features.shape[1]
    n_feat, n_ent = lax.axis_size("feat"), lax.axis_size("ent")
    owners = lax.axis_size("rows") * n_ent
    capacity = 2 * rows_here // owners
    mine = lax.axis_index(HOME).astype(jnp.int32)
    on_item = (lax.axis_index("feat") >= n_feat // 2).astype(jnp.int32)
    where = jnp.stack([mine, on_item])
    member, item = member_owner.reshape(1, rows_here), item_owner.reshape(1, rows_here)

    def shape(*dims, dtype=F32):
        return jax.ShapeDtypeStruct(dims, dtype)

    def partial(kernel, *args):
        return lambda *refs: kernel(*args, *refs)

    row = pltpu.VMEM((1, rows_here), jnp.int32)
    half, early = owners // 2, 3 * owners // 4
    first, second, near = list(range(half, early)), list(range(early, owners)), list(reversed(range(half)))
    chunk = shape(capacity + IDS, width, dtype=BF16)
    flops = len(first) * 2 * capacity * rows_here * width

    def in_hbm(x):
        return pltpu.with_memory_space_constraint(x, pltpu.HBM)

    ranks, place, ids, feats, *chunks = call(
        partial(far_kernel, owners, capacity, first),
        [
            shape(2, rows_here, dtype=jnp.int32),
            shape(1, rows_here, dtype=jnp.int32),
            shape(IDS, rows_here, dtype=BF16),
            shape(rows_here, width, dtype=BF16),
        ]
        + [chunk] * len(first),
        (
            where,
            in_hbm(member),
            in_hbm(item),
            in_hbm(member_local.reshape(1, rows_here)),
            in_hbm(item_local.reshape(1, rows_here)),
            in_hbm(entity_feats),
        ),
        [SMEM] + [HBM] * 5,
        flops=flops,
        scratch=[row, row, row, row, pltpu.SemaphoreType.DMA((5,))],
    )
    chunks += call(
        partial(rest_kernel, capacity, second),
        [chunk] * len(second),
        (place, ids, feats),
        [VMEM] * 3,
        flops=flops,
    )
    chunks = [xor_send(x, HOME, owners, k) for k, x in zip(first + second, chunks)]
    weight = global_weight.astype(F32).reshape(1, columns)
    parts = 4
    global_part, kept = call(
        partial(margin_kernel, parts),
        [shape(1, rows_here), shape(rows_here, columns, dtype=BF16)],
        (place, weight, in_hbm(features)),
        [VMEM, VMEM, HBM],
        hidden=True,
        scratch=[pltpu.SemaphoreType.DMA((parts,))],
    )
    global_total = lax.psum(global_part, "feat")
    near_chunks = call(
        partial(rest_kernel, capacity, near),
        [chunk] * len(near),
        (place, ids, feats, global_total),
        [VMEM] * 4,
        hidden=True,
    )
    near_chunks = [xor_send(x, HOME, owners, k) for k, x in zip(near, near_chunks)]
    order = first + near[-1:] + second + near[:-1]
    chunks = chunks[: len(first)] + near_chunks[-1:] + chunks[len(first) :] + near_chunks[:-1]
    came_early = len(first) + 1
    scores = call(
        partial(early_kernel, capacity),
        [shape(1, capacity)] * came_early,
        (coefs, *chunks[:came_early]),
        [VMEM] * (1 + came_early),
        hidden=True,
    )
    (scores,) = call(
        partial(scores_kernel, order, capacity, n_feat, n_ent),
        [shape(n_feat * owners, 1, capacity)],
        (where, coefs, *scores, *chunks[came_early:]),
        [SMEM] + [VMEM] * (1 + owners),
        flops=2 * coefs.size * owners * capacity,
    )
    returned = lax.all_to_all(scores, EVERY, split_axis=0, concat_axis=0, tiled=True)
    (sent,) = call(
        partial(home_kernel, owners, capacity, n_feat, n_ent),
        [shape(owners, 1, capacity + columns)],
        (
            where,
            member,
            item,
            ranks,
            clicks.reshape(1, rows_here),
            valid.reshape(1, rows_here),
            global_total,
            returned,
            kept,
        ),
        [SMEM] + [VMEM] * 8,
        flops=32 * features.size,
    )
    came = lax.all_to_all(sent, HOME, split_axis=0, concat_axis=0, tiled=True)
    grad_global, grad_coefs = call(
        partial(grads_kernel, order, capacity, 1.0 / math.sqrt(rows_here * owners)),
        [shape(1, columns), shape(*coefs.shape)],
        (where, coefs, weight, came, *chunks),
        [SMEM] + [VMEM] * (3 + owners),
        flops=4 * coefs.size * owners * capacity,
    )
    return (grad_global.reshape(columns), grad_coefs)


def solution(mesh):
    by_row = P(("groups", "rows", "ent"))
    by_both = P(("groups", "rows", "ent"), "feat")
    column = P(("groups", "rows", "ent"), None)
    by_feat = P(("groups", "feat"))
    return jax.shard_map(
        body,
        mesh=mesh,
        in_specs=(by_both, by_feat, by_both, by_both, column, by_row, column, by_row, by_row, by_row),
        out_specs=(by_feat, by_both),
        check_vma=False,
    )
```

```python
import math

import jax
import jax.numpy as jnp
from jax import lax
from jax.experimental import pallas as pl
from jax.experimental.pallas import tpu as pltpu
from jax.sharding import PartitionSpec as P

F32 = jnp.float32
BF16 = jnp.bfloat16
HOME = ("rows", "ent")
EVERY = ("rows", "feat", "ent")
IDS = 8
PARAMS = pltpu.CompilerParams(vmem_limit_bytes=24 * 2**20)
SMEM = pl.BlockSpec(memory_space=pltpu.SMEM)
VMEM = pl.BlockSpec(memory_space=pltpu.VMEM)
HBM = pl.BlockSpec(memory_space=pltpu.HBM)


def lanes_dot(a, b):
    return lax.dot_general(a, b, (((1,), (1,)), ((), ())), preferred_element_type=F32)


def plain_dot(a, b):
    return lax.dot_general(a, b, (((1,), (0,)), ((), ())), preferred_element_type=F32)


def halves(x):
    high = x.astype(BF16)
    return high, (x - high.astype(F32)).astype(BF16)


def one_hot(row, count):
    return row == lax.broadcasted_iota(jnp.int32, (count, row.shape[1]), 0)


def ranks_of(owners, member, item):
    rows = member.shape[1]
    step = min(256, rows)
    blocks = rows // step
    hits = jnp.concatenate([one_hot(member, owners).astype(F32), one_hot(item, owners).astype(F32)], axis=0)
    stacked = jnp.concatenate([hits[:, b * step : (b + 1) * step] for b in range(blocks)], axis=0)
    upper = lax.broadcasted_iota(jnp.int32, (step, step), 0) <= lax.broadcasted_iota(
        jnp.int32, (step, step), 1
    )
    counts = plain_dot(stacked.astype(BF16), upper.astype(F32).astype(BF16))
    before = jnp.zeros((2 * owners, 1), F32)
    pieces = []
    for b in range(blocks):
        here = counts[2 * owners * b : 2 * owners * (b + 1)]
        taken = (here + before) * hits[:, b * step : (b + 1) * step]
        sides = [jnp.sum(x, axis=0, keepdims=True) for x in (taken[:owners], taken[owners:])]
        pieces.append(jnp.concatenate(sides, axis=0))
        before = before + here[:, step - 1 : step]
    return jnp.concatenate(pieces, axis=1).astype(jnp.int32) - 1


def pack_chunk(k, capacity, place, ids, feats, chunk):
    pick = one_hot(place - k * capacity, capacity).astype(F32).astype(BF16)
    chunk[:capacity] = plain_dot(pick, feats).astype(BF16)
    chunk[capacity:, :capacity] = lanes_dot(ids, pick).astype(BF16)


def far_kernel(owners, capacity, far, where, *refs):
    sources, ranks, place_out, ids_out, feats = refs[:5], refs[5], refs[6], refs[7], refs[8]
    chunks, copies, sems = refs[9 : 9 + len(far)], refs[9 + len(far) : 13 + len(far)], refs[13 + len(far)]
    copies = (*copies, feats)
    moves = [pltpu.make_async_copy(sources[i], copies[i], sems.at[i]) for i in range(5)]
    for move in moves:
        move.start()
    for move in moves[:4]:
        move.wait()
    member, item, member_local, item_local = [copy[...] for copy in copies[:4]]
    rows = member.shape[1]
    mine, on_item = where[0], where[1] > 0
    rank = ranks_of(owners, member, item)
    ranks[...] = rank
    own = jnp.where(on_item, item, member)
    place = (own ^ mine) * capacity + jnp.where(on_item, rank[1:2], rank[0:1])
    place_out[...] = place
    local = jnp.where(on_item, item_local, member_local)
    high = local >> 8
    ids = jnp.concatenate([high, local - (high << 8), jnp.zeros((IDS - 2, rows), jnp.int32)], axis=0)
    ids = ids.astype(F32).astype(BF16)
    ids_out[...] = ids
    moves[4].wait()
    for chunk, k in zip(chunks, far):
        pack_chunk(k, capacity, place, ids, feats[...], chunk)


def rest_kernel(capacity, rest, place, ids, feats, *refs):
    chunks = refs[-len(rest) :]
    for chunk, k in zip(chunks, rest):
        pack_chunk(k, capacity, place[...], ids[...], feats[...], chunk)


def margin_kernel(place, weight, features, margin, copies, sems):
    parts = copies.shape[0]
    step = copies.shape[1]
    moves = [
        pltpu.make_async_copy(features.at[pl.ds(i * step, step)], copies.at[i], sems.at[i]) for i in range(parts)
    ]
    for move in moves:
        move.start()
    wide = jnp.broadcast_to(weight[...], (16, weight.shape[1])).astype(BF16)
    for i in range(parts):
        moves[i].wait()
        margin[:, i * step : (i + 1) * step] = lanes_dot(wide, copies[i])[0:1]


def chunk_ids(chunk, capacity):
    pair = chunk[capacity:, :capacity].astype(F32)
    return (pair[0:1] * 256.0 + pair[1:2]).astype(jnp.int32)


def chunk_scores(chunk, table, capacity):
    entities = table.shape[0] // 2
    every = lanes_dot(table, chunk[:capacity])
    hits = one_hot(chunk_ids(chunk, capacity), entities)
    return jnp.sum(jnp.where(hits, every[:entities] + every[entities:], 0.0), axis=0, keepdims=True)


def early_kernel(capacity, coefs, *refs):
    half = len(refs) // 2
    table = jnp.concatenate(halves(coefs[...]), axis=0)
    for chunk, out in zip(refs[:half], refs[half:]):
        out[...] = chunk_scores(chunk, table, capacity)


def scores_kernel(order, capacity, n_feat, n_ent, where, coefs, *refs):
    out, mine = refs[-1], where[0]
    table = jnp.concatenate(halves(coefs[...]), axis=0)
    scores = [
        x[...] if x.shape[0] == 1 else chunk_scores(x, table, capacity) for x in refs[:-1]
    ]
    for k, score in zip(order, scores):
        home = mine ^ k
        for f in range(n_feat):
            out[(home // n_ent * n_feat + f) * n_ent + home % n_ent] = score


def home_kernel(
    owners, capacity, n_feat, n_ent, where, member, item, ranks, clicks, valid, margin, scores, features, out
):
    on_item = where[1] > 0
    total = margin[...]
    hits_of = [one_hot(owner[...], owners).astype(F32) for owner in (member, item)]
    spot_of = [one_hot(ranks[side : side + 1], capacity).astype(F32).astype(BF16) for side in (0, 1)]
    for side in (0, 1):
        table = None
        for f in range(side * n_feat // 2, (side + 1) * n_feat // 2):
            part = jnp.concatenate(
                [scores[(h // n_ent * n_feat + f) * n_ent + h % n_ent] for h in range(owners)], axis=0
            )
            table = part if table is None else table + part
        found = plain_dot(jnp.concatenate(halves(table), axis=0), spot_of[side])
        total = total + jnp.sum((found[:owners] + found[owners:]) * hits_of[side], axis=0, keepdims=True)
    resid = valid[...].astype(F32) * (jax.nn.sigmoid(total) - clicks[...].astype(F32))
    hits = jnp.where(on_item, hits_of[1], hits_of[0])
    spot = jnp.where(on_item, spot_of[1], spot_of[0])
    sent = lanes_dot(jnp.concatenate(halves(hits * resid), axis=0), spot)
    sent = sent[:owners] + sent[owners:]
    low = jnp.broadcast_to(resid, (16, resid.shape[1])).astype(BF16)
    grad = plain_dot(low, features[...])[0:1]
    for h in range(owners):
        out[h, :, :capacity] = sent[h : h + 1]
        out[h, :, capacity:] = grad


def grads_kernel(order, capacity, scale, where, coefs, weight, came, *refs):
    chunks, grad_global, grad_coefs = refs[:-2], refs[-2], refs[-1]
    entities = coefs.shape[0]
    mine = where[0]
    resids = [came[mine ^ k][:, :capacity] for k in order]
    summed = came[0][:, capacity:]
    for h in range(1, len(order)):
        summed = summed + came[h][:, capacity:]
    grad_global[...] = summed * scale + 4.0 * weight[...]
    highs, lows, feats = [], [], []
    for chunk, resid in zip(chunks, resids):
        hits = one_hot(chunk_ids(chunk, capacity), entities)
        high, low = halves(resid)
        highs.append(jnp.where(hits, high.astype(F32), 0.0).astype(BF16))
        lows.append(jnp.where(hits, low.astype(F32), 0.0).astype(BF16))
        feats.append(chunk[:capacity])
    spread = jnp.concatenate([jnp.concatenate(highs, axis=1), jnp.concatenate(lows, axis=1)], axis=0)
    both = plain_dot(spread, jnp.concatenate(feats, axis=0))
    grad_coefs[...] = coefs[...] + both[:entities] + both[entities:]


def xor_send(x, axes, size, k):
    return x if k == 0 else lax.ppermute(x, axes, [(i, i ^ k) for i in range(size)])


def call(kernel, out_shape, operands, in_specs, flops=0, scratch=(), hidden=False):
    moved = 0 if hidden else sum(x.size * x.dtype.itemsize for x in (*operands, *out_shape))
    return pl.pallas_call(
        kernel,
        out_shape=out_shape,
        in_specs=in_specs,
        out_specs=[VMEM] * len(out_shape),
        scratch_shapes=scratch,
        compiler_params=PARAMS,
        cost_estimate=pl.CostEstimate(flops=flops, bytes_accessed=moved, transcendentals=0),
    )(*operands)


def body(
    features,
    global_weight,
    entity_feats,
    coefs,
    member_owner,
    member_local,
    item_owner,
    item_local,
    clicks,
    valid,
):
    rows_here, width = entity_feats.shape
    columns = features.shape[1]
    n_feat, n_ent = lax.axis_size("feat"), lax.axis_size("ent")
    owners = lax.axis_size("rows") * n_ent
    capacity = 2 * rows_here // owners
    mine = lax.axis_index(HOME).astype(jnp.int32)
    on_item = (lax.axis_index("feat") >= n_feat // 2).astype(jnp.int32)
    where = jnp.stack([mine, on_item])
    member, item = member_owner.reshape(1, rows_here), item_owner.reshape(1, rows_here)

    def shape(*dims, dtype=F32):
        return jax.ShapeDtypeStruct(dims, dtype)

    def partial(kernel, *args):
        return lambda *refs: kernel(*args, *refs)

    row = pltpu.VMEM((1, rows_here), jnp.int32)
    half, early = owners // 2, 3 * owners // 4
    first, second, near = list(range(half, early)), list(range(early, owners)), list(reversed(range(half)))
    chunk = shape(capacity + IDS, width, dtype=BF16)
    flops = len(first) * 2 * capacity * rows_here * width

    def in_hbm(x):
        return pltpu.with_memory_space_constraint(x, pltpu.HBM)

    ranks, place, ids, feats, *chunks = call(
        partial(far_kernel, owners, capacity, first),
        [
            shape(2, rows_here, dtype=jnp.int32),
            shape(1, rows_here, dtype=jnp.int32),
            shape(IDS, rows_here, dtype=BF16),
            shape(rows_here, width, dtype=BF16),
        ]
        + [chunk] * len(first),
        (
            where,
            in_hbm(member),
            in_hbm(item),
            in_hbm(member_local.reshape(1, rows_here)),
            in_hbm(item_local.reshape(1, rows_here)),
            in_hbm(entity_feats),
        ),
        [SMEM] + [HBM] * 5,
        flops=flops,
        scratch=[row, row, row, row, pltpu.SemaphoreType.DMA((5,))],
    )
    chunks += call(
        partial(rest_kernel, capacity, second),
        [chunk] * len(second),
        (place, ids, feats),
        [VMEM] * 3,
        flops=flops,
    )
    chunks = [xor_send(x, HOME, owners, k) for k, x in zip(first + second, chunks)]
    weight = global_weight.astype(F32).reshape(1, columns)
    parts = 4
    (global_part,) = call(
        margin_kernel,
        [shape(1, rows_here)],
        (place, weight, in_hbm(features)),
        [VMEM, VMEM, HBM],
        hidden=True,
        scratch=[pltpu.VMEM((parts, rows_here // parts, columns), BF16), pltpu.SemaphoreType.DMA((parts,))],
    )
    global_total = lax.psum(global_part, "feat")
    near_chunks = call(
        partial(rest_kernel, capacity, near),
        [chunk] * len(near),
        (place, ids, feats, global_total),
        [VMEM] * 4,
        hidden=True,
    )
    near_chunks = [xor_send(x, HOME, owners, k) for k, x in zip(near, near_chunks)]
    order = first + near[-1:] + second + near[:-1]
    chunks = chunks[: len(first)] + near_chunks[-1:] + chunks[len(first) :] + near_chunks[:-1]
    came_early = len(first) + 1
    scores = call(
        partial(early_kernel, capacity),
        [shape(1, capacity)] * came_early,
        (coefs, *chunks[:came_early]),
        [VMEM] * (1 + came_early),
        hidden=True,
    )
    (scores,) = call(
        partial(scores_kernel, order, capacity, n_feat, n_ent),
        [shape(n_feat * owners, 1, capacity)],
        (where, coefs, *scores, *chunks[came_early:]),
        [SMEM] + [VMEM] * (1 + owners),
        flops=16 * coefs.size * owners * capacity,
    )
    returned = lax.all_to_all(scores, EVERY, split_axis=0, concat_axis=0, tiled=True)
    (sent,) = call(
        partial(home_kernel, owners, capacity, n_feat, n_ent),
        [shape(owners, 1, capacity + columns)],
        (
            where,
            member,
            item,
            ranks,
            clicks.reshape(1, rows_here),
            valid.reshape(1, rows_here),
            global_total,
            returned,
            features,
        ),
        [SMEM] + [VMEM] * 8,
        flops=32 * features.size,
    )
    came = lax.all_to_all(sent, HOME, split_axis=0, concat_axis=0, tiled=True)
    grad_global, grad_coefs = call(
        partial(grads_kernel, order, capacity, 1.0 / math.sqrt(rows_here * owners)),
        [shape(1, columns), shape(*coefs.shape)],
        (where, coefs, weight, came, *chunks),
        [SMEM] + [VMEM] * (3 + owners),
        flops=4 * coefs.size * owners * capacity,
    )
    return (grad_global.reshape(columns), grad_coefs)


def solution(mesh):
    by_row = P(("groups", "rows", "ent"))
    by_both = P(("groups", "rows", "ent"), "feat")
    column = P(("groups", "rows", "ent"), None)
    by_feat = P(("groups", "feat"))
    return jax.shard_map(
        body,
        mesh=mesh,
        in_specs=(by_both, by_feat, by_both, by_both, column, by_row, column, by_row, by_row, by_row),
        out_specs=(by_feat, by_both),
        check_vma=False,
    )
```

```python
import math

import jax
import jax.numpy as jnp
from jax import lax
from jax.experimental import pallas as pl
from jax.experimental.pallas import tpu as pltpu
from jax.sharding import PartitionSpec as P

F32 = jnp.float32
BF16 = jnp.bfloat16
HOME = ("rows", "ent")
EVERY = ("rows", "feat", "ent")
IDS = 8
PARAMS = pltpu.CompilerParams(vmem_limit_bytes=24 * 2**20)
SMEM = pl.BlockSpec(memory_space=pltpu.SMEM)
VMEM = pl.BlockSpec(memory_space=pltpu.VMEM)
HBM = pl.BlockSpec(memory_space=pltpu.HBM)


def lanes_dot(a, b):
    return lax.dot_general(a, b, (((1,), (1,)), ((), ())), preferred_element_type=F32)


def plain_dot(a, b):
    return lax.dot_general(a, b, (((1,), (0,)), ((), ())), preferred_element_type=F32)


def halves(x):
    high = x.astype(BF16)
    return high, (x - high.astype(F32)).astype(BF16)


def one_hot(row, count):
    return row == lax.broadcasted_iota(jnp.int32, (count, row.shape[1]), 0)


def ranks_of(owners, member, item):
    rows = member.shape[1]
    step = min(256, rows)
    blocks = rows // step
    hits = jnp.concatenate([one_hot(member, owners).astype(F32), one_hot(item, owners).astype(F32)], axis=0)
    stacked = jnp.concatenate([hits[:, b * step : (b + 1) * step] for b in range(blocks)], axis=0)
    upper = lax.broadcasted_iota(jnp.int32, (step, step), 0) <= lax.broadcasted_iota(
        jnp.int32, (step, step), 1
    )
    counts = plain_dot(stacked.astype(BF16), upper.astype(F32).astype(BF16))
    before = jnp.zeros((2 * owners, 1), F32)
    pieces = []
    for b in range(blocks):
        here = counts[2 * owners * b : 2 * owners * (b + 1)]
        taken = (here + before) * hits[:, b * step : (b + 1) * step]
        sides = [jnp.sum(x, axis=0, keepdims=True) for x in (taken[:owners], taken[owners:])]
        pieces.append(jnp.concatenate(sides, axis=0))
        before = before + here[:, step - 1 : step]
    return jnp.concatenate(pieces, axis=1).astype(jnp.int32) - 1


def pack_chunk(k, capacity, place, ids, feats, chunk):
    pick = one_hot(place - k * capacity, capacity).astype(F32).astype(BF16)
    chunk[:capacity] = plain_dot(pick, feats).astype(BF16)
    chunk[capacity:, :capacity] = lanes_dot(ids, pick).astype(BF16)


def far_kernel(owners, capacity, far, where, *refs):
    sources, ranks, place_out, ids_out, feats = refs[:5], refs[5], refs[6], refs[7], refs[8]
    chunks, copies, sems = refs[9 : 9 + len(far)], refs[9 + len(far) : 13 + len(far)], refs[13 + len(far)]
    copies = (*copies, feats)
    moves = [pltpu.make_async_copy(sources[i], copies[i], sems.at[i]) for i in range(5)]
    for move in moves:
        move.start()
    for move in moves[:4]:
        move.wait()
    member, item, member_local, item_local = [copy[...] for copy in copies[:4]]
    rows = member.shape[1]
    mine, on_item = where[0], where[1] > 0
    rank = ranks_of(owners, member, item)
    ranks[...] = rank
    own = jnp.where(on_item, item, member)
    place = (own ^ mine) * capacity + jnp.where(on_item, rank[1:2], rank[0:1])
    place_out[...] = place
    local = jnp.where(on_item, item_local, member_local)
    high = local >> 8
    ids = jnp.concatenate([high, local - (high << 8), jnp.zeros((IDS - 2, rows), jnp.int32)], axis=0)
    ids = ids.astype(F32).astype(BF16)
    ids_out[...] = ids
    moves[4].wait()
    for chunk, k in zip(chunks, far):
        pack_chunk(k, capacity, place, ids, feats[...], chunk)


def rest_kernel(capacity, rest, place, ids, feats, *refs):
    chunks = refs[-len(rest) :]
    for chunk, k in zip(chunks, rest):
        pack_chunk(k, capacity, place[...], ids[...], feats[...], chunk)


def margin_kernel(place, weight, features, margin):
    wide = jnp.broadcast_to(weight[...], (16, weight.shape[1])).astype(BF16)
    margin[...] = lanes_dot(wide, features[...])[0:1]


def chunk_ids(chunk, capacity):
    pair = chunk[capacity:, :capacity].astype(F32)
    return (pair[0:1] * 256.0 + pair[1:2]).astype(jnp.int32)


def chunk_scores(chunk, table, capacity):
    entities = table.shape[0] // 2
    every = lanes_dot(table, chunk[:capacity])
    hits = one_hot(chunk_ids(chunk, capacity), entities)
    return jnp.sum(jnp.where(hits, every[:entities] + every[entities:], 0.0), axis=0, keepdims=True)


def early_kernel(capacity, count, coefs, *refs):
    table = jnp.concatenate(halves(coefs[...]), axis=0)
    for chunk, out in zip(refs[:count], refs[-count:]):
        out[...] = chunk_scores(chunk, table, capacity)


def scores_kernel(order, capacity, n_feat, n_ent, where, coefs, *refs):
    out, mine = refs[-1], where[0]
    table = jnp.concatenate(halves(coefs[...]), axis=0)
    scores = [x[...] if x.shape[0] == 1 else chunk_scores(x, table, capacity) for x in refs[:-1]]
    scores.append(jnp.zeros((1, capacity), F32))
    for k, score in zip(order, scores):
        home = mine ^ k
        for f in range(n_feat):
            out[(home // n_ent * n_feat + f) * n_ent + home % n_ent] = score


def home_kernel(
    owners, capacity, n_feat, n_ent, where, member, item, ranks, clicks, valid, margin, scores, features, *refs
):
    lates, out = refs[:-1], refs[-1]
    mine, on_item = where[0], where[1] > 0
    total = margin[...]
    hits_of = [one_hot(owner[...], owners).astype(F32) for owner in (member, item)]
    spot_of = [one_hot(ranks[side : side + 1], capacity).astype(F32).astype(BF16) for side in (0, 1)]
    late = lax.broadcasted_iota(jnp.int32, (owners, capacity), 0) == (mine ^ (owners - 1))
    for side in (0, 1):
        table = None
        for f in range(side * n_feat // 2, (side + 1) * n_feat // 2):
            part = jnp.concatenate(
                [scores[(h // n_ent * n_feat + f) * n_ent + h % n_ent] for h in range(owners)], axis=0
            )
            table = part if table is None else table + part
        for q in range(n_feat):
            on_side = where[1 + q] == side
            table = table + jnp.where(late & on_side, lates[q][...], 0.0)
        found = plain_dot(jnp.concatenate(halves(table), axis=0), spot_of[side])
        total = total + jnp.sum((found[:owners] + found[owners:]) * hits_of[side], axis=0, keepdims=True)
    resid = valid[...].astype(F32) * (jax.nn.sigmoid(total) - clicks[...].astype(F32))
    hits = jnp.where(on_item, hits_of[1], hits_of[0])
    spot = jnp.where(on_item, spot_of[1], spot_of[0])
    sent = lanes_dot(jnp.concatenate(halves(hits * resid), axis=0), spot)
    sent = sent[:owners] + sent[owners:]
    low = jnp.broadcast_to(resid, (16, resid.shape[1])).astype(BF16)
    grad = plain_dot(low, features[...])[0:1]
    for h in range(owners):
        out[h, :, :capacity] = sent[h : h + 1]
        out[h, :, capacity:] = grad


def grads_kernel(order, capacity, scale, where, coefs, weight, came, *refs):
    chunks, grad_global, grad_coefs = refs[:-2], refs[-2], refs[-1]
    entities = coefs.shape[0]
    mine = where[0]
    resids = [came[mine ^ k][:, :capacity] for k in order]
    summed = came[0][:, capacity:]
    for h in range(1, len(order)):
        summed = summed + came[h][:, capacity:]
    grad_global[...] = summed * scale + 4.0 * weight[...]
    highs, lows, feats = [], [], []
    for chunk, resid in zip(chunks, resids):
        hits = one_hot(chunk_ids(chunk, capacity), entities)
        high, low = halves(resid)
        highs.append(jnp.where(hits, high.astype(F32), 0.0).astype(BF16))
        lows.append(jnp.where(hits, low.astype(F32), 0.0).astype(BF16))
        feats.append(chunk[:capacity])
    spread = jnp.concatenate([jnp.concatenate(highs, axis=1), jnp.concatenate(lows, axis=1)], axis=0)
    both = plain_dot(spread, jnp.concatenate(feats, axis=0))
    grad_coefs[...] = coefs[...] + both[:entities] + both[entities:]


def xor_send(x, axes, size, k):
    return x if k == 0 else lax.ppermute(x, axes, [(i, i ^ k) for i in range(size)])


def call(kernel, out_shape, operands, in_specs, flops=0, scratch=(), hidden=False):
    moved = 0 if hidden else sum(x.size * x.dtype.itemsize for x in (*operands, *out_shape))
    return pl.pallas_call(
        kernel,
        out_shape=out_shape,
        in_specs=in_specs,
        out_specs=[VMEM] * len(out_shape),
        scratch_shapes=scratch,
        compiler_params=PARAMS,
        cost_estimate=pl.CostEstimate(flops=flops, bytes_accessed=moved, transcendentals=0),
    )(*operands)


def body(
    features,
    global_weight,
    entity_feats,
    coefs,
    member_owner,
    member_local,
    item_owner,
    item_local,
    clicks,
    valid,
):
    rows_here, width = entity_feats.shape
    columns = features.shape[1]
    n_feat, n_ent = lax.axis_size("feat"), lax.axis_size("ent")
    owners = lax.axis_size("rows") * n_ent
    capacity = 2 * rows_here // owners
    mine = lax.axis_index(HOME).astype(jnp.int32)
    feat = lax.axis_index("feat")
    where = jnp.stack([mine, *(((feat ^ q) >= n_feat // 2).astype(jnp.int32) for q in range(n_feat))])
    member, item = member_owner.reshape(1, rows_here), item_owner.reshape(1, rows_here)

    def shape(*dims, dtype=F32):
        return jax.ShapeDtypeStruct(dims, dtype)

    def partial(kernel, *args):
        return lambda *refs: kernel(*args, *refs)

    row = pltpu.VMEM((1, rows_here), jnp.int32)
    half, early, late = owners // 2, 3 * owners // 4, owners - 1
    first, second = list(range(half, early)), list(range(early, owners))
    last = list(reversed(range(half)))
    chunk = shape(capacity + IDS, width, dtype=BF16)
    flops = len(first) * 2 * capacity * rows_here * width

    def in_hbm(x):
        return pltpu.with_memory_space_constraint(x, pltpu.HBM)

    ranks, place, ids, feats, *chunks = call(
        partial(far_kernel, owners, capacity, first),
        [
            shape(2, rows_here, dtype=jnp.int32),
            shape(1, rows_here, dtype=jnp.int32),
            shape(IDS, rows_here, dtype=BF16),
            shape(rows_here, width, dtype=BF16),
        ]
        + [chunk] * len(first),
        (
            where,
            in_hbm(member),
            in_hbm(item),
            in_hbm(member_local.reshape(1, rows_here)),
            in_hbm(item_local.reshape(1, rows_here)),
            in_hbm(entity_feats),
        ),
        [SMEM] + [HBM] * 5,
        flops=1 * flops,
        scratch=[row, row, row, row, pltpu.SemaphoreType.DMA((5,))],
    )
    chunks += call(
        partial(rest_kernel, capacity, second),
        [chunk] * len(second),
        (place, ids, feats),
        [VMEM] * 3,
        flops=16 * flops,
    )
    chunks = [xor_send(x, HOME, owners, k) for k, x in zip(first + second, chunks)]
    weight = global_weight.astype(F32).reshape(1, columns)
    (global_part,) = call(
        margin_kernel, [shape(1, rows_here)], (place, weight, features), [VMEM] * 3, hidden=True
    )
    global_total = lax.psum(global_part, "feat")
    last_chunks = call(
        partial(rest_kernel, capacity, last),
        [chunk] * len(last),
        (place, ids, feats, global_total),
        [VMEM] * 4,
        hidden=True,
    )
    last_chunks = [xor_send(x, HOME, owners, k) for k, x in zip(last, last_chunks)]
    chunks = dict(zip(first + second + last, chunks + last_chunks))
    came_early = first + [0]
    scores = call(
        partial(early_kernel, capacity, len(came_early)),
        [shape(1, capacity)] * len(came_early),
        (coefs, *(chunks[k] for k in came_early)),
        [VMEM] * (1 + len(came_early)),
        hidden=True,
    )
    came_next = second[:-1] + last[:-1]
    order = came_early + came_next + [late]
    (scores,) = call(
        partial(scores_kernel, order, capacity, n_feat, n_ent),
        [shape(n_feat * owners, 1, capacity)],
        (where, coefs, *scores, *(chunks[k] for k in came_next)),
        [SMEM] + [VMEM] * owners,
        flops=16 * coefs.size * owners * capacity,
    )
    returned = lax.all_to_all(scores, EVERY, split_axis=0, concat_axis=0, tiled=True)
    (late_score,) = call(
        partial(early_kernel, capacity, 1), [shape(1, capacity)], (coefs, chunks[late], scores), [VMEM] * 3, hidden=True
    )
    lates = []
    for q in range(n_feat):
        apart = (late // n_ent * n_feat + q) * n_ent + late % n_ent
        lates.append(xor_send(late_score, EVERY, n_feat * owners, apart))
    (sent,) = call(
        partial(home_kernel, owners, capacity, n_feat, n_ent),
        [shape(owners, 1, capacity + columns)],
        (
            where,
            member,
            item,
            ranks,
            clicks.reshape(1, rows_here),
            valid.reshape(1, rows_here),
            global_total,
            returned,
            features,
            *lates,
        ),
        [SMEM] + [VMEM] * (8 + n_feat),
        flops=32 * features.size,
    )
    came = lax.all_to_all(sent, HOME, split_axis=0, concat_axis=0, tiled=True)
    grad_global, grad_coefs = call(
        partial(grads_kernel, order, capacity, 1.0 / math.sqrt(rows_here * owners)),
        [shape(1, columns), shape(*coefs.shape)],
        (where, coefs, weight, came, *(chunks[k] for k in order)),
        [SMEM] + [VMEM] * (3 + owners),
        flops=4 * coefs.size * owners * capacity,
    )
    return (grad_global.reshape(columns), grad_coefs)


def solution(mesh):
    by_row = P(("groups", "rows", "ent"))
    by_both = P(("groups", "rows", "ent"), "feat")
    column = P(("groups", "rows", "ent"), None)
    by_feat = P(("groups", "feat"))
    return jax.shard_map(
        body,
        mesh=mesh,
        in_specs=(by_both, by_feat, by_both, by_both, column, by_row, column, by_row, by_row, by_row),
        out_specs=(by_feat, by_both),
        check_vma=False,
    )
```

```python
import math

import jax
import jax.numpy as jnp
from jax import lax
from jax.experimental import pallas as pl
from jax.experimental.pallas import tpu as pltpu
from jax.sharding import PartitionSpec as P

F32 = jnp.float32
BF16 = jnp.bfloat16
HOME = ("rows", "ent")
EVERY = ("rows", "feat", "ent")
IDS = 8
PARAMS = pltpu.CompilerParams(vmem_limit_bytes=24 * 2**20)
SMEM = pl.BlockSpec(memory_space=pltpu.SMEM)
VMEM = pl.BlockSpec(memory_space=pltpu.VMEM)
HBM = pl.BlockSpec(memory_space=pltpu.HBM)


def lanes_dot(a, b):
    return lax.dot_general(a, b, (((1,), (1,)), ((), ())), preferred_element_type=F32)


def plain_dot(a, b):
    return lax.dot_general(a, b, (((1,), (0,)), ((), ())), preferred_element_type=F32)


def halves(x):
    high = x.astype(BF16)
    return high, (x - high.astype(F32)).astype(BF16)


def one_hot(row, count):
    return row == lax.broadcasted_iota(jnp.int32, (count, row.shape[1]), 0)


def low_hot(row, count):
    row = jnp.where((row >= 0) & (row < count), row, -1).astype(F32).astype(BF16)
    return row == lax.broadcasted_iota(jnp.int32, (count, row.shape[1]), 0).astype(F32).astype(BF16)


def ones(mask):
    return jnp.where(mask, jnp.ones((), BF16), jnp.zeros((), BF16))


def xor_rows(rows, mine):
    count = rows.shape[0]
    bit = 1
    while bit < count:
        swapped = jnp.concatenate([rows[(k ^ bit) : (k ^ bit) + 1] for k in range(count)], axis=0)
        rows = jnp.where((mine & bit) > 0, swapped, rows)
        bit *= 2
    return rows


def ranks_of(owners, member, item):
    rows = member.shape[1]
    step = min(256, rows)
    blocks = rows // step
    hits = jnp.concatenate([one_hot(member, owners).astype(F32), one_hot(item, owners).astype(F32)], axis=0)
    stacked = jnp.concatenate([hits[:, b * step : (b + 1) * step] for b in range(blocks)], axis=0)
    upper = lax.broadcasted_iota(jnp.int32, (step, step), 0) <= lax.broadcasted_iota(
        jnp.int32, (step, step), 1
    )
    counts = plain_dot(stacked.astype(BF16), upper.astype(F32).astype(BF16))
    before = jnp.zeros((2 * owners, 1), F32)
    pieces = []
    for b in range(blocks):
        here = counts[2 * owners * b : 2 * owners * (b + 1)]
        taken = (here + before) * hits[:, b * step : (b + 1) * step]
        sides = [jnp.sum(x, axis=0, keepdims=True) for x in (taken[:owners], taken[owners:])]
        pieces.append(jnp.concatenate(sides, axis=0))
        before = before + here[:, step - 1 : step]
    return jnp.concatenate(pieces, axis=1).astype(jnp.int32) - 1


def pack_chunk(k, capacity, place, ids, feats, chunk):
    pick = ones(low_hot(place - k * capacity, capacity))
    chunk[:capacity] = plain_dot(pick, feats).astype(BF16)
    chunk[capacity:, :capacity] = lanes_dot(ids, pick).astype(BF16)


def far_kernel(owners, capacity, far, where, *refs):
    sources, ranks, place_out, ids_out, feats = refs[:5], refs[5], refs[6], refs[7], refs[8]
    chunks, copies, sems = refs[9 : 9 + len(far)], refs[9 + len(far) : 13 + len(far)], refs[13 + len(far)]
    copies = (*copies, feats)
    moves = [pltpu.make_async_copy(sources[i], copies[i], sems.at[i]) for i in range(5)]
    for move in moves:
        move.start()
    for move in moves[:4]:
        move.wait()
    member, item, member_local, item_local = [copy[...] for copy in copies[:4]]
    rows = member.shape[1]
    mine, on_item = where[0], where[1] > 0
    rank = ranks_of(owners, member, item)
    ranks[...] = rank
    own = jnp.where(on_item, item, member)
    place = (own ^ mine) * capacity + jnp.where(on_item, rank[1:2], rank[0:1])
    place_out[...] = place
    local = jnp.where(on_item, item_local, member_local)
    high = local >> 8
    ids = jnp.concatenate([high, local - (high << 8), jnp.zeros((IDS - 2, rows), jnp.int32)], axis=0)
    ids = ids.astype(F32).astype(BF16)
    ids_out[...] = ids
    moves[4].wait()
    for chunk, k in zip(chunks, far):
        pack_chunk(k, capacity, place, ids, feats[...], chunk)


def rest_kernel(capacity, rest, place, ids, feats, *refs):
    chunks = refs[-len(rest) :]
    for chunk, k in zip(chunks, rest):
        pack_chunk(k, capacity, place[...], ids[...], feats[...], chunk)


def margin_kernel(place, weight, features, margin, copies, sems):
    parts = copies.shape[0]
    step = copies.shape[1]
    moves = [
        pltpu.make_async_copy(features.at[pl.ds(i * step, step)], copies.at[i], sems.at[i]) for i in range(parts)
    ]
    for move in moves:
        move.start()
    wide = jnp.broadcast_to(weight[...], (16, weight.shape[1])).astype(BF16)
    for i in range(parts):
        moves[i].wait()
        margin[:, i * step : (i + 1) * step] = lanes_dot(wide, copies[i])[0:1]


def chunk_ids(chunk, capacity):
    pair = chunk[capacity:, :capacity].astype(F32)
    return (pair[0:1] * 256.0 + pair[1:2]).astype(jnp.int32)


def chunk_scores(chunk, table, capacity):
    entities = table.shape[0] // 2
    every = lanes_dot(table, chunk[:capacity])
    hits = one_hot(chunk_ids(chunk, capacity), entities)
    return jnp.sum(jnp.where(hits, every[:entities] + every[entities:], 0.0), axis=0, keepdims=True)


def early_kernel(capacity, coefs, *refs):
    half = len(refs) // 2
    table = jnp.concatenate(halves(coefs[...]), axis=0)
    for chunk, out in zip(refs[:half], refs[half:]):
        out[...] = chunk_scores(chunk, table, capacity)


def scores_kernel(order, capacity, n_feat, n_ent, where, coefs, *refs):
    out, mine = refs[-1], where[0]
    table = jnp.concatenate(halves(coefs[...]), axis=0)
    scores = [
        x[...] if x.shape[0] == 1 else chunk_scores(x, table, capacity) for x in refs[:-1]
    ]
    scores = dict(zip(order, scores))
    scores = xor_rows(jnp.concatenate([scores[k] for k in range(len(order))], axis=0), mine)
    for home in range(len(order)):
        for f in range(n_feat):
            out[(home // n_ent * n_feat + f) * n_ent + home % n_ent] = scores[home : home + 1]


def home_kernel(
    owners, capacity, n_feat, n_ent, where, member, item, ranks, clicks, valid, margin, scores, features, out
):
    on_item = where[1] > 0
    total = margin[...]
    hits_of = [one_hot(owner[...], owners).astype(F32) for owner in (member, item)]
    spot_of = [ones(low_hot(ranks[side : side + 1], capacity)) for side in (0, 1)]
    for side in (0, 1):
        table = None
        for f in range(side * n_feat // 2, (side + 1) * n_feat // 2):
            part = jnp.concatenate(
                [scores[(h // n_ent * n_feat + f) * n_ent + h % n_ent] for h in range(owners)], axis=0
            )
            table = part if table is None else table + part
        found = plain_dot(jnp.concatenate(halves(table), axis=0), spot_of[side])
        total = total + jnp.sum((found[:owners] + found[owners:]) * hits_of[side], axis=0, keepdims=True)
    resid = valid[...].astype(F32) * (jax.nn.sigmoid(total) - clicks[...].astype(F32))
    hits = jnp.where(on_item, hits_of[1], hits_of[0])
    spot = jnp.where(on_item, spot_of[1], spot_of[0])
    sent = lanes_dot(jnp.concatenate(halves(hits * resid), axis=0), spot)
    sent = sent[:owners] + sent[owners:]
    low = jnp.broadcast_to(resid, (16, resid.shape[1])).astype(BF16)
    grad = plain_dot(low, features[...])[0:1]
    for h in range(owners):
        out[h, :, :capacity] = sent[h : h + 1]
        out[h, :, capacity:] = grad


def grads_kernel(order, capacity, scale, where, coefs, weight, came, *refs):
    chunks, grad_global, grad_coefs = refs[:-2], refs[-2], refs[-1]
    entities = coefs.shape[0]
    mine = where[0]
    resids = xor_rows(jnp.concatenate([came[h][:, :capacity] for h in range(len(order))], axis=0), mine)
    summed = came[0][:, capacity:]
    for h in range(1, len(order)):
        summed = summed + came[h][:, capacity:]
    grad_global[...] = summed * scale + 4.0 * weight[...]
    highs, lows, feats = [], [], []
    for chunk, k in zip(chunks, order):
        here = chunk_ids(chunk, capacity)
        blocks = [low_hot(here - first, min(256, entities)) for first in range(0, entities, 256)]
        high, low = halves(resids[k : k + 1])
        highs.append(jnp.concatenate([jnp.where(hits, high, jnp.zeros((), BF16)) for hits in blocks], axis=0))
        lows.append(jnp.concatenate([jnp.where(hits, low, jnp.zeros((), BF16)) for hits in blocks], axis=0))
        feats.append(chunk[:capacity])
    spread = jnp.concatenate([jnp.concatenate(highs, axis=1), jnp.concatenate(lows, axis=1)], axis=0)
    both = plain_dot(spread, jnp.concatenate(feats, axis=0))
    grad_coefs[...] = coefs[...] + both[:entities] + both[entities:]


def xor_send(x, axes, size, k):
    return x if k == 0 else lax.ppermute(x, axes, [(i, i ^ k) for i in range(size)])


def call(kernel, out_shape, operands, in_specs, flops=0, scratch=(), hidden=False):
    moved = 0 if hidden else sum(x.size * x.dtype.itemsize for x in (*operands, *out_shape))
    return pl.pallas_call(
        kernel,
        out_shape=out_shape,
        in_specs=in_specs,
        out_specs=[VMEM] * len(out_shape),
        scratch_shapes=scratch,
        compiler_params=PARAMS,
        cost_estimate=pl.CostEstimate(flops=flops, bytes_accessed=moved, transcendentals=0),
    )(*operands)


def body(
    features,
    global_weight,
    entity_feats,
    coefs,
    member_owner,
    member_local,
    item_owner,
    item_local,
    clicks,
    valid,
):
    rows_here, width = entity_feats.shape
    columns = features.shape[1]
    n_feat, n_ent = lax.axis_size("feat"), lax.axis_size("ent")
    owners = lax.axis_size("rows") * n_ent
    capacity = 2 * rows_here // owners
    mine = lax.axis_index(HOME).astype(jnp.int32)
    on_item = (lax.axis_index("feat") >= n_feat // 2).astype(jnp.int32)
    where = jnp.stack([mine, on_item])
    member, item = member_owner.reshape(1, rows_here), item_owner.reshape(1, rows_here)

    def shape(*dims, dtype=F32):
        return jax.ShapeDtypeStruct(dims, dtype)

    def partial(kernel, *args):
        return lambda *refs: kernel(*args, *refs)

    row = pltpu.VMEM((1, rows_here), jnp.int32)
    half, early = owners // 2, 3 * owners // 4
    first, second, near = list(range(half, early)), list(range(early, owners)), list(reversed(range(half)))
    chunk = shape(capacity + IDS, width, dtype=BF16)
    flops = len(first) * 2 * capacity * rows_here * width

    def in_hbm(x):
        return pltpu.with_memory_space_constraint(x, pltpu.HBM)

    ranks, place, ids, feats, *chunks = call(
        partial(far_kernel, owners, capacity, first),
        [
            shape(2, rows_here, dtype=jnp.int32),
            shape(1, rows_here, dtype=jnp.int32),
            shape(IDS, rows_here, dtype=BF16),
            shape(rows_here, width, dtype=BF16),
        ]
        + [chunk] * len(first),
        (
            where,
            in_hbm(member),
            in_hbm(item),
            in_hbm(member_local.reshape(1, rows_here)),
            in_hbm(item_local.reshape(1, rows_here)),
            in_hbm(entity_feats),
        ),
        [SMEM] + [HBM] * 5,
        flops=flops,
        scratch=[row, row, row, row, pltpu.SemaphoreType.DMA((5,))],
    )
    chunks += call(
        partial(rest_kernel, capacity, second),
        [chunk] * len(second),
        (place, ids, feats),
        [VMEM] * 3,
        flops=flops,
    )
    chunks = [xor_send(x, HOME, owners, k) for k, x in zip(first + second, chunks)]
    weight = global_weight.astype(F32).reshape(1, columns)
    parts = 4
    (global_part,) = call(
        margin_kernel,
        [shape(1, rows_here)],
        (place, weight, in_hbm(features)),
        [VMEM, VMEM, HBM],
        hidden=True,
        scratch=[pltpu.VMEM((parts, rows_here // parts, columns), BF16), pltpu.SemaphoreType.DMA((parts,))],
    )
    global_total = lax.psum(global_part, "feat")
    near_chunks = call(
        partial(rest_kernel, capacity, near),
        [chunk] * len(near),
        (place, ids, feats, global_total),
        [VMEM] * 4,
        hidden=True,
    )
    near_chunks = [xor_send(x, HOME, owners, k) for k, x in zip(near, near_chunks)]
    order = first + near[-1:] + second + near[:-1]
    chunks = chunks[: len(first)] + near_chunks[-1:] + chunks[len(first) :] + near_chunks[:-1]
    came_early = len(first) + 1
    scores = call(
        partial(early_kernel, capacity),
        [shape(1, capacity)] * came_early,
        (coefs, *chunks[:came_early]),
        [VMEM] * (1 + came_early),
        hidden=True,
    )
    (scores,) = call(
        partial(scores_kernel, order, capacity, n_feat, n_ent),
        [shape(n_feat * owners, 1, capacity)],
        (where, coefs, *scores, *chunks[came_early:]),
        [SMEM] + [VMEM] * (1 + owners),
        flops=16 * coefs.size * owners * capacity,
    )
    returned = lax.all_to_all(scores, EVERY, split_axis=0, concat_axis=0, tiled=True)
    (sent,) = call(
        partial(home_kernel, owners, capacity, n_feat, n_ent),
        [shape(owners, 1, capacity + columns)],
        (
            where,
            member,
            item,
            ranks,
            clicks.reshape(1, rows_here),
            valid.reshape(1, rows_here),
            global_total,
            returned,
            features,
        ),
        [SMEM] + [VMEM] * 8,
        flops=32 * features.size,
    )
    came = lax.all_to_all(sent, HOME, split_axis=0, concat_axis=0, tiled=True)
    grad_global, grad_coefs = call(
        partial(grads_kernel, order, capacity, 1.0 / math.sqrt(rows_here * owners)),
        [shape(1, columns), shape(*coefs.shape)],
        (where, coefs, weight, came, *chunks),
        [SMEM] + [VMEM] * (3 + owners),
        flops=4 * coefs.size * owners * capacity,
    )
    return (grad_global.reshape(columns), grad_coefs)


def solution(mesh):
    by_row = P(("groups", "rows", "ent"))
    by_both = P(("groups", "rows", "ent"), "feat")
    column = P(("groups", "rows", "ent"), None)
    by_feat = P(("groups", "feat"))
    return jax.shard_map(
        body,
        mesh=mesh,
        in_specs=(by_both, by_feat, by_both, by_both, column, by_row, column, by_row, by_row, by_row),
        out_specs=(by_feat, by_both),
        check_vma=False,
    )
```

```python
import math

import jax
import jax.numpy as jnp
from jax import lax
from jax.experimental import pallas as pl
from jax.experimental.pallas import tpu as pltpu
from jax.sharding import PartitionSpec as P

F32 = jnp.float32
BF16 = jnp.bfloat16
HOME = ("rows", "ent")
EVERY = ("rows", "feat", "ent")
IDS = 8
PARAMS = pltpu.CompilerParams(vmem_limit_bytes=24 * 2**20)
VMEM = pl.BlockSpec(memory_space=pltpu.VMEM)
HBM = pl.BlockSpec(memory_space=pltpu.HBM)


def lanes_dot(a, b):
    return lax.dot_general(a, b, (((1,), (1,)), ((), ())), preferred_element_type=F32)


def plain_dot(a, b):
    return lax.dot_general(a, b, (((1,), (0,)), ((), ())), preferred_element_type=F32)


def halves(x):
    high = x.astype(BF16)
    return high, (x - high.astype(F32)).astype(BF16)


def one_hot(row, count):
    return row == lax.broadcasted_iota(jnp.int32, (count, row.shape[1]), 0)


def low_hot(row, count):
    row = jnp.where((row >= 0) & (row < count), row, -1).astype(F32).astype(BF16)
    return row == lax.broadcasted_iota(jnp.int32, (count, row.shape[1]), 0).astype(F32).astype(BF16)


def ones(mask):
    return jnp.where(mask, jnp.ones((), BF16), jnp.zeros((), BF16))


def xor_rows(rows, mine):
    count = rows.shape[0]
    bit = 1
    while bit < count:
        swapped = jnp.concatenate([rows[(k ^ bit) : (k ^ bit) + 1] for k in range(count)], axis=0)
        rows = jnp.where((mine & bit) > 0, swapped, rows)
        bit *= 2
    return rows


def ranks_of(owners, member, item):
    rows = member.shape[1]
    step = min(256, rows)
    blocks = rows // step
    hits = jnp.concatenate([one_hot(member, owners).astype(F32), one_hot(item, owners).astype(F32)], axis=0)
    stacked = jnp.concatenate([hits[:, b * step : (b + 1) * step] for b in range(blocks)], axis=0)
    upper = lax.broadcasted_iota(jnp.int32, (step, step), 0) <= lax.broadcasted_iota(
        jnp.int32, (step, step), 1
    )
    counts = plain_dot(stacked.astype(BF16), upper.astype(F32).astype(BF16))
    before = jnp.zeros((2 * owners, 1), F32)
    pieces = []
    for b in range(blocks):
        here = counts[2 * owners * b : 2 * owners * (b + 1)]
        taken = (here + before) * hits[:, b * step : (b + 1) * step]
        sides = [jnp.sum(x, axis=0, keepdims=True) for x in (taken[:owners], taken[owners:])]
        pieces.append(jnp.concatenate(sides, axis=0))
        before = before + here[:, step - 1 : step]
    return jnp.concatenate(pieces, axis=1).astype(jnp.int32) - 1


def pack_chunk(k, capacity, place, ids, feats, chunk):
    pick = ones(low_hot(place - k * capacity, capacity))
    chunk[:capacity] = plain_dot(pick, feats).astype(BF16)
    chunk[capacity:, :capacity] = lanes_dot(ids, pick).astype(BF16)


def position(n_feat):
    return lax.axis_index(HOME), lax.axis_index("feat") >= n_feat // 2


def far_kernel(owners, capacity, n_feat, far, *refs):
    sources, ranks, place_out, ids_out, feats = refs[:5], refs[5], refs[6], refs[7], refs[8]
    chunks, copies, sems = refs[9 : 9 + len(far)], refs[9 + len(far) : 13 + len(far)], refs[13 + len(far)]
    copies = (*copies, feats)
    moves = [pltpu.make_async_copy(sources[i], copies[i], sems.at[i]) for i in range(5)]
    for move in moves:
        move.start()
    for move in moves[:4]:
        move.wait()
    member, item, member_local, item_local = [copy[...] for copy in copies[:4]]
    rows = member.shape[1]
    mine, on_item = position(n_feat)
    rank = ranks_of(owners, member, item)
    ranks[...] = rank
    own = jnp.where(on_item, item, member)
    place = (own ^ mine) * capacity + jnp.where(on_item, rank[1:2], rank[0:1])
    place_out[...] = place
    local = jnp.where(on_item, item_local, member_local)
    high = local >> 8
    ids = jnp.concatenate([high, local - (high << 8), jnp.zeros((IDS - 2, rows), jnp.int32)], axis=0)
    ids = ids.astype(F32).astype(BF16)
    ids_out[...] = ids
    moves[4].wait()
    for chunk, k in zip(chunks, far):
        pack_chunk(k, capacity, place, ids, feats[...], chunk)


def rest_kernel(capacity, rest, place, ids, feats, *refs):
    chunks = refs[-len(rest) :]
    for chunk, k in zip(chunks, rest):
        pack_chunk(k, capacity, place[...], ids[...], feats[...], chunk)


def margin_kernel(place, weight, features, margin, copies, sems):
    parts = copies.shape[0]
    step = copies.shape[1]
    moves = [
        pltpu.make_async_copy(features.at[pl.ds(i * step, step)], copies.at[i], sems.at[i]) for i in range(parts)
    ]
    for move in moves:
        move.start()
    wide = jnp.broadcast_to(weight[...], (16, weight.shape[1])).astype(BF16)
    for i in range(parts):
        moves[i].wait()
        margin[:, i * step : (i + 1) * step] = lanes_dot(wide, copies[i])[0:1]


def chunk_ids(chunk, capacity):
    pair = chunk[capacity:, :capacity].astype(F32)
    return (pair[0:1] * 256.0 + pair[1:2]).astype(jnp.int32)


def chunk_scores(chunk, table, capacity):
    entities = table.shape[0] // 2
    every = lanes_dot(table, chunk[:capacity])
    hits = one_hot(chunk_ids(chunk, capacity), entities)
    return jnp.sum(jnp.where(hits, every[:entities] + every[entities:], 0.0), axis=0, keepdims=True)


def early_kernel(capacity, coefs, *refs):
    half = len(refs) // 2
    table = jnp.concatenate(halves(coefs[...]), axis=0)
    for chunk, out in zip(refs[:half], refs[half:]):
        out[...] = chunk_scores(chunk, table, capacity)


def scores_kernel(order, capacity, n_feat, n_ent, coefs, *refs):
    out, mine = refs[-1], lax.axis_index(HOME)
    table = jnp.concatenate(halves(coefs[...]), axis=0)
    scores = [
        x[...] if x.shape[0] == 1 else chunk_scores(x, table, capacity) for x in refs[:-1]
    ]
    scores = dict(zip(order, scores))
    scores = xor_rows(jnp.concatenate([scores[k] for k in range(len(order))], axis=0), mine)
    for home in range(len(order)):
        for f in range(n_feat):
            out[(home // n_ent * n_feat + f) * n_ent + home % n_ent] = scores[home : home + 1]


def home_kernel(
    owners, capacity, n_feat, n_ent, member, item, ranks, clicks, valid, margin, scores, features, out
):
    on_item = position(n_feat)[1]
    total = margin[...]
    hits_of = [one_hot(owner[...], owners).astype(F32) for owner in (member, item)]
    spot_of = [ones(low_hot(ranks[side : side + 1], capacity)) for side in (0, 1)]
    for side in (0, 1):
        table = None
        for f in range(side * n_feat // 2, (side + 1) * n_feat // 2):
            part = jnp.concatenate(
                [scores[(h // n_ent * n_feat + f) * n_ent + h % n_ent] for h in range(owners)], axis=0
            )
            table = part if table is None else table + part
        found = plain_dot(jnp.concatenate(halves(table), axis=0), spot_of[side])
        total = total + jnp.sum((found[:owners] + found[owners:]) * hits_of[side], axis=0, keepdims=True)
    resid = valid[...].astype(F32) * (jax.nn.sigmoid(total) - clicks[...].astype(F32))
    hits = jnp.where(on_item, hits_of[1], hits_of[0])
    spot = jnp.where(on_item, spot_of[1], spot_of[0])
    sent = lanes_dot(jnp.concatenate(halves(hits * resid), axis=0), spot)
    sent = sent[:owners] + sent[owners:]
    low = jnp.broadcast_to(resid, (16, resid.shape[1])).astype(BF16)
    grad = plain_dot(low, features[...])[0:1]
    for h in range(owners):
        out[h, :, :capacity] = sent[h : h + 1]
        out[h, :, capacity:] = grad


def grads_kernel(order, capacity, scale, coefs, weight, came, *refs):
    chunks, grad_global, grad_coefs = refs[:-2], refs[-2], refs[-1]
    entities = coefs.shape[0]
    mine = lax.axis_index(HOME)
    resids = xor_rows(jnp.concatenate([came[h][:, :capacity] for h in range(len(order))], axis=0), mine)
    summed = came[0][:, capacity:]
    for h in range(1, len(order)):
        summed = summed + came[h][:, capacity:]
    grad_global[...] = summed * scale + 4.0 * weight[...]
    highs, lows, feats = [], [], []
    for chunk, k in zip(chunks, order):
        here = chunk_ids(chunk, capacity)
        blocks = [low_hot(here - first, min(256, entities)) for first in range(0, entities, 256)]
        high, low = halves(resids[k : k + 1])
        highs.append(jnp.concatenate([jnp.where(hits, high, jnp.zeros((), BF16)) for hits in blocks], axis=0))
        lows.append(jnp.concatenate([jnp.where(hits, low, jnp.zeros((), BF16)) for hits in blocks], axis=0))
        feats.append(chunk[:capacity])
    spread = jnp.concatenate([jnp.concatenate(highs, axis=1), jnp.concatenate(lows, axis=1)], axis=0)
    both = plain_dot(spread, jnp.concatenate(feats, axis=0))
    grad_coefs[...] = coefs[...] + both[:entities] + both[entities:]


def xor_send(x, axes, size, k):
    return x if k == 0 else lax.ppermute(x, axes, [(i, i ^ k) for i in range(size)])


def call(kernel, out_shape, operands, in_specs, flops=0, scratch=(), hidden=False):
    moved = 0 if hidden else sum(x.size * x.dtype.itemsize for x in (*operands, *out_shape))
    return pl.pallas_call(
        kernel,
        out_shape=out_shape,
        in_specs=in_specs,
        out_specs=[VMEM] * len(out_shape),
        scratch_shapes=scratch,
        compiler_params=PARAMS,
        cost_estimate=pl.CostEstimate(flops=flops, bytes_accessed=moved, transcendentals=0),
    )(*operands)


def body(
    features,
    global_weight,
    entity_feats,
    coefs,
    member_owner,
    member_local,
    item_owner,
    item_local,
    clicks,
    valid,
):
    rows_here, width = entity_feats.shape
    columns = features.shape[1]
    n_feat, n_ent = lax.axis_size("feat"), lax.axis_size("ent")
    owners = lax.axis_size("rows") * n_ent
    capacity = 2 * rows_here // owners
    member, item = member_owner.reshape(1, rows_here), item_owner.reshape(1, rows_here)

    def shape(*dims, dtype=F32):
        return jax.ShapeDtypeStruct(dims, dtype)

    def partial(kernel, *args):
        return lambda *refs: kernel(*args, *refs)

    row = pltpu.VMEM((1, rows_here), jnp.int32)
    half, early = owners // 2, 3 * owners // 4
    first, second, near = list(range(half, early)), list(range(early, owners)), list(reversed(range(half)))
    chunk = shape(capacity + IDS, width, dtype=BF16)
    flops = len(first) * 2 * capacity * rows_here * width

    def in_hbm(x):
        return pltpu.with_memory_space_constraint(x, pltpu.HBM)

    ranks, place, ids, feats, *chunks = call(
        partial(far_kernel, owners, capacity, n_feat, first),
        [
            shape(2, rows_here, dtype=jnp.int32),
            shape(1, rows_here, dtype=jnp.int32),
            shape(IDS, rows_here, dtype=BF16),
            shape(rows_here, width, dtype=BF16),
        ]
        + [chunk] * len(first),
        (
            in_hbm(member),
            in_hbm(item),
            in_hbm(member_local.reshape(1, rows_here)),
            in_hbm(item_local.reshape(1, rows_here)),
            in_hbm(entity_feats),
        ),
        [HBM] * 5,
        flops=flops,
        scratch=[row, row, row, row, pltpu.SemaphoreType.DMA((5,))],
    )
    chunks += call(
        partial(rest_kernel, capacity, second),
        [chunk] * len(second),
        (place, ids, feats),
        [VMEM] * 3,
        flops=flops,
    )
    chunks = [xor_send(x, HOME, owners, k) for k, x in zip(first + second, chunks)]
    weight = global_weight.astype(F32).reshape(1, columns)
    parts = 4
    (global_part,) = call(
        margin_kernel,
        [shape(1, rows_here)],
        (place, weight, in_hbm(features)),
        [VMEM, VMEM, HBM],
        hidden=True,
        scratch=[pltpu.VMEM((parts, rows_here // parts, columns), BF16), pltpu.SemaphoreType.DMA((parts,))],
    )
    global_total = lax.psum(global_part, "feat")
    near_chunks = call(
        partial(rest_kernel, capacity, near),
        [chunk] * len(near),
        (place, ids, feats, global_total),
        [VMEM] * 4,
        hidden=True,
    )
    near_chunks = [xor_send(x, HOME, owners, k) for k, x in zip(near, near_chunks)]
    order = first + near[-1:] + second + near[:-1]
    chunks = chunks[: len(first)] + near_chunks[-1:] + chunks[len(first) :] + near_chunks[:-1]
    came_early = len(first) + 1
    scores = call(
        partial(early_kernel, capacity),
        [shape(1, capacity)] * came_early,
        (coefs, *chunks[:came_early]),
        [VMEM] * (1 + came_early),
        hidden=True,
    )
    (scores,) = call(
        partial(scores_kernel, order, capacity, n_feat, n_ent),
        [shape(n_feat * owners, 1, capacity)],
        (coefs, *scores, *chunks[came_early:]),
        [VMEM] * (1 + owners),
        flops=16 * coefs.size * owners * capacity,
    )
    returned = lax.all_to_all(scores, EVERY, split_axis=0, concat_axis=0, tiled=True)
    (sent,) = call(
        partial(home_kernel, owners, capacity, n_feat, n_ent),
        [shape(owners, 1, capacity + columns)],
        (
            member,
            item,
            ranks,
            clicks.reshape(1, rows_here),
            valid.reshape(1, rows_here),
            global_total,
            returned,
            features,
        ),
        [VMEM] * 8,
        flops=32 * features.size,
    )
    came = lax.all_to_all(sent, HOME, split_axis=0, concat_axis=0, tiled=True)
    grad_global, grad_coefs = call(
        partial(grads_kernel, order, capacity, 1.0 / math.sqrt(rows_here * owners)),
        [shape(1, columns), shape(*coefs.shape)],
        (coefs, weight, came, *chunks),
        [VMEM] * (3 + owners),
        flops=4 * coefs.size * owners * capacity,
    )
    return (grad_global.reshape(columns), grad_coefs)


def solution(mesh):
    by_row = P(("groups", "rows", "ent"))
    by_both = P(("groups", "rows", "ent"), "feat")
    column = P(("groups", "rows", "ent"), None)
    by_feat = P(("groups", "feat"))
    return jax.shard_map(
        body,
        mesh=mesh,
        in_specs=(by_both, by_feat, by_both, by_both, column, by_row, column, by_row, by_row, by_row),
        out_specs=(by_feat, by_both),
        check_vma=False,
    )
```

```python
import math

import jax
import jax.numpy as jnp
from jax import lax
from jax.experimental import pallas as pl
from jax.experimental.pallas import tpu as pltpu
from jax.sharding import PartitionSpec as P

F32 = jnp.float32
BF16 = jnp.bfloat16
HOME = ("rows", "ent")
EVERY = ("rows", "feat", "ent")
IDS = 8
PARAMS = pltpu.CompilerParams(vmem_limit_bytes=24 * 2**20)
VMEM = pl.BlockSpec(memory_space=pltpu.VMEM)
HBM = pl.BlockSpec(memory_space=pltpu.HBM)


def lanes_dot(a, b):
    return lax.dot_general(a, b, (((1,), (1,)), ((), ())), preferred_element_type=F32)


def plain_dot(a, b):
    return lax.dot_general(a, b, (((1,), (0,)), ((), ())), preferred_element_type=F32)


def halves(x):
    high = x.astype(BF16)
    return high, (x - high.astype(F32)).astype(BF16)


def one_hot(row, count):
    return row == lax.broadcasted_iota(jnp.int32, (count, row.shape[1]), 0)


def low_hot(row, count):
    row = jnp.where((row >= 0) & (row < count), row, -1).astype(F32).astype(BF16)
    return row == lax.broadcasted_iota(jnp.int32, (count, row.shape[1]), 0).astype(F32).astype(BF16)


def ones(mask):
    return jnp.where(mask, jnp.ones((), BF16), jnp.zeros((), BF16))


def xor_rows(rows, mine):
    count = rows.shape[0]
    bit = 1
    while bit < count:
        swapped = jnp.concatenate([rows[(k ^ bit) : (k ^ bit) + 1] for k in range(count)], axis=0)
        rows = jnp.where((mine & bit) > 0, swapped, rows)
        bit *= 2
    return rows


def ranks_of(owners, member, item):
    rows = member.shape[1]
    step = min(256, rows)
    blocks = rows // step
    hits = jnp.concatenate([one_hot(member, owners).astype(F32), one_hot(item, owners).astype(F32)], axis=0)
    stacked = jnp.concatenate([hits[:, b * step : (b + 1) * step] for b in range(blocks)], axis=0)
    upper = lax.broadcasted_iota(jnp.int32, (step, step), 0) <= lax.broadcasted_iota(
        jnp.int32, (step, step), 1
    )
    counts = plain_dot(stacked.astype(BF16), upper.astype(F32).astype(BF16))
    before = jnp.zeros((2 * owners, 1), F32)
    pieces = []
    for b in range(blocks):
        here = counts[2 * owners * b : 2 * owners * (b + 1)]
        taken = (here + before) * hits[:, b * step : (b + 1) * step]
        sides = [jnp.sum(x, axis=0, keepdims=True) for x in (taken[:owners], taken[owners:])]
        pieces.append(jnp.concatenate(sides, axis=0))
        before = before + here[:, step - 1 : step]
    return jnp.concatenate(pieces, axis=1).astype(jnp.int32) - 1


def pack_chunk(k, capacity, place, ids, feats, chunk):
    pick = ones(low_hot(place - k * capacity, capacity))
    chunk[:capacity] = plain_dot(pick, feats).astype(BF16)
    chunk[capacity:, :capacity] = lanes_dot(ids, pick).astype(BF16)


def position(n_feat):
    return lax.axis_index(HOME), lax.axis_index("feat") >= n_feat // 2


def far_kernel(owners, capacity, n_feat, far, *refs):
    sources, ranks, place_out, ids_out, feats = refs[:5], refs[5], refs[6], refs[7], refs[8]
    chunks, copies, sems = refs[9 : 9 + len(far)], refs[9 + len(far) : 13 + len(far)], refs[13 + len(far)]
    copies = (*copies, feats)
    moves = [pltpu.make_async_copy(sources[i], copies[i], sems.at[i]) for i in range(5)]
    for move in moves:
        move.start()
    for move in moves[:4]:
        move.wait()
    member, item, member_local, item_local = [copy[...] for copy in copies[:4]]
    rows = member.shape[1]
    mine, on_item = position(n_feat)
    rank = ranks_of(owners, member, item)
    ranks[...] = rank
    own = jnp.where(on_item, item, member)
    place = (own ^ mine) * capacity + jnp.where(on_item, rank[1:2], rank[0:1])
    place_out[...] = place
    local = jnp.where(on_item, item_local, member_local)
    high = local >> 8
    ids = jnp.concatenate([high, local - (high << 8), jnp.zeros((IDS - 2, rows), jnp.int32)], axis=0)
    ids = ids.astype(F32).astype(BF16)
    ids_out[...] = ids
    moves[4].wait()
    for chunk, k in zip(chunks, far):
        pack_chunk(k, capacity, place, ids, feats[...], chunk)


def rest_kernel(capacity, rest, place, ids, feats, *refs):
    chunks = refs[-len(rest) :]
    for chunk, k in zip(chunks, rest):
        pack_chunk(k, capacity, place[...], ids[...], feats[...], chunk)


def margin_kernel(place, weight, features, margin, copies, sems):
    parts, step = copies.shape[0], copies.shape[1]
    moves = [
        pltpu.make_async_copy(features.at[pl.ds(i * step, step)], copies.at[i], sems.at[i]) for i in range(parts)
    ]
    for move in moves[:2]:
        move.start()
    wide = jnp.broadcast_to(weight[...], (16, weight.shape[1])).astype(BF16)
    for i in range(parts):
        moves[i].wait()
        if i + 2 < parts:
            moves[i + 2].start()
        margin[:, i * step : (i + 1) * step] = lanes_dot(wide, copies[i])[0:1]


def chunk_ids(chunk, capacity):
    pair = chunk[capacity:, :capacity].astype(F32)
    return (pair[0:1] * 256.0 + pair[1:2]).astype(jnp.int32)


def chunk_scores(chunk, table, capacity):
    entities = table.shape[0] // 2
    every = lanes_dot(table, chunk[:capacity])
    hits = one_hot(chunk_ids(chunk, capacity), entities)
    return jnp.sum(jnp.where(hits, every[:entities] + every[entities:], 0.0), axis=0, keepdims=True)


def early_kernel(capacity, coefs, *refs):
    half = len(refs) // 2
    table = jnp.concatenate(halves(coefs[...]), axis=0)
    for chunk, out in zip(refs[:half], refs[half:]):
        out[...] = chunk_scores(chunk, table, capacity)


def scores_kernel(order, capacity, n_feat, n_ent, coefs, *refs):
    out, mine = refs[-1], lax.axis_index(HOME)
    table = jnp.concatenate(halves(coefs[...]), axis=0)
    scores = [
        x[...] if x.shape[0] == 1 else chunk_scores(x, table, capacity) for x in refs[:-1]
    ]
    scores = dict(zip(order, scores))
    scores = xor_rows(jnp.concatenate([scores[k] for k in range(len(order))], axis=0), mine)
    for home in range(len(order)):
        for f in range(n_feat):
            out[(home // n_ent * n_feat + f) * n_ent + home % n_ent] = scores[home : home + 1]


def home_kernel(
    owners, capacity, n_feat, n_ent, member, item, ranks, clicks, valid, margin, scores, features, out
):
    on_item = position(n_feat)[1]
    total = margin[...]
    hits_of = [one_hot(owner[...], owners).astype(F32) for owner in (member, item)]
    spot_of = [ones(low_hot(ranks[side : side + 1], capacity)) for side in (0, 1)]
    for side in (0, 1):
        table = None
        for f in range(side * n_feat // 2, (side + 1) * n_feat // 2):
            part = jnp.concatenate(
                [scores[(h // n_ent * n_feat + f) * n_ent + h % n_ent] for h in range(owners)], axis=0
            )
            table = part if table is None else table + part
        found = plain_dot(jnp.concatenate(halves(table), axis=0), spot_of[side])
        total = total + jnp.sum((found[:owners] + found[owners:]) * hits_of[side], axis=0, keepdims=True)
    resid = valid[...].astype(F32) * (jax.nn.sigmoid(total) - clicks[...].astype(F32))
    hits = jnp.where(on_item, hits_of[1], hits_of[0])
    spot = jnp.where(on_item, spot_of[1], spot_of[0])
    sent = lanes_dot(jnp.concatenate(halves(hits * resid), axis=0), spot)
    sent = sent[:owners] + sent[owners:]
    low = jnp.broadcast_to(resid, (16, resid.shape[1])).astype(BF16)
    grad = plain_dot(low, features[...])[0:1]
    for h in range(owners):
        out[h, :, :capacity] = sent[h : h + 1]
        out[h, :, capacity:] = grad


def grads_kernel(order, capacity, scale, coefs, weight, came, *refs):
    chunks, grad_global, grad_coefs, done, sems = refs[:-4], refs[-4], refs[-3], refs[-2], refs[-1]
    entities = coefs.shape[0]
    mine = lax.axis_index(HOME)
    resids = xor_rows(jnp.concatenate([came[h][:, :capacity] for h in range(len(order))], axis=0), mine)
    summed = came[0][:, capacity:]
    for h in range(1, len(order)):
        summed = summed + came[h][:, capacity:]
    grad_global[...] = summed * scale + 4.0 * weight[...]
    step = min(256, entities)
    feats = jnp.concatenate([chunk[:capacity] for chunk in chunks], axis=0)
    ids = jnp.concatenate([chunk_ids(chunk, capacity) for chunk in chunks], axis=1)
    high, low = halves(jnp.concatenate([resids[k : k + 1] for k in order], axis=1))
    moves = []
    for i in range(entities // step):
        hits = low_hot(ids - i * step, step)
        spread = [jnp.where(hits, part, jnp.zeros((), BF16)) for part in (high, low)]
        both = plain_dot(jnp.concatenate(spread, axis=0), feats)
        here = slice(i * step, (i + 1) * step)
        done[here] = coefs[here] + both[:step] + both[step:]
        moves.append(pltpu.make_async_copy(done.at[here], grad_coefs.at[here], sems.at[i]))
        moves[i].start()
    for move in moves:
        move.wait()


def xor_send(x, axes, size, k):
    return x if k == 0 else lax.ppermute(x, axes, [(i, i ^ k) for i in range(size)])


def call(kernel, out_shape, operands, in_specs, flops=0, scratch=(), hidden=False, out_specs=None):
    moved = 0 if hidden else sum(x.size * x.dtype.itemsize for x in (*operands, *out_shape))
    return pl.pallas_call(
        kernel,
        out_shape=out_shape,
        in_specs=in_specs,
        out_specs=out_specs or [VMEM] * len(out_shape),
        scratch_shapes=scratch,
        compiler_params=PARAMS,
        cost_estimate=pl.CostEstimate(flops=flops, bytes_accessed=moved, transcendentals=0),
    )(*operands)


def body(
    features,
    global_weight,
    entity_feats,
    coefs,
    member_owner,
    member_local,
    item_owner,
    item_local,
    clicks,
    valid,
):
    rows_here, width = entity_feats.shape
    columns = features.shape[1]
    n_feat, n_ent = lax.axis_size("feat"), lax.axis_size("ent")
    owners = lax.axis_size("rows") * n_ent
    capacity = 2 * rows_here // owners
    member, item = member_owner.reshape(1, rows_here), item_owner.reshape(1, rows_here)

    def shape(*dims, dtype=F32):
        return jax.ShapeDtypeStruct(dims, dtype)

    def partial(kernel, *args):
        return lambda *refs: kernel(*args, *refs)

    row = pltpu.VMEM((1, rows_here), jnp.int32)
    half = owners // 2
    first, second, near = [half], list(range(half + 1, owners)), list(reversed(range(half)))
    chunk = shape(capacity + IDS, width, dtype=BF16)
    flops = len(first) * 2 * capacity * rows_here * width

    def in_hbm(x):
        return pltpu.with_memory_space_constraint(x, pltpu.HBM)

    ranks, place, ids, feats, *chunks = call(
        partial(far_kernel, owners, capacity, n_feat, first),
        [
            shape(2, rows_here, dtype=jnp.int32),
            shape(1, rows_here, dtype=jnp.int32),
            shape(IDS, rows_here, dtype=BF16),
            shape(rows_here, width, dtype=BF16),
        ]
        + [chunk] * len(first),
        (
            in_hbm(member),
            in_hbm(item),
            in_hbm(member_local.reshape(1, rows_here)),
            in_hbm(item_local.reshape(1, rows_here)),
            in_hbm(entity_feats),
        ),
        [HBM] * 5,
        flops=flops,
        scratch=[row, row, row, row, pltpu.SemaphoreType.DMA((5,))],
    )
    chunks += call(
        partial(rest_kernel, capacity, second),
        [chunk] * len(second),
        (place, ids, feats),
        [VMEM] * 3,
        flops=flops,
    )
    chunks = [xor_send(x, HOME, owners, k) for k, x in zip(first + second, chunks)]
    weight = global_weight.astype(F32).reshape(1, columns)
    parts = 4
    (global_part,) = call(
        margin_kernel,
        [shape(1, rows_here)],
        (place, weight, in_hbm(features)),
        [VMEM, VMEM, HBM],
        hidden=True,
        scratch=[pltpu.VMEM((parts, rows_here // parts, columns), BF16), pltpu.SemaphoreType.DMA((parts,))],
    )
    global_total = lax.psum(global_part, "feat")
    near_chunks = call(
        partial(rest_kernel, capacity, near),
        [chunk] * len(near),
        (place, ids, feats, global_total),
        [VMEM] * 4,
        hidden=True,
    )
    near_chunks = [xor_send(x, HOME, owners, k) for k, x in zip(near, near_chunks)]
    chunks = dict(zip(first + second + near, chunks + near_chunks))
    early = (first + second)[: half // 2] + near[-1:]
    late = (first + second)[half // 2 :] + near[:-1]
    order = early + late
    scores = call(
        partial(early_kernel, capacity),
        [shape(1, capacity)] * len(early),
        (coefs, *(chunks[k] for k in early)),
        [VMEM] * (1 + len(early)),
        hidden=True,
    )
    (scores,) = call(
        partial(scores_kernel, order, capacity, n_feat, n_ent),
        [shape(n_feat * owners, 1, capacity)],
        (coefs, *scores, *(chunks[k] for k in late)),
        [VMEM] * (1 + owners),
        flops=16 * coefs.size * owners * capacity,
    )
    returned = lax.all_to_all(scores, EVERY, split_axis=0, concat_axis=0, tiled=True)
    (sent,) = call(
        partial(home_kernel, owners, capacity, n_feat, n_ent),
        [shape(owners, 1, capacity + columns)],
        (
            member,
            item,
            ranks,
            clicks.reshape(1, rows_here),
            valid.reshape(1, rows_here),
            global_total,
            returned,
            features,
        ),
        [VMEM] * 8,
        flops=32 * features.size,
    )
    came = lax.all_to_all(sent, HOME, split_axis=0, concat_axis=0, tiled=True)
    grad_global, grad_coefs = call(
        partial(grads_kernel, order, capacity, 1.0 / math.sqrt(rows_here * owners)),
        [shape(1, columns), shape(*coefs.shape)],
        (coefs, weight, came, *(chunks[k] for k in order)),
        [VMEM] * (3 + owners),
        out_specs=[VMEM, HBM],
        scratch=[pltpu.VMEM(coefs.shape, F32), pltpu.SemaphoreType.DMA((-(-coefs.shape[0] // 256),))],
        flops=4 * coefs.size * owners * capacity,
    )
    return (grad_global.reshape(columns), grad_coefs)


def solution(mesh):
    by_row = P(("groups", "rows", "ent"))
    by_both = P(("groups", "rows", "ent"), "feat")
    column = P(("groups", "rows", "ent"), None)
    by_feat = P(("groups", "feat"))
    return jax.shard_map(
        body,
        mesh=mesh,
        in_specs=(by_both, by_feat, by_both, by_both, column, by_row, column, by_row, by_row, by_row),
        out_specs=(by_feat, by_both),
        check_vma=False,
    )
```

```python
import math

import jax
import jax.numpy as jnp
from jax import lax
from jax.experimental import pallas as pl
from jax.experimental.pallas import tpu as pltpu
from jax.sharding import PartitionSpec as P

F32 = jnp.float32
BF16 = jnp.bfloat16
HOME = ("rows", "ent")
EVERY = ("rows", "feat", "ent")
IDS = 8
PARAMS = pltpu.CompilerParams(vmem_limit_bytes=24 * 2**20)
VMEM = pl.BlockSpec(memory_space=pltpu.VMEM)
HBM = pl.BlockSpec(memory_space=pltpu.HBM)


def lanes_dot(a, b):
    return lax.dot_general(a, b, (((1,), (1,)), ((), ())), preferred_element_type=F32)


def plain_dot(a, b):
    return lax.dot_general(a, b, (((1,), (0,)), ((), ())), preferred_element_type=F32)


def halves(x):
    high = x.astype(BF16)
    return high, (x - high.astype(F32)).astype(BF16)


def one_hot(row, count):
    return row == lax.broadcasted_iota(jnp.int32, (count, row.shape[1]), 0)


def low_hot(row, count):
    row = jnp.where((row >= 0) & (row < count), row, -1).astype(F32).astype(BF16)
    return row == lax.broadcasted_iota(jnp.int32, (count, row.shape[1]), 0).astype(F32).astype(BF16)


def ones(mask):
    return jnp.where(mask, jnp.ones((), BF16), jnp.zeros((), BF16))


def xor_rows(rows, mine):
    count = rows.shape[0]
    bit = 1
    while bit < count:
        swapped = jnp.concatenate([rows[(k ^ bit) : (k ^ bit) + 1] for k in range(count)], axis=0)
        rows = jnp.where((mine & bit) > 0, swapped, rows)
        bit *= 2
    return rows


def ranks_of(owners, member, item):
    rows = member.shape[1]
    step = min(256, rows)
    blocks = rows // step
    hits = jnp.concatenate([one_hot(member, owners).astype(F32), one_hot(item, owners).astype(F32)], axis=0)
    stacked = jnp.concatenate([hits[:, b * step : (b + 1) * step] for b in range(blocks)], axis=0)
    upper = lax.broadcasted_iota(jnp.int32, (step, step), 0) <= lax.broadcasted_iota(
        jnp.int32, (step, step), 1
    )
    counts = plain_dot(stacked.astype(BF16), upper.astype(F32).astype(BF16))
    before = jnp.zeros((2 * owners, 1), F32)
    pieces = []
    for b in range(blocks):
        here = counts[2 * owners * b : 2 * owners * (b + 1)]
        taken = (here + before) * hits[:, b * step : (b + 1) * step]
        sides = [jnp.sum(x, axis=0, keepdims=True) for x in (taken[:owners], taken[owners:])]
        pieces.append(jnp.concatenate(sides, axis=0))
        before = before + here[:, step - 1 : step]
    return jnp.concatenate(pieces, axis=1).astype(jnp.int32) - 1


def pack_chunk(k, capacity, place, ids, feats, chunk):
    pick = ones(low_hot(place - k * capacity, capacity))
    chunk[:capacity] = plain_dot(pick, feats).astype(BF16)
    chunk[capacity:, :capacity] = lanes_dot(ids, pick).astype(BF16)


def position(n_feat):
    return lax.axis_index(HOME), lax.axis_index("feat") >= n_feat // 2


def far_kernel(owners, capacity, n_feat, far, *refs):
    sources, ranks, place_out, ids_out, feats = refs[:5], refs[5], refs[6], refs[7], refs[8]
    chunks, copies, sems = refs[9 : 9 + len(far)], refs[9 + len(far) : 13 + len(far)], refs[13 + len(far)]
    copies = (*copies, feats)
    moves = [pltpu.make_async_copy(sources[i], copies[i], sems.at[i]) for i in range(5)]
    for move in moves:
        move.start()
    for move in moves[:4]:
        move.wait()
    member, item, member_local, item_local = [copy[...] for copy in copies[:4]]
    rows = member.shape[1]
    mine, on_item = position(n_feat)
    rank = ranks_of(owners, member, item)
    ranks[...] = rank
    own = jnp.where(on_item, item, member)
    place = (own ^ mine) * capacity + jnp.where(on_item, rank[1:2], rank[0:1])
    place_out[...] = place
    local = jnp.where(on_item, item_local, member_local)
    high = local >> 8
    ids = jnp.concatenate([high, local - (high << 8), jnp.zeros((IDS - 2, rows), jnp.int32)], axis=0)
    ids = ids.astype(F32).astype(BF16)
    ids_out[...] = ids
    moves[4].wait()
    for chunk, k in zip(chunks, far):
        pack_chunk(k, capacity, place, ids, feats[...], chunk)


def rest_kernel(capacity, rest, place, ids, feats, *refs):
    chunks = refs[-len(rest) :]
    for chunk, k in zip(chunks, rest):
        pack_chunk(k, capacity, place[...], ids[...], feats[...], chunk)


def margin_kernel(place, weight, features, margin, copies, sems):
    parts, step = copies.shape[0], copies.shape[1]
    moves = [
        pltpu.make_async_copy(features.at[pl.ds(i * step, step)], copies.at[i], sems.at[i]) for i in range(parts)
    ]
    for move in moves[:2]:
        move.start()
    wide = jnp.broadcast_to(weight[...], (16, weight.shape[1])).astype(BF16)
    for i in range(parts):
        moves[i].wait()
        if i + 2 < parts:
            moves[i + 2].start()
        margin[:, i * step : (i + 1) * step] = lanes_dot(wide, copies[i])[0:1]


def chunk_ids(chunk, capacity):
    pair = chunk[capacity:, :capacity].astype(F32)
    return (pair[0:1] * 256.0 + pair[1:2]).astype(jnp.int32)


def chunk_scores(chunk, table, capacity):
    entities = table.shape[0] // 2
    every = lanes_dot(table, chunk[:capacity])
    hits = one_hot(chunk_ids(chunk, capacity), entities)
    return jnp.sum(jnp.where(hits, every[:entities] + every[entities:], 0.0), axis=0, keepdims=True)


def early_kernel(capacity, coefs, *refs):
    half = len(refs) // 2
    kept = refs[half]
    entities = coefs.shape[0]
    kept[:entities], kept[entities:] = halves(coefs[...])
    table = kept[...]
    for chunk, out in zip(refs[:half], refs[half + 1 :]):
        out[...] = chunk_scores(chunk, table, capacity)


def scores_kernel(order, capacity, n_feat, n_ent, table, *refs):
    out, mine = refs[-1], lax.axis_index(HOME)
    scores = [x[...] if x.shape[0] == 1 else chunk_scores(x, table[...], capacity) for x in refs[:-1]]
    scores = dict(zip(order, scores))
    scores = xor_rows(jnp.concatenate([scores[k] for k in range(len(order))], axis=0), mine)
    for home in range(len(order)):
        for f in range(n_feat):
            out[(home // n_ent * n_feat + f) * n_ent + home % n_ent] = scores[home : home + 1]


def home_kernel(
    owners, capacity, n_feat, n_ent, member, item, ranks, clicks, valid, margin, scores, features, out
):
    on_item = position(n_feat)[1]
    total = margin[...]
    hits_of = [one_hot(owner[...], owners).astype(F32) for owner in (member, item)]
    spot_of = [ones(low_hot(ranks[side : side + 1], capacity)) for side in (0, 1)]
    for side in (0, 1):
        table = None
        for f in range(side * n_feat // 2, (side + 1) * n_feat // 2):
            part = jnp.concatenate(
                [scores[(h // n_ent * n_feat + f) * n_ent + h % n_ent] for h in range(owners)], axis=0
            )
            table = part if table is None else table + part
        found = plain_dot(jnp.concatenate(halves(table), axis=0), spot_of[side])
        total = total + jnp.sum((found[:owners] + found[owners:]) * hits_of[side], axis=0, keepdims=True)
    resid = valid[...].astype(F32) * (jax.nn.sigmoid(total) - clicks[...].astype(F32))
    hits = jnp.where(on_item, hits_of[1], hits_of[0])
    spot = jnp.where(on_item, spot_of[1], spot_of[0])
    sent = lanes_dot(jnp.concatenate(halves(hits * resid), axis=0), spot)
    sent = sent[:owners] + sent[owners:]
    low = jnp.broadcast_to(resid, (16, resid.shape[1])).astype(BF16)
    grad = plain_dot(low, features[...])[0:1]
    for h in range(owners):
        out[h, :, :capacity] = sent[h : h + 1]
        out[h, :, capacity:] = grad


def grads_kernel(order, capacity, scale, coefs, weight, came, *refs):
    chunks, grad_global, grad_coefs = refs[:-2], refs[-2], refs[-1]
    entities = coefs.shape[0]
    mine = lax.axis_index(HOME)
    resids = xor_rows(jnp.concatenate([came[h][:, :capacity] for h in range(len(order))], axis=0), mine)
    summed = came[0][:, capacity:]
    for h in range(1, len(order)):
        summed = summed + came[h][:, capacity:]
    grad_global[...] = summed * scale + 4.0 * weight[...]
    highs, lows, feats = [], [], []
    for chunk, k in zip(chunks, order):
        here = chunk_ids(chunk, capacity)
        blocks = [low_hot(here - first, min(256, entities)) for first in range(0, entities, 256)]
        high, low = halves(resids[k : k + 1])
        highs.append(jnp.concatenate([jnp.where(hits, high, jnp.zeros((), BF16)) for hits in blocks], axis=0))
        lows.append(jnp.concatenate([jnp.where(hits, low, jnp.zeros((), BF16)) for hits in blocks], axis=0))
        feats.append(chunk[:capacity])
    spread = jnp.concatenate([jnp.concatenate(highs, axis=1), jnp.concatenate(lows, axis=1)], axis=0)
    both = plain_dot(spread, jnp.concatenate(feats, axis=0))
    grad_coefs[...] = coefs[...] + both[:entities] + both[entities:]


def xor_send(x, axes, size, k):
    return x if k == 0 else lax.ppermute(x, axes, [(i, i ^ k) for i in range(size)])


def call(kernel, out_shape, operands, in_specs, flops=0, scratch=(), hidden=False):
    moved = 0 if hidden else sum(x.size * x.dtype.itemsize for x in (*operands, *out_shape))
    return pl.pallas_call(
        kernel,
        out_shape=out_shape,
        in_specs=in_specs,
        out_specs=[VMEM] * len(out_shape),
        scratch_shapes=scratch,
        compiler_params=PARAMS,
        cost_estimate=pl.CostEstimate(flops=flops, bytes_accessed=moved, transcendentals=0),
    )(*operands)


def body(
    features,
    global_weight,
    entity_feats,
    coefs,
    member_owner,
    member_local,
    item_owner,
    item_local,
    clicks,
    valid,
):
    rows_here, width = entity_feats.shape
    columns = features.shape[1]
    n_feat, n_ent = lax.axis_size("feat"), lax.axis_size("ent")
    owners = lax.axis_size("rows") * n_ent
    capacity = 2 * rows_here // owners
    member, item = member_owner.reshape(1, rows_here), item_owner.reshape(1, rows_here)

    def shape(*dims, dtype=F32):
        return jax.ShapeDtypeStruct(dims, dtype)

    def partial(kernel, *args):
        return lambda *refs: kernel(*args, *refs)

    row = pltpu.VMEM((1, rows_here), jnp.int32)
    half = owners // 2
    first, second, near = [half], list(range(half + 1, owners)), list(reversed(range(half)))
    chunk = shape(capacity + IDS, width, dtype=BF16)
    flops = len(first) * 2 * capacity * rows_here * width

    def in_hbm(x):
        return pltpu.with_memory_space_constraint(x, pltpu.HBM)

    ranks, place, ids, feats, *chunks = call(
        partial(far_kernel, owners, capacity, n_feat, first),
        [
            shape(2, rows_here, dtype=jnp.int32),
            shape(1, rows_here, dtype=jnp.int32),
            shape(IDS, rows_here, dtype=BF16),
            shape(rows_here, width, dtype=BF16),
        ]
        + [chunk] * len(first),
        (
            in_hbm(member),
            in_hbm(item),
            in_hbm(member_local.reshape(1, rows_here)),
            in_hbm(item_local.reshape(1, rows_here)),
            in_hbm(entity_feats),
        ),
        [HBM] * 5,
        flops=flops,
        scratch=[row, row, row, row, pltpu.SemaphoreType.DMA((5,))],
    )
    chunks += call(
        partial(rest_kernel, capacity, second),
        [chunk] * len(second),
        (place, ids, feats),
        [VMEM] * 3,
        flops=flops,
    )
    chunks = [xor_send(x, HOME, owners, k) for k, x in zip(first + second, chunks)]
    weight = global_weight.astype(F32).reshape(1, columns)
    parts = 4
    (global_part,) = call(
        margin_kernel,
        [shape(1, rows_here)],
        (place, weight, in_hbm(features)),
        [VMEM, VMEM, HBM],
        hidden=True,
        scratch=[pltpu.VMEM((parts, rows_here // parts, columns), BF16), pltpu.SemaphoreType.DMA((parts,))],
    )
    global_total = lax.psum(global_part, "feat")
    near_chunks = call(
        partial(rest_kernel, capacity, near),
        [chunk] * len(near),
        (place, ids, feats, global_total),
        [VMEM] * 4,
        hidden=True,
    )
    near_chunks = [xor_send(x, HOME, owners, k) for k, x in zip(near, near_chunks)]
    chunks = dict(zip(first + second + near, chunks + near_chunks))
    early = (first + second)[: half // 2] + near[-1:]
    late = (first + second)[half // 2 :] + near[:-1]
    order = early + late
    table, *scores = call(
        partial(early_kernel, capacity),
        [shape(2 * coefs.shape[0], width, dtype=BF16)] + [shape(1, capacity)] * len(early),
        (coefs, *(chunks[k] for k in early)),
        [VMEM] * (1 + len(early)),
        hidden=True,
    )
    (scores,) = call(
        partial(scores_kernel, order, capacity, n_feat, n_ent),
        [shape(n_feat * owners, 1, capacity)],
        (table, *scores, *(chunks[k] for k in late)),
        [VMEM] * (1 + owners),
        flops=16 * coefs.size * owners * capacity,
    )
    returned = lax.all_to_all(scores, EVERY, split_axis=0, concat_axis=0, tiled=True)
    (sent,) = call(
        partial(home_kernel, owners, capacity, n_feat, n_ent),
        [shape(owners, 1, capacity + columns)],
        (
            member,
            item,
            ranks,
            clicks.reshape(1, rows_here),
            valid.reshape(1, rows_here),
            global_total,
            returned,
            features,
        ),
        [VMEM] * 8,
        flops=32 * features.size,
    )
    came = lax.all_to_all(sent, HOME, split_axis=0, concat_axis=0, tiled=True)
    grad_global, grad_coefs = call(
        partial(grads_kernel, order, capacity, 1.0 / math.sqrt(rows_here * owners)),
        [shape(1, columns), shape(*coefs.shape)],
        (coefs, weight, came, *(chunks[k] for k in order)),
        [VMEM] * (3 + owners),
        flops=4 * coefs.size * owners * capacity,
    )
    return (grad_global.reshape(columns), grad_coefs)


def solution(mesh):
    by_row = P(("groups", "rows", "ent"))
    by_both = P(("groups", "rows", "ent"), "feat")
    column = P(("groups", "rows", "ent"), None)
    by_feat = P(("groups", "feat"))
    return jax.shard_map(
        body,
        mesh=mesh,
        in_specs=(by_both, by_feat, by_both, by_both, column, by_row, column, by_row, by_row, by_row),
        out_specs=(by_feat, by_both),
        check_vma=False,
    )
```

```python
import math

import jax
import jax.numpy as jnp
from jax import lax
from jax.experimental import pallas as pl
from jax.experimental.pallas import tpu as pltpu
from jax.sharding import PartitionSpec as P

F32 = jnp.float32
BF16 = jnp.bfloat16
HOME = ("rows", "ent")
EVERY = ("rows", "feat", "ent")
IDS = 8
PARAMS = pltpu.CompilerParams(vmem_limit_bytes=24 * 2**20)
VMEM = pl.BlockSpec(memory_space=pltpu.VMEM)
HBM = pl.BlockSpec(memory_space=pltpu.HBM)


def lanes_dot(a, b):
    return lax.dot_general(a, b, (((1,), (1,)), ((), ())), preferred_element_type=F32)


def plain_dot(a, b):
    return lax.dot_general(a, b, (((1,), (0,)), ((), ())), preferred_element_type=F32)


def halves(x):
    high = x.astype(BF16)
    return high, (x - high.astype(F32)).astype(BF16)


def one_hot(row, count):
    return row == lax.broadcasted_iota(jnp.int32, (count, row.shape[1]), 0)


def low_hot(row, count):
    row = jnp.where((row >= 0) & (row < count), row, -1).astype(F32).astype(BF16)
    return row == lax.broadcasted_iota(jnp.int32, (count, row.shape[1]), 0).astype(F32).astype(BF16)


def ones(mask):
    return jnp.where(mask, jnp.ones((), BF16), jnp.zeros((), BF16))


def xor_rows(rows, mine):
    count = rows.shape[0]
    bit = 1
    while bit < count:
        swapped = jnp.concatenate([rows[(k ^ bit) : (k ^ bit) + 1] for k in range(count)], axis=0)
        rows = jnp.where((mine & bit) > 0, swapped, rows)
        bit *= 2
    return rows


def ranks_of(owners, member, item):
    rows = member.shape[1]
    step = min(256, rows)
    blocks = rows // step
    hits = jnp.concatenate([one_hot(member, owners).astype(F32), one_hot(item, owners).astype(F32)], axis=0)
    stacked = jnp.concatenate([hits[:, b * step : (b + 1) * step] for b in range(blocks)], axis=0)
    upper = lax.broadcasted_iota(jnp.int32, (step, step), 0) <= lax.broadcasted_iota(
        jnp.int32, (step, step), 1
    )
    counts = plain_dot(stacked.astype(BF16), upper.astype(F32).astype(BF16))
    before = jnp.zeros((2 * owners, 1), F32)
    pieces = []
    for b in range(blocks):
        here = counts[2 * owners * b : 2 * owners * (b + 1)]
        taken = (here + before) * hits[:, b * step : (b + 1) * step]
        sides = [jnp.sum(x, axis=0, keepdims=True) for x in (taken[:owners], taken[owners:])]
        pieces.append(jnp.concatenate(sides, axis=0))
        before = before + here[:, step - 1 : step]
    return jnp.concatenate(pieces, axis=1).astype(jnp.int32) - 1


def pack_chunk(k, capacity, place, ids, feats, chunk):
    pick = ones(low_hot(place - k * capacity, capacity))
    chunk[:capacity] = plain_dot(pick, feats).astype(BF16)
    chunk[capacity:, :capacity] = lanes_dot(ids, pick).astype(BF16)


def position(n_feat):
    return lax.axis_index(HOME), lax.axis_index("feat") >= n_feat // 2


def far_kernel(owners, capacity, n_feat, far, *refs):
    sources, ranks, place_out, ids_out, feats = refs[:5], refs[5], refs[6], refs[7], refs[8]
    chunks, copies, sems = refs[9 : 9 + len(far)], refs[9 + len(far) : 13 + len(far)], refs[13 + len(far)]
    copies = (*copies, feats)
    moves = [pltpu.make_async_copy(sources[i], copies[i], sems.at[i]) for i in range(5)]
    for move in moves:
        move.start()
    for move in moves[:4]:
        move.wait()
    member, item, member_local, item_local = [copy[...] for copy in copies[:4]]
    rows = member.shape[1]
    mine, on_item = position(n_feat)
    rank = ranks_of(owners, member, item)
    ranks[...] = rank
    own = jnp.where(on_item, item, member)
    place = (own ^ mine) * capacity + jnp.where(on_item, rank[1:2], rank[0:1])
    place_out[...] = place
    local = jnp.where(on_item, item_local, member_local)
    high = local >> 8
    ids = jnp.concatenate([high, local - (high << 8), jnp.zeros((IDS - 2, rows), jnp.int32)], axis=0)
    ids = ids.astype(F32).astype(BF16)
    ids_out[...] = ids
    moves[4].wait()
    for chunk, k in zip(chunks, far):
        pack_chunk(k, capacity, place, ids, feats[...], chunk)


def rest_kernel(capacity, rest, place, ids, feats, *refs):
    chunks = refs[-len(rest) :]
    for chunk, k in zip(chunks, rest):
        pack_chunk(k, capacity, place[...], ids[...], feats[...], chunk)


def margin_kernel(place, weight, features, margin):
    wide = jnp.broadcast_to(weight[...], (16, weight.shape[1])).astype(BF16)
    margin[...] = lanes_dot(wide, features[...])[0:1]


def chunk_ids(chunk, capacity):
    pair = chunk[capacity:, :capacity].astype(F32)
    return (pair[0:1] * 256.0 + pair[1:2]).astype(jnp.int32)


def chunk_scores(chunk, table, capacity):
    entities = table.shape[0] // 2
    every = lanes_dot(table, chunk[:capacity])
    hits = one_hot(chunk_ids(chunk, capacity), entities)
    return jnp.sum(jnp.where(hits, every[:entities] + every[entities:], 0.0), axis=0, keepdims=True)


def early_kernel(capacity, coefs, *refs):
    half = len(refs) // 2
    kept = refs[half]
    entities = coefs.shape[0]
    kept[:entities], kept[entities:] = halves(coefs[...])
    table = kept[...]
    for chunk, out in zip(refs[:half], refs[half + 1 :]):
        out[...] = chunk_scores(chunk, table, capacity)


def scores_kernel(order, capacity, n_feat, n_ent, table, *refs):
    out, mine = refs[-1], lax.axis_index(HOME)
    scores = [x[...] if x.shape[0] == 1 else chunk_scores(x, table[...], capacity) for x in refs[:-1]]
    scores = dict(zip(order, scores))
    scores = xor_rows(jnp.concatenate([scores[k] for k in range(len(order))], axis=0), mine)
    for home in range(len(order)):
        for f in range(n_feat):
            out[(home // n_ent * n_feat + f) * n_ent + home % n_ent] = scores[home : home + 1]


def home_kernel(
    owners, capacity, n_feat, n_ent, member, item, ranks, clicks, valid, margin, scores, features, out
):
    on_item = position(n_feat)[1]
    total = margin[...]
    hits_of = [one_hot(owner[...], owners).astype(F32) for owner in (member, item)]
    spot_of = [ones(low_hot(ranks[side : side + 1], capacity)) for side in (0, 1)]
    for side in (0, 1):
        table = None
        for f in range(side * n_feat // 2, (side + 1) * n_feat // 2):
            part = jnp.concatenate(
                [scores[(h // n_ent * n_feat + f) * n_ent + h % n_ent] for h in range(owners)], axis=0
            )
            table = part if table is None else table + part
        found = plain_dot(jnp.concatenate(halves(table), axis=0), spot_of[side])
        total = total + jnp.sum((found[:owners] + found[owners:]) * hits_of[side], axis=0, keepdims=True)
    resid = valid[...].astype(F32) * (jax.nn.sigmoid(total) - clicks[...].astype(F32))
    hits = jnp.where(on_item, hits_of[1], hits_of[0])
    spot = jnp.where(on_item, spot_of[1], spot_of[0])
    sent = lanes_dot(jnp.concatenate(halves(hits * resid), axis=0), spot)
    sent = sent[:owners] + sent[owners:]
    low = jnp.broadcast_to(resid, (16, resid.shape[1])).astype(BF16)
    grad = plain_dot(low, features[...])[0:1]
    for h in range(owners):
        out[h, :, :capacity] = sent[h : h + 1]
        out[h, :, capacity:] = grad


def grads_kernel(order, capacity, scale, coefs, weight, came, *refs):
    chunks, grad_global, grad_coefs = refs[:-2], refs[-2], refs[-1]
    entities = coefs.shape[0]
    mine = lax.axis_index(HOME)
    resids = xor_rows(jnp.concatenate([came[h][:, :capacity] for h in range(len(order))], axis=0), mine)
    summed = came[0][:, capacity:]
    for h in range(1, len(order)):
        summed = summed + came[h][:, capacity:]
    grad_global[...] = summed * scale + 4.0 * weight[...]
    highs, lows, feats = [], [], []
    for chunk, k in zip(chunks, order):
        here = chunk_ids(chunk, capacity)
        blocks = [low_hot(here - first, min(256, entities)) for first in range(0, entities, 256)]
        high, low = halves(resids[k : k + 1])
        highs.append(jnp.concatenate([jnp.where(hits, high, jnp.zeros((), BF16)) for hits in blocks], axis=0))
        lows.append(jnp.concatenate([jnp.where(hits, low, jnp.zeros((), BF16)) for hits in blocks], axis=0))
        feats.append(chunk[:capacity])
    spread = jnp.concatenate([jnp.concatenate(highs, axis=1), jnp.concatenate(lows, axis=1)], axis=0)
    both = plain_dot(spread, jnp.concatenate(feats, axis=0))
    grad_coefs[...] = coefs[...] + both[:entities] + both[entities:]


def xor_send(x, axes, size, k):
    return x if k == 0 else lax.ppermute(x, axes, [(i, i ^ k) for i in range(size)])


def call(kernel, out_shape, operands, in_specs, flops=0, scratch=(), hidden=False):
    moved = 0 if hidden else sum(x.size * x.dtype.itemsize for x in (*operands, *out_shape))
    return pl.pallas_call(
        kernel,
        out_shape=out_shape,
        in_specs=in_specs,
        out_specs=[VMEM] * len(out_shape),
        scratch_shapes=scratch,
        compiler_params=PARAMS,
        cost_estimate=pl.CostEstimate(flops=flops, bytes_accessed=moved, transcendentals=0),
    )(*operands)


def body(
    features,
    global_weight,
    entity_feats,
    coefs,
    member_owner,
    member_local,
    item_owner,
    item_local,
    clicks,
    valid,
):
    rows_here, width = entity_feats.shape
    columns = features.shape[1]
    n_feat, n_ent = lax.axis_size("feat"), lax.axis_size("ent")
    owners = lax.axis_size("rows") * n_ent
    capacity = 2 * rows_here // owners
    member, item = member_owner.reshape(1, rows_here), item_owner.reshape(1, rows_here)

    def shape(*dims, dtype=F32):
        return jax.ShapeDtypeStruct(dims, dtype)

    def partial(kernel, *args):
        return lambda *refs: kernel(*args, *refs)

    row = pltpu.VMEM((1, rows_here), jnp.int32)
    half = owners // 2
    first, second, near = [half], list(range(half + 1, owners)), list(reversed(range(half)))
    chunk = shape(capacity + IDS, width, dtype=BF16)
    flops = len(first) * 2 * capacity * rows_here * width

    def in_hbm(x):
        return pltpu.with_memory_space_constraint(x, pltpu.HBM)

    ranks, place, ids, feats, *chunks = call(
        partial(far_kernel, owners, capacity, n_feat, first),
        [
            shape(2, rows_here, dtype=jnp.int32),
            shape(1, rows_here, dtype=jnp.int32),
            shape(IDS, rows_here, dtype=BF16),
            shape(rows_here, width, dtype=BF16),
        ]
        + [chunk] * len(first),
        (
            in_hbm(member),
            in_hbm(item),
            in_hbm(member_local.reshape(1, rows_here)),
            in_hbm(item_local.reshape(1, rows_here)),
            in_hbm(entity_feats),
        ),
        [HBM] * 5,
        flops=flops,
        scratch=[row, row, row, row, pltpu.SemaphoreType.DMA((5,))],
    )
    chunks += call(
        partial(rest_kernel, capacity, second),
        [chunk] * len(second),
        (place, ids, feats),
        [VMEM] * 3,
        flops=32 * flops,
    )
    chunks = [xor_send(x, HOME, owners, k) for k, x in zip(first + second, chunks)]
    weight = global_weight.astype(F32).reshape(1, columns)
    (global_part,) = call(
        margin_kernel, [shape(1, rows_here)], (place, weight, features), [VMEM] * 3, hidden=True
    )
    global_total = lax.psum(global_part, "feat")
    near_chunks = call(
        partial(rest_kernel, capacity, near),
        [chunk] * len(near),
        (place, ids, feats, global_total),
        [VMEM] * 4,
        hidden=True,
    )
    near_chunks = [xor_send(x, HOME, owners, k) for k, x in zip(near, near_chunks)]
    chunks = dict(zip(first + second + near, chunks + near_chunks))
    early = (first + second)[: half // 2] + near[-1:]
    late = (first + second)[half // 2 :] + near[:-1]
    order = early + late
    table, *scores = call(
        partial(early_kernel, capacity),
        [shape(2 * coefs.shape[0], width, dtype=BF16)] + [shape(1, capacity)] * len(early),
        (coefs, *(chunks[k] for k in early)),
        [VMEM] * (1 + len(early)),
        hidden=True,
    )
    (scores,) = call(
        partial(scores_kernel, order, capacity, n_feat, n_ent),
        [shape(n_feat * owners, 1, capacity)],
        (table, *scores, *(chunks[k] for k in late)),
        [VMEM] * (1 + owners),
        flops=16 * coefs.size * owners * capacity,
    )
    returned = lax.all_to_all(scores, EVERY, split_axis=0, concat_axis=0, tiled=True)
    (sent,) = call(
        partial(home_kernel, owners, capacity, n_feat, n_ent),
        [shape(owners, 1, capacity + columns)],
        (
            member,
            item,
            ranks,
            clicks.reshape(1, rows_here),
            valid.reshape(1, rows_here),
            global_total,
            returned,
            features,
        ),
        [VMEM] * 8,
        flops=32 * features.size,
    )
    came = lax.all_to_all(sent, HOME, split_axis=0, concat_axis=0, tiled=True)
    grad_global, grad_coefs = call(
        partial(grads_kernel, order, capacity, 1.0 / math.sqrt(rows_here * owners)),
        [shape(1, columns), shape(*coefs.shape)],
        (coefs, weight, came, *(chunks[k] for k in order)),
        [VMEM] * (3 + owners),
        flops=4 * coefs.size * owners * capacity,
    )
    return (grad_global.reshape(columns), grad_coefs)


def solution(mesh):
    by_row = P(("groups", "rows", "ent"))
    by_both = P(("groups", "rows", "ent"), "feat")
    column = P(("groups", "rows", "ent"), None)
    by_feat = P(("groups", "feat"))
    return jax.shard_map(
        body,
        mesh=mesh,
        in_specs=(by_both, by_feat, by_both, by_both, column, by_row, column, by_row, by_row, by_row),
        out_specs=(by_feat, by_both),
        check_vma=False,
    )
```

```python
import math

import jax
import jax.numpy as jnp
from jax import lax
from jax.experimental import pallas as pl
from jax.experimental.pallas import tpu as pltpu
from jax.sharding import PartitionSpec as P

F32 = jnp.float32
BF16 = jnp.bfloat16
HOME = ("rows", "ent")
EVERY = ("rows", "feat", "ent")
IDS = 8
PARAMS = pltpu.CompilerParams(vmem_limit_bytes=24 * 2**20)
VMEM = pl.BlockSpec(memory_space=pltpu.VMEM)
HBM = pl.BlockSpec(memory_space=pltpu.HBM)


def lanes_dot(a, b):
    return lax.dot_general(a, b, (((1,), (1,)), ((), ())), preferred_element_type=F32)


def plain_dot(a, b):
    return lax.dot_general(a, b, (((1,), (0,)), ((), ())), preferred_element_type=F32)


def halves(x):
    high = x.astype(BF16)
    return high, (x - high.astype(F32)).astype(BF16)


def one_hot(row, count):
    return row == lax.broadcasted_iota(jnp.int32, (count, row.shape[1]), 0)


def low_hot(row, count):
    row = jnp.where((row >= 0) & (row < count), row, -1).astype(F32).astype(BF16)
    return row == lax.broadcasted_iota(jnp.int32, (count, row.shape[1]), 0).astype(F32).astype(BF16)


def ones(mask):
    return jnp.where(mask, jnp.ones((), BF16), jnp.zeros((), BF16))


def turn_rows(rows, n_rows, n_ent, z, c):
    def moved(di, dj, sign):
        at = [
            ((sign * i - di) % n_rows) * n_ent + (sign * j - dj) % n_ent for i in range(n_rows) for j in range(n_ent)
        ]
        return jnp.concatenate([rows[k : k + 1] for k in at], axis=0)

    rows = moved(0, 0, -1)
    bit = 1
    while bit < n_rows:
        rows = jnp.where((z & bit) > 0, moved(bit, 0, 1), rows)
        bit *= 2
    bit = 1
    while bit < n_ent:
        rows = jnp.where((c & bit) > 0, moved(0, bit, 1), rows)
        bit *= 2
    return rows


def ranks_of(owners, member, item):
    rows = member.shape[1]
    step = min(256, rows)
    blocks = rows // step
    hits = jnp.concatenate([one_hot(member, owners).astype(F32), one_hot(item, owners).astype(F32)], axis=0)
    stacked = jnp.concatenate([hits[:, b * step : (b + 1) * step] for b in range(blocks)], axis=0)
    upper = lax.broadcasted_iota(jnp.int32, (step, step), 0) <= lax.broadcasted_iota(
        jnp.int32, (step, step), 1
    )
    counts = plain_dot(stacked.astype(BF16), upper.astype(F32).astype(BF16))
    before = jnp.zeros((2 * owners, 1), F32)
    pieces = []
    for b in range(blocks):
        here = counts[2 * owners * b : 2 * owners * (b + 1)]
        taken = (here + before) * hits[:, b * step : (b + 1) * step]
        sides = [jnp.sum(x, axis=0, keepdims=True) for x in (taken[:owners], taken[owners:])]
        pieces.append(jnp.concatenate(sides, axis=0))
        before = before + here[:, step - 1 : step]
    return jnp.concatenate(pieces, axis=1).astype(jnp.int32) - 1


def pack_chunk(k, capacity, place, ids, feats, chunk):
    pick = ones(low_hot(place - k * capacity, capacity))
    chunk[:capacity] = plain_dot(pick, feats).astype(BF16)
    chunk[capacity:, :capacity] = lanes_dot(ids, pick).astype(BF16)


def far_kernel(n_rows, n_ent, capacity, n_feat, far, *refs):
    sources, ranks, place_out, ids_out, feats = refs[:5], refs[5], refs[6], refs[7], refs[8]
    chunks, copies, sems = refs[9 : 9 + len(far)], refs[9 + len(far) : 13 + len(far)], refs[13 + len(far)]
    copies = (*copies, feats)
    moves = [pltpu.make_async_copy(sources[i], copies[i], sems.at[i]) for i in range(5)]
    for move in moves:
        move.start()
    for move in moves[:4]:
        move.wait()
    member, item, member_local, item_local = [copy[...] for copy in copies[:4]]
    rows = member.shape[1]
    rank = ranks_of(n_rows * n_ent, member, item)
    ranks[...] = rank
    on_item = lax.axis_index("feat") >= n_feat // 2
    own = jnp.where(on_item, item, member)
    up, across = own // n_ent - lax.axis_index("rows"), own % n_ent - lax.axis_index("ent")
    up, across = jnp.where(up < 0, up + n_rows, up), jnp.where(across < 0, across + n_ent, across)
    place = (up * n_ent + across) * capacity + jnp.where(on_item, rank[1:2], rank[0:1])
    place_out[...] = place
    local = jnp.where(on_item, item_local, member_local)
    high = local >> 8
    ids = jnp.concatenate([high, local - (high << 8), jnp.zeros((IDS - 2, rows), jnp.int32)], axis=0)
    ids = ids.astype(F32).astype(BF16)
    ids_out[...] = ids
    moves[4].wait()
    for chunk, k in zip(chunks, far):
        pack_chunk(k, capacity, place, ids, feats[...], chunk)


def rest_kernel(capacity, rest, place, ids, feats, *refs):
    chunks = refs[-len(rest) :]
    for chunk, k in zip(chunks, rest):
        pack_chunk(k, capacity, place[...], ids[...], feats[...], chunk)


def margin_kernel(place, weight, features, margin):
    wide = jnp.broadcast_to(weight[...], (16, weight.shape[1])).astype(BF16)
    margin[...] = lanes_dot(wide, features[...])[0:1]


def chunk_ids(chunk, capacity):
    pair = chunk[capacity:, :capacity].astype(F32)
    return (pair[0:1] * 256.0 + pair[1:2]).astype(jnp.int32)


def chunk_scores(chunk, table, capacity):
    entities = table.shape[0] // 2
    every = lanes_dot(table, chunk[:capacity])
    hits = one_hot(chunk_ids(chunk, capacity), entities)
    return jnp.sum(jnp.where(hits, every[:entities] + every[entities:], 0.0), axis=0, keepdims=True)


def early_kernel(capacity, coefs, *refs):
    half = len(refs) // 2
    kept = refs[half]
    entities = coefs.shape[0]
    kept[:entities], kept[entities:] = halves(coefs[...])
    table = kept[...]
    for chunk, out in zip(refs[:half], refs[half + 1 :]):
        out[...] = chunk_scores(chunk, table, capacity)


def scores_kernel(order, capacity, n_feat, n_rows, n_ent, table, *refs):
    out = refs[-1]
    scores = [x[...] if x.shape[0] == 1 else chunk_scores(x, table[...], capacity) for x in refs[:-1]]
    scores = dict(zip(order, scores))
    scores = jnp.concatenate([scores[k] for k in range(len(order))], axis=0)
    scores = turn_rows(scores, n_rows, n_ent, lax.axis_index("rows"), lax.axis_index("ent"))
    for home in range(len(order)):
        for f in range(n_feat):
            out[(home // n_ent * n_feat + f) * n_ent + home % n_ent] = scores[home : home + 1]


def home_kernel(
    owners, capacity, n_feat, n_ent, member, item, ranks, clicks, valid, margin, scores, features, out
):
    on_item = lax.axis_index("feat") >= n_feat // 2
    total = margin[...]
    hits_of = [one_hot(owner[...], owners).astype(F32) for owner in (member, item)]
    spot_of = [ones(low_hot(ranks[side : side + 1], capacity)) for side in (0, 1)]
    for side in (0, 1):
        table = None
        for f in range(side * n_feat // 2, (side + 1) * n_feat // 2):
            part = jnp.concatenate(
                [scores[(h // n_ent * n_feat + f) * n_ent + h % n_ent] for h in range(owners)], axis=0
            )
            table = part if table is None else table + part
        found = plain_dot(jnp.concatenate(halves(table), axis=0), spot_of[side])
        total = total + jnp.sum((found[:owners] + found[owners:]) * hits_of[side], axis=0, keepdims=True)
    resid = valid[...].astype(F32) * (jax.nn.sigmoid(total) - clicks[...].astype(F32))
    hits = jnp.where(on_item, hits_of[1], hits_of[0])
    spot = jnp.where(on_item, spot_of[1], spot_of[0])
    sent = lanes_dot(jnp.concatenate(halves(hits * resid), axis=0), spot)
    sent = sent[:owners] + sent[owners:]
    low = jnp.broadcast_to(resid, (16, resid.shape[1])).astype(BF16)
    grad = plain_dot(low, features[...])[0:1]
    for h in range(owners):
        out[h, :, :capacity] = sent[h : h + 1]
        out[h, :, capacity:] = grad


def grads_kernel(order, capacity, n_rows, n_ent, scale, coefs, weight, came, *refs):
    chunks, grad_global, grad_coefs = refs[:-2], refs[-2], refs[-1]
    entities = coefs.shape[0]
    resids = jnp.concatenate([came[h][:, :capacity] for h in range(len(order))], axis=0)
    resids = turn_rows(resids, n_rows, n_ent, lax.axis_index("rows"), lax.axis_index("ent"))
    summed = came[0][:, capacity:]
    for h in range(1, len(order)):
        summed = summed + came[h][:, capacity:]
    grad_global[...] = summed * scale + 4.0 * weight[...]
    highs, lows, feats = [], [], []
    for chunk, k in zip(chunks, order):
        here = chunk_ids(chunk, capacity)
        blocks = [low_hot(here - first, min(256, entities)) for first in range(0, entities, 256)]
        high, low = halves(resids[k : k + 1])
        highs.append(jnp.concatenate([jnp.where(hits, high, jnp.zeros((), BF16)) for hits in blocks], axis=0))
        lows.append(jnp.concatenate([jnp.where(hits, low, jnp.zeros((), BF16)) for hits in blocks], axis=0))
        feats.append(chunk[:capacity])
    spread = jnp.concatenate([jnp.concatenate(highs, axis=1), jnp.concatenate(lows, axis=1)], axis=0)
    both = plain_dot(spread, jnp.concatenate(feats, axis=0))
    grad_coefs[...] = coefs[...] + both[:entities] + both[entities:]


def shift_send(x, n_rows, n_ent, k):
    if k == 0:
        return x
    up, across = divmod(k, n_ent)
    pairs = [
        (z * n_ent + c, (z + up) % n_rows * n_ent + (c + across) % n_ent)
        for z in range(n_rows)
        for c in range(n_ent)
    ]
    return lax.ppermute(x, HOME, pairs)


def call(kernel, out_shape, operands, in_specs, flops=0, scratch=(), hidden=False):
    moved = 0 if hidden else sum(x.size * x.dtype.itemsize for x in (*operands, *out_shape))
    return pl.pallas_call(
        kernel,
        out_shape=out_shape,
        in_specs=in_specs,
        out_specs=[VMEM] * len(out_shape),
        scratch_shapes=scratch,
        compiler_params=PARAMS,
        cost_estimate=pl.CostEstimate(flops=flops, bytes_accessed=moved, transcendentals=0),
    )(*operands)


def body(
    features,
    global_weight,
    entity_feats,
    coefs,
    member_owner,
    member_local,
    item_owner,
    item_local,
    clicks,
    valid,
):
    rows_here, width = entity_feats.shape
    columns = features.shape[1]
    n_feat, n_ent = lax.axis_size("feat"), lax.axis_size("ent")
    n_rows = lax.axis_size("rows")
    owners = n_rows * n_ent
    capacity = 2 * rows_here // owners
    member, item = member_owner.reshape(1, rows_here), item_owner.reshape(1, rows_here)

    def shape(*dims, dtype=F32):
        return jax.ShapeDtypeStruct(dims, dtype)

    def partial(kernel, *args):
        return lambda *refs: kernel(*args, *refs)

    row = pltpu.VMEM((1, rows_here), jnp.int32)
    middle = n_rows // 2
    away = [middle * n_ent + c for c in range(n_ent)]
    for c in range(n_ent):
        for up in range(1, middle):
            away += [up * n_ent + c, (n_rows - up) * n_ent + c]
    first, second, near = away[:1], away[1:-2], [*away[-2:], *reversed(range(n_ent))]
    chunk = shape(capacity + IDS, width, dtype=BF16)
    flops = len(first) * 2 * capacity * rows_here * width

    def in_hbm(x):
        return pltpu.with_memory_space_constraint(x, pltpu.HBM)

    ranks, place, ids, feats, *chunks = call(
        partial(far_kernel, n_rows, n_ent, capacity, n_feat, first),
        [
            shape(2, rows_here, dtype=jnp.int32),
            shape(1, rows_here, dtype=jnp.int32),
            shape(IDS, rows_here, dtype=BF16),
            shape(rows_here, width, dtype=BF16),
        ]
        + [chunk] * len(first),
        (
            in_hbm(member),
            in_hbm(item),
            in_hbm(member_local.reshape(1, rows_here)),
            in_hbm(item_local.reshape(1, rows_here)),
            in_hbm(entity_feats),
        ),
        [HBM] * 5,
        flops=flops,
        scratch=[row, row, row, row, pltpu.SemaphoreType.DMA((5,))],
    )
    chunks += call(
        partial(rest_kernel, capacity, second),
        [chunk] * len(second),
        (place, ids, feats),
        [VMEM] * 3,
        flops=32 * flops,
    )
    chunks = [shift_send(x, n_rows, n_ent, k) for k, x in zip(first + second, chunks)]
    weight = global_weight.astype(F32).reshape(1, columns)
    (global_part,) = call(
        margin_kernel, [shape(1, rows_here)], (place, weight, features), [VMEM] * 3, hidden=True
    )
    global_total = lax.psum(global_part, "feat")
    near_chunks = call(
        partial(rest_kernel, capacity, near),
        [chunk] * len(near),
        (place, ids, feats, global_total),
        [VMEM] * 4,
        hidden=True,
    )
    near_chunks = [shift_send(x, n_rows, n_ent, k) for k, x in zip(near, near_chunks)]
    chunks = dict(zip(first + second + near, chunks + near_chunks))
    early = away[:n_ent] + near[-1:]
    late = away[n_ent:-2] + near[:-1]
    order = early + late
    table, *scores = call(
        partial(early_kernel, capacity),
        [shape(2 * coefs.shape[0], width, dtype=BF16)] + [shape(1, capacity)] * len(early),
        (coefs, *(chunks[k] for k in early)),
        [VMEM] * (1 + len(early)),
        hidden=True,
    )
    (scores,) = call(
        partial(scores_kernel, order, capacity, n_feat, n_rows, n_ent),
        [shape(n_feat * owners, 1, capacity)],
        (table, *scores, *(chunks[k] for k in late)),
        [VMEM] * (1 + owners),
        flops=16 * coefs.size * owners * capacity,
    )
    returned = lax.all_to_all(scores, EVERY, split_axis=0, concat_axis=0, tiled=True)
    (sent,) = call(
        partial(home_kernel, owners, capacity, n_feat, n_ent),
        [shape(owners, 1, capacity + columns)],
        (
            member,
            item,
            ranks,
            clicks.reshape(1, rows_here),
            valid.reshape(1, rows_here),
            global_total,
            returned,
            features,
        ),
        [VMEM] * 8,
        flops=32 * features.size,
    )
    came = lax.all_to_all(sent, HOME, split_axis=0, concat_axis=0, tiled=True)
    grad_global, grad_coefs = call(
        partial(grads_kernel, order, capacity, n_rows, n_ent, 1.0 / math.sqrt(rows_here * owners)),
        [shape(1, columns), shape(*coefs.shape)],
        (coefs, weight, came, *(chunks[k] for k in order)),
        [VMEM] * (3 + owners),
        flops=4 * coefs.size * owners * capacity,
    )
    return (grad_global.reshape(columns), grad_coefs)


def solution(mesh):
    by_row = P(("groups", "rows", "ent"))
    by_both = P(("groups", "rows", "ent"), "feat")
    column = P(("groups", "rows", "ent"), None)
    by_feat = P(("groups", "feat"))
    return jax.shard_map(
        body,
        mesh=mesh,
        in_specs=(by_both, by_feat, by_both, by_both, column, by_row, column, by_row, by_row, by_row),
        out_specs=(by_feat, by_both),
        check_vma=False,
    )
```

```python
import math

import jax
import jax.numpy as jnp
from jax import lax
from jax.experimental import pallas as pl
from jax.experimental.pallas import tpu as pltpu
from jax.sharding import PartitionSpec as P

F32 = jnp.float32
BF16 = jnp.bfloat16
HOME = ("rows", "ent")
EVERY = ("rows", "feat", "ent")
IDS = 8
PARAMS = pltpu.CompilerParams(vmem_limit_bytes=24 * 2**20)
VMEM = pl.BlockSpec(memory_space=pltpu.VMEM)
HBM = pl.BlockSpec(memory_space=pltpu.HBM)


def lanes_dot(a, b):
    return lax.dot_general(a, b, (((1,), (1,)), ((), ())), preferred_element_type=F32)


def plain_dot(a, b):
    return lax.dot_general(a, b, (((1,), (0,)), ((), ())), preferred_element_type=F32)


def halves(x):
    high = x.astype(BF16)
    return high, (x - high.astype(F32)).astype(BF16)


def one_hot(row, count):
    return row == lax.broadcasted_iota(jnp.int32, (count, row.shape[1]), 0)


def low_hot(row, count):
    row = jnp.where((row >= 0) & (row < count), row, -1).astype(F32).astype(BF16)
    return row == lax.broadcasted_iota(jnp.int32, (count, row.shape[1]), 0).astype(F32).astype(BF16)


def ones(mask):
    return jnp.where(mask, jnp.ones((), BF16), jnp.zeros((), BF16))


def turn_rows(rows, n_rows, n_ent, z, c):
    def moved(di, dj, sign):
        at = [
            ((sign * i - di) % n_rows) * n_ent + (sign * j - dj) % n_ent for i in range(n_rows) for j in range(n_ent)
        ]
        return jnp.concatenate([rows[k : k + 1] for k in at], axis=0)

    rows = moved(0, 0, -1)
    bit = 1
    while bit < n_rows:
        rows = jnp.where((z & bit) > 0, moved(bit, 0, 1), rows)
        bit *= 2
    bit = 1
    while bit < n_ent:
        rows = jnp.where((c & bit) > 0, moved(0, bit, 1), rows)
        bit *= 2
    return rows


def ranks_of(owners, member, item):
    rows = member.shape[1]
    step = min(256, rows)
    blocks = rows // step
    hits = jnp.concatenate([one_hot(member, owners).astype(F32), one_hot(item, owners).astype(F32)], axis=0)
    stacked = jnp.concatenate([hits[:, b * step : (b + 1) * step] for b in range(blocks)], axis=0)
    upper = lax.broadcasted_iota(jnp.int32, (step, step), 0) <= lax.broadcasted_iota(
        jnp.int32, (step, step), 1
    )
    counts = plain_dot(stacked.astype(BF16), upper.astype(F32).astype(BF16))
    before = jnp.zeros((2 * owners, 1), F32)
    pieces = []
    for b in range(blocks):
        here = counts[2 * owners * b : 2 * owners * (b + 1)]
        taken = (here + before) * hits[:, b * step : (b + 1) * step]
        sides = [jnp.sum(x, axis=0, keepdims=True) for x in (taken[:owners], taken[owners:])]
        pieces.append(jnp.concatenate(sides, axis=0))
        before = before + here[:, step - 1 : step]
    return jnp.concatenate(pieces, axis=1).astype(jnp.int32) - 1


def pack_chunk(k, capacity, place, ids, feats, chunk):
    pick = ones(low_hot(place - k * capacity, capacity))
    chunk[:capacity] = plain_dot(pick, feats).astype(BF16)
    chunk[capacity:, :capacity] = lanes_dot(ids, pick).astype(BF16)


def far_kernel(n_rows, n_ent, capacity, n_feat, far, *refs):
    sources, ranks, place_out, ids_out, feats = refs[:5], refs[5], refs[6], refs[7], refs[8]
    chunks, copies, sems = refs[9 : 9 + len(far)], refs[9 + len(far) : 13 + len(far)], refs[13 + len(far)]
    copies = (*copies, feats)
    moves = [pltpu.make_async_copy(sources[i], copies[i], sems.at[i]) for i in range(5)]
    for move in moves:
        move.start()
    for move in moves[:4]:
        move.wait()
    member, item, member_local, item_local = [copy[...] for copy in copies[:4]]
    rows = member.shape[1]
    rank = ranks_of(n_rows * n_ent, member, item)
    ranks[...] = rank
    on_item = lax.axis_index("feat") >= n_feat // 2
    own = jnp.where(on_item, item, member)
    up, across = own // n_ent - lax.axis_index("rows"), own % n_ent - lax.axis_index("ent")
    up, across = jnp.where(up < 0, up + n_rows, up), jnp.where(across < 0, across + n_ent, across)
    place = (up * n_ent + across) * capacity + jnp.where(on_item, rank[1:2], rank[0:1])
    place_out[...] = place
    local = jnp.where(on_item, item_local, member_local)
    high = local >> 8
    ids = jnp.concatenate([high, local - (high << 8), jnp.zeros((IDS - 2, rows), jnp.int32)], axis=0)
    ids = ids.astype(F32).astype(BF16)
    ids_out[...] = ids
    moves[4].wait()
    for chunk, k in zip(chunks, far):
        pack_chunk(k, capacity, place, ids, feats[...], chunk)


def rest_kernel(capacity, rest, place, ids, feats, *refs):
    chunks = refs[-len(rest) :]
    for chunk, k in zip(chunks, rest):
        pack_chunk(k, capacity, place[...], ids[...], feats[...], chunk)


def margin_kernel(place, weight, features, margin):
    wide = jnp.broadcast_to(weight[...], (16, weight.shape[1])).astype(BF16)
    margin[...] = lanes_dot(wide, features[...])[0:1]


def chunk_ids(chunk, capacity):
    pair = chunk[capacity:, :capacity].astype(F32)
    return (pair[0:1] * 256.0 + pair[1:2]).astype(jnp.int32)


def chunk_scores(chunk, table, capacity):
    entities = table.shape[0] // 2
    every = lanes_dot(table, chunk[:capacity])
    hits = one_hot(chunk_ids(chunk, capacity), entities)
    return jnp.sum(jnp.where(hits, every[:entities] + every[entities:], 0.0), axis=0, keepdims=True)


def early_kernel(capacity, coefs, *refs):
    half = len(refs) // 2
    kept = refs[half]
    entities = coefs.shape[0]
    kept[:entities], kept[entities:] = halves(coefs[...])
    table = kept[...]
    for chunk, out in zip(refs[:half], refs[half + 1 :]):
        out[...] = chunk_scores(chunk, table, capacity)


def scores_kernel(order, capacity, n_feat, n_rows, n_ent, table, *refs):
    out = refs[-1]
    scores = [x[...] if x.shape[0] == 1 else chunk_scores(x, table[...], capacity) for x in refs[:-1]]
    scores = dict(zip(order, scores))
    scores = jnp.concatenate([scores[k] for k in range(len(order))], axis=0)
    scores = turn_rows(scores, n_rows, n_ent, lax.axis_index("rows"), lax.axis_index("ent"))
    for home in range(len(order)):
        for f in range(n_feat):
            out[(home // n_ent * n_feat + f) * n_ent + home % n_ent] = scores[home : home + 1]


def home_kernel(
    owners, capacity, n_feat, n_ent, member, item, ranks, clicks, valid, margin, scores, features, out
):
    on_item = lax.axis_index("feat") >= n_feat // 2
    total = margin[...]
    hits_of = [one_hot(owner[...], owners).astype(F32) for owner in (member, item)]
    spot_of = [ones(low_hot(ranks[side : side + 1], capacity)) for side in (0, 1)]
    for side in (0, 1):
        table = None
        for f in range(side * n_feat // 2, (side + 1) * n_feat // 2):
            part = jnp.concatenate(
                [scores[(h // n_ent * n_feat + f) * n_ent + h % n_ent] for h in range(owners)], axis=0
            )
            table = part if table is None else table + part
        found = plain_dot(jnp.concatenate(halves(table), axis=0), spot_of[side])
        total = total + jnp.sum((found[:owners] + found[owners:]) * hits_of[side], axis=0, keepdims=True)
    resid = valid[...].astype(F32) * (jax.nn.sigmoid(total) - clicks[...].astype(F32))
    hits = jnp.where(on_item, hits_of[1], hits_of[0])
    spot = jnp.where(on_item, spot_of[1], spot_of[0])
    sent = lanes_dot(jnp.concatenate(halves(hits * resid), axis=0), spot)
    sent = sent[:owners] + sent[owners:]
    low = jnp.broadcast_to(resid, (16, resid.shape[1])).astype(BF16)
    grad = plain_dot(low, features[...])[0:1]
    for h in range(owners):
        out[h, :, :capacity] = sent[h : h + 1]
        out[h, :, capacity:] = grad


def grads_kernel(order, capacity, n_rows, n_ent, scale, coefs, weight, came, *refs):
    chunks, grad_global, grad_coefs = refs[:-2], refs[-2], refs[-1]
    entities = coefs.shape[0]
    resids = jnp.concatenate([came[h][:, :capacity] for h in range(len(order))], axis=0)
    resids = turn_rows(resids, n_rows, n_ent, lax.axis_index("rows"), lax.axis_index("ent"))
    summed = came[0][:, capacity:]
    for h in range(1, len(order)):
        summed = summed + came[h][:, capacity:]
    grad_global[...] = summed * scale + 4.0 * weight[...]
    highs, lows, feats = [], [], []
    for chunk, k in zip(chunks, order):
        here = chunk_ids(chunk, capacity)
        blocks = [low_hot(here - first, min(256, entities)) for first in range(0, entities, 256)]
        high, low = halves(resids[k : k + 1])
        highs.append(jnp.concatenate([jnp.where(hits, high, jnp.zeros((), BF16)) for hits in blocks], axis=0))
        lows.append(jnp.concatenate([jnp.where(hits, low, jnp.zeros((), BF16)) for hits in blocks], axis=0))
        feats.append(chunk[:capacity])
    spread = jnp.concatenate([jnp.concatenate(highs, axis=1), jnp.concatenate(lows, axis=1)], axis=0)
    both = plain_dot(spread, jnp.concatenate(feats, axis=0))
    grad_coefs[...] = coefs[...] + both[:entities] + both[entities:]


def shift_send(x, n_rows, n_ent, k):
    if k == 0:
        return x
    up, across = divmod(k, n_ent)
    pairs = [
        (z * n_ent + c, (z + up) % n_rows * n_ent + (c + across) % n_ent)
        for z in range(n_rows)
        for c in range(n_ent)
    ]
    return lax.ppermute(x, HOME, pairs)


def call(kernel, out_shape, operands, in_specs, flops=0, scratch=(), hidden=False):
    moved = 0 if hidden else sum(x.size * x.dtype.itemsize for x in (*operands, *out_shape))
    return pl.pallas_call(
        kernel,
        out_shape=out_shape,
        in_specs=in_specs,
        out_specs=[VMEM] * len(out_shape),
        scratch_shapes=scratch,
        compiler_params=PARAMS,
        cost_estimate=pl.CostEstimate(flops=flops, bytes_accessed=moved, transcendentals=0),
    )(*operands)


def body(
    features,
    global_weight,
    entity_feats,
    coefs,
    member_owner,
    member_local,
    item_owner,
    item_local,
    clicks,
    valid,
):
    rows_here, width = entity_feats.shape
    columns = features.shape[1]
    n_feat, n_ent = lax.axis_size("feat"), lax.axis_size("ent")
    n_rows = lax.axis_size("rows")
    owners = n_rows * n_ent
    capacity = 2 * rows_here // owners
    member, item = member_owner.reshape(1, rows_here), item_owner.reshape(1, rows_here)

    def shape(*dims, dtype=F32):
        return jax.ShapeDtypeStruct(dims, dtype)

    def partial(kernel, *args):
        return lambda *refs: kernel(*args, *refs)

    row = pltpu.VMEM((1, rows_here), jnp.int32)
    middle = n_rows // 2
    away = [middle * n_ent + c for c in range(n_ent)]
    for c in range(n_ent):
        for up in range(1, middle):
            away += [up * n_ent + c, (n_rows - up) * n_ent + c]
    first, second, near = away[:1], away[1:-2], [*away[-2:], *reversed(range(n_ent))]
    chunk = shape(capacity + IDS, width, dtype=BF16)
    flops = len(first) * 2 * capacity * rows_here * width

    def in_hbm(x):
        return pltpu.with_memory_space_constraint(x, pltpu.HBM)

    ranks, place, ids, feats, *chunks = call(
        partial(far_kernel, n_rows, n_ent, capacity, n_feat, first),
        [
            shape(2, rows_here, dtype=jnp.int32),
            shape(1, rows_here, dtype=jnp.int32),
            shape(IDS, rows_here, dtype=BF16),
            shape(rows_here, width, dtype=BF16),
        ]
        + [chunk] * len(first),
        (
            in_hbm(member),
            in_hbm(item),
            in_hbm(member_local.reshape(1, rows_here)),
            in_hbm(item_local.reshape(1, rows_here)),
            in_hbm(entity_feats),
        ),
        [HBM] * 5,
        flops=flops,
        scratch=[row, row, row, row, pltpu.SemaphoreType.DMA((5,))],
    )
    chunks += call(
        partial(rest_kernel, capacity, second),
        [chunk] * len(second),
        (place, ids, feats),
        [VMEM] * 3,
        flops=32 * flops,
    )
    chunks = [shift_send(x, n_rows, n_ent, k) for k, x in zip(first + second, chunks)]
    weight = global_weight.astype(F32).reshape(1, columns)
    (global_part,) = call(
        margin_kernel, [shape(1, rows_here)], (place, weight, features), [VMEM] * 3, hidden=True
    )
    global_total = lax.psum(global_part, "feat")
    near_chunks = call(
        partial(rest_kernel, capacity, near),
        [chunk] * len(near),
        (place, ids, feats, global_part),
        [VMEM] * 4,
        hidden=True,
    )
    near_chunks = [shift_send(x, n_rows, n_ent, k) for k, x in zip(near, near_chunks)]
    chunks = dict(zip(first + second + near, chunks + near_chunks))
    early = away[:n_ent] + near[-1:]
    late = away[n_ent:-2] + near[:-1]
    order = early + late
    table, *scores = call(
        partial(early_kernel, capacity),
        [shape(2 * coefs.shape[0], width, dtype=BF16)] + [shape(1, capacity)] * len(early),
        (coefs, *(chunks[k] for k in early)),
        [VMEM] * (1 + len(early)),
        hidden=True,
    )
    (scores,) = call(
        partial(scores_kernel, order, capacity, n_feat, n_rows, n_ent),
        [shape(n_feat * owners, 1, capacity)],
        (table, *scores, *(chunks[k] for k in late)),
        [VMEM] * (1 + owners),
        flops=16 * coefs.size * owners * capacity,
    )
    returned = lax.all_to_all(scores, EVERY, split_axis=0, concat_axis=0, tiled=True)
    (sent,) = call(
        partial(home_kernel, owners, capacity, n_feat, n_ent),
        [shape(owners, 1, capacity + columns)],
        (
            member,
            item,
            ranks,
            clicks.reshape(1, rows_here),
            valid.reshape(1, rows_here),
            global_total,
            returned,
            features,
        ),
        [VMEM] * 8,
        flops=32 * features.size,
    )
    came = lax.all_to_all(sent, HOME, split_axis=0, concat_axis=0, tiled=True)
    grad_global, grad_coefs = call(
        partial(grads_kernel, order, capacity, n_rows, n_ent, 1.0 / math.sqrt(rows_here * owners)),
        [shape(1, columns), shape(*coefs.shape)],
        (coefs, weight, came, *(chunks[k] for k in order)),
        [VMEM] * (3 + owners),
        flops=4 * coefs.size * owners * capacity,
    )
    return (grad_global.reshape(columns), grad_coefs)


def solution(mesh):
    by_row = P(("groups", "rows", "ent"))
    by_both = P(("groups", "rows", "ent"), "feat")
    column = P(("groups", "rows", "ent"), None)
    by_feat = P(("groups", "feat"))
    return jax.shard_map(
        body,
        mesh=mesh,
        in_specs=(by_both, by_feat, by_both, by_both, column, by_row, column, by_row, by_row, by_row),
        out_specs=(by_feat, by_both),
        check_vma=False,
    )
```

```python
import math

import jax
import jax.numpy as jnp
from jax import lax
from jax.experimental import pallas as pl
from jax.experimental.pallas import tpu as pltpu
from jax.sharding import PartitionSpec as P

F32 = jnp.float32
BF16 = jnp.bfloat16
HOME = ("rows", "ent")
EVERY = ("rows", "feat", "ent")
IDS = 8
PARAMS = pltpu.CompilerParams(vmem_limit_bytes=24 * 2**20)
VMEM = pl.BlockSpec(memory_space=pltpu.VMEM)
HBM = pl.BlockSpec(memory_space=pltpu.HBM)


def lanes_dot(a, b):
    return lax.dot_general(a, b, (((1,), (1,)), ((), ())), preferred_element_type=F32)


def plain_dot(a, b):
    return lax.dot_general(a, b, (((1,), (0,)), ((), ())), preferred_element_type=F32)


def halves(x):
    high = x.astype(BF16)
    return high, (x - high.astype(F32)).astype(BF16)


def one_hot(row, count):
    return row == lax.broadcasted_iota(jnp.int32, (count, row.shape[1]), 0)


def low_hot(row, count):
    row = jnp.where((row >= 0) & (row < count), row, -1).astype(F32).astype(BF16)
    return row == lax.broadcasted_iota(jnp.int32, (count, row.shape[1]), 0).astype(F32).astype(BF16)


def ones(mask):
    return jnp.where(mask, jnp.ones((), BF16), jnp.zeros((), BF16))


def turn_rows(rows, n_rows, n_ent, z, c):
    def moved(di, dj, sign):
        at = [
            ((sign * i - di) % n_rows) * n_ent + (sign * j - dj) % n_ent for i in range(n_rows) for j in range(n_ent)
        ]
        return jnp.concatenate([rows[k : k + 1] for k in at], axis=0)

    rows = moved(0, 0, -1)
    bit = 1
    while bit < n_rows:
        rows = jnp.where((z & bit) > 0, moved(bit, 0, 1), rows)
        bit *= 2
    bit = 1
    while bit < n_ent:
        rows = jnp.where((c & bit) > 0, moved(0, bit, 1), rows)
        bit *= 2
    return rows


def ranks_of(owners, member, item):
    rows = member.shape[1]
    step = min(256, rows)
    blocks = rows // step
    hits = jnp.concatenate([one_hot(member, owners).astype(F32), one_hot(item, owners).astype(F32)], axis=0)
    stacked = jnp.concatenate([hits[:, b * step : (b + 1) * step] for b in range(blocks)], axis=0)
    upper = lax.broadcasted_iota(jnp.int32, (step, step), 0) <= lax.broadcasted_iota(
        jnp.int32, (step, step), 1
    )
    counts = plain_dot(stacked.astype(BF16), upper.astype(F32).astype(BF16))
    before = jnp.zeros((2 * owners, 1), F32)
    pieces = []
    for b in range(blocks):
        here = counts[2 * owners * b : 2 * owners * (b + 1)]
        taken = (here + before) * hits[:, b * step : (b + 1) * step]
        sides = [jnp.sum(x, axis=0, keepdims=True) for x in (taken[:owners], taken[owners:])]
        pieces.append(jnp.concatenate(sides, axis=0))
        before = before + here[:, step - 1 : step]
    return jnp.concatenate(pieces, axis=1).astype(jnp.int32) - 1


def pack_chunk(k, capacity, place, ids, feats, chunk):
    pick = ones(low_hot(place - k * capacity, capacity))
    chunk[:capacity] = plain_dot(pick, feats).astype(BF16)
    chunk[capacity:, :capacity] = lanes_dot(ids, pick).astype(BF16)


def far_kernel(n_rows, n_ent, capacity, n_feat, far, *refs):
    sources, ranks, place_out, ids_out, feats = refs[:5], refs[5], refs[6], refs[7], refs[8]
    chunks, copies, sems = refs[9 : 9 + len(far)], refs[9 + len(far) : 13 + len(far)], refs[13 + len(far)]
    copies = (*copies, feats)
    moves = [pltpu.make_async_copy(sources[i], copies[i], sems.at[i]) for i in range(5)]
    for move in moves:
        move.start()
    for move in moves[:4]:
        move.wait()
    member, item, member_local, item_local = [copy[...] for copy in copies[:4]]
    rows = member.shape[1]
    rank = ranks_of(n_rows * n_ent, member, item)
    ranks[...] = rank
    on_item = lax.axis_index("feat") >= n_feat // 2
    own = jnp.where(on_item, item, member)
    up, across = own // n_ent - lax.axis_index("rows"), own % n_ent - lax.axis_index("ent")
    up, across = jnp.where(up < 0, up + n_rows, up), jnp.where(across < 0, across + n_ent, across)
    place = (up * n_ent + across) * capacity + jnp.where(on_item, rank[1:2], rank[0:1])
    place_out[...] = place
    local = jnp.where(on_item, item_local, member_local)
    high = local >> 8
    ids = jnp.concatenate([high, local - (high << 8), jnp.zeros((IDS - 2, rows), jnp.int32)], axis=0)
    ids = ids.astype(F32).astype(BF16)
    ids_out[...] = ids
    moves[4].wait()
    for chunk, k in zip(chunks, far):
        pack_chunk(k, capacity, place, ids, feats[...], chunk)


def rest_kernel(capacity, rest, place, ids, feats, *refs):
    chunks = refs[-len(rest) :]
    for chunk, k in zip(chunks, rest):
        pack_chunk(k, capacity, place[...], ids[...], feats[...], chunk)


def margin_kernel(place, weight, features, margin):
    wide = jnp.broadcast_to(weight[...], (16, weight.shape[1])).astype(BF16)
    margin[...] = lanes_dot(wide, features[...])[0:1]


def chunk_ids(chunk, capacity):
    pair = chunk[capacity:, :capacity].astype(F32)
    return (pair[0:1] * 256.0 + pair[1:2]).astype(jnp.int32)


def chunk_scores(chunk, table, capacity):
    entities = table.shape[0] // 2
    every = lanes_dot(table, chunk[:capacity])
    hits = one_hot(chunk_ids(chunk, capacity), entities)
    return jnp.sum(jnp.where(hits, every[:entities] + every[entities:], 0.0), axis=0, keepdims=True)


def early_kernel(capacity, coefs, *refs):
    half = len(refs) // 2
    kept = refs[half]
    entities = coefs.shape[0]
    kept[:entities], kept[entities:] = halves(coefs[...])
    table = kept[...]
    for chunk, out in zip(refs[:half], refs[half + 1 :]):
        out[...] = chunk_scores(chunk, table, capacity)


def later_kernel(capacity, table, *refs):
    half = len(refs) // 2
    for chunk, out in zip(refs[:half], refs[half:]):
        out[...] = chunk_scores(chunk, table[...], capacity)


def scores_kernel(order, capacity, n_feat, n_rows, n_ent, table, *refs):
    out = refs[-1]
    scores = [x[...] if x.shape[0] == 1 else chunk_scores(x, table[...], capacity) for x in refs[:-1]]
    scores = dict(zip(order, scores))
    scores = jnp.concatenate([scores[k] for k in range(len(order))], axis=0)
    scores = turn_rows(scores, n_rows, n_ent, lax.axis_index("rows"), lax.axis_index("ent"))
    for home in range(len(order)):
        for f in range(n_feat):
            out[(home // n_ent * n_feat + f) * n_ent + home % n_ent] = scores[home : home + 1]


def home_kernel(
    owners, capacity, n_feat, n_ent, member, item, ranks, clicks, valid, margin, scores, features, out
):
    on_item = lax.axis_index("feat") >= n_feat // 2
    total = margin[...]
    hits_of = [one_hot(owner[...], owners).astype(F32) for owner in (member, item)]
    spot_of = [ones(low_hot(ranks[side : side + 1], capacity)) for side in (0, 1)]
    for side in (0, 1):
        table = None
        for f in range(side * n_feat // 2, (side + 1) * n_feat // 2):
            part = jnp.concatenate(
                [scores[(h // n_ent * n_feat + f) * n_ent + h % n_ent] for h in range(owners)], axis=0
            )
            table = part if table is None else table + part
        found = plain_dot(jnp.concatenate(halves(table), axis=0), spot_of[side])
        total = total + jnp.sum((found[:owners] + found[owners:]) * hits_of[side], axis=0, keepdims=True)
    resid = valid[...].astype(F32) * (jax.nn.sigmoid(total) - clicks[...].astype(F32))
    hits = jnp.where(on_item, hits_of[1], hits_of[0])
    spot = jnp.where(on_item, spot_of[1], spot_of[0])
    sent = lanes_dot(jnp.concatenate(halves(hits * resid), axis=0), spot)
    sent = sent[:owners] + sent[owners:]
    low = jnp.broadcast_to(resid, (16, resid.shape[1])).astype(BF16)
    grad = plain_dot(low, features[...])[0:1]
    for h in range(owners):
        out[h, :, :capacity] = sent[h : h + 1]
        out[h, :, capacity:] = grad


def grads_kernel(order, capacity, n_rows, n_ent, scale, coefs, weight, came, *refs):
    chunks, grad_global, grad_coefs = refs[:-2], refs[-2], refs[-1]
    entities = coefs.shape[0]
    resids = jnp.concatenate([came[h][:, :capacity] for h in range(len(order))], axis=0)
    resids = turn_rows(resids, n_rows, n_ent, lax.axis_index("rows"), lax.axis_index("ent"))
    summed = came[0][:, capacity:]
    for h in range(1, len(order)):
        summed = summed + came[h][:, capacity:]
    grad_global[...] = summed * scale + 4.0 * weight[...]
    highs, lows, feats = [], [], []
    for chunk, k in zip(chunks, order):
        here = chunk_ids(chunk, capacity)
        blocks = [low_hot(here - first, min(256, entities)) for first in range(0, entities, 256)]
        high, low = halves(resids[k : k + 1])
        highs.append(jnp.concatenate([jnp.where(hits, high, jnp.zeros((), BF16)) for hits in blocks], axis=0))
        lows.append(jnp.concatenate([jnp.where(hits, low, jnp.zeros((), BF16)) for hits in blocks], axis=0))
        feats.append(chunk[:capacity])
    spread = jnp.concatenate([jnp.concatenate(highs, axis=1), jnp.concatenate(lows, axis=1)], axis=0)
    both = plain_dot(spread, jnp.concatenate(feats, axis=0))
    grad_coefs[...] = coefs[...] + both[:entities] + both[entities:]


def shift_send(x, n_rows, n_ent, k):
    if k == 0:
        return x
    up, across = divmod(k, n_ent)
    pairs = [
        (z * n_ent + c, (z + up) % n_rows * n_ent + (c + across) % n_ent)
        for z in range(n_rows)
        for c in range(n_ent)
    ]
    return lax.ppermute(x, HOME, pairs)


def call(kernel, out_shape, operands, in_specs, flops=0, scratch=(), hidden=False):
    moved = 0 if hidden else sum(x.size * x.dtype.itemsize for x in (*operands, *out_shape))
    return pl.pallas_call(
        kernel,
        out_shape=out_shape,
        in_specs=in_specs,
        out_specs=[VMEM] * len(out_shape),
        scratch_shapes=scratch,
        compiler_params=PARAMS,
        cost_estimate=pl.CostEstimate(flops=flops, bytes_accessed=moved, transcendentals=0),
    )(*operands)


def body(
    features,
    global_weight,
    entity_feats,
    coefs,
    member_owner,
    member_local,
    item_owner,
    item_local,
    clicks,
    valid,
):
    rows_here, width = entity_feats.shape
    columns = features.shape[1]
    n_feat, n_ent = lax.axis_size("feat"), lax.axis_size("ent")
    n_rows = lax.axis_size("rows")
    owners = n_rows * n_ent
    capacity = 2 * rows_here // owners
    member, item = member_owner.reshape(1, rows_here), item_owner.reshape(1, rows_here)

    def shape(*dims, dtype=F32):
        return jax.ShapeDtypeStruct(dims, dtype)

    def partial(kernel, *args):
        return lambda *refs: kernel(*args, *refs)

    row = pltpu.VMEM((1, rows_here), jnp.int32)
    middle = n_rows // 2
    away = [middle * n_ent + c for c in range(n_ent)]
    for c in range(n_ent):
        for up in range(1, middle):
            away += [up * n_ent + c, (n_rows - up) * n_ent + c]
    first, second, near = away[:1], away[1:-2], [*away[-2:], *reversed(range(n_ent))]
    chunk = shape(capacity + IDS, width, dtype=BF16)
    flops = len(first) * 2 * capacity * rows_here * width

    def in_hbm(x):
        return pltpu.with_memory_space_constraint(x, pltpu.HBM)

    ranks, place, ids, feats, *chunks = call(
        partial(far_kernel, n_rows, n_ent, capacity, n_feat, first),
        [
            shape(2, rows_here, dtype=jnp.int32),
            shape(1, rows_here, dtype=jnp.int32),
            shape(IDS, rows_here, dtype=BF16),
            shape(rows_here, width, dtype=BF16),
        ]
        + [chunk] * len(first),
        (
            in_hbm(member),
            in_hbm(item),
            in_hbm(member_local.reshape(1, rows_here)),
            in_hbm(item_local.reshape(1, rows_here)),
            in_hbm(entity_feats),
        ),
        [HBM] * 5,
        flops=flops,
        scratch=[row, row, row, row, pltpu.SemaphoreType.DMA((5,))],
    )
    chunks += call(
        partial(rest_kernel, capacity, second),
        [chunk] * len(second),
        (place, ids, feats),
        [VMEM] * 3,
        flops=32 * flops,
    )
    chunks = [shift_send(x, n_rows, n_ent, k) for k, x in zip(first + second, chunks)]
    weight = global_weight.astype(F32).reshape(1, columns)
    (global_part,) = call(
        margin_kernel, [shape(1, rows_here)], (place, weight, features), [VMEM] * 3, hidden=True
    )
    global_total = lax.psum(global_part, "feat")
    near_chunks = call(
        partial(rest_kernel, capacity, near),
        [chunk] * len(near),
        (place, ids, feats, global_total),
        [VMEM] * 4,
        hidden=True,
    )
    near_chunks = [shift_send(x, n_rows, n_ent, k) for k, x in zip(near, near_chunks)]
    chunks = dict(zip(first + second + near, chunks + near_chunks))
    early = away[:n_ent] + near[-1:]
    later, late = away[n_ent:-2], near[:-1]
    order = early + later + late
    table, *scores = call(
        partial(early_kernel, capacity),
        [shape(2 * coefs.shape[0], width, dtype=BF16)] + [shape(1, capacity)] * len(early),
        (coefs, *(chunks[k] for k in early)),
        [VMEM] * (1 + len(early)),
        hidden=True,
    )
    scores += call(
        partial(later_kernel, capacity),
        [shape(1, capacity)] * len(later),
        (table, *(chunks[k] for k in later)),
        [VMEM] * (1 + len(later)),
        hidden=True,
    )
    (scores,) = call(
        partial(scores_kernel, order, capacity, n_feat, n_rows, n_ent),
        [shape(n_feat * owners, 1, capacity)],
        (table, *scores, *(chunks[k] for k in late)),
        [VMEM] * (1 + owners),
        flops=16 * coefs.size * owners * capacity,
    )
    returned = lax.all_to_all(scores, EVERY, split_axis=0, concat_axis=0, tiled=True)
    (sent,) = call(
        partial(home_kernel, owners, capacity, n_feat, n_ent),
        [shape(owners, 1, capacity + columns)],
        (
            member,
            item,
            ranks,
            clicks.reshape(1, rows_here),
            valid.reshape(1, rows_here),
            global_total,
            returned,
            features,
        ),
        [VMEM] * 8,
        flops=32 * features.size,
    )
    came = lax.all_to_all(sent, HOME, split_axis=0, concat_axis=0, tiled=True)
    grad_global, grad_coefs = call(
        partial(grads_kernel, order, capacity, n_rows, n_ent, 1.0 / math.sqrt(rows_here * owners)),
        [shape(1, columns), shape(*coefs.shape)],
        (coefs, weight, came, *(chunks[k] for k in order)),
        [VMEM] * (3 + owners),
        flops=4 * coefs.size * owners * capacity,
    )
    return (grad_global.reshape(columns), grad_coefs)


def solution(mesh):
    by_row = P(("groups", "rows", "ent"))
    by_both = P(("groups", "rows", "ent"), "feat")
    column = P(("groups", "rows", "ent"), None)
    by_feat = P(("groups", "feat"))
    return jax.shard_map(
        body,
        mesh=mesh,
        in_specs=(by_both, by_feat, by_both, by_both, column, by_row, column, by_row, by_row, by_row),
        out_specs=(by_feat, by_both),
        check_vma=False,
    )
```

```python
import math

import jax
import jax.numpy as jnp
from jax import lax
from jax.experimental import pallas as pl
from jax.experimental.pallas import tpu as pltpu
from jax.sharding import PartitionSpec as P

F32 = jnp.float32
BF16 = jnp.bfloat16
HOME = ("rows", "ent")
EVERY = ("rows", "feat", "ent")
IDS = 8
PARAMS = pltpu.CompilerParams(vmem_limit_bytes=24 * 2**20)
VMEM = pl.BlockSpec(memory_space=pltpu.VMEM)
HBM = pl.BlockSpec(memory_space=pltpu.HBM)


def lanes_dot(a, b):
    return lax.dot_general(a, b, (((1,), (1,)), ((), ())), preferred_element_type=F32)


def plain_dot(a, b):
    return lax.dot_general(a, b, (((1,), (0,)), ((), ())), preferred_element_type=F32)


def halves(x):
    high = x.astype(BF16)
    return high, (x - high.astype(F32)).astype(BF16)


def one_hot(row, count):
    return row == lax.broadcasted_iota(jnp.int32, (count, row.shape[1]), 0)


def low_hot(row, count):
    row = jnp.where((row >= 0) & (row < count), row, -1).astype(F32).astype(BF16)
    return row == lax.broadcasted_iota(jnp.int32, (count, row.shape[1]), 0).astype(F32).astype(BF16)


def ones(mask):
    return jnp.where(mask, jnp.ones((), BF16), jnp.zeros((), BF16))


def turn_rows(rows, n_rows, n_ent, z, c):
    def moved(di, dj, sign):
        at = [
            ((sign * i - di) % n_rows) * n_ent + (sign * j - dj) % n_ent for i in range(n_rows) for j in range(n_ent)
        ]
        return jnp.concatenate([rows[k : k + 1] for k in at], axis=0)

    rows = moved(0, 0, -1)
    bit = 1
    while bit < n_rows:
        rows = jnp.where((z & bit) > 0, moved(bit, 0, 1), rows)
        bit *= 2
    bit = 1
    while bit < n_ent:
        rows = jnp.where((c & bit) > 0, moved(0, bit, 1), rows)
        bit *= 2
    return rows


def ranks_of(owners, member, item):
    rows = member.shape[1]
    step = min(256, rows)
    blocks = rows // step
    hits = jnp.concatenate([one_hot(member, owners).astype(F32), one_hot(item, owners).astype(F32)], axis=0)
    stacked = jnp.concatenate([hits[:, b * step : (b + 1) * step] for b in range(blocks)], axis=0)
    upper = lax.broadcasted_iota(jnp.int32, (step, step), 0) <= lax.broadcasted_iota(
        jnp.int32, (step, step), 1
    )
    counts = plain_dot(stacked.astype(BF16), upper.astype(F32).astype(BF16))
    before = jnp.zeros((2 * owners, 1), F32)
    pieces = []
    for b in range(blocks):
        here = counts[2 * owners * b : 2 * owners * (b + 1)]
        taken = (here + before) * hits[:, b * step : (b + 1) * step]
        sides = [jnp.sum(x, axis=0, keepdims=True) for x in (taken[:owners], taken[owners:])]
        pieces.append(jnp.concatenate(sides, axis=0))
        before = before + here[:, step - 1 : step]
    return jnp.concatenate(pieces, axis=1).astype(jnp.int32) - 1


def pack_chunk(k, capacity, place, ids, feats, chunk):
    pick = ones(low_hot(place - k * capacity, capacity))
    chunk[:capacity] = plain_dot(pick, feats).astype(BF16)
    chunk[capacity:, :capacity] = lanes_dot(ids, pick).astype(BF16)


def far_kernel(n_rows, n_ent, capacity, n_feat, far, *refs):
    sources, ranks, place_out, ids_out, feats = refs[:5], refs[5], refs[6], refs[7], refs[8]
    chunks, copies, sems = refs[9 : 9 + len(far)], refs[9 + len(far) : 13 + len(far)], refs[13 + len(far)]
    copies = (*copies, feats)
    moves = [pltpu.make_async_copy(sources[i], copies[i], sems.at[i]) for i in range(5)]
    for move in moves:
        move.start()
    for move in moves[:4]:
        move.wait()
    member, item, member_local, item_local = [copy[...] for copy in copies[:4]]
    rows = member.shape[1]
    rank = ranks_of(n_rows * n_ent, member, item)
    ranks[...] = rank
    on_item = lax.axis_index("feat") >= n_feat // 2
    own = jnp.where(on_item, item, member)
    up, across = own // n_ent - lax.axis_index("rows"), own % n_ent - lax.axis_index("ent")
    up, across = jnp.where(up < 0, up + n_rows, up), jnp.where(across < 0, across + n_ent, across)
    place = (up * n_ent + across) * capacity + jnp.where(on_item, rank[1:2], rank[0:1])
    place_out[...] = place
    local = jnp.where(on_item, item_local, member_local)
    high = local >> 8
    ids = jnp.concatenate([high, local - (high << 8), jnp.zeros((IDS - 2, rows), jnp.int32)], axis=0)
    ids = ids.astype(F32).astype(BF16)
    ids_out[...] = ids
    moves[4].wait()
    for chunk, k in zip(chunks, far):
        pack_chunk(k, capacity, place, ids, feats[...], chunk)


def rest_kernel(capacity, rest, place, ids, feats, *refs):
    chunks = refs[-len(rest) :]
    for chunk, k in zip(chunks, rest):
        pack_chunk(k, capacity, place[...], ids[...], feats[...], chunk)


def margin_kernel(place, weight, features, margin):
    wide = jnp.broadcast_to(weight[...], (16, weight.shape[1])).astype(BF16)
    margin[...] = lanes_dot(wide, features[...])[0:1]


def chunk_ids(chunk, capacity):
    pair = chunk[capacity:, :capacity].astype(F32)
    return (pair[0:1] * 256.0 + pair[1:2]).astype(jnp.int32)


def chunk_scores(chunk, table, capacity):
    entities = table.shape[0] // 2
    every = lanes_dot(table, chunk[:capacity])
    hits = one_hot(chunk_ids(chunk, capacity), entities)
    return jnp.sum(jnp.where(hits, every[:entities] + every[entities:], 0.0), axis=0, keepdims=True)


def early_kernel(capacity, coefs, *refs):
    half = len(refs) // 2
    kept = refs[half]
    entities = coefs.shape[0]
    kept[:entities], kept[entities:] = halves(coefs[...])
    table = kept[...]
    for chunk, out in zip(refs[:half], refs[half + 1 :]):
        out[...] = chunk_scores(chunk, table, capacity)


def later_kernel(capacity, table, *refs):
    half = len(refs) // 2
    for chunk, out in zip(refs[:half], refs[half:]):
        out[...] = chunk_scores(chunk, table[...], capacity)


def scores_kernel(order, capacity, n_feat, n_rows, n_ent, table, *refs):
    out = refs[-1]
    scores = [x[...] if x.shape[0] == 1 else chunk_scores(x, table[...], capacity) for x in refs[:-1]]
    scores = dict(zip(order, scores))
    scores = jnp.concatenate([scores[k] for k in range(len(order))], axis=0)
    scores = turn_rows(scores, n_rows, n_ent, lax.axis_index("rows"), lax.axis_index("ent"))
    for home in range(len(order)):
        for f in range(n_feat):
            out[(home // n_ent * n_feat + f) * n_ent + home % n_ent] = scores[home : home + 1]


def home_kernel(
    owners, capacity, n_feat, n_ent, member, item, ranks, clicks, valid, margin, scores, features, out
):
    on_item = lax.axis_index("feat") >= n_feat // 2
    total = margin[...]
    hits_of = [one_hot(owner[...], owners).astype(F32) for owner in (member, item)]
    spot_of = [ones(low_hot(ranks[side : side + 1], capacity)) for side in (0, 1)]
    for side in (0, 1):
        table = None
        for f in range(side * n_feat // 2, (side + 1) * n_feat // 2):
            part = jnp.concatenate(
                [scores[(h // n_ent * n_feat + f) * n_ent + h % n_ent] for h in range(owners)], axis=0
            )
            table = part if table is None else table + part
        found = plain_dot(jnp.concatenate(halves(table), axis=0), spot_of[side])
        total = total + jnp.sum((found[:owners] + found[owners:]) * hits_of[side], axis=0, keepdims=True)
    resid = valid[...].astype(F32) * (jax.nn.sigmoid(total) - clicks[...].astype(F32))
    hits = jnp.where(on_item, hits_of[1], hits_of[0])
    spot = jnp.where(on_item, spot_of[1], spot_of[0])
    sent = lanes_dot(jnp.concatenate(halves(hits * resid), axis=0), spot)
    sent = sent[:owners] + sent[owners:]
    low = jnp.broadcast_to(resid, (16, resid.shape[1])).astype(BF16)
    grad = plain_dot(low, features[...])[0:1]
    for h in range(owners):
        out[h, :, :capacity] = sent[h : h + 1]
        out[h, :, capacity:] = grad


def grads_kernel(order, capacity, n_rows, n_ent, scale, coefs, weight, came, *refs):
    chunks, grad_global, grad_coefs = refs[:-2], refs[-2], refs[-1]
    entities = coefs.shape[0]
    resids = jnp.concatenate([came[h][:, :capacity] for h in range(len(order))], axis=0)
    resids = turn_rows(resids, n_rows, n_ent, lax.axis_index("rows"), lax.axis_index("ent"))
    summed = came[0][:, capacity:]
    for h in range(1, len(order)):
        summed = summed + came[h][:, capacity:]
    grad_global[...] = summed * scale + 4.0 * weight[...]
    highs, lows, feats = [], [], []
    for chunk, k in zip(chunks, order):
        here = chunk_ids(chunk, capacity)
        blocks = [low_hot(here - first, min(256, entities)) for first in range(0, entities, 256)]
        high, low = halves(resids[k : k + 1])
        highs.append(jnp.concatenate([jnp.where(hits, high, jnp.zeros((), BF16)) for hits in blocks], axis=0))
        lows.append(jnp.concatenate([jnp.where(hits, low, jnp.zeros((), BF16)) for hits in blocks], axis=0))
        feats.append(chunk[:capacity])
    spread = jnp.concatenate([jnp.concatenate(highs, axis=1), jnp.concatenate(lows, axis=1)], axis=0)
    both = plain_dot(spread, jnp.concatenate(feats, axis=0))
    grad_coefs[...] = coefs[...] + both[:entities] + both[entities:]


def shift_send(x, n_rows, n_ent, k):
    if k == 0:
        return x
    up, across = divmod(k, n_ent)
    pairs = [
        (z * n_ent + c, (z + up) % n_rows * n_ent + (c + across) % n_ent)
        for z in range(n_rows)
        for c in range(n_ent)
    ]
    return lax.ppermute(x, HOME, pairs)


def call(kernel, out_shape, operands, in_specs, flops=0, scratch=(), hidden=False):
    moved = 0 if hidden else sum(x.size * x.dtype.itemsize for x in (*operands, *out_shape))
    return pl.pallas_call(
        kernel,
        out_shape=out_shape,
        in_specs=in_specs,
        out_specs=[VMEM] * len(out_shape),
        scratch_shapes=scratch,
        compiler_params=PARAMS,
        cost_estimate=pl.CostEstimate(flops=flops, bytes_accessed=moved, transcendentals=0),
    )(*operands)


def body(
    features,
    global_weight,
    entity_feats,
    coefs,
    member_owner,
    member_local,
    item_owner,
    item_local,
    clicks,
    valid,
):
    rows_here, width = entity_feats.shape
    columns = features.shape[1]
    n_feat, n_ent = lax.axis_size("feat"), lax.axis_size("ent")
    n_rows = lax.axis_size("rows")
    owners = n_rows * n_ent
    capacity = 2 * rows_here // owners
    member, item = member_owner.reshape(1, rows_here), item_owner.reshape(1, rows_here)

    def shape(*dims, dtype=F32):
        return jax.ShapeDtypeStruct(dims, dtype)

    def partial(kernel, *args):
        return lambda *refs: kernel(*args, *refs)

    row = pltpu.VMEM((1, rows_here), jnp.int32)
    middle = n_rows // 2
    away = [up * n_ent for half in range(1, middle) for up in (half, n_rows - half)]
    away += [middle * n_ent + c for c in range(n_ent)]
    away += [up * n_ent + c for c in range(1, n_ent) for half in range(1, middle) for up in (half, n_rows - half)]
    first, second, near = away[:1], away[1:-2], [*away[-2:], *reversed(range(n_ent))]
    chunk = shape(capacity + IDS, width, dtype=BF16)
    flops = len(first) * 2 * capacity * rows_here * width

    def in_hbm(x):
        return pltpu.with_memory_space_constraint(x, pltpu.HBM)

    ranks, place, ids, feats, *chunks = call(
        partial(far_kernel, n_rows, n_ent, capacity, n_feat, first),
        [
            shape(2, rows_here, dtype=jnp.int32),
            shape(1, rows_here, dtype=jnp.int32),
            shape(IDS, rows_here, dtype=BF16),
            shape(rows_here, width, dtype=BF16),
        ]
        + [chunk] * len(first),
        (
            in_hbm(member),
            in_hbm(item),
            in_hbm(member_local.reshape(1, rows_here)),
            in_hbm(item_local.reshape(1, rows_here)),
            in_hbm(entity_feats),
        ),
        [HBM] * 5,
        flops=flops,
        scratch=[row, row, row, row, pltpu.SemaphoreType.DMA((5,))],
    )
    chunks += call(
        partial(rest_kernel, capacity, second),
        [chunk] * len(second),
        (place, ids, feats),
        [VMEM] * 3,
        flops=32 * flops,
    )
    chunks = [shift_send(x, n_rows, n_ent, k) for k, x in zip(first + second, chunks)]
    weight = global_weight.astype(F32).reshape(1, columns)
    (global_part,) = call(
        margin_kernel, [shape(1, rows_here)], (place, weight, features), [VMEM] * 3, hidden=True
    )
    global_total = lax.psum(global_part, "feat")
    near_chunks = call(
        partial(rest_kernel, capacity, near),
        [chunk] * len(near),
        (place, ids, feats, global_total),
        [VMEM] * 4,
        hidden=True,
    )
    near_chunks = [shift_send(x, n_rows, n_ent, k) for k, x in zip(near, near_chunks)]
    chunks = dict(zip(first + second + near, chunks + near_chunks))
    early = away[:n_ent] + near[-1:]
    later, late = away[n_ent:-2], near[:-1]
    order = early + later + late
    table, *scores = call(
        partial(early_kernel, capacity),
        [shape(2 * coefs.shape[0], width, dtype=BF16)] + [shape(1, capacity)] * len(early),
        (coefs, *(chunks[k] for k in early)),
        [VMEM] * (1 + len(early)),
        hidden=True,
    )
    scores += call(
        partial(later_kernel, capacity),
        [shape(1, capacity)] * len(later),
        (table, *(chunks[k] for k in later)),
        [VMEM] * (1 + len(later)),
        hidden=True,
    )
    (scores,) = call(
        partial(scores_kernel, order, capacity, n_feat, n_rows, n_ent),
        [shape(n_feat * owners, 1, capacity)],
        (table, *scores, *(chunks[k] for k in late)),
        [VMEM] * (1 + owners),
        flops=16 * coefs.size * owners * capacity,
    )
    returned = lax.all_to_all(scores, EVERY, split_axis=0, concat_axis=0, tiled=True)
    (sent,) = call(
        partial(home_kernel, owners, capacity, n_feat, n_ent),
        [shape(owners, 1, capacity + columns)],
        (
            member,
            item,
            ranks,
            clicks.reshape(1, rows_here),
            valid.reshape(1, rows_here),
            global_total,
            returned,
            features,
        ),
        [VMEM] * 8,
        flops=32 * features.size,
    )
    came = lax.all_to_all(sent, HOME, split_axis=0, concat_axis=0, tiled=True)
    grad_global, grad_coefs = call(
        partial(grads_kernel, order, capacity, n_rows, n_ent, 1.0 / math.sqrt(rows_here * owners)),
        [shape(1, columns), shape(*coefs.shape)],
        (coefs, weight, came, *(chunks[k] for k in order)),
        [VMEM] * (3 + owners),
        flops=4 * coefs.size * owners * capacity,
    )
    return (grad_global.reshape(columns), grad_coefs)


def solution(mesh):
    by_row = P(("groups", "rows", "ent"))
    by_both = P(("groups", "rows", "ent"), "feat")
    column = P(("groups", "rows", "ent"), None)
    by_feat = P(("groups", "feat"))
    return jax.shard_map(
        body,
        mesh=mesh,
        in_specs=(by_both, by_feat, by_both, by_both, column, by_row, column, by_row, by_row, by_row),
        out_specs=(by_feat, by_both),
        check_vma=False,
    )
```

```python
import math

import jax
import jax.numpy as jnp
from jax import lax
from jax.experimental import pallas as pl
from jax.experimental.pallas import tpu as pltpu
from jax.sharding import PartitionSpec as P

F32 = jnp.float32
BF16 = jnp.bfloat16
HOME = ("rows", "ent")
EVERY = ("rows", "feat", "ent")
IDS = 8
PARAMS = pltpu.CompilerParams(vmem_limit_bytes=24 * 2**20)
VMEM = pl.BlockSpec(memory_space=pltpu.VMEM)
HBM = pl.BlockSpec(memory_space=pltpu.HBM)


def lanes_dot(a, b):
    return lax.dot_general(a, b, (((1,), (1,)), ((), ())), preferred_element_type=F32)


def plain_dot(a, b):
    return lax.dot_general(a, b, (((1,), (0,)), ((), ())), preferred_element_type=F32)


def halves(x):
    high = x.astype(BF16)
    return high, (x - high.astype(F32)).astype(BF16)


def one_hot(row, count):
    return row == lax.broadcasted_iota(jnp.int32, (count, row.shape[1]), 0)


def low_hot(row, count):
    row = jnp.where((row >= 0) & (row < count), row, -1).astype(F32).astype(BF16)
    return row == lax.broadcasted_iota(jnp.int32, (count, row.shape[1]), 0).astype(F32).astype(BF16)


def ones(mask):
    return jnp.where(mask, jnp.ones((), BF16), jnp.zeros((), BF16))


def turn_rows(rows, n_rows, n_ent, z, c):
    def moved(di, dj, sign):
        at = [
            ((sign * i - di) % n_rows) * n_ent + (sign * j - dj) % n_ent for i in range(n_rows) for j in range(n_ent)
        ]
        return jnp.concatenate([rows[k : k + 1] for k in at], axis=0)

    rows = moved(0, 0, -1)
    bit = 1
    while bit < n_rows:
        rows = jnp.where((z & bit) > 0, moved(bit, 0, 1), rows)
        bit *= 2
    bit = 1
    while bit < n_ent:
        rows = jnp.where((c & bit) > 0, moved(0, bit, 1), rows)
        bit *= 2
    return rows


def ranks_of(owners, member, item):
    rows = member.shape[1]
    step = min(256, rows)
    blocks = rows // step
    hits = jnp.concatenate([one_hot(member, owners).astype(F32), one_hot(item, owners).astype(F32)], axis=0)
    stacked = jnp.concatenate([hits[:, b * step : (b + 1) * step] for b in range(blocks)], axis=0)
    upper = lax.broadcasted_iota(jnp.int32, (step, step), 0) <= lax.broadcasted_iota(
        jnp.int32, (step, step), 1
    )
    counts = plain_dot(stacked.astype(BF16), upper.astype(F32).astype(BF16))
    before = jnp.zeros((2 * owners, 1), F32)
    pieces = []
    for b in range(blocks):
        here = counts[2 * owners * b : 2 * owners * (b + 1)]
        taken = (here + before) * hits[:, b * step : (b + 1) * step]
        sides = [jnp.sum(x, axis=0, keepdims=True) for x in (taken[:owners], taken[owners:])]
        pieces.append(jnp.concatenate(sides, axis=0))
        before = before + here[:, step - 1 : step]
    return jnp.concatenate(pieces, axis=1).astype(jnp.int32) - 1


def pack_chunk(k, capacity, place, ids, feats, chunk):
    pick = ones(low_hot(place - k * capacity, capacity))
    chunk[:capacity] = plain_dot(pick, feats).astype(BF16)
    chunk[capacity:, :capacity] = lanes_dot(ids, pick).astype(BF16)


def far_kernel(n_rows, n_ent, capacity, n_feat, far, *refs):
    sources, ranks, place_out, ids_out, feats = refs[:5], refs[5], refs[6], refs[7], refs[8]
    chunks, copies, sems = refs[9 : 9 + len(far)], refs[9 + len(far) : 13 + len(far)], refs[13 + len(far)]
    copies = (*copies, feats)
    moves = [pltpu.make_async_copy(sources[i], copies[i], sems.at[i]) for i in range(5)]
    for move in moves:
        move.start()
    for move in moves[:4]:
        move.wait()
    member, item, member_local, item_local = [copy[...] for copy in copies[:4]]
    rows = member.shape[1]
    rank = ranks_of(n_rows * n_ent, member, item)
    ranks[...] = rank
    on_item = lax.axis_index("feat") >= n_feat // 2
    own = jnp.where(on_item, item, member)
    up, across = own // n_ent - lax.axis_index("rows"), own % n_ent - lax.axis_index("ent")
    up, across = jnp.where(up < 0, up + n_rows, up), jnp.where(across < 0, across + n_ent, across)
    place = (up * n_ent + across) * capacity + jnp.where(on_item, rank[1:2], rank[0:1])
    place_out[...] = place
    local = jnp.where(on_item, item_local, member_local)
    high = local >> 8
    ids = jnp.concatenate([high, local - (high << 8), jnp.zeros((IDS - 2, rows), jnp.int32)], axis=0)
    ids = ids.astype(F32).astype(BF16)
    ids_out[...] = ids
    moves[4].wait()
    for chunk, k in zip(chunks, far):
        pack_chunk(k, capacity, place, ids, feats[...], chunk)


def rest_kernel(capacity, rest, place, ids, feats, *refs):
    chunks = refs[-len(rest) :]
    for chunk, k in zip(chunks, rest):
        pack_chunk(k, capacity, place[...], ids[...], feats[...], chunk)


def margin_kernel(place, weight, features, margin):
    wide = jnp.broadcast_to(weight[...], (16, weight.shape[1])).astype(BF16)
    margin[...] = lanes_dot(wide, features[...])[0:1]


def chunk_ids(chunk, capacity):
    pair = chunk[capacity:, :capacity].astype(F32)
    return (pair[0:1] * 256.0 + pair[1:2]).astype(jnp.int32)


def chunk_scores(chunk, table, capacity):
    entities = table.shape[0] // 2
    every = lanes_dot(table, chunk[:capacity])
    hits = one_hot(chunk_ids(chunk, capacity), entities)
    return jnp.sum(jnp.where(hits, every[:entities] + every[entities:], 0.0), axis=0, keepdims=True)


def early_kernel(capacity, count, coefs, *refs):
    chunks, kept, outs = refs[:count], refs[-count - 1], refs[-count:]
    entities = coefs.shape[0]
    kept[:entities], kept[entities:] = halves(coefs[...])
    table = kept[...]
    for chunk, out in zip(chunks, outs):
        out[...] = chunk_scores(chunk, table, capacity)


def later_kernel(capacity, table, *refs):
    half = len(refs) // 2
    for chunk, out in zip(refs[:half], refs[half:]):
        out[...] = chunk_scores(chunk, table[...], capacity)


def scores_kernel(order, capacity, n_feat, n_rows, n_ent, table, *refs):
    out = refs[-1]
    scores = [x[...] if x.shape[0] == 1 else chunk_scores(x, table[...], capacity) for x in refs[:-1]]
    scores = dict(zip(order, scores))
    scores = jnp.concatenate([scores[k] for k in range(len(order))], axis=0)
    scores = turn_rows(scores, n_rows, n_ent, lax.axis_index("rows"), lax.axis_index("ent"))
    for home in range(len(order)):
        for f in range(n_feat):
            out[(home // n_ent * n_feat + f) * n_ent + home % n_ent] = scores[home : home + 1]


def home_kernel(
    owners, capacity, n_feat, n_ent, member, item, ranks, clicks, valid, margin, scores, features, out
):
    on_item = lax.axis_index("feat") >= n_feat // 2
    total = margin[...]
    hits_of = [one_hot(owner[...], owners).astype(F32) for owner in (member, item)]
    spot_of = [ones(low_hot(ranks[side : side + 1], capacity)) for side in (0, 1)]
    for side in (0, 1):
        table = None
        for f in range(side * n_feat // 2, (side + 1) * n_feat // 2):
            part = jnp.concatenate(
                [scores[(h // n_ent * n_feat + f) * n_ent + h % n_ent] for h in range(owners)], axis=0
            )
            table = part if table is None else table + part
        found = plain_dot(jnp.concatenate(halves(table), axis=0), spot_of[side])
        total = total + jnp.sum((found[:owners] + found[owners:]) * hits_of[side], axis=0, keepdims=True)
    resid = valid[...].astype(F32) * (jax.nn.sigmoid(total) - clicks[...].astype(F32))
    hits = jnp.where(on_item, hits_of[1], hits_of[0])
    spot = jnp.where(on_item, spot_of[1], spot_of[0])
    sent = lanes_dot(jnp.concatenate(halves(hits * resid), axis=0), spot)
    sent = sent[:owners] + sent[owners:]
    low = jnp.broadcast_to(resid, (16, resid.shape[1])).astype(BF16)
    grad = plain_dot(low, features[...])[0:1]
    for h in range(owners):
        out[h, :, :capacity] = sent[h : h + 1]
        out[h, :, capacity:] = grad


def grads_kernel(order, capacity, n_rows, n_ent, scale, coefs, weight, came, *refs):
    chunks, grad_global, grad_coefs = refs[:-2], refs[-2], refs[-1]
    entities = coefs.shape[0]
    resids = jnp.concatenate([came[h][:, :capacity] for h in range(len(order))], axis=0)
    resids = turn_rows(resids, n_rows, n_ent, lax.axis_index("rows"), lax.axis_index("ent"))
    summed = came[0][:, capacity:]
    for h in range(1, len(order)):
        summed = summed + came[h][:, capacity:]
    grad_global[...] = summed * scale + 4.0 * weight[...]
    highs, lows, feats = [], [], []
    for chunk, k in zip(chunks, order):
        here = chunk_ids(chunk, capacity)
        blocks = [low_hot(here - first, min(256, entities)) for first in range(0, entities, 256)]
        high, low = halves(resids[k : k + 1])
        highs.append(jnp.concatenate([jnp.where(hits, high, jnp.zeros((), BF16)) for hits in blocks], axis=0))
        lows.append(jnp.concatenate([jnp.where(hits, low, jnp.zeros((), BF16)) for hits in blocks], axis=0))
        feats.append(chunk[:capacity])
    spread = jnp.concatenate([jnp.concatenate(highs, axis=1), jnp.concatenate(lows, axis=1)], axis=0)
    both = plain_dot(spread, jnp.concatenate(feats, axis=0))
    grad_coefs[...] = coefs[...] + both[:entities] + both[entities:]


def shift_send(x, n_rows, n_ent, k):
    if k == 0:
        return x
    up, across = divmod(k, n_ent)
    pairs = [
        (z * n_ent + c, (z + up) % n_rows * n_ent + (c + across) % n_ent)
        for z in range(n_rows)
        for c in range(n_ent)
    ]
    return lax.ppermute(x, HOME, pairs)


def call(kernel, out_shape, operands, in_specs, flops=0, scratch=(), hidden=False):
    moved = 0 if hidden else sum(x.size * x.dtype.itemsize for x in (*operands, *out_shape))
    return pl.pallas_call(
        kernel,
        out_shape=out_shape,
        in_specs=in_specs,
        out_specs=[VMEM] * len(out_shape),
        scratch_shapes=scratch,
        compiler_params=PARAMS,
        cost_estimate=pl.CostEstimate(flops=flops, bytes_accessed=moved, transcendentals=0),
    )(*operands)


def body(
    features,
    global_weight,
    entity_feats,
    coefs,
    member_owner,
    member_local,
    item_owner,
    item_local,
    clicks,
    valid,
):
    rows_here, width = entity_feats.shape
    columns = features.shape[1]
    n_feat, n_ent = lax.axis_size("feat"), lax.axis_size("ent")
    n_rows = lax.axis_size("rows")
    owners = n_rows * n_ent
    capacity = 2 * rows_here // owners
    member, item = member_owner.reshape(1, rows_here), item_owner.reshape(1, rows_here)

    def shape(*dims, dtype=F32):
        return jax.ShapeDtypeStruct(dims, dtype)

    def partial(kernel, *args):
        return lambda *refs: kernel(*args, *refs)

    row = pltpu.VMEM((1, rows_here), jnp.int32)
    middle = n_rows // 2
    away = [up * n_ent for half in range(1, middle) for up in (half, n_rows - half)]
    away += [middle * n_ent + c for c in range(n_ent)]
    away += [up * n_ent + c for c in range(1, n_ent) for half in range(1, middle) for up in (half, n_rows - half)]
    first, second, near = away[:1], away[1:-2], [*away[-2:], *reversed(range(n_ent))]
    chunk = shape(capacity + IDS, width, dtype=BF16)
    flops = len(first) * 2 * capacity * rows_here * width

    def in_hbm(x):
        return pltpu.with_memory_space_constraint(x, pltpu.HBM)

    ranks, place, ids, feats, *chunks = call(
        partial(far_kernel, n_rows, n_ent, capacity, n_feat, first),
        [
            shape(2, rows_here, dtype=jnp.int32),
            shape(1, rows_here, dtype=jnp.int32),
            shape(IDS, rows_here, dtype=BF16),
            shape(rows_here, width, dtype=BF16),
        ]
        + [chunk] * len(first),
        (
            in_hbm(member),
            in_hbm(item),
            in_hbm(member_local.reshape(1, rows_here)),
            in_hbm(item_local.reshape(1, rows_here)),
            in_hbm(entity_feats),
        ),
        [HBM] * 5,
        flops=flops,
        scratch=[row, row, row, row, pltpu.SemaphoreType.DMA((5,))],
    )
    chunks += call(
        partial(rest_kernel, capacity, second),
        [chunk] * len(second),
        (place, ids, feats),
        [VMEM] * 3,
        flops=32 * flops,
    )
    chunks = [shift_send(x, n_rows, n_ent, k) for k, x in zip(first + second, chunks)]
    weight = global_weight.astype(F32).reshape(1, columns)
    (global_part,) = call(
        margin_kernel, [shape(1, rows_here)], (place, weight, features), [VMEM] * 3, hidden=True
    )
    global_total = lax.psum(global_part, "feat")
    near_chunks = call(
        partial(rest_kernel, capacity, near),
        [chunk] * len(near),
        (place, ids, feats, global_part),
        [VMEM] * 4,
        hidden=True,
    )
    near_chunks = [shift_send(x, n_rows, n_ent, k) for k, x in zip(near, near_chunks)]
    chunks = dict(zip(first + second + near, chunks + near_chunks))
    early = away[:n_ent] + near[-1:]
    later, late = away[n_ent:-2], near[:-1]
    order = early + later + late
    table, *scores = call(
        partial(early_kernel, capacity, len(early)),
        [shape(2 * coefs.shape[0], width, dtype=BF16)] + [shape(1, capacity)] * len(early),
        (coefs, *(chunks[k] for k in early), global_total),
        [VMEM] * (2 + len(early)),
        hidden=True,
    )
    scores += call(
        partial(later_kernel, capacity),
        [shape(1, capacity)] * len(later),
        (table, *(chunks[k] for k in later)),
        [VMEM] * (1 + len(later)),
        hidden=True,
    )
    (scores,) = call(
        partial(scores_kernel, order, capacity, n_feat, n_rows, n_ent),
        [shape(n_feat * owners, 1, capacity)],
        (table, *scores, *(chunks[k] for k in late)),
        [VMEM] * (1 + owners),
        flops=16 * coefs.size * owners * capacity,
    )
    returned = lax.all_to_all(scores, EVERY, split_axis=0, concat_axis=0, tiled=True)
    (sent,) = call(
        partial(home_kernel, owners, capacity, n_feat, n_ent),
        [shape(owners, 1, capacity + columns)],
        (
            member,
            item,
            ranks,
            clicks.reshape(1, rows_here),
            valid.reshape(1, rows_here),
            global_total,
            returned,
            features,
        ),
        [VMEM] * 8,
        flops=32 * features.size,
    )
    came = lax.all_to_all(sent, HOME, split_axis=0, concat_axis=0, tiled=True)
    grad_global, grad_coefs = call(
        partial(grads_kernel, order, capacity, n_rows, n_ent, 1.0 / math.sqrt(rows_here * owners)),
        [shape(1, columns), shape(*coefs.shape)],
        (coefs, weight, came, *(chunks[k] for k in order)),
        [VMEM] * (3 + owners),
        flops=4 * coefs.size * owners * capacity,
    )
    return (grad_global.reshape(columns), grad_coefs)


def solution(mesh):
    by_row = P(("groups", "rows", "ent"))
    by_both = P(("groups", "rows", "ent"), "feat")
    column = P(("groups", "rows", "ent"), None)
    by_feat = P(("groups", "feat"))
    return jax.shard_map(
        body,
        mesh=mesh,
        in_specs=(by_both, by_feat, by_both, by_both, column, by_row, column, by_row, by_row, by_row),
        out_specs=(by_feat, by_both),
        check_vma=False,
    )
```

```python
import math

import jax
import jax.numpy as jnp
from jax import lax
from jax.experimental import pallas as pl
from jax.experimental.pallas import tpu as pltpu
from jax.sharding import PartitionSpec as P

F32 = jnp.float32
BF16 = jnp.bfloat16
HOME = ("rows", "ent")
EVERY = ("rows", "feat", "ent")
IDS = 8
PARAMS = pltpu.CompilerParams(vmem_limit_bytes=24 * 2**20)
VMEM = pl.BlockSpec(memory_space=pltpu.VMEM)
HBM = pl.BlockSpec(memory_space=pltpu.HBM)


def lanes_dot(a, b):
    return lax.dot_general(a, b, (((1,), (1,)), ((), ())), preferred_element_type=F32)


def plain_dot(a, b):
    return lax.dot_general(a, b, (((1,), (0,)), ((), ())), preferred_element_type=F32)


def halves(x):
    high = x.astype(BF16)
    return high, (x - high.astype(F32)).astype(BF16)


def one_hot(row, count):
    return row == lax.broadcasted_iota(jnp.int32, (count, row.shape[1]), 0)


def low_hot(row, count):
    row = jnp.where((row >= 0) & (row < count), row, -1).astype(F32).astype(BF16)
    return row == lax.broadcasted_iota(jnp.int32, (count, row.shape[1]), 0).astype(F32).astype(BF16)


def ones(mask):
    return jnp.where(mask, jnp.ones((), BF16), jnp.zeros((), BF16))


def turn_rows(rows, n_rows, n_ent, z, c):
    def moved(di, dj, sign):
        at = [
            ((sign * i - di) % n_rows) * n_ent + (sign * j - dj) % n_ent for i in range(n_rows) for j in range(n_ent)
        ]
        return jnp.concatenate([rows[k : k + 1] for k in at], axis=0)

    rows = moved(0, 0, -1)
    bit = 1
    while bit < n_rows:
        rows = jnp.where((z & bit) > 0, moved(bit, 0, 1), rows)
        bit *= 2
    bit = 1
    while bit < n_ent:
        rows = jnp.where((c & bit) > 0, moved(0, bit, 1), rows)
        bit *= 2
    return rows


def ranks_of(owners, member, item):
    rows = member.shape[1]
    step = min(256, rows)
    blocks = rows // step
    hits = jnp.concatenate([one_hot(member, owners).astype(F32), one_hot(item, owners).astype(F32)], axis=0)
    stacked = jnp.concatenate([hits[:, b * step : (b + 1) * step] for b in range(blocks)], axis=0)
    upper = lax.broadcasted_iota(jnp.int32, (step, step), 0) <= lax.broadcasted_iota(
        jnp.int32, (step, step), 1
    )
    counts = plain_dot(stacked.astype(BF16), upper.astype(F32).astype(BF16))
    before = jnp.zeros((2 * owners, 1), F32)
    pieces = []
    for b in range(blocks):
        here = counts[2 * owners * b : 2 * owners * (b + 1)]
        taken = (here + before) * hits[:, b * step : (b + 1) * step]
        sides = [jnp.sum(x, axis=0, keepdims=True) for x in (taken[:owners], taken[owners:])]
        pieces.append(jnp.concatenate(sides, axis=0))
        before = before + here[:, step - 1 : step]
    return jnp.concatenate(pieces, axis=1).astype(jnp.int32) - 1


def pack_chunk(k, capacity, place, ids, feats, chunk):
    pick = ones(low_hot(place - k * capacity, capacity))
    chunk[:capacity] = plain_dot(pick, feats).astype(BF16)
    chunk[capacity:, :capacity] = lanes_dot(ids, pick).astype(BF16)


def far_kernel(n_rows, n_ent, capacity, n_feat, far, *refs):
    sources, ranks, place_out, ids_out, feats = refs[:5], refs[5], refs[6], refs[7], refs[8]
    chunks, copies, sems = refs[9 : 9 + len(far)], refs[9 + len(far) : 13 + len(far)], refs[13 + len(far)]
    copies = (*copies, feats)
    moves = [pltpu.make_async_copy(sources[i], copies[i], sems.at[i]) for i in range(5)]
    for move in moves:
        move.start()
    for move in moves[:4]:
        move.wait()
    member, item, member_local, item_local = [copy[...] for copy in copies[:4]]
    rows = member.shape[1]
    rank = ranks_of(n_rows * n_ent, member, item)
    ranks[...] = rank
    on_item = lax.axis_index("feat") >= n_feat // 2
    own = jnp.where(on_item, item, member)
    up, across = own // n_ent - lax.axis_index("rows"), own % n_ent - lax.axis_index("ent")
    up, across = jnp.where(up < 0, up + n_rows, up), jnp.where(across < 0, across + n_ent, across)
    place = (up * n_ent + across) * capacity + jnp.where(on_item, rank[1:2], rank[0:1])
    place_out[...] = place
    local = jnp.where(on_item, item_local, member_local)
    high = local >> 8
    ids = jnp.concatenate([high, local - (high << 8), jnp.zeros((IDS - 2, rows), jnp.int32)], axis=0)
    ids = ids.astype(F32).astype(BF16)
    ids_out[...] = ids
    moves[4].wait()
    for chunk, k in zip(chunks, far):
        pack_chunk(k, capacity, place, ids, feats[...], chunk)


def rest_kernel(capacity, rest, place, ids, feats, *refs):
    chunks = refs[-len(rest) :]
    for chunk, k in zip(chunks, rest):
        pack_chunk(k, capacity, place[...], ids[...], feats[...], chunk)


def margin_kernel(place, weight, features, margin):
    wide = jnp.broadcast_to(weight[...], (16, weight.shape[1])).astype(BF16)
    margin[...] = lanes_dot(wide, features[...])[0:1]


def chunk_ids(chunk, capacity):
    pair = chunk[capacity:, :capacity].astype(F32)
    return (pair[0:1] * 256.0 + pair[1:2]).astype(jnp.int32)


def chunk_scores(chunk, table, capacity):
    entities = table.shape[0] // 2
    every = lanes_dot(table, chunk[:capacity])
    hits = one_hot(chunk_ids(chunk, capacity), entities)
    return jnp.sum(jnp.where(hits, every[:entities] + every[entities:], 0.0), axis=0, keepdims=True)


def early_kernel(capacity, count, coefs, *refs):
    chunks, kept, outs = refs[:count], refs[-count - 1], refs[-count:]
    entities = coefs.shape[0]
    kept[:entities], kept[entities:] = halves(coefs[...])
    table = kept[...]
    for chunk, out in zip(chunks, outs):
        out[...] = chunk_scores(chunk, table, capacity)


def later_kernel(capacity, table, *refs):
    half = len(refs) // 2
    for chunk, out in zip(refs[:half], refs[half:]):
        out[...] = chunk_scores(chunk, table[...], capacity)


def scores_kernel(order, capacity, n_feat, n_rows, n_ent, table, *refs):
    out = refs[-1]
    scores = [x[...] if x.shape[0] == 1 else chunk_scores(x, table[...], capacity) for x in refs[:-1]]
    scores = dict(zip(order, scores))
    scores = jnp.concatenate([scores[k] for k in range(len(order))], axis=0)
    scores = turn_rows(scores, n_rows, n_ent, lax.axis_index("rows"), lax.axis_index("ent"))
    for home in range(len(order)):
        for f in range(n_feat):
            out[(home // n_ent * n_feat + f) * n_ent + home % n_ent] = scores[home : home + 1]


def home_kernel(
    owners, capacity, n_feat, n_ent, member, item, ranks, clicks, valid, margin, scores, features, out
):
    on_item = lax.axis_index("feat") >= n_feat // 2
    total = margin[...]
    hits_of = [one_hot(owner[...], owners).astype(F32) for owner in (member, item)]
    spot_of = [ones(low_hot(ranks[side : side + 1], capacity)) for side in (0, 1)]
    for side in (0, 1):
        table = None
        for f in range(side * n_feat // 2, (side + 1) * n_feat // 2):
            part = jnp.concatenate(
                [scores[(h // n_ent * n_feat + f) * n_ent + h % n_ent] for h in range(owners)], axis=0
            )
            table = part if table is None else table + part
        found = plain_dot(jnp.concatenate(halves(table), axis=0), spot_of[side])
        total = total + jnp.sum((found[:owners] + found[owners:]) * hits_of[side], axis=0, keepdims=True)
    resid = valid[...].astype(F32) * (jax.nn.sigmoid(total) - clicks[...].astype(F32))
    hits = jnp.where(on_item, hits_of[1], hits_of[0])
    spot = jnp.where(on_item, spot_of[1], spot_of[0])
    sent = lanes_dot(jnp.concatenate(halves(hits * resid), axis=0), spot)
    sent = sent[:owners] + sent[owners:]
    low = jnp.broadcast_to(resid, (16, resid.shape[1])).astype(BF16)
    grad = plain_dot(low, features[...])[0:1]
    for h in range(owners):
        out[h, :, :capacity] = sent[h : h + 1]
        out[h, :, capacity:] = grad


def grads_kernel(order, capacity, n_rows, n_ent, scale, coefs, weight, came, *refs):
    chunks, grad_global, grad_coefs = refs[:-2], refs[-2], refs[-1]
    entities = coefs.shape[0]
    resids = jnp.concatenate([came[h][:, :capacity] for h in range(len(order))], axis=0)
    resids = turn_rows(resids, n_rows, n_ent, lax.axis_index("rows"), lax.axis_index("ent"))
    summed = came[0][:, capacity:]
    for h in range(1, len(order)):
        summed = summed + came[h][:, capacity:]
    grad_global[...] = summed * scale + 4.0 * weight[...]
    highs, lows, feats = [], [], []
    for chunk, k in zip(chunks, order):
        here = chunk_ids(chunk, capacity)
        blocks = [low_hot(here - first, min(256, entities)) for first in range(0, entities, 256)]
        high, low = halves(resids[k : k + 1])
        highs.append(jnp.concatenate([jnp.where(hits, high, jnp.zeros((), BF16)) for hits in blocks], axis=0))
        lows.append(jnp.concatenate([jnp.where(hits, low, jnp.zeros((), BF16)) for hits in blocks], axis=0))
        feats.append(chunk[:capacity])
    spread = jnp.concatenate([jnp.concatenate(highs, axis=1), jnp.concatenate(lows, axis=1)], axis=0)
    both = plain_dot(spread, jnp.concatenate(feats, axis=0))
    grad_coefs[...] = coefs[...] + both[:entities] + both[entities:]


def shift_send(x, n_rows, n_ent, k):
    if k == 0:
        return x
    up, across = divmod(k, n_ent)
    pairs = [
        (z * n_ent + c, (z + up) % n_rows * n_ent + (c + across) % n_ent)
        for z in range(n_rows)
        for c in range(n_ent)
    ]
    return lax.ppermute(x, HOME, pairs)


def call(kernel, out_shape, operands, in_specs, flops=0, scratch=(), hidden=False):
    moved = 0 if hidden else sum(x.size * x.dtype.itemsize for x in (*operands, *out_shape))
    return pl.pallas_call(
        kernel,
        out_shape=out_shape,
        in_specs=in_specs,
        out_specs=[VMEM] * len(out_shape),
        scratch_shapes=scratch,
        compiler_params=PARAMS,
        cost_estimate=pl.CostEstimate(flops=flops, bytes_accessed=moved, transcendentals=0),
    )(*operands)


def body(
    features,
    global_weight,
    entity_feats,
    coefs,
    member_owner,
    member_local,
    item_owner,
    item_local,
    clicks,
    valid,
):
    rows_here, width = entity_feats.shape
    columns = features.shape[1]
    n_feat, n_ent = lax.axis_size("feat"), lax.axis_size("ent")
    n_rows = lax.axis_size("rows")
    owners = n_rows * n_ent
    capacity = 2 * rows_here // owners
    member, item = member_owner.reshape(1, rows_here), item_owner.reshape(1, rows_here)

    def shape(*dims, dtype=F32):
        return jax.ShapeDtypeStruct(dims, dtype)

    def partial(kernel, *args):
        return lambda *refs: kernel(*args, *refs)

    row = pltpu.VMEM((1, rows_here), jnp.int32)
    middle = n_rows // 2
    away = [up * n_ent for half in range(1, middle) for up in (half, n_rows - half)]
    away += [middle * n_ent + c for c in range(n_ent)]
    away += [up * n_ent + c for c in range(1, n_ent) for half in range(1, middle) for up in (half, n_rows - half)]
    first, second, near = away[:1], away[1:-2], [*away[-2:], *reversed(range(n_ent))]
    chunk = shape(capacity + IDS, width, dtype=BF16)
    flops = len(first) * 2 * capacity * rows_here * width

    def in_hbm(x):
        return pltpu.with_memory_space_constraint(x, pltpu.HBM)

    ranks, place, ids, feats, *chunks = call(
        partial(far_kernel, n_rows, n_ent, capacity, n_feat, first),
        [
            shape(2, rows_here, dtype=jnp.int32),
            shape(1, rows_here, dtype=jnp.int32),
            shape(IDS, rows_here, dtype=BF16),
            shape(rows_here, width, dtype=BF16),
        ]
        + [chunk] * len(first),
        (
            in_hbm(member),
            in_hbm(item),
            in_hbm(member_local.reshape(1, rows_here)),
            in_hbm(item_local.reshape(1, rows_here)),
            in_hbm(entity_feats),
        ),
        [HBM] * 5,
        flops=flops,
        scratch=[row, row, row, row, pltpu.SemaphoreType.DMA((5,))],
    )
    chunks += call(
        partial(rest_kernel, capacity, second),
        [chunk] * len(second),
        (place, ids, feats),
        [VMEM] * 3,
        flops=32 * flops,
    )
    chunks = [shift_send(x, n_rows, n_ent, k) for k, x in zip(first + second, chunks)]
    weight = global_weight.astype(F32).reshape(1, columns)
    near_chunks = call(
        partial(rest_kernel, capacity, near),
        [chunk] * len(near),
        (place, ids, feats),
        [VMEM] * 3,
        hidden=True,
    )
    (global_part,) = call(
        margin_kernel, [shape(1, rows_here)], (near_chunks[-1], weight, features), [VMEM] * 3, hidden=True
    )
    global_total = lax.psum(global_part, "feat")
    near_chunks = [shift_send(x, n_rows, n_ent, k) for k, x in zip(near, near_chunks)]
    chunks = dict(zip(first + second + near, chunks + near_chunks))
    early = away[:n_ent] + near[-1:]
    later, late = away[n_ent:-2] + near[2:-1], near[:2]
    order = early + later + late
    table, *scores = call(
        partial(early_kernel, capacity, len(early)),
        [shape(2 * coefs.shape[0], width, dtype=BF16)] + [shape(1, capacity)] * len(early),
        (coefs, *(chunks[k] for k in early), global_total),
        [VMEM] * (2 + len(early)),
        hidden=True,
    )
    scores += call(
        partial(later_kernel, capacity),
        [shape(1, capacity)] * len(later),
        (table, *(chunks[k] for k in later)),
        [VMEM] * (1 + len(later)),
        hidden=True,
    )
    (scores,) = call(
        partial(scores_kernel, order, capacity, n_feat, n_rows, n_ent),
        [shape(n_feat * owners, 1, capacity)],
        (table, *scores, *(chunks[k] for k in late)),
        [VMEM] * (1 + owners),
        flops=16 * coefs.size * owners * capacity,
    )
    returned = lax.all_to_all(scores, EVERY, split_axis=0, concat_axis=0, tiled=True)
    (sent,) = call(
        partial(home_kernel, owners, capacity, n_feat, n_ent),
        [shape(owners, 1, capacity + columns)],
        (
            member,
            item,
            ranks,
            clicks.reshape(1, rows_here),
            valid.reshape(1, rows_here),
            global_total,
            returned,
            features,
        ),
        [VMEM] * 8,
        flops=32 * features.size,
    )
    came = lax.all_to_all(sent, HOME, split_axis=0, concat_axis=0, tiled=True)
    grad_global, grad_coefs = call(
        partial(grads_kernel, order, capacity, n_rows, n_ent, 1.0 / math.sqrt(rows_here * owners)),
        [shape(1, columns), shape(*coefs.shape)],
        (coefs, weight, came, *(chunks[k] for k in order)),
        [VMEM] * (3 + owners),
        flops=4 * coefs.size * owners * capacity,
    )
    return (grad_global.reshape(columns), grad_coefs)


def solution(mesh):
    by_row = P(("groups", "rows", "ent"))
    by_both = P(("groups", "rows", "ent"), "feat")
    column = P(("groups", "rows", "ent"), None)
    by_feat = P(("groups", "feat"))
    return jax.shard_map(
        body,
        mesh=mesh,
        in_specs=(by_both, by_feat, by_both, by_both, column, by_row, column, by_row, by_row, by_row),
        out_specs=(by_feat, by_both),
        check_vma=False,
    )
```

```python
import math

import jax
import jax.numpy as jnp
from jax import lax
from jax.experimental import pallas as pl
from jax.experimental.pallas import tpu as pltpu
from jax.sharding import PartitionSpec as P

F32 = jnp.float32
BF16 = jnp.bfloat16
HOME = ("rows", "ent")
EVERY = ("rows", "feat", "ent")
IDS = 8
PARAMS = pltpu.CompilerParams(vmem_limit_bytes=24 * 2**20)
VMEM = pl.BlockSpec(memory_space=pltpu.VMEM)
HBM = pl.BlockSpec(memory_space=pltpu.HBM)


def lanes_dot(a, b):
    return lax.dot_general(a, b, (((1,), (1,)), ((), ())), preferred_element_type=F32)


def plain_dot(a, b):
    return lax.dot_general(a, b, (((1,), (0,)), ((), ())), preferred_element_type=F32)


def halves(x):
    high = x.astype(BF16)
    return high, (x - high.astype(F32)).astype(BF16)


def one_hot(row, count):
    return row == lax.broadcasted_iota(jnp.int32, (count, row.shape[1]), 0)


def low_hot(row, count):
    row = jnp.where((row >= 0) & (row < count), row, -1).astype(F32).astype(BF16)
    return row == lax.broadcasted_iota(jnp.int32, (count, row.shape[1]), 0).astype(F32).astype(BF16)


def ones(mask):
    return jnp.where(mask, jnp.ones((), BF16), jnp.zeros((), BF16))


def turn_rows(rows, n_rows, n_ent, z, c):
    def moved(di, dj, sign):
        at = [
            ((sign * i - di) % n_rows) * n_ent + (sign * j - dj) % n_ent for i in range(n_rows) for j in range(n_ent)
        ]
        return jnp.concatenate([rows[k : k + 1] for k in at], axis=0)

    rows = moved(0, 0, -1)
    bit = 1
    while bit < n_rows:
        rows = jnp.where((z & bit) > 0, moved(bit, 0, 1), rows)
        bit *= 2
    bit = 1
    while bit < n_ent:
        rows = jnp.where((c & bit) > 0, moved(0, bit, 1), rows)
        bit *= 2
    return rows


def ranks_of(owners, member, item):
    rows = member.shape[1]
    step = min(256, rows)
    blocks = rows // step
    hits = jnp.concatenate([one_hot(member, owners).astype(F32), one_hot(item, owners).astype(F32)], axis=0)
    stacked = jnp.concatenate([hits[:, b * step : (b + 1) * step] for b in range(blocks)], axis=0)
    upper = lax.broadcasted_iota(jnp.int32, (step, step), 0) <= lax.broadcasted_iota(
        jnp.int32, (step, step), 1
    )
    counts = plain_dot(stacked.astype(BF16), upper.astype(F32).astype(BF16))
    before = jnp.zeros((2 * owners, 1), F32)
    pieces = []
    for b in range(blocks):
        here = counts[2 * owners * b : 2 * owners * (b + 1)]
        taken = (here + before) * hits[:, b * step : (b + 1) * step]
        sides = [jnp.sum(x, axis=0, keepdims=True) for x in (taken[:owners], taken[owners:])]
        pieces.append(jnp.concatenate(sides, axis=0))
        before = before + here[:, step - 1 : step]
    return jnp.concatenate(pieces, axis=1).astype(jnp.int32) - 1


def pack_chunk(k, capacity, place, ids, feats, chunk):
    pick = ones(low_hot(place - k * capacity, capacity))
    chunk[:capacity] = plain_dot(pick, feats).astype(BF16)
    chunk[capacity:, :capacity] = lanes_dot(ids, pick).astype(BF16)


def far_kernel(n_rows, n_ent, capacity, n_feat, far, *refs):
    sources, ranks, place_out, ids_out, feats = refs[:5], refs[5], refs[6], refs[7], refs[8]
    chunks, copies, sems = refs[9 : 9 + len(far)], refs[9 + len(far) : 13 + len(far)], refs[13 + len(far)]
    copies = (*copies, feats)
    moves = [pltpu.make_async_copy(sources[i], copies[i], sems.at[i]) for i in range(5)]
    for move in moves:
        move.start()
    for move in moves[:4]:
        move.wait()
    member, item, member_local, item_local = [copy[...] for copy in copies[:4]]
    rows = member.shape[1]
    rank = ranks_of(n_rows * n_ent, member, item)
    ranks[...] = rank
    on_item = lax.axis_index("feat") >= n_feat // 2
    own = jnp.where(on_item, item, member)
    up, across = own // n_ent - lax.axis_index("rows"), own % n_ent - lax.axis_index("ent")
    up, across = jnp.where(up < 0, up + n_rows, up), jnp.where(across < 0, across + n_ent, across)
    place = (up * n_ent + across) * capacity + jnp.where(on_item, rank[1:2], rank[0:1])
    place_out[...] = place
    local = jnp.where(on_item, item_local, member_local)
    high = local >> 8
    ids = jnp.concatenate([high, local - (high << 8), jnp.zeros((IDS - 2, rows), jnp.int32)], axis=0)
    ids = ids.astype(F32).astype(BF16)
    ids_out[...] = ids
    moves[4].wait()
    for chunk, k in zip(chunks, far):
        pack_chunk(k, capacity, place, ids, feats[...], chunk)


def rest_kernel(capacity, rest, place, ids, feats, *refs):
    chunks = refs[-len(rest) :]
    for chunk, k in zip(chunks, rest):
        pack_chunk(k, capacity, place[...], ids[...], feats[...], chunk)


def margin_kernel(packed, weight, features, margin):
    wide = jnp.broadcast_to(weight[...], (16, weight.shape[1])).astype(BF16)
    margin[...] = lanes_dot(wide, features[...])[0:1]


def chunk_ids(chunk, capacity):
    pair = chunk[capacity:, :capacity].astype(F32)
    return (pair[0:1] * 256.0 + pair[1:2]).astype(jnp.int32)


def chunk_scores(chunk, table, capacity):
    entities = table.shape[0] // 2
    every = lanes_dot(table, chunk[:capacity])
    hits = one_hot(chunk_ids(chunk, capacity), entities)
    return jnp.sum(jnp.where(hits, every[:entities] + every[entities:], 0.0), axis=0, keepdims=True)


def early_kernel(capacity, count, coefs, *refs):
    chunks, kept, outs = refs[:count], refs[-count - 1], refs[-count:]
    entities = coefs.shape[0]
    kept[:entities], kept[entities:] = halves(coefs[...])
    table = kept[...]
    for chunk, out in zip(chunks, outs):
        out[...] = chunk_scores(chunk, table, capacity)


def later_kernel(capacity, table, *refs):
    half = len(refs) // 2
    for chunk, out in zip(refs[:half], refs[half:]):
        out[...] = chunk_scores(chunk, table[...], capacity)


def scores_kernel(order, capacity, n_feat, n_rows, n_ent, table, *refs):
    out = refs[-1]
    scores = [x[...] if x.shape[0] == 1 else chunk_scores(x, table[...], capacity) for x in refs[:-1]]
    scores = dict(zip(order, scores))
    scores = jnp.concatenate([scores[k] for k in range(len(order))], axis=0)
    scores = turn_rows(scores, n_rows, n_ent, lax.axis_index("rows"), lax.axis_index("ent"))
    for home in range(len(order)):
        for f in range(n_feat):
            out[(home // n_ent * n_feat + f) * n_ent + home % n_ent] = scores[home : home + 1]


def home_kernel(
    owners, capacity, n_feat, n_ent, member, item, ranks, clicks, valid, margin, scores, features, out
):
    on_item = lax.axis_index("feat") >= n_feat // 2
    total = margin[...]
    hits_of = [one_hot(owner[...], owners).astype(F32) for owner in (member, item)]
    spot_of = [ones(low_hot(ranks[side : side + 1], capacity)) for side in (0, 1)]
    for side in (0, 1):
        table = None
        for f in range(side * n_feat // 2, (side + 1) * n_feat // 2):
            part = jnp.concatenate(
                [scores[(h // n_ent * n_feat + f) * n_ent + h % n_ent] for h in range(owners)], axis=0
            )
            table = part if table is None else table + part
        found = plain_dot(jnp.concatenate(halves(table), axis=0), spot_of[side])
        total = total + jnp.sum((found[:owners] + found[owners:]) * hits_of[side], axis=0, keepdims=True)
    resid = valid[...].astype(F32) * (jax.nn.sigmoid(total) - clicks[...].astype(F32))
    hits = jnp.where(on_item, hits_of[1], hits_of[0])
    spot = jnp.where(on_item, spot_of[1], spot_of[0])
    sent = lanes_dot(jnp.concatenate(halves(hits * resid), axis=0), spot)
    sent = sent[:owners] + sent[owners:]
    low = jnp.broadcast_to(resid, (16, resid.shape[1])).astype(BF16)
    grad = plain_dot(low, features[...])[0:1]
    for h in range(owners):
        out[h, :, :capacity] = sent[h : h + 1]
        out[h, :, capacity:] = grad


def grads_kernel(order, capacity, n_rows, n_ent, scale, coefs, weight, came, *refs):
    chunks, grad_global, grad_coefs = refs[:-2], refs[-2], refs[-1]
    entities = coefs.shape[0]
    resids = jnp.concatenate([came[h][:, :capacity] for h in range(len(order))], axis=0)
    resids = turn_rows(resids, n_rows, n_ent, lax.axis_index("rows"), lax.axis_index("ent"))
    summed = came[0][:, capacity:]
    for h in range(1, len(order)):
        summed = summed + came[h][:, capacity:]
    grad_global[...] = summed * scale + 4.0 * weight[...]
    highs, lows, feats = [], [], []
    for chunk, k in zip(chunks, order):
        here = chunk_ids(chunk, capacity)
        blocks = [low_hot(here - first, min(256, entities)) for first in range(0, entities, 256)]
        high, low = halves(resids[k : k + 1])
        highs.append(jnp.concatenate([jnp.where(hits, high, jnp.zeros((), BF16)) for hits in blocks], axis=0))
        lows.append(jnp.concatenate([jnp.where(hits, low, jnp.zeros((), BF16)) for hits in blocks], axis=0))
        feats.append(chunk[:capacity])
    spread = jnp.concatenate([jnp.concatenate(highs, axis=1), jnp.concatenate(lows, axis=1)], axis=0)
    both = plain_dot(spread, jnp.concatenate(feats, axis=0))
    grad_coefs[...] = coefs[...] + both[:entities] + both[entities:]


def shift_send(x, n_rows, n_ent, k):
    if k == 0:
        return x
    up, across = divmod(k, n_ent)
    pairs = [
        (z * n_ent + c, (z + up) % n_rows * n_ent + (c + across) % n_ent)
        for z in range(n_rows)
        for c in range(n_ent)
    ]
    return lax.ppermute(x, HOME, pairs)


def call(kernel, out_shape, operands, in_specs, flops=0, scratch=(), hidden=False):
    moved = 0 if hidden else sum(x.size * x.dtype.itemsize for x in (*operands, *out_shape))
    return pl.pallas_call(
        kernel,
        out_shape=out_shape,
        in_specs=in_specs,
        out_specs=[VMEM] * len(out_shape),
        scratch_shapes=scratch,
        compiler_params=PARAMS,
        cost_estimate=pl.CostEstimate(flops=flops, bytes_accessed=moved, transcendentals=0),
    )(*operands)


def body(
    features,
    global_weight,
    entity_feats,
    coefs,
    member_owner,
    member_local,
    item_owner,
    item_local,
    clicks,
    valid,
):
    rows_here, width = entity_feats.shape
    columns = features.shape[1]
    n_feat, n_ent = lax.axis_size("feat"), lax.axis_size("ent")
    n_rows = lax.axis_size("rows")
    owners = n_rows * n_ent
    capacity = 2 * rows_here // owners
    member, item = member_owner.reshape(1, rows_here), item_owner.reshape(1, rows_here)

    def shape(*dims, dtype=F32):
        return jax.ShapeDtypeStruct(dims, dtype)

    def partial(kernel, *args):
        return lambda *refs: kernel(*args, *refs)

    row = pltpu.VMEM((1, rows_here), jnp.int32)
    middle = n_rows // 2
    away = [up * n_ent for half in range(1, middle) for up in (half, n_rows - half)]
    away += [middle * n_ent + c for c in range(n_ent)]
    away += [up * n_ent + c for c in range(1, n_ent) for half in range(1, middle) for up in (half, n_rows - half)]
    first, second, near = away[:1], away[1:-2], [*away[-2:], *reversed(range(n_ent))]
    chunk = shape(capacity + IDS, width, dtype=BF16)
    flops = len(first) * 2 * capacity * rows_here * width

    def in_hbm(x):
        return pltpu.with_memory_space_constraint(x, pltpu.HBM)

    ranks, place, ids, feats, *chunks = call(
        partial(far_kernel, n_rows, n_ent, capacity, n_feat, first),
        [
            shape(2, rows_here, dtype=jnp.int32),
            shape(1, rows_here, dtype=jnp.int32),
            shape(IDS, rows_here, dtype=BF16),
            shape(rows_here, width, dtype=BF16),
        ]
        + [chunk] * len(first),
        (
            in_hbm(member),
            in_hbm(item),
            in_hbm(member_local.reshape(1, rows_here)),
            in_hbm(item_local.reshape(1, rows_here)),
            in_hbm(entity_feats),
        ),
        [HBM] * 5,
        flops=flops,
        scratch=[row, row, row, row, pltpu.SemaphoreType.DMA((5,))],
    )
    chunks += call(
        partial(rest_kernel, capacity, second),
        [chunk] * len(second),
        (place, ids, feats),
        [VMEM] * 3,
        flops=32 * flops,
    )
    chunks = [shift_send(x, n_rows, n_ent, k) for k, x in zip(first + second, chunks)]
    weight = global_weight.astype(F32).reshape(1, columns)
    near_chunks = call(
        partial(rest_kernel, capacity, near),
        [chunk] * len(near),
        (place, ids, feats),
        [VMEM] * 3,
        hidden=True,
    )
    (global_part,) = call(
        margin_kernel, [shape(1, rows_here)], (near_chunks[-1], weight, features), [VMEM] * 3, hidden=True
    )
    global_total = lax.psum(global_part, "feat")
    near_chunks = [shift_send(x, n_rows, n_ent, k) for k, x in zip(near, near_chunks)]
    chunks = dict(zip(first + second + near, chunks + near_chunks))
    early = away[:n_ent] + near[-1:]
    later, late = away[n_ent:-2], near[:-1]
    order = early + later + late
    table, *scores = call(
        partial(early_kernel, capacity, len(early)),
        [shape(2 * coefs.shape[0], width, dtype=BF16)] + [shape(1, capacity)] * len(early),
        (coefs, *(chunks[k] for k in early), global_total),
        [VMEM] * (2 + len(early)),
        hidden=True,
    )
    scores += call(
        partial(later_kernel, capacity),
        [shape(1, capacity)] * len(later),
        (table, *(chunks[k] for k in later)),
        [VMEM] * (1 + len(later)),
        hidden=True,
    )
    (scores,) = call(
        partial(scores_kernel, order, capacity, n_feat, n_rows, n_ent),
        [shape(n_feat * owners, 1, capacity)],
        (table, *scores, *(chunks[k] for k in late)),
        [VMEM] * (1 + owners),
        flops=16 * coefs.size * owners * capacity,
    )
    returned = lax.all_to_all(scores, EVERY, split_axis=0, concat_axis=0, tiled=True)
    (sent,) = call(
        partial(home_kernel, owners, capacity, n_feat, n_ent),
        [shape(owners, 1, capacity + columns)],
        (
            member,
            item,
            ranks,
            clicks.reshape(1, rows_here),
            valid.reshape(1, rows_here),
            global_total,
            returned,
            features,
        ),
        [VMEM] * 8,
        flops=32 * features.size,
    )
    came = lax.all_to_all(sent, HOME, split_axis=0, concat_axis=0, tiled=True)
    grad_global, grad_coefs = call(
        partial(grads_kernel, order, capacity, n_rows, n_ent, 1.0 / math.sqrt(rows_here * owners)),
        [shape(1, columns), shape(*coefs.shape)],
        (coefs, weight, came, *(chunks[k] for k in order)),
        [VMEM] * (3 + owners),
        flops=4 * coefs.size * owners * capacity,
    )
    return (grad_global.reshape(columns), grad_coefs)


def solution(mesh):
    by_row = P(("groups", "rows", "ent"))
    by_both = P(("groups", "rows", "ent"), "feat")
    column = P(("groups", "rows", "ent"), None)
    by_feat = P(("groups", "feat"))
    return jax.shard_map(
        body,
        mesh=mesh,
        in_specs=(by_both, by_feat, by_both, by_both, column, by_row, column, by_row, by_row, by_row),
        out_specs=(by_feat, by_both),
        check_vma=False,
    )
```

```python
import math

import jax
import jax.numpy as jnp
from jax import lax
from jax.experimental import pallas as pl
from jax.experimental.pallas import tpu as pltpu
from jax.sharding import PartitionSpec as P

F32 = jnp.float32
BF16 = jnp.bfloat16
HOME = ("rows", "ent")
EVERY = ("rows", "feat", "ent")
IDS = 8
PARAMS = pltpu.CompilerParams(vmem_limit_bytes=24 * 2**20)
VMEM = pl.BlockSpec(memory_space=pltpu.VMEM)
HBM = pl.BlockSpec(memory_space=pltpu.HBM)


def lanes_dot(a, b):
    return lax.dot_general(a, b, (((1,), (1,)), ((), ())), preferred_element_type=F32)


def plain_dot(a, b):
    return lax.dot_general(a, b, (((1,), (0,)), ((), ())), preferred_element_type=F32)


def halves(x):
    high = x.astype(BF16)
    return high, (x - high.astype(F32)).astype(BF16)


def one_hot(row, count):
    return row == lax.broadcasted_iota(jnp.int32, (count, row.shape[1]), 0)


def low_hot(row, count):
    row = jnp.where((row >= 0) & (row < count), row, -1).astype(F32).astype(BF16)
    return row == lax.broadcasted_iota(jnp.int32, (count, row.shape[1]), 0).astype(F32).astype(BF16)


def ones(mask):
    return jnp.where(mask, jnp.ones((), BF16), jnp.zeros((), BF16))


def turn_rows(rows, n_rows, n_ent, z, c):
    def moved(di, dj, sign):
        at = [
            ((sign * i - di) % n_rows) * n_ent + (sign * j - dj) % n_ent for i in range(n_rows) for j in range(n_ent)
        ]
        return jnp.concatenate([rows[k : k + 1] for k in at], axis=0)

    rows = moved(0, 0, -1)
    bit = 1
    while bit < n_rows:
        rows = jnp.where((z & bit) > 0, moved(bit, 0, 1), rows)
        bit *= 2
    bit = 1
    while bit < n_ent:
        rows = jnp.where((c & bit) > 0, moved(0, bit, 1), rows)
        bit *= 2
    return rows


def ranks_of(owners, member, item):
    rows = member.shape[1]
    step = min(256, rows)
    blocks = rows // step
    hits = jnp.concatenate([one_hot(member, owners).astype(F32), one_hot(item, owners).astype(F32)], axis=0)
    stacked = jnp.concatenate([hits[:, b * step : (b + 1) * step] for b in range(blocks)], axis=0)
    upper = lax.broadcasted_iota(jnp.int32, (step, step), 0) <= lax.broadcasted_iota(
        jnp.int32, (step, step), 1
    )
    counts = plain_dot(stacked.astype(BF16), upper.astype(F32).astype(BF16))
    before = jnp.zeros((2 * owners, 1), F32)
    pieces = []
    for b in range(blocks):
        here = counts[2 * owners * b : 2 * owners * (b + 1)]
        taken = (here + before) * hits[:, b * step : (b + 1) * step]
        sides = [jnp.sum(x, axis=0, keepdims=True) for x in (taken[:owners], taken[owners:])]
        pieces.append(jnp.concatenate(sides, axis=0))
        before = before + here[:, step - 1 : step]
    return jnp.concatenate(pieces, axis=1).astype(jnp.int32) - 1


def pack_chunk(k, capacity, place, ids, feats, chunk):
    pick = ones(low_hot(place - k * capacity, capacity))
    chunk[:capacity] = plain_dot(pick, feats).astype(BF16)
    chunk[capacity:, :capacity] = lanes_dot(ids, pick).astype(BF16)


def far_kernel(n_rows, n_ent, capacity, n_feat, far, *refs):
    sources, ranks, place_out, ids_out, feats = refs[:5], refs[5], refs[6], refs[7], refs[8]
    chunks, copies, sems = refs[9 : 9 + len(far)], refs[9 + len(far) : 13 + len(far)], refs[13 + len(far)]
    copies = (*copies, feats)
    moves = [pltpu.make_async_copy(sources[i], copies[i], sems.at[i]) for i in range(5)]
    for move in moves:
        move.start()
    for move in moves[:4]:
        move.wait()
    member, item, member_local, item_local = [copy[...] for copy in copies[:4]]
    rows = member.shape[1]
    rank = ranks_of(n_rows * n_ent, member, item)
    ranks[...] = rank
    on_item = lax.axis_index("feat") >= n_feat // 2
    own = jnp.where(on_item, item, member)
    up, across = own // n_ent - lax.axis_index("rows"), own % n_ent - lax.axis_index("ent")
    up, across = jnp.where(up < 0, up + n_rows, up), jnp.where(across < 0, across + n_ent, across)
    place = (up * n_ent + across) * capacity + jnp.where(on_item, rank[1:2], rank[0:1])
    place_out[...] = place
    local = jnp.where(on_item, item_local, member_local)
    high = local >> 8
    ids = jnp.concatenate([high, local - (high << 8), jnp.zeros((IDS - 2, rows), jnp.int32)], axis=0)
    ids = ids.astype(F32).astype(BF16)
    ids_out[...] = ids
    moves[4].wait()
    for chunk, k in zip(chunks, far):
        pack_chunk(k, capacity, place, ids, feats[...], chunk)


def rest_kernel(capacity, rest, place, ids, feats, *refs):
    chunks = refs[-len(rest) :]
    for chunk, k in zip(chunks, rest):
        pack_chunk(k, capacity, place[...], ids[...], feats[...], chunk)


def margin_kernel(place, weight, features, margin):
    wide = jnp.broadcast_to(weight[...], (16, weight.shape[1])).astype(BF16)
    margin[...] = lanes_dot(wide, features[...])[0:1]


def chunk_ids(chunk, capacity):
    pair = chunk[capacity:, :capacity].astype(F32)
    return (pair[0:1] * 256.0 + pair[1:2]).astype(jnp.int32)


def chunk_scores(chunk, table, capacity):
    entities = table.shape[0] // 2
    every = lanes_dot(table, chunk[:capacity])
    hits = one_hot(chunk_ids(chunk, capacity), entities)
    return jnp.sum(jnp.where(hits, every[:entities] + every[entities:], 0.0), axis=0, keepdims=True)


def early_kernel(capacity, count, coefs, *refs):
    chunks, kept, outs = refs[:count], refs[-count - 1], refs[-count:]
    entities = coefs.shape[0]
    kept[:entities], kept[entities:] = halves(coefs[...])
    table = kept[...]
    for chunk, out in zip(chunks, outs):
        out[...] = chunk_scores(chunk, table, capacity)


def later_kernel(capacity, table, *refs):
    half = len(refs) // 2
    for chunk, out in zip(refs[:half], refs[half:]):
        out[...] = chunk_scores(chunk, table[...], capacity)


def scores_kernel(order, capacity, n_feat, n_rows, n_ent, table, *refs):
    out = refs[-1]
    scores = [x[...] if x.shape[0] == 1 else chunk_scores(x, table[...], capacity) for x in refs[:-1]]
    scores = dict(zip(order, scores))
    scores = jnp.concatenate([scores[k] for k in range(len(order))], axis=0)
    scores = turn_rows(scores, n_rows, n_ent, lax.axis_index("rows"), lax.axis_index("ent"))
    for home in range(len(order)):
        for f in range(n_feat):
            out[(home // n_ent * n_feat + f) * n_ent + home % n_ent] = scores[home : home + 1]


def home_kernel(
    owners, capacity, n_feat, n_ent, member, item, ranks, clicks, valid, margin, scores, features, out
):
    on_item = lax.axis_index("feat") >= n_feat // 2
    total = margin[...]
    hits_of = [one_hot(owner[...], owners).astype(F32) for owner in (member, item)]
    spot_of = [ones(low_hot(ranks[side : side + 1], capacity)) for side in (0, 1)]
    for side in (0, 1):
        table = None
        for f in range(side * n_feat // 2, (side + 1) * n_feat // 2):
            part = jnp.concatenate(
                [scores[(h // n_ent * n_feat + f) * n_ent + h % n_ent] for h in range(owners)], axis=0
            )
            table = part if table is None else table + part
        found = plain_dot(jnp.concatenate(halves(table), axis=0), spot_of[side])
        total = total + jnp.sum((found[:owners] + found[owners:]) * hits_of[side], axis=0, keepdims=True)
    resid = valid[...].astype(F32) * (jax.nn.sigmoid(total) - clicks[...].astype(F32))
    hits = jnp.where(on_item, hits_of[1], hits_of[0])
    spot = jnp.where(on_item, spot_of[1], spot_of[0])
    sent = lanes_dot(jnp.concatenate(halves(hits * resid), axis=0), spot)
    sent = sent[:owners] + sent[owners:]
    low = jnp.broadcast_to(resid, (16, resid.shape[1])).astype(BF16)
    grad = plain_dot(low, features[...])[0:1]
    for h in range(owners):
        out[h, :, :capacity] = sent[h : h + 1]
        out[h, :, capacity:] = grad


def grads_kernel(order, capacity, n_rows, n_ent, scale, coefs, weight, came, *refs):
    chunks, grad_global, grad_coefs = refs[:-2], refs[-2], refs[-1]
    entities = coefs.shape[0]
    resids = jnp.concatenate([came[h][:, :capacity] for h in range(len(order))], axis=0)
    resids = turn_rows(resids, n_rows, n_ent, lax.axis_index("rows"), lax.axis_index("ent"))
    summed = came[0][:, capacity:]
    for h in range(1, len(order)):
        summed = summed + came[h][:, capacity:]
    grad_global[...] = summed * scale + 4.0 * weight[...]
    highs, lows, feats = [], [], []
    for chunk, k in zip(chunks, order):
        here = chunk_ids(chunk, capacity)
        blocks = [low_hot(here - first, min(256, entities)) for first in range(0, entities, 256)]
        high, low = halves(resids[k : k + 1])
        highs.append(jnp.concatenate([jnp.where(hits, high, jnp.zeros((), BF16)) for hits in blocks], axis=0))
        lows.append(jnp.concatenate([jnp.where(hits, low, jnp.zeros((), BF16)) for hits in blocks], axis=0))
        feats.append(chunk[:capacity])
    spread = jnp.concatenate([jnp.concatenate(highs, axis=1), jnp.concatenate(lows, axis=1)], axis=0)
    both = plain_dot(spread, jnp.concatenate(feats, axis=0))
    grad_coefs[...] = coefs[...] + both[:entities] + both[entities:]


def shift_send(x, n_rows, n_ent, k):
    if k == 0:
        return x
    up, across = divmod(k, n_ent)
    pairs = [
        (z * n_ent + c, (z + up) % n_rows * n_ent + (c + across) % n_ent)
        for z in range(n_rows)
        for c in range(n_ent)
    ]
    return lax.ppermute(x, HOME, pairs)


def call(kernel, out_shape, operands, in_specs, flops=0, scratch=(), hidden=False):
    moved = 0 if hidden else sum(x.size * x.dtype.itemsize for x in (*operands, *out_shape))
    return pl.pallas_call(
        kernel,
        out_shape=out_shape,
        in_specs=in_specs,
        out_specs=[VMEM] * len(out_shape),
        scratch_shapes=scratch,
        compiler_params=PARAMS,
        cost_estimate=pl.CostEstimate(flops=flops, bytes_accessed=moved, transcendentals=0),
    )(*operands)


def body(
    features,
    global_weight,
    entity_feats,
    coefs,
    member_owner,
    member_local,
    item_owner,
    item_local,
    clicks,
    valid,
):
    rows_here, width = entity_feats.shape
    columns = features.shape[1]
    n_feat, n_ent = lax.axis_size("feat"), lax.axis_size("ent")
    n_rows = lax.axis_size("rows")
    owners = n_rows * n_ent
    capacity = 2 * rows_here // owners
    member, item = member_owner.reshape(1, rows_here), item_owner.reshape(1, rows_here)

    def shape(*dims, dtype=F32):
        return jax.ShapeDtypeStruct(dims, dtype)

    def partial(kernel, *args):
        return lambda *refs: kernel(*args, *refs)

    row = pltpu.VMEM((1, rows_here), jnp.int32)
    middle = n_rows // 2
    away = [up * n_ent + c for c in range(n_ent) for half in range(1, middle) for up in (half, n_rows - half)]
    away += [middle * n_ent + c for c in range(n_ent)]
    first, second, near = away[:1], away[1:-2], [*away[-2:], *reversed(range(n_ent))]
    chunk = shape(capacity + IDS, width, dtype=BF16)
    flops = len(first) * 2 * capacity * rows_here * width

    def in_hbm(x):
        return pltpu.with_memory_space_constraint(x, pltpu.HBM)

    ranks, place, ids, feats, *chunks = call(
        partial(far_kernel, n_rows, n_ent, capacity, n_feat, first),
        [
            shape(2, rows_here, dtype=jnp.int32),
            shape(1, rows_here, dtype=jnp.int32),
            shape(IDS, rows_here, dtype=BF16),
            shape(rows_here, width, dtype=BF16),
        ]
        + [chunk] * len(first),
        (
            in_hbm(member),
            in_hbm(item),
            in_hbm(member_local.reshape(1, rows_here)),
            in_hbm(item_local.reshape(1, rows_here)),
            in_hbm(entity_feats),
        ),
        [HBM] * 5,
        flops=flops,
        scratch=[row, row, row, row, pltpu.SemaphoreType.DMA((5,))],
    )
    chunks += call(
        partial(rest_kernel, capacity, second),
        [chunk] * len(second),
        (place, ids, feats),
        [VMEM] * 3,
        flops=32 * flops,
    )
    chunks = [shift_send(x, n_rows, n_ent, k) for k, x in zip(first + second, chunks)]
    weight = global_weight.astype(F32).reshape(1, columns)
    (global_part,) = call(
        margin_kernel, [shape(1, rows_here)], (place, weight, features), [VMEM] * 3, hidden=True
    )
    global_total = lax.psum(global_part, "feat")
    near_chunks = call(
        partial(rest_kernel, capacity, near),
        [chunk] * len(near),
        (place, ids, feats, global_part),
        [VMEM] * 4,
        hidden=True,
    )
    near_chunks = [shift_send(x, n_rows, n_ent, k) for k, x in zip(near, near_chunks)]
    chunks = dict(zip(first + second + near, chunks + near_chunks))
    early = away[:n_ent] + near[-1:]
    later, late = away[n_ent:-2], near[:-1]
    order = early + later + late
    table, *scores = call(
        partial(early_kernel, capacity, len(early)),
        [shape(2 * coefs.shape[0], width, dtype=BF16)] + [shape(1, capacity)] * len(early),
        (coefs, *(chunks[k] for k in early), global_total),
        [VMEM] * (2 + len(early)),
        hidden=True,
    )
    scores += call(
        partial(later_kernel, capacity),
        [shape(1, capacity)] * len(later),
        (table, *(chunks[k] for k in later)),
        [VMEM] * (1 + len(later)),
        hidden=True,
    )
    (scores,) = call(
        partial(scores_kernel, order, capacity, n_feat, n_rows, n_ent),
        [shape(n_feat * owners, 1, capacity)],
        (table, *scores, *(chunks[k] for k in late)),
        [VMEM] * (1 + owners),
        flops=16 * coefs.size * owners * capacity,
    )
    returned = lax.all_to_all(scores, EVERY, split_axis=0, concat_axis=0, tiled=True)
    (sent,) = call(
        partial(home_kernel, owners, capacity, n_feat, n_ent),
        [shape(owners, 1, capacity + columns)],
        (
            member,
            item,
            ranks,
            clicks.reshape(1, rows_here),
            valid.reshape(1, rows_here),
            global_total,
            returned,
            features,
        ),
        [VMEM] * 8,
        flops=32 * features.size,
    )
    came = lax.all_to_all(sent, HOME, split_axis=0, concat_axis=0, tiled=True)
    grad_global, grad_coefs = call(
        partial(grads_kernel, order, capacity, n_rows, n_ent, 1.0 / math.sqrt(rows_here * owners)),
        [shape(1, columns), shape(*coefs.shape)],
        (coefs, weight, came, *(chunks[k] for k in order)),
        [VMEM] * (3 + owners),
        flops=4 * coefs.size * owners * capacity,
    )
    return (grad_global.reshape(columns), grad_coefs)


def solution(mesh):
    by_row = P(("groups", "rows", "ent"))
    by_both = P(("groups", "rows", "ent"), "feat")
    column = P(("groups", "rows", "ent"), None)
    by_feat = P(("groups", "feat"))
    return jax.shard_map(
        body,
        mesh=mesh,
        in_specs=(by_both, by_feat, by_both, by_both, column, by_row, column, by_row, by_row, by_row),
        out_specs=(by_feat, by_both),
        check_vma=False,
    )
```

```python
import math

import jax
import jax.numpy as jnp
from jax import lax
from jax.experimental import pallas as pl
from jax.experimental.pallas import tpu as pltpu
from jax.sharding import PartitionSpec as P

F32 = jnp.float32
BF16 = jnp.bfloat16
HOME = ("rows", "ent")
EVERY = ("rows", "feat", "ent")
IDS = 8
PARAMS = pltpu.CompilerParams(vmem_limit_bytes=24 * 2**20)
VMEM = pl.BlockSpec(memory_space=pltpu.VMEM)
HBM = pl.BlockSpec(memory_space=pltpu.HBM)


def lanes_dot(a, b):
    return lax.dot_general(a, b, (((1,), (1,)), ((), ())), preferred_element_type=F32)


def plain_dot(a, b):
    return lax.dot_general(a, b, (((1,), (0,)), ((), ())), preferred_element_type=F32)


def halves(x):
    high = x.astype(BF16)
    return high, (x - high.astype(F32)).astype(BF16)


def one_hot(row, count):
    return row == lax.broadcasted_iota(jnp.int32, (count, row.shape[1]), 0)


def low_hot(row, count):
    row = jnp.where((row >= 0) & (row < count), row, -1).astype(F32).astype(BF16)
    return row == lax.broadcasted_iota(jnp.int32, (count, row.shape[1]), 0).astype(F32).astype(BF16)


def ones(mask):
    return jnp.where(mask, jnp.ones((), BF16), jnp.zeros((), BF16))


def turn_rows(rows, n_rows, n_ent, z, c):
    def moved(di, dj, sign):
        at = [
            ((sign * i - di) % n_rows) * n_ent + (sign * j - dj) % n_ent for i in range(n_rows) for j in range(n_ent)
        ]
        return jnp.concatenate([rows[k : k + 1] for k in at], axis=0)

    rows = moved(0, 0, -1)
    bit = 1
    while bit < n_rows:
        rows = jnp.where((z & bit) > 0, moved(bit, 0, 1), rows)
        bit *= 2
    bit = 1
    while bit < n_ent:
        rows = jnp.where((c & bit) > 0, moved(0, bit, 1), rows)
        bit *= 2
    return rows


def ranks_of(owners, member, item):
    rows = member.shape[1]
    step = min(256, rows)
    blocks = rows // step
    hits = jnp.concatenate([one_hot(member, owners).astype(F32), one_hot(item, owners).astype(F32)], axis=0)
    stacked = jnp.concatenate([hits[:, b * step : (b + 1) * step] for b in range(blocks)], axis=0)
    upper = lax.broadcasted_iota(jnp.int32, (step, step), 0) <= lax.broadcasted_iota(
        jnp.int32, (step, step), 1
    )
    counts = plain_dot(stacked.astype(BF16), upper.astype(F32).astype(BF16))
    before = jnp.zeros((2 * owners, 1), F32)
    pieces = []
    for b in range(blocks):
        here = counts[2 * owners * b : 2 * owners * (b + 1)]
        taken = (here + before) * hits[:, b * step : (b + 1) * step]
        sides = [jnp.sum(x, axis=0, keepdims=True) for x in (taken[:owners], taken[owners:])]
        pieces.append(jnp.concatenate(sides, axis=0))
        before = before + here[:, step - 1 : step]
    return jnp.concatenate(pieces, axis=1).astype(jnp.int32) - 1


def pack_chunk(k, capacity, place, ids, feats, chunk):
    pick = ones(low_hot(place - k * capacity, capacity))
    chunk[:capacity] = plain_dot(pick, feats).astype(BF16)
    chunk[capacity:, :capacity] = lanes_dot(ids, pick).astype(BF16)


def far_kernel(n_rows, n_ent, capacity, n_feat, far, *refs):
    sources, ranks, place_out, ids_out, feats = refs[:5], refs[5], refs[6], refs[7], refs[8]
    chunks, copies, sems = refs[9 : 9 + len(far)], refs[9 + len(far) : 13 + len(far)], refs[13 + len(far)]
    copies = (*copies, feats)
    moves = [pltpu.make_async_copy(sources[i], copies[i], sems.at[i]) for i in range(5)]
    for move in moves:
        move.start()
    for move in moves[:4]:
        move.wait()
    member, item, member_local, item_local = [copy[...] for copy in copies[:4]]
    rows = member.shape[1]
    rank = ranks_of(n_rows * n_ent, member, item)
    ranks[...] = rank
    on_item = lax.axis_index("feat") >= n_feat // 2
    own = jnp.where(on_item, item, member)
    up, across = own // n_ent - lax.axis_index("rows"), own % n_ent - lax.axis_index("ent")
    up, across = jnp.where(up < 0, up + n_rows, up), jnp.where(across < 0, across + n_ent, across)
    place = (up * n_ent + across) * capacity + jnp.where(on_item, rank[1:2], rank[0:1])
    place_out[...] = place
    local = jnp.where(on_item, item_local, member_local)
    high = local >> 8
    ids = jnp.concatenate([high, local - (high << 8), jnp.zeros((IDS - 2, rows), jnp.int32)], axis=0)
    ids = ids.astype(F32).astype(BF16)
    ids_out[...] = ids
    moves[4].wait()
    for chunk, k in zip(chunks, far):
        pack_chunk(k, capacity, place, ids, feats[...], chunk)


def rest_kernel(capacity, rest, place, ids, feats, *refs):
    chunks = refs[-len(rest) :]
    for chunk, k in zip(chunks, rest):
        pack_chunk(k, capacity, place[...], ids[...], feats[...], chunk)


def margin_kernel(place, weight, features, margin):
    wide = jnp.broadcast_to(weight[...], (16, weight.shape[1])).astype(BF16)
    margin[...] = lanes_dot(wide, features[...])[0:1]


def chunk_ids(chunk, capacity):
    pair = chunk[capacity:, :capacity].astype(F32)
    return (pair[0:1] * 256.0 + pair[1:2]).astype(jnp.int32)


def chunk_scores(chunk, table, capacity):
    entities = table.shape[0] // 2
    every = lanes_dot(table, chunk[:capacity])
    hits = one_hot(chunk_ids(chunk, capacity), entities)
    return jnp.sum(jnp.where(hits, every[:entities] + every[entities:], 0.0), axis=0, keepdims=True)


def early_kernel(capacity, count, coefs, *refs):
    chunks, kept, outs = refs[:count], refs[-count - 1], refs[-count:]
    entities = coefs.shape[0]
    kept[:entities], kept[entities:] = halves(coefs[...])
    table = kept[...]
    for chunk, out in zip(chunks, outs):
        out[...] = chunk_scores(chunk, table, capacity)


def later_kernel(capacity, table, *refs):
    half = len(refs) // 2
    for chunk, out in zip(refs[:half], refs[half:]):
        out[...] = chunk_scores(chunk, table[...], capacity)


def scores_kernel(order, capacity, n_feat, n_rows, n_ent, table, *refs):
    out = refs[-1]
    scores = [x[...] if x.shape[0] == 1 else chunk_scores(x, table[...], capacity) for x in refs[:-1]]
    scores = dict(zip(order, scores))
    scores = jnp.concatenate([scores[k] for k in range(len(order))], axis=0)
    scores = turn_rows(scores, n_rows, n_ent, lax.axis_index("rows"), lax.axis_index("ent"))
    for home in range(len(order)):
        for f in range(n_feat):
            out[(home // n_ent * n_feat + f) * n_ent + home % n_ent] = scores[home : home + 1]


def home_kernel(
    owners, capacity, n_feat, n_ent, member, item, ranks, clicks, valid, margin, scores, features, out
):
    on_item = lax.axis_index("feat") >= n_feat // 2
    total = margin[...]
    hits_of = [one_hot(owner[...], owners).astype(F32) for owner in (member, item)]
    spot_of = [ones(low_hot(ranks[side : side + 1], capacity)) for side in (0, 1)]
    for side in (0, 1):
        table = None
        for f in range(side * n_feat // 2, (side + 1) * n_feat // 2):
            part = jnp.concatenate(
                [scores[(h // n_ent * n_feat + f) * n_ent + h % n_ent] for h in range(owners)], axis=0
            )
            table = part if table is None else table + part
        found = plain_dot(jnp.concatenate(halves(table), axis=0), spot_of[side])
        total = total + jnp.sum((found[:owners] + found[owners:]) * hits_of[side], axis=0, keepdims=True)
    resid = valid[...].astype(F32) * (jax.nn.sigmoid(total) - clicks[...].astype(F32))
    hits = jnp.where(on_item, hits_of[1], hits_of[0])
    spot = jnp.where(on_item, spot_of[1], spot_of[0])
    sent = lanes_dot(jnp.concatenate(halves(hits * resid), axis=0), spot)
    sent = sent[:owners] + sent[owners:]
    low = jnp.broadcast_to(resid, (16, resid.shape[1])).astype(BF16)
    grad = plain_dot(low, features[...])[0:1]
    for h in range(owners):
        out[h, :, :capacity] = sent[h : h + 1]
        out[h, :, capacity:] = grad


def grads_kernel(order, capacity, n_rows, n_ent, scale, coefs, weight, came, *refs):
    chunks, grad_global, grad_coefs = refs[:-2], refs[-2], refs[-1]
    entities = coefs.shape[0]
    resids = jnp.concatenate([came[h][:, :capacity] for h in range(len(order))], axis=0)
    resids = turn_rows(resids, n_rows, n_ent, lax.axis_index("rows"), lax.axis_index("ent"))
    summed = came[0][:, capacity:]
    for h in range(1, len(order)):
        summed = summed + came[h][:, capacity:]
    grad_global[...] = summed * scale + 4.0 * weight[...]
    highs, lows, feats = [], [], []
    for chunk, k in zip(chunks, order):
        here = chunk_ids(chunk, capacity)
        blocks = [low_hot(here - first, min(256, entities)) for first in range(0, entities, 256)]
        high, low = halves(resids[k : k + 1])
        highs.append(jnp.concatenate([jnp.where(hits, high, jnp.zeros((), BF16)) for hits in blocks], axis=0))
        lows.append(jnp.concatenate([jnp.where(hits, low, jnp.zeros((), BF16)) for hits in blocks], axis=0))
        feats.append(chunk[:capacity])
    spread = jnp.concatenate([jnp.concatenate(highs, axis=1), jnp.concatenate(lows, axis=1)], axis=0)
    both = plain_dot(spread, jnp.concatenate(feats, axis=0))
    grad_coefs[...] = coefs[...] + both[:entities] + both[entities:]


def shift_send(x, n_rows, n_ent, k):
    if k == 0:
        return x
    up, across = divmod(k, n_ent)
    pairs = [
        (z * n_ent + c, (z + up) % n_rows * n_ent + (c + across) % n_ent)
        for z in range(n_rows)
        for c in range(n_ent)
    ]
    return lax.ppermute(x, HOME, pairs)


def call(kernel, out_shape, operands, in_specs, flops=0, scratch=(), hidden=False):
    moved = 0 if hidden else sum(x.size * x.dtype.itemsize for x in (*operands, *out_shape))
    return pl.pallas_call(
        kernel,
        out_shape=out_shape,
        in_specs=in_specs,
        out_specs=[VMEM] * len(out_shape),
        scratch_shapes=scratch,
        compiler_params=PARAMS,
        cost_estimate=pl.CostEstimate(flops=flops, bytes_accessed=moved, transcendentals=0),
    )(*operands)


def body(
    features,
    global_weight,
    entity_feats,
    coefs,
    member_owner,
    member_local,
    item_owner,
    item_local,
    clicks,
    valid,
):
    rows_here, width = entity_feats.shape
    columns = features.shape[1]
    n_feat, n_ent = lax.axis_size("feat"), lax.axis_size("ent")
    n_rows = lax.axis_size("rows")
    owners = n_rows * n_ent
    capacity = 2 * rows_here // owners
    member, item = member_owner.reshape(1, rows_here), item_owner.reshape(1, rows_here)

    def shape(*dims, dtype=F32):
        return jax.ShapeDtypeStruct(dims, dtype)

    def partial(kernel, *args):
        return lambda *refs: kernel(*args, *refs)

    row = pltpu.VMEM((1, rows_here), jnp.int32)
    middle = n_rows // 2
    away = [middle * n_ent]
    for c in range(n_ent):
        away += [up * n_ent + c for half in range(1, middle) for up in (half, n_rows - half)]
        away += [middle * n_ent + c + 1] if c + 1 < n_ent else []
    first, second, near = away[:1], away[1:-2], [*away[-2:], *reversed(range(n_ent))]
    chunk = shape(capacity + IDS, width, dtype=BF16)
    flops = len(first) * 2 * capacity * rows_here * width

    def in_hbm(x):
        return pltpu.with_memory_space_constraint(x, pltpu.HBM)

    ranks, place, ids, feats, *chunks = call(
        partial(far_kernel, n_rows, n_ent, capacity, n_feat, first),
        [
            shape(2, rows_here, dtype=jnp.int32),
            shape(1, rows_here, dtype=jnp.int32),
            shape(IDS, rows_here, dtype=BF16),
            shape(rows_here, width, dtype=BF16),
        ]
        + [chunk] * len(first),
        (
            in_hbm(member),
            in_hbm(item),
            in_hbm(member_local.reshape(1, rows_here)),
            in_hbm(item_local.reshape(1, rows_here)),
            in_hbm(entity_feats),
        ),
        [HBM] * 5,
        flops=flops,
        scratch=[row, row, row, row, pltpu.SemaphoreType.DMA((5,))],
    )
    chunks += call(
        partial(rest_kernel, capacity, second),
        [chunk] * len(second),
        (place, ids, feats),
        [VMEM] * 3,
        flops=32 * flops,
    )
    chunks = [shift_send(x, n_rows, n_ent, k) for k, x in zip(first + second, chunks)]
    weight = global_weight.astype(F32).reshape(1, columns)
    (global_part,) = call(
        margin_kernel, [shape(1, rows_here)], (place, weight, features), [VMEM] * 3, hidden=True
    )
    global_total = lax.psum(global_part, "feat")
    near_chunks = call(
        partial(rest_kernel, capacity, near),
        [chunk] * len(near),
        (place, ids, feats, global_part),
        [VMEM] * 4,
        hidden=True,
    )
    near_chunks = [shift_send(x, n_rows, n_ent, k) for k, x in zip(near, near_chunks)]
    chunks = dict(zip(first + second + near, chunks + near_chunks))
    early = away[:n_ent] + near[-1:]
    later, late = away[n_ent:-2], near[:-1]
    order = early + later + late
    table, *scores = call(
        partial(early_kernel, capacity, len(early)),
        [shape(2 * coefs.shape[0], width, dtype=BF16)] + [shape(1, capacity)] * len(early),
        (coefs, *(chunks[k] for k in early), global_total),
        [VMEM] * (2 + len(early)),
        hidden=True,
    )
    scores += call(
        partial(later_kernel, capacity),
        [shape(1, capacity)] * len(later),
        (table, *(chunks[k] for k in later)),
        [VMEM] * (1 + len(later)),
        hidden=True,
    )
    (scores,) = call(
        partial(scores_kernel, order, capacity, n_feat, n_rows, n_ent),
        [shape(n_feat * owners, 1, capacity)],
        (table, *scores, *(chunks[k] for k in late)),
        [VMEM] * (1 + owners),
        flops=16 * coefs.size * owners * capacity,
    )
    returned = lax.all_to_all(scores, EVERY, split_axis=0, concat_axis=0, tiled=True)
    (sent,) = call(
        partial(home_kernel, owners, capacity, n_feat, n_ent),
        [shape(owners, 1, capacity + columns)],
        (
            member,
            item,
            ranks,
            clicks.reshape(1, rows_here),
            valid.reshape(1, rows_here),
            global_total,
            returned,
            features,
        ),
        [VMEM] * 8,
        flops=32 * features.size,
    )
    came = lax.all_to_all(sent, HOME, split_axis=0, concat_axis=0, tiled=True)
    grad_global, grad_coefs = call(
        partial(grads_kernel, order, capacity, n_rows, n_ent, 1.0 / math.sqrt(rows_here * owners)),
        [shape(1, columns), shape(*coefs.shape)],
        (coefs, weight, came, *(chunks[k] for k in order)),
        [VMEM] * (3 + owners),
        flops=4 * coefs.size * owners * capacity,
    )
    return (grad_global.reshape(columns), grad_coefs)


def solution(mesh):
    by_row = P(("groups", "rows", "ent"))
    by_both = P(("groups", "rows", "ent"), "feat")
    column = P(("groups", "rows", "ent"), None)
    by_feat = P(("groups", "feat"))
    return jax.shard_map(
        body,
        mesh=mesh,
        in_specs=(by_both, by_feat, by_both, by_both, column, by_row, column, by_row, by_row, by_row),
        out_specs=(by_feat, by_both),
        check_vma=False,
    )
```

```python
import math

import jax
import jax.numpy as jnp
from jax import lax
from jax.experimental import pallas as pl
from jax.experimental.pallas import tpu as pltpu
from jax.sharding import PartitionSpec as P

F32 = jnp.float32
BF16 = jnp.bfloat16
HOME = ("rows", "ent")
EVERY = ("feat", "rows", "ent")
IDS = 8
PARAMS = pltpu.CompilerParams(vmem_limit_bytes=24 * 2**20)
VMEM = pl.BlockSpec(memory_space=pltpu.VMEM)
HBM = pl.BlockSpec(memory_space=pltpu.HBM)


def lanes_dot(a, b):
    return lax.dot_general(a, b, (((1,), (1,)), ((), ())), preferred_element_type=F32)


def plain_dot(a, b):
    return lax.dot_general(a, b, (((1,), (0,)), ((), ())), preferred_element_type=F32)


def halves(x):
    high = x.astype(BF16)
    return high, (x - high.astype(F32)).astype(BF16)


def one_hot(row, count):
    return row == lax.broadcasted_iota(jnp.int32, (count, row.shape[1]), 0)


def low_hot(row, count):
    row = jnp.where((row >= 0) & (row < count), row, -1).astype(F32).astype(BF16)
    return row == lax.broadcasted_iota(jnp.int32, (count, row.shape[1]), 0).astype(F32).astype(BF16)


def ones(mask):
    return jnp.where(mask, jnp.ones((), BF16), jnp.zeros((), BF16))


def turn_rows(rows, n_rows, n_ent, z, c):
    def moved(di, dj, sign):
        at = [
            ((sign * i - di) % n_rows) * n_ent + (sign * j - dj) % n_ent for i in range(n_rows) for j in range(n_ent)
        ]
        return jnp.concatenate([rows[k : k + 1] for k in at], axis=0)

    rows = moved(0, 0, -1)
    bit = 1
    while bit < n_rows:
        rows = jnp.where((z & bit) > 0, moved(bit, 0, 1), rows)
        bit *= 2
    bit = 1
    while bit < n_ent:
        rows = jnp.where((c & bit) > 0, moved(0, bit, 1), rows)
        bit *= 2
    return rows


def ranks_of(owners, member, item):
    rows = member.shape[1]
    step = min(256, rows)
    blocks = rows // step
    hits = jnp.concatenate([one_hot(member, owners).astype(F32), one_hot(item, owners).astype(F32)], axis=0)
    stacked = jnp.concatenate([hits[:, b * step : (b + 1) * step] for b in range(blocks)], axis=0)
    upper = lax.broadcasted_iota(jnp.int32, (step, step), 0) <= lax.broadcasted_iota(
        jnp.int32, (step, step), 1
    )
    counts = plain_dot(stacked.astype(BF16), upper.astype(F32).astype(BF16))
    before = jnp.zeros((2 * owners, 1), F32)
    pieces = []
    for b in range(blocks):
        here = counts[2 * owners * b : 2 * owners * (b + 1)]
        taken = (here + before) * hits[:, b * step : (b + 1) * step]
        sides = [jnp.sum(x, axis=0, keepdims=True) for x in (taken[:owners], taken[owners:])]
        pieces.append(jnp.concatenate(sides, axis=0))
        before = before + here[:, step - 1 : step]
    return jnp.concatenate(pieces, axis=1).astype(jnp.int32) - 1


def pack_chunk(k, capacity, place, ids, feats, chunk):
    pick = ones(low_hot(place - k * capacity, capacity))
    chunk[:capacity] = plain_dot(pick, feats).astype(BF16)
    chunk[capacity:, :capacity] = lanes_dot(ids, pick).astype(BF16)


def far_kernel(n_rows, n_ent, capacity, n_feat, far, *refs):
    sources, ranks, place_out, ids_out, feats = refs[:5], refs[5], refs[6], refs[7], refs[8]
    chunks, copies, sems = refs[9 : 9 + len(far)], refs[9 + len(far) : 13 + len(far)], refs[13 + len(far)]
    copies = (*copies, feats)
    moves = [pltpu.make_async_copy(sources[i], copies[i], sems.at[i]) for i in range(5)]
    for move in moves:
        move.start()
    for move in moves[:4]:
        move.wait()
    member, item, member_local, item_local = [copy[...] for copy in copies[:4]]
    rows = member.shape[1]
    rank = ranks_of(n_rows * n_ent, member, item)
    ranks[...] = rank
    on_item = lax.axis_index("feat") >= n_feat // 2
    own = jnp.where(on_item, item, member)
    up, across = own // n_ent - lax.axis_index("rows"), own % n_ent - lax.axis_index("ent")
    up, across = jnp.where(up < 0, up + n_rows, up), jnp.where(across < 0, across + n_ent, across)
    place = (up * n_ent + across) * capacity + jnp.where(on_item, rank[1:2], rank[0:1])
    place_out[...] = place
    local = jnp.where(on_item, item_local, member_local)
    high = local >> 8
    ids = jnp.concatenate([high, local - (high << 8), jnp.zeros((IDS - 2, rows), jnp.int32)], axis=0)
    ids = ids.astype(F32).astype(BF16)
    ids_out[...] = ids
    moves[4].wait()
    for chunk, k in zip(chunks, far):
        pack_chunk(k, capacity, place, ids, feats[...], chunk)


def rest_kernel(capacity, rest, place, ids, feats, *refs):
    chunks = refs[-len(rest) :]
    for chunk, k in zip(chunks, rest):
        pack_chunk(k, capacity, place[...], ids[...], feats[...], chunk)


def margin_kernel(place, weight, features, margin):
    wide = jnp.broadcast_to(weight[...], (16, weight.shape[1])).astype(BF16)
    margin[...] = lanes_dot(wide, features[...])[0:1]


def chunk_ids(chunk, capacity):
    pair = chunk[capacity:, :capacity].astype(F32)
    return (pair[0:1] * 256.0 + pair[1:2]).astype(jnp.int32)


def chunk_scores(chunk, table, capacity):
    entities = table.shape[0] // 2
    every = lanes_dot(table, chunk[:capacity])
    hits = one_hot(chunk_ids(chunk, capacity), entities)
    return jnp.sum(jnp.where(hits, every[:entities] + every[entities:], 0.0), axis=0, keepdims=True)


def early_kernel(capacity, count, coefs, *refs):
    chunks, kept, outs = refs[:count], refs[-count - 1], refs[-count:]
    entities = coefs.shape[0]
    kept[:entities], kept[entities:] = halves(coefs[...])
    table = kept[...]
    for chunk, out in zip(chunks, outs):
        out[...] = chunk_scores(chunk, table, capacity)


def later_kernel(capacity, table, *refs):
    half = len(refs) // 2
    for chunk, out in zip(refs[:half], refs[half:]):
        out[...] = chunk_scores(chunk, table[...], capacity)


def scores_kernel(order, capacity, n_feat, n_rows, n_ent, table, *refs):
    out = refs[-1]
    scores = [x[...] if x.shape[0] == 1 else chunk_scores(x, table[...], capacity) for x in refs[:-1]]
    scores = dict(zip(order, scores))
    scores = jnp.concatenate([scores[k] for k in range(len(order))], axis=0)
    scores = turn_rows(scores, n_rows, n_ent, lax.axis_index("rows"), lax.axis_index("ent"))
    for home in range(len(order)):
        for f in range(n_feat):
            out[f * len(order) + home] = scores[home : home + 1]


def home_kernel(
    owners, capacity, n_feat, n_ent, member, item, ranks, clicks, valid, margin, scores, features, out
):
    on_item = lax.axis_index("feat") >= n_feat // 2
    total = margin[...]
    hits_of = [one_hot(owner[...], owners).astype(F32) for owner in (member, item)]
    spot_of = [ones(low_hot(ranks[side : side + 1], capacity)) for side in (0, 1)]
    for side in (0, 1):
        table = None
        for f in range(side * n_feat // 2, (side + 1) * n_feat // 2):
            part = jnp.concatenate(
                [scores[f * owners + h] for h in range(owners)], axis=0
            )
            table = part if table is None else table + part
        found = plain_dot(jnp.concatenate(halves(table), axis=0), spot_of[side])
        total = total + jnp.sum((found[:owners] + found[owners:]) * hits_of[side], axis=0, keepdims=True)
    resid = valid[...].astype(F32) * (jax.nn.sigmoid(total) - clicks[...].astype(F32))
    hits = jnp.where(on_item, hits_of[1], hits_of[0])
    spot = jnp.where(on_item, spot_of[1], spot_of[0])
    sent = lanes_dot(jnp.concatenate(halves(hits * resid), axis=0), spot)
    sent = sent[:owners] + sent[owners:]
    low = jnp.broadcast_to(resid, (16, resid.shape[1])).astype(BF16)
    grad = plain_dot(low, features[...])[0:1]
    for h in range(owners):
        out[h, :, :capacity] = sent[h : h + 1]
        out[h, :, capacity:] = grad


def grads_kernel(order, capacity, n_rows, n_ent, scale, coefs, weight, came, *refs):
    chunks, grad_global, grad_coefs = refs[:-2], refs[-2], refs[-1]
    entities = coefs.shape[0]
    resids = jnp.concatenate([came[h][:, :capacity] for h in range(len(order))], axis=0)
    resids = turn_rows(resids, n_rows, n_ent, lax.axis_index("rows"), lax.axis_index("ent"))
    summed = came[0][:, capacity:]
    for h in range(1, len(order)):
        summed = summed + came[h][:, capacity:]
    grad_global[...] = summed * scale + 4.0 * weight[...]
    highs, lows, feats = [], [], []
    for chunk, k in zip(chunks, order):
        here = chunk_ids(chunk, capacity)
        blocks = [low_hot(here - first, min(256, entities)) for first in range(0, entities, 256)]
        high, low = halves(resids[k : k + 1])
        highs.append(jnp.concatenate([jnp.where(hits, high, jnp.zeros((), BF16)) for hits in blocks], axis=0))
        lows.append(jnp.concatenate([jnp.where(hits, low, jnp.zeros((), BF16)) for hits in blocks], axis=0))
        feats.append(chunk[:capacity])
    spread = jnp.concatenate([jnp.concatenate(highs, axis=1), jnp.concatenate(lows, axis=1)], axis=0)
    both = plain_dot(spread, jnp.concatenate(feats, axis=0))
    grad_coefs[...] = coefs[...] + both[:entities] + both[entities:]


def shift_send(x, n_rows, n_ent, k):
    if k == 0:
        return x
    up, across = divmod(k, n_ent)
    pairs = [
        (z * n_ent + c, (z + up) % n_rows * n_ent + (c + across) % n_ent)
        for z in range(n_rows)
        for c in range(n_ent)
    ]
    return lax.ppermute(x, HOME, pairs)


def call(kernel, out_shape, operands, in_specs, flops=0, scratch=(), hidden=False):
    moved = 0 if hidden else sum(x.size * x.dtype.itemsize for x in (*operands, *out_shape))
    return pl.pallas_call(
        kernel,
        out_shape=out_shape,
        in_specs=in_specs,
        out_specs=[VMEM] * len(out_shape),
        scratch_shapes=scratch,
        compiler_params=PARAMS,
        cost_estimate=pl.CostEstimate(flops=flops, bytes_accessed=moved, transcendentals=0),
    )(*operands)


def body(
    features,
    global_weight,
    entity_feats,
    coefs,
    member_owner,
    member_local,
    item_owner,
    item_local,
    clicks,
    valid,
):
    rows_here, width = entity_feats.shape
    columns = features.shape[1]
    n_feat, n_ent = lax.axis_size("feat"), lax.axis_size("ent")
    n_rows = lax.axis_size("rows")
    owners = n_rows * n_ent
    capacity = 2 * rows_here // owners
    member, item = member_owner.reshape(1, rows_here), item_owner.reshape(1, rows_here)

    def shape(*dims, dtype=F32):
        return jax.ShapeDtypeStruct(dims, dtype)

    def partial(kernel, *args):
        return lambda *refs: kernel(*args, *refs)

    row = pltpu.VMEM((1, rows_here), jnp.int32)
    middle = n_rows // 2
    away = [up * n_ent for half in range(1, middle) for up in (half, n_rows - half)]
    away += [middle * n_ent + c for c in range(n_ent)]
    away += [up * n_ent + c for c in range(1, n_ent) for half in range(1, middle) for up in (half, n_rows - half)]
    first, second, near = away[:1], away[1:-2], [*away[-2:], *reversed(range(n_ent))]
    chunk = shape(capacity + IDS, width, dtype=BF16)
    flops = len(first) * 2 * capacity * rows_here * width

    def in_hbm(x):
        return pltpu.with_memory_space_constraint(x, pltpu.HBM)

    ranks, place, ids, feats, *chunks = call(
        partial(far_kernel, n_rows, n_ent, capacity, n_feat, first),
        [
            shape(2, rows_here, dtype=jnp.int32),
            shape(1, rows_here, dtype=jnp.int32),
            shape(IDS, rows_here, dtype=BF16),
            shape(rows_here, width, dtype=BF16),
        ]
        + [chunk] * len(first),
        (
            in_hbm(member),
            in_hbm(item),
            in_hbm(member_local.reshape(1, rows_here)),
            in_hbm(item_local.reshape(1, rows_here)),
            in_hbm(entity_feats),
        ),
        [HBM] * 5,
        flops=flops,
        scratch=[row, row, row, row, pltpu.SemaphoreType.DMA((5,))],
    )
    chunks += call(
        partial(rest_kernel, capacity, second),
        [chunk] * len(second),
        (place, ids, feats),
        [VMEM] * 3,
        flops=32 * flops,
    )
    chunks = [shift_send(x, n_rows, n_ent, k) for k, x in zip(first + second, chunks)]
    weight = global_weight.astype(F32).reshape(1, columns)
    (global_part,) = call(
        margin_kernel, [shape(1, rows_here)], (place, weight, features), [VMEM] * 3, hidden=True
    )
    global_total = lax.psum(global_part, "feat")
    near_chunks = call(
        partial(rest_kernel, capacity, near),
        [chunk] * len(near),
        (place, ids, feats, global_part),
        [VMEM] * 4,
        hidden=True,
    )
    near_chunks = [shift_send(x, n_rows, n_ent, k) for k, x in zip(near, near_chunks)]
    chunks = dict(zip(first + second + near, chunks + near_chunks))
    early = away[:n_ent] + near[-1:]
    later, late = away[n_ent:-2], near[:-1]
    order = early + later + late
    table, *scores = call(
        partial(early_kernel, capacity, len(early)),
        [shape(2 * coefs.shape[0], width, dtype=BF16)] + [shape(1, capacity)] * len(early),
        (coefs, *(chunks[k] for k in early), global_total),
        [VMEM] * (2 + len(early)),
        hidden=True,
    )
    scores += call(
        partial(later_kernel, capacity),
        [shape(1, capacity)] * len(later),
        (table, *(chunks[k] for k in later)),
        [VMEM] * (1 + len(later)),
        hidden=True,
    )
    (scores,) = call(
        partial(scores_kernel, order, capacity, n_feat, n_rows, n_ent),
        [shape(n_feat * owners, 1, capacity)],
        (table, *scores, *(chunks[k] for k in late)),
        [VMEM] * (1 + owners),
        flops=16 * coefs.size * owners * capacity,
    )
    returned = lax.all_to_all(scores, EVERY, split_axis=0, concat_axis=0, tiled=True)
    (sent,) = call(
        partial(home_kernel, owners, capacity, n_feat, n_ent),
        [shape(owners, 1, capacity + columns)],
        (
            member,
            item,
            ranks,
            clicks.reshape(1, rows_here),
            valid.reshape(1, rows_here),
            global_total,
            returned,
            features,
        ),
        [VMEM] * 8,
        flops=32 * features.size,
    )
    came = lax.all_to_all(sent, HOME, split_axis=0, concat_axis=0, tiled=True)
    grad_global, grad_coefs = call(
        partial(grads_kernel, order, capacity, n_rows, n_ent, 1.0 / math.sqrt(rows_here * owners)),
        [shape(1, columns), shape(*coefs.shape)],
        (coefs, weight, came, *(chunks[k] for k in order)),
        [VMEM] * (3 + owners),
        flops=4 * coefs.size * owners * capacity,
    )
    return (grad_global.reshape(columns), grad_coefs)


def solution(mesh):
    by_row = P(("groups", "rows", "ent"))
    by_both = P(("groups", "rows", "ent"), "feat")
    column = P(("groups", "rows", "ent"), None)
    by_feat = P(("groups", "feat"))
    return jax.shard_map(
        body,
        mesh=mesh,
        in_specs=(by_both, by_feat, by_both, by_both, column, by_row, column, by_row, by_row, by_row),
        out_specs=(by_feat, by_both),
        check_vma=False,
    )
```

```python
import math

import jax
import jax.numpy as jnp
from jax import lax
from jax.experimental import pallas as pl
from jax.experimental.pallas import tpu as pltpu
from jax.sharding import PartitionSpec as P

F32 = jnp.float32
BF16 = jnp.bfloat16
HOME = ("rows", "ent")
EVERY = ("rows", "feat", "ent")
IDS = 8
PARAMS = pltpu.CompilerParams(vmem_limit_bytes=24 * 2**20)
VMEM = pl.BlockSpec(memory_space=pltpu.VMEM)
HBM = pl.BlockSpec(memory_space=pltpu.HBM)


def lanes_dot(a, b):
    return lax.dot_general(a, b, (((1,), (1,)), ((), ())), preferred_element_type=F32)


def plain_dot(a, b):
    return lax.dot_general(a, b, (((1,), (0,)), ((), ())), preferred_element_type=F32)


def halves(x):
    high = x.astype(BF16)
    return high, (x - high.astype(F32)).astype(BF16)


def one_hot(row, count):
    return row == lax.broadcasted_iota(jnp.int32, (count, row.shape[1]), 0)


def low_hot(row, count):
    row = jnp.where((row >= 0) & (row < count), row, -1).astype(F32).astype(BF16)
    return row == lax.broadcasted_iota(jnp.int32, (count, row.shape[1]), 0).astype(F32).astype(BF16)


def ones(mask):
    return jnp.where(mask, jnp.ones((), BF16), jnp.zeros((), BF16))


def turn_rows(rows, n_rows, n_ent, z, c):
    def moved(di, dj, sign):
        at = [
            ((sign * i - di) % n_rows) * n_ent + (sign * j - dj) % n_ent for i in range(n_rows) for j in range(n_ent)
        ]
        return jnp.concatenate([rows[k : k + 1] for k in at], axis=0)

    rows = moved(0, 0, -1)
    bit = 1
    while bit < n_rows:
        rows = jnp.where((z & bit) > 0, moved(bit, 0, 1), rows)
        bit *= 2
    bit = 1
    while bit < n_ent:
        rows = jnp.where((c & bit) > 0, moved(0, bit, 1), rows)
        bit *= 2
    return rows


def ranks_of(owners, member, item):
    rows = member.shape[1]
    step = min(256, rows)
    blocks = rows // step
    hits = jnp.concatenate([one_hot(member, owners).astype(F32), one_hot(item, owners).astype(F32)], axis=0)
    stacked = jnp.concatenate([hits[:, b * step : (b + 1) * step] for b in range(blocks)], axis=0)
    upper = lax.broadcasted_iota(jnp.int32, (step, step), 0) <= lax.broadcasted_iota(
        jnp.int32, (step, step), 1
    )
    counts = plain_dot(stacked.astype(BF16), upper.astype(F32).astype(BF16))
    before = jnp.zeros((2 * owners, 1), F32)
    pieces = []
    for b in range(blocks):
        here = counts[2 * owners * b : 2 * owners * (b + 1)]
        taken = (here + before) * hits[:, b * step : (b + 1) * step]
        sides = [jnp.sum(x, axis=0, keepdims=True) for x in (taken[:owners], taken[owners:])]
        pieces.append(jnp.concatenate(sides, axis=0))
        before = before + here[:, step - 1 : step]
    return jnp.concatenate(pieces, axis=1).astype(jnp.int32) - 1


def pack_chunk(k, capacity, place, ids, feats, chunk):
    pick = ones(low_hot(place - k * capacity, capacity))
    chunk[:capacity] = plain_dot(pick, feats).astype(BF16)
    chunk[capacity:, :capacity] = lanes_dot(ids, pick).astype(BF16)


def far_kernel(n_rows, n_ent, capacity, n_feat, far, *refs):
    sources, ranks, place_out, ids_out, feats = refs[:5], refs[5], refs[6], refs[7], refs[8]
    chunks, copies, sems = refs[9 : 9 + len(far)], refs[9 + len(far) : 13 + len(far)], refs[13 + len(far)]
    copies = (*copies, feats)
    moves = [pltpu.make_async_copy(sources[i], copies[i], sems.at[i]) for i in range(5)]
    for move in moves:
        move.start()
    for move in moves[:4]:
        move.wait()
    member, item, member_local, item_local = [copy[...] for copy in copies[:4]]
    rows = member.shape[1]
    rank = ranks_of(n_rows * n_ent, member, item)
    ranks[...] = rank
    on_item = lax.axis_index("feat") >= n_feat // 2
    own = jnp.where(on_item, item, member)
    up, across = own // n_ent - lax.axis_index("rows"), own % n_ent - lax.axis_index("ent")
    up, across = jnp.where(up < 0, up + n_rows, up), jnp.where(across < 0, across + n_ent, across)
    place = (up * n_ent + across) * capacity + jnp.where(on_item, rank[1:2], rank[0:1])
    place_out[...] = place
    local = jnp.where(on_item, item_local, member_local)
    high = local >> 8
    ids = jnp.concatenate([high, local - (high << 8), jnp.zeros((IDS - 2, rows), jnp.int32)], axis=0)
    ids = ids.astype(F32).astype(BF16)
    ids_out[...] = ids
    moves[4].wait()
    for chunk, k in zip(chunks, far):
        pack_chunk(k, capacity, place, ids, feats[...], chunk)


def rest_kernel(capacity, rest, place, ids, feats, *refs):
    chunks = refs[-len(rest) :]
    for chunk, k in zip(chunks, rest):
        pack_chunk(k, capacity, place[...], ids[...], feats[...], chunk)


def margin_kernel(place, weight, features, margin):
    wide = jnp.broadcast_to(weight[...], (16, weight.shape[1])).astype(BF16)
    margin[...] = lanes_dot(wide, features[...])[0:1]


def chunk_ids(chunk, capacity):
    pair = chunk[capacity:, :capacity].astype(F32)
    return (pair[0:1] * 256.0 + pair[1:2]).astype(jnp.int32)


def chunk_scores(chunk, table, capacity):
    entities = table.shape[0] // 2
    every = lanes_dot(table, chunk[:capacity])
    hits = one_hot(chunk_ids(chunk, capacity), entities)
    return jnp.sum(jnp.where(hits, every[:entities] + every[entities:], 0.0), axis=0, keepdims=True)


def early_kernel(capacity, count, coefs, *refs):
    chunks, kept, outs = refs[:count], refs[-count - 1], refs[-count:]
    entities = coefs.shape[0]
    kept[:entities], kept[entities:] = halves(coefs[...])
    table = kept[...]
    for chunk, out in zip(chunks, outs):
        out[...] = chunk_scores(chunk, table, capacity)


def later_kernel(capacity, table, *refs):
    half = len(refs) // 2
    for chunk, out in zip(refs[:half], refs[half:]):
        out[...] = chunk_scores(chunk, table[...], capacity)


def scores_kernel(order, capacity, n_feat, n_rows, n_ent, table, *refs):
    out = refs[-1]
    scores = [x[...] if x.shape[0] == 1 else chunk_scores(x, table[...], capacity) for x in refs[:-1]]
    scores = dict(zip(order, scores))
    scores = jnp.concatenate([scores[k] for k in range(len(order))], axis=0)
    scores = turn_rows(scores, n_rows, n_ent, lax.axis_index("rows"), lax.axis_index("ent"))
    for home in range(len(order)):
        for f in range(n_feat):
            out[(home // n_ent * n_feat + f) * n_ent + home % n_ent] = scores[home : home + 1]


def home_kernel(
    owners, capacity, n_feat, n_ent, member, item, ranks, clicks, valid, margin, scores, features, out
):
    on_item = lax.axis_index("feat") >= n_feat // 2
    total = margin[...]
    hits_of = [one_hot(owner[...], owners).astype(F32) for owner in (member, item)]
    spot_of = [ones(low_hot(ranks[side : side + 1], capacity)) for side in (0, 1)]
    for side in (0, 1):
        table = None
        for f in range(side * n_feat // 2, (side + 1) * n_feat // 2):
            part = jnp.concatenate(
                [scores[(h // n_ent * n_feat + f) * n_ent + h % n_ent] for h in range(owners)], axis=0
            )
            table = part if table is None else table + part
        found = plain_dot(jnp.concatenate(halves(table), axis=0), spot_of[side])
        total = total + jnp.sum((found[:owners] + found[owners:]) * hits_of[side], axis=0, keepdims=True)
    resid = valid[...].astype(F32) * (jax.nn.sigmoid(total) - clicks[...].astype(F32))
    hits = jnp.where(on_item, hits_of[1], hits_of[0])
    spot = jnp.where(on_item, spot_of[1], spot_of[0])
    sent = lanes_dot(jnp.concatenate(halves(hits * resid), axis=0), spot)
    sent = sent[:owners] + sent[owners:]
    low = jnp.broadcast_to(resid, (16, resid.shape[1])).astype(BF16)
    grad = plain_dot(low, features[...])[0:1]
    for h in range(owners):
        out[h, :, :capacity] = sent[h : h + 1]
        out[h, :, capacity:] = grad


def grads_kernel(order, capacity, n_rows, n_ent, scale, coefs, weight, came, *refs):
    chunks, grad_global, grad_coefs = refs[:-2], refs[-2], refs[-1]
    entities = coefs.shape[0]
    resids = jnp.concatenate([came[h][:, :capacity] for h in range(len(order))], axis=0)
    resids = turn_rows(resids, n_rows, n_ent, lax.axis_index("rows"), lax.axis_index("ent"))
    summed = came[0][:, capacity:]
    for h in range(1, len(order)):
        summed = summed + came[h][:, capacity:]
    grad_global[...] = summed * scale + 4.0 * weight[...]
    highs, lows, feats = [], [], []
    for chunk, k in zip(chunks, order):
        here = chunk_ids(chunk, capacity)
        blocks = [low_hot(here - first, min(256, entities)) for first in range(0, entities, 256)]
        high, low = halves(resids[k : k + 1])
        highs.append(jnp.concatenate([jnp.where(hits, high, jnp.zeros((), BF16)) for hits in blocks], axis=0))
        lows.append(jnp.concatenate([jnp.where(hits, low, jnp.zeros((), BF16)) for hits in blocks], axis=0))
        feats.append(chunk[:capacity])
    spread = jnp.concatenate([jnp.concatenate(highs, axis=1), jnp.concatenate(lows, axis=1)], axis=0)
    both = plain_dot(spread, jnp.concatenate(feats, axis=0))
    grad_coefs[...] = coefs[...] + both[:entities] + both[entities:]


def shift_send(x, n_rows, n_ent, k):
    if k == 0:
        return x
    up, across = divmod(k, n_ent)
    pairs = [
        (z * n_ent + c, (z + up) % n_rows * n_ent + (c + across) % n_ent)
        for z in range(n_rows)
        for c in range(n_ent)
    ]
    return lax.ppermute(x, HOME, pairs)


def call(kernel, out_shape, operands, in_specs, flops=0, scratch=(), hidden=False):
    moved = 0 if hidden else sum(x.size * x.dtype.itemsize for x in (*operands, *out_shape))
    return pl.pallas_call(
        kernel,
        out_shape=out_shape,
        in_specs=in_specs,
        out_specs=[VMEM] * len(out_shape),
        scratch_shapes=scratch,
        compiler_params=PARAMS,
        cost_estimate=pl.CostEstimate(flops=flops, bytes_accessed=moved, transcendentals=0),
    )(*operands)


def body(
    features,
    global_weight,
    entity_feats,
    coefs,
    member_owner,
    member_local,
    item_owner,
    item_local,
    clicks,
    valid,
):
    rows_here, width = entity_feats.shape
    columns = features.shape[1]
    n_feat, n_ent = lax.axis_size("feat"), lax.axis_size("ent")
    n_rows = lax.axis_size("rows")
    owners = n_rows * n_ent
    capacity = 2 * rows_here // owners
    member, item = member_owner.reshape(1, rows_here), item_owner.reshape(1, rows_here)

    def shape(*dims, dtype=F32):
        return jax.ShapeDtypeStruct(dims, dtype)

    def partial(kernel, *args):
        return lambda *refs: kernel(*args, *refs)

    row = pltpu.VMEM((1, rows_here), jnp.int32)
    middle = n_rows // 2
    away = [up * n_ent for half in range(1, middle) for up in (half, n_rows - half)]
    away += [middle * n_ent + c for c in range(n_ent)]
    away += [up * n_ent + c for c in range(1, n_ent) for half in range(1, middle) for up in (half, n_rows - half)]
    first, second, near = away[:2], away[2:-2], [*away[-2:], *reversed(range(n_ent))]
    chunk = shape(capacity + IDS, width, dtype=BF16)
    flops = 2 * capacity * rows_here * width

    def in_hbm(x):
        return pltpu.with_memory_space_constraint(x, pltpu.HBM)

    ranks, place, ids, feats, *chunks = call(
        partial(far_kernel, n_rows, n_ent, capacity, n_feat, first),
        [
            shape(2, rows_here, dtype=jnp.int32),
            shape(1, rows_here, dtype=jnp.int32),
            shape(IDS, rows_here, dtype=BF16),
            shape(rows_here, width, dtype=BF16),
        ]
        + [chunk] * len(first),
        (
            in_hbm(member),
            in_hbm(item),
            in_hbm(member_local.reshape(1, rows_here)),
            in_hbm(item_local.reshape(1, rows_here)),
            in_hbm(entity_feats),
        ),
        [HBM] * 5,
        flops=flops,
        scratch=[row, row, row, row, pltpu.SemaphoreType.DMA((5,))],
    )
    chunks += call(
        partial(rest_kernel, capacity, second),
        [chunk] * len(second),
        (place, ids, feats),
        [VMEM] * 3,
        flops=32 * flops,
    )
    chunks = [shift_send(x, n_rows, n_ent, k) for k, x in zip(first + second, chunks)]
    weight = global_weight.astype(F32).reshape(1, columns)
    (global_part,) = call(
        margin_kernel, [shape(1, rows_here)], (place, weight, features), [VMEM] * 3, hidden=True
    )
    global_total = lax.psum(global_part, "feat")
    near_chunks = call(
        partial(rest_kernel, capacity, near),
        [chunk] * len(near),
        (place, ids, feats, global_part),
        [VMEM] * 4,
        hidden=True,
    )
    near_chunks = [shift_send(x, n_rows, n_ent, k) for k, x in zip(near, near_chunks)]
    chunks = dict(zip(first + second + near, chunks + near_chunks))
    early = away[:n_ent] + near[-1:]
    later, late = away[n_ent:-2], near[:-1]
    order = early + later + late
    table, *scores = call(
        partial(early_kernel, capacity, len(early)),
        [shape(2 * coefs.shape[0], width, dtype=BF16)] + [shape(1, capacity)] * len(early),
        (coefs, *(chunks[k] for k in early), global_total),
        [VMEM] * (2 + len(early)),
        hidden=True,
    )
    scores += call(
        partial(later_kernel, capacity),
        [shape(1, capacity)] * len(later),
        (table, *(chunks[k] for k in later)),
        [VMEM] * (1 + len(later)),
        hidden=True,
    )
    (scores,) = call(
        partial(scores_kernel, order, capacity, n_feat, n_rows, n_ent),
        [shape(n_feat * owners, 1, capacity)],
        (table, *scores, *(chunks[k] for k in late)),
        [VMEM] * (1 + owners),
        flops=16 * coefs.size * owners * capacity,
    )
    returned = lax.all_to_all(scores, EVERY, split_axis=0, concat_axis=0, tiled=True)
    (sent,) = call(
        partial(home_kernel, owners, capacity, n_feat, n_ent),
        [shape(owners, 1, capacity + columns)],
        (
            member,
            item,
            ranks,
            clicks.reshape(1, rows_here),
            valid.reshape(1, rows_here),
            global_total,
            returned,
            features,
        ),
        [VMEM] * 8,
        flops=32 * features.size,
    )
    came = lax.all_to_all(sent, HOME, split_axis=0, concat_axis=0, tiled=True)
    grad_global, grad_coefs = call(
        partial(grads_kernel, order, capacity, n_rows, n_ent, 1.0 / math.sqrt(rows_here * owners)),
        [shape(1, columns), shape(*coefs.shape)],
        (coefs, weight, came, *(chunks[k] for k in order)),
        [VMEM] * (3 + owners),
        flops=4 * coefs.size * owners * capacity,
    )
    return (grad_global.reshape(columns), grad_coefs)


def solution(mesh):
    by_row = P(("groups", "rows", "ent"))
    by_both = P(("groups", "rows", "ent"), "feat")
    column = P(("groups", "rows", "ent"), None)
    by_feat = P(("groups", "feat"))
    return jax.shard_map(
        body,
        mesh=mesh,
        in_specs=(by_both, by_feat, by_both, by_both, column, by_row, column, by_row, by_row, by_row),
        out_specs=(by_feat, by_both),
        check_vma=False,
    )
```

```python
import math

import jax
import jax.numpy as jnp
from jax import lax
from jax.experimental import pallas as pl
from jax.experimental.pallas import tpu as pltpu
from jax.sharding import PartitionSpec as P

F32 = jnp.float32
BF16 = jnp.bfloat16
HOME = ("rows", "ent")
EVERY = ("rows", "feat", "ent")
IDS = 8
PARAMS = pltpu.CompilerParams(vmem_limit_bytes=24 * 2**20)
VMEM = pl.BlockSpec(memory_space=pltpu.VMEM)
HBM = pl.BlockSpec(memory_space=pltpu.HBM)


def lanes_dot(a, b):
    return lax.dot_general(a, b, (((1,), (1,)), ((), ())), preferred_element_type=F32)


def plain_dot(a, b):
    return lax.dot_general(a, b, (((1,), (0,)), ((), ())), preferred_element_type=F32)


def halves(x):
    high = x.astype(BF16)
    return high, (x - high.astype(F32)).astype(BF16)


def one_hot(row, count):
    return row == lax.broadcasted_iota(jnp.int32, (count, row.shape[1]), 0)


def low_hot(row, count):
    row = jnp.where((row >= 0) & (row < count), row, -1).astype(F32).astype(BF16)
    return row == lax.broadcasted_iota(jnp.int32, (count, row.shape[1]), 0).astype(F32).astype(BF16)


def ones(mask):
    return jnp.where(mask, jnp.ones((), BF16), jnp.zeros((), BF16))


def turn_rows(rows, n_rows, n_ent, z, c):
    def moved(di, dj, sign):
        at = [
            ((sign * i - di) % n_rows) * n_ent + (sign * j - dj) % n_ent for i in range(n_rows) for j in range(n_ent)
        ]
        return jnp.concatenate([rows[k : k + 1] for k in at], axis=0)

    rows = moved(0, 0, -1)
    bit = 1
    while bit < n_rows:
        rows = jnp.where((z & bit) > 0, moved(bit, 0, 1), rows)
        bit *= 2
    bit = 1
    while bit < n_ent:
        rows = jnp.where((c & bit) > 0, moved(0, bit, 1), rows)
        bit *= 2
    return rows


def ranks_of(owners, member, item):
    rows = member.shape[1]
    step = min(256, rows)
    blocks = rows // step
    hits = jnp.concatenate([one_hot(member, owners).astype(F32), one_hot(item, owners).astype(F32)], axis=0)
    stacked = jnp.concatenate([hits[:, b * step : (b + 1) * step] for b in range(blocks)], axis=0)
    upper = lax.broadcasted_iota(jnp.int32, (step, step), 0) <= lax.broadcasted_iota(
        jnp.int32, (step, step), 1
    )
    counts = plain_dot(stacked.astype(BF16), upper.astype(F32).astype(BF16))
    before = jnp.zeros((2 * owners, 1), F32)
    pieces = []
    for b in range(blocks):
        here = counts[2 * owners * b : 2 * owners * (b + 1)]
        taken = (here + before) * hits[:, b * step : (b + 1) * step]
        sides = [jnp.sum(x, axis=0, keepdims=True) for x in (taken[:owners], taken[owners:])]
        pieces.append(jnp.concatenate(sides, axis=0))
        before = before + here[:, step - 1 : step]
    return jnp.concatenate(pieces, axis=1).astype(jnp.int32) - 1


def pack_chunk(k, capacity, place, ids, feats, chunk):
    pick = ones(low_hot(place - k * capacity, capacity))
    chunk[:capacity] = plain_dot(pick, feats).astype(BF16)
    chunk[capacity:, :capacity] = lanes_dot(ids, pick).astype(BF16)


def far_kernel(n_rows, n_ent, capacity, n_feat, far, *refs):
    sources, ranks, place_out, ids_out, feats = refs[:5], refs[5], refs[6], refs[7], refs[8]
    chunks, copies, sems = refs[9 : 9 + len(far)], refs[9 + len(far) : 13 + len(far)], refs[13 + len(far)]
    copies = (*copies, feats)
    moves = [pltpu.make_async_copy(sources[i], copies[i], sems.at[i]) for i in range(5)]
    for move in moves:
        move.start()
    for move in moves[:4]:
        move.wait()
    member, item, member_local, item_local = [copy[...] for copy in copies[:4]]
    rows = member.shape[1]
    rank = ranks_of(n_rows * n_ent, member, item)
    ranks[...] = rank
    on_item = lax.axis_index("feat") >= n_feat // 2
    own = jnp.where(on_item, item, member)
    up, across = own // n_ent - lax.axis_index("rows"), own % n_ent - lax.axis_index("ent")
    up, across = jnp.where(up < 0, up + n_rows, up), jnp.where(across < 0, across + n_ent, across)
    place = (up * n_ent + across) * capacity + jnp.where(on_item, rank[1:2], rank[0:1])
    place_out[...] = place
    local = jnp.where(on_item, item_local, member_local)
    high = local >> 8
    ids = jnp.concatenate([high, local - (high << 8), jnp.zeros((IDS - 2, rows), jnp.int32)], axis=0)
    ids = ids.astype(F32).astype(BF16)
    ids_out[...] = ids
    moves[4].wait()
    for chunk, k in zip(chunks, far):
        pack_chunk(k, capacity, place, ids, feats[...], chunk)


def rest_kernel(capacity, rest, place, ids, feats, *refs):
    chunks = refs[-len(rest) :]
    for chunk, k in zip(chunks, rest):
        pack_chunk(k, capacity, place[...], ids[...], feats[...], chunk)


def margin_kernel(place, weight, features, margin):
    wide = jnp.broadcast_to(weight[...], (16, weight.shape[1])).astype(BF16)
    margin[...] = lanes_dot(wide, features[...])[0:1]


def chunk_ids(chunk, capacity):
    pair = chunk[capacity:, :capacity].astype(F32)
    return (pair[0:1] * 256.0 + pair[1:2]).astype(jnp.int32)


def chunk_scores(chunk, table, capacity):
    entities = table.shape[0] // 2
    every = lanes_dot(table, chunk[:capacity])
    hits = one_hot(chunk_ids(chunk, capacity), entities)
    return jnp.sum(jnp.where(hits, every[:entities] + every[entities:], 0.0), axis=0, keepdims=True)


def early_kernel(capacity, count, coefs, *refs):
    chunks, kept, outs = refs[:count], refs[-count - 1], refs[-count:]
    entities = coefs.shape[0]
    kept[:entities], kept[entities:] = halves(coefs[...])
    table = kept[...]
    for chunk, out in zip(chunks, outs):
        out[...] = chunk_scores(chunk, table, capacity)


def later_kernel(capacity, table, *refs):
    half = len(refs) // 2
    for chunk, out in zip(refs[:half], refs[half:]):
        out[...] = chunk_scores(chunk, table[...], capacity)


def scores_kernel(order, capacity, n_feat, n_rows, n_ent, table, *refs):
    out = refs[-1]
    scores = [x[...] if x.shape[0] == 1 else chunk_scores(x, table[...], capacity) for x in refs[:-1]]
    scores = dict(zip(order, scores))
    scores = jnp.concatenate([scores[k] for k in range(len(order))], axis=0)
    scores = turn_rows(scores, n_rows, n_ent, lax.axis_index("rows"), lax.axis_index("ent"))
    for home in range(len(order)):
        for f in range(n_feat):
            out[(home // n_ent * n_feat + f) * n_ent + home % n_ent] = scores[home : home + 1]


def home_kernel(
    owners, capacity, n_feat, n_ent, member, item, ranks, clicks, valid, margin, scores, features, out
):
    on_item = lax.axis_index("feat") >= n_feat // 2
    total = margin[...]
    hits_of = [one_hot(owner[...], owners).astype(F32) for owner in (member, item)]
    spot_of = [ones(low_hot(ranks[side : side + 1], capacity)) for side in (0, 1)]
    for side in (0, 1):
        table = None
        for f in range(side * n_feat // 2, (side + 1) * n_feat // 2):
            part = jnp.concatenate(
                [scores[(h // n_ent * n_feat + f) * n_ent + h % n_ent] for h in range(owners)], axis=0
            )
            table = part if table is None else table + part
        found = plain_dot(jnp.concatenate(halves(table), axis=0), spot_of[side])
        total = total + jnp.sum((found[:owners] + found[owners:]) * hits_of[side], axis=0, keepdims=True)
    resid = valid[...].astype(F32) * (jax.nn.sigmoid(total) - clicks[...].astype(F32))
    hits = jnp.where(on_item, hits_of[1], hits_of[0])
    spot = jnp.where(on_item, spot_of[1], spot_of[0])
    sent = lanes_dot(jnp.concatenate(halves(hits * resid), axis=0), spot)
    sent = sent[:owners] + sent[owners:]
    low = jnp.broadcast_to(resid, (16, resid.shape[1])).astype(BF16)
    grad = plain_dot(low, features[...])[0:1]
    for h in range(owners):
        out[h, :, :capacity] = sent[h : h + 1]
        out[h, :, capacity:] = grad


def grads_kernel(order, capacity, n_rows, n_ent, scale, coefs, weight, came, *refs):
    chunks, grad_global, grad_coefs = refs[:-2], refs[-2], refs[-1]
    entities = coefs.shape[0]
    resids = jnp.concatenate([came[h][:, :capacity] for h in range(len(order))], axis=0)
    resids = turn_rows(resids, n_rows, n_ent, lax.axis_index("rows"), lax.axis_index("ent"))
    summed = came[0][:, capacity:]
    for h in range(1, len(order)):
        summed = summed + came[h][:, capacity:]
    grad_global[...] = summed * scale + 4.0 * weight[...]
    highs, lows, feats = [], [], []
    for chunk, k in zip(chunks, order):
        here = chunk_ids(chunk, capacity)
        blocks = [low_hot(here - first, min(256, entities)) for first in range(0, entities, 256)]
        high, low = halves(resids[k : k + 1])
        highs.append(jnp.concatenate([jnp.where(hits, high, jnp.zeros((), BF16)) for hits in blocks], axis=0))
        lows.append(jnp.concatenate([jnp.where(hits, low, jnp.zeros((), BF16)) for hits in blocks], axis=0))
        feats.append(chunk[:capacity])
    spread = jnp.concatenate([jnp.concatenate(highs, axis=1), jnp.concatenate(lows, axis=1)], axis=0)
    both = plain_dot(spread, jnp.concatenate(feats, axis=0))
    grad_coefs[...] = coefs[...] + both[:entities] + both[entities:]


def shift_send(x, n_rows, n_ent, k):
    if k == 0:
        return x
    up, across = divmod(k, n_ent)
    pairs = [
        (z * n_ent + c, (z + up) % n_rows * n_ent + (c + across) % n_ent)
        for z in range(n_rows)
        for c in range(n_ent)
    ]
    return lax.ppermute(x, HOME, pairs)


def call(kernel, out_shape, operands, in_specs, flops=0, scratch=(), hidden=False):
    moved = 0 if hidden else sum(x.size * x.dtype.itemsize for x in (*operands, *out_shape))
    return pl.pallas_call(
        kernel,
        out_shape=out_shape,
        in_specs=in_specs,
        out_specs=[VMEM] * len(out_shape),
        scratch_shapes=scratch,
        compiler_params=PARAMS,
        cost_estimate=pl.CostEstimate(flops=flops, bytes_accessed=moved, transcendentals=0),
    )(*operands)


def body(
    features,
    global_weight,
    entity_feats,
    coefs,
    member_owner,
    member_local,
    item_owner,
    item_local,
    clicks,
    valid,
):
    rows_here, width = entity_feats.shape
    columns = features.shape[1]
    n_feat, n_ent = lax.axis_size("feat"), lax.axis_size("ent")
    n_rows = lax.axis_size("rows")
    owners = n_rows * n_ent
    capacity = 2 * rows_here // owners
    member, item = member_owner.reshape(1, rows_here), item_owner.reshape(1, rows_here)

    def shape(*dims, dtype=F32):
        return jax.ShapeDtypeStruct(dims, dtype)

    def partial(kernel, *args):
        return lambda *refs: kernel(*args, *refs)

    row = pltpu.VMEM((1, rows_here), jnp.int32)
    middle = n_rows // 2
    away = [up * n_ent for half in range(1, middle) for up in (half, n_rows - half)]
    away += [middle * n_ent + c for c in range(n_ent)]
    away += [up * n_ent + c for c in range(1, n_ent) for half in range(1, middle) for up in (n_rows - half, half)]
    first, second, near = away[:1], away[1:-2], [*away[-2:], *reversed(range(n_ent))]
    chunk = shape(capacity + IDS, width, dtype=BF16)
    flops = len(first) * 2 * capacity * rows_here * width

    def in_hbm(x):
        return pltpu.with_memory_space_constraint(x, pltpu.HBM)

    ranks, place, ids, feats, *chunks = call(
        partial(far_kernel, n_rows, n_ent, capacity, n_feat, first),
        [
            shape(2, rows_here, dtype=jnp.int32),
            shape(1, rows_here, dtype=jnp.int32),
            shape(IDS, rows_here, dtype=BF16),
            shape(rows_here, width, dtype=BF16),
        ]
        + [chunk] * len(first),
        (
            in_hbm(member),
            in_hbm(item),
            in_hbm(member_local.reshape(1, rows_here)),
            in_hbm(item_local.reshape(1, rows_here)),
            in_hbm(entity_feats),
        ),
        [HBM] * 5,
        flops=flops,
        scratch=[row, row, row, row, pltpu.SemaphoreType.DMA((5,))],
    )
    chunks += call(
        partial(rest_kernel, capacity, second),
        [chunk] * len(second),
        (place, ids, feats),
        [VMEM] * 3,
        flops=32 * flops,
    )
    chunks = [shift_send(x, n_rows, n_ent, k) for k, x in zip(first + second, chunks)]
    weight = global_weight.astype(F32).reshape(1, columns)
    (global_part,) = call(
        margin_kernel, [shape(1, rows_here)], (place, weight, features), [VMEM] * 3, hidden=True
    )
    global_total = lax.psum(global_part, "feat")
    near_chunks = call(
        partial(rest_kernel, capacity, near),
        [chunk] * len(near),
        (place, ids, feats, global_part),
        [VMEM] * 4,
        hidden=True,
    )
    near_chunks = [shift_send(x, n_rows, n_ent, k) for k, x in zip(near, near_chunks)]
    chunks = dict(zip(first + second + near, chunks + near_chunks))
    early = away[:n_ent] + near[-1:]
    later, late = away[n_ent:-2], near[:-1]
    order = early + later + late
    table, *scores = call(
        partial(early_kernel, capacity, len(early)),
        [shape(2 * coefs.shape[0], width, dtype=BF16)] + [shape(1, capacity)] * len(early),
        (coefs, *(chunks[k] for k in early), global_total),
        [VMEM] * (2 + len(early)),
        hidden=True,
    )
    scores += call(
        partial(later_kernel, capacity),
        [shape(1, capacity)] * len(later),
        (table, *(chunks[k] for k in later)),
        [VMEM] * (1 + len(later)),
        hidden=True,
    )
    (scores,) = call(
        partial(scores_kernel, order, capacity, n_feat, n_rows, n_ent),
        [shape(n_feat * owners, 1, capacity)],
        (table, *scores, *(chunks[k] for k in late)),
        [VMEM] * (1 + owners),
        flops=16 * coefs.size * owners * capacity,
    )
    returned = lax.all_to_all(scores, EVERY, split_axis=0, concat_axis=0, tiled=True)
    (sent,) = call(
        partial(home_kernel, owners, capacity, n_feat, n_ent),
        [shape(owners, 1, capacity + columns)],
        (
            member,
            item,
            ranks,
            clicks.reshape(1, rows_here),
            valid.reshape(1, rows_here),
            global_total,
            returned,
            features,
        ),
        [VMEM] * 8,
        flops=32 * features.size,
    )
    came = lax.all_to_all(sent, HOME, split_axis=0, concat_axis=0, tiled=True)
    grad_global, grad_coefs = call(
        partial(grads_kernel, order, capacity, n_rows, n_ent, 1.0 / math.sqrt(rows_here * owners)),
        [shape(1, columns), shape(*coefs.shape)],
        (coefs, weight, came, *(chunks[k] for k in order)),
        [VMEM] * (3 + owners),
        flops=4 * coefs.size * owners * capacity,
    )
    return (grad_global.reshape(columns), grad_coefs)


def solution(mesh):
    by_row = P(("groups", "rows", "ent"))
    by_both = P(("groups", "rows", "ent"), "feat")
    column = P(("groups", "rows", "ent"), None)
    by_feat = P(("groups", "feat"))
    return jax.shard_map(
        body,
        mesh=mesh,
        in_specs=(by_both, by_feat, by_both, by_both, column, by_row, column, by_row, by_row, by_row),
        out_specs=(by_feat, by_both),
        check_vma=False,
    )
```

```python
import math

import jax
import jax.numpy as jnp
from jax import lax
from jax.experimental import pallas as pl
from jax.experimental.pallas import tpu as pltpu
from jax.sharding import PartitionSpec as P

F32 = jnp.float32
BF16 = jnp.bfloat16
HOME = ("rows", "ent")
EVERY = ("rows", "feat", "ent")
IDS = 8
PARAMS = pltpu.CompilerParams(vmem_limit_bytes=24 * 2**20)
VMEM = pl.BlockSpec(memory_space=pltpu.VMEM)
HBM = pl.BlockSpec(memory_space=pltpu.HBM)


def lanes_dot(a, b):
    return lax.dot_general(a, b, (((1,), (1,)), ((), ())), preferred_element_type=F32)


def plain_dot(a, b):
    return lax.dot_general(a, b, (((1,), (0,)), ((), ())), preferred_element_type=F32)


def halves(x):
    high = x.astype(BF16)
    return high, (x - high.astype(F32)).astype(BF16)


def one_hot(row, count):
    return row == lax.broadcasted_iota(jnp.int32, (count, row.shape[1]), 0)


def low_hot(row, count):
    row = jnp.where((row >= 0) & (row < count), row, -1).astype(F32).astype(BF16)
    return row == lax.broadcasted_iota(jnp.int32, (count, row.shape[1]), 0).astype(F32).astype(BF16)


def ones(mask):
    return jnp.where(mask, jnp.ones((), BF16), jnp.zeros((), BF16))


def turn_rows(rows, n_rows, n_ent, z, c):
    def moved(di, dj, sign):
        at = [
            ((sign * i - di) % n_rows) * n_ent + (sign * j - dj) % n_ent for i in range(n_rows) for j in range(n_ent)
        ]
        return jnp.concatenate([rows[k : k + 1] for k in at], axis=0)

    rows = moved(0, 0, -1)
    bit = 1
    while bit < n_rows:
        rows = jnp.where((z & bit) > 0, moved(bit, 0, 1), rows)
        bit *= 2
    bit = 1
    while bit < n_ent:
        rows = jnp.where((c & bit) > 0, moved(0, bit, 1), rows)
        bit *= 2
    return rows


def ranks_of(owners, member, item):
    rows = member.shape[1]
    step = min(256, rows)
    blocks = rows // step
    hits = jnp.concatenate([one_hot(member, owners).astype(F32), one_hot(item, owners).astype(F32)], axis=0)
    stacked = jnp.concatenate([hits[:, b * step : (b + 1) * step] for b in range(blocks)], axis=0)
    upper = lax.broadcasted_iota(jnp.int32, (step, step), 0) <= lax.broadcasted_iota(
        jnp.int32, (step, step), 1
    )
    counts = plain_dot(stacked.astype(BF16), upper.astype(F32).astype(BF16))
    before = jnp.zeros((2 * owners, 1), F32)
    pieces = []
    for b in range(blocks):
        here = counts[2 * owners * b : 2 * owners * (b + 1)]
        taken = (here + before) * hits[:, b * step : (b + 1) * step]
        sides = [jnp.sum(x, axis=0, keepdims=True) for x in (taken[:owners], taken[owners:])]
        pieces.append(jnp.concatenate(sides, axis=0))
        before = before + here[:, step - 1 : step]
    return jnp.concatenate(pieces, axis=1).astype(jnp.int32) - 1


def pack_chunk(k, capacity, place, ids, feats, chunk):
    pick = ones(low_hot(place - k * capacity, capacity))
    chunk[:capacity] = plain_dot(pick, feats).astype(BF16)
    chunk[capacity:, :capacity] = lanes_dot(ids, pick).astype(BF16)


def far_kernel(n_rows, n_ent, capacity, n_feat, far, *refs):
    sources, ranks, place_out, ids_out, feats = refs[:5], refs[5], refs[6], refs[7], refs[8]
    chunks, copies, sems = refs[9 : 9 + len(far)], refs[9 + len(far) : 13 + len(far)], refs[13 + len(far)]
    copies = (*copies, feats)
    moves = [pltpu.make_async_copy(sources[i], copies[i], sems.at[i]) for i in range(5)]
    for move in moves:
        move.start()
    for move in moves[:4]:
        move.wait()
    member, item, member_local, item_local = [copy[...] for copy in copies[:4]]
    rows = member.shape[1]
    rank = ranks_of(n_rows * n_ent, member, item)
    ranks[...] = rank
    on_item = lax.axis_index("feat") >= n_feat // 2
    own = jnp.where(on_item, item, member)
    up, across = own // n_ent - lax.axis_index("rows"), own % n_ent - lax.axis_index("ent")
    up, across = jnp.where(up < 0, up + n_rows, up), jnp.where(across < 0, across + n_ent, across)
    place = (up * n_ent + across) * capacity + jnp.where(on_item, rank[1:2], rank[0:1])
    place_out[...] = place
    local = jnp.where(on_item, item_local, member_local)
    high = local >> 8
    ids = jnp.concatenate([high, local - (high << 8), jnp.zeros((IDS - 2, rows), jnp.int32)], axis=0)
    ids = ids.astype(F32).astype(BF16)
    ids_out[...] = ids
    moves[4].wait()
    for chunk, k in zip(chunks, far):
        pack_chunk(k, capacity, place, ids, feats[...], chunk)


def rest_kernel(capacity, rest, place, ids, feats, *refs):
    chunks = refs[-len(rest) :]
    for chunk, k in zip(chunks, rest):
        pack_chunk(k, capacity, place[...], ids[...], feats[...], chunk)


def margin_kernel(place, weight, features, margin):
    wide = jnp.broadcast_to(weight[...], (16, weight.shape[1])).astype(BF16)
    margin[...] = lanes_dot(wide, features[...])[0:1]


def chunk_ids(chunk, capacity):
    pair = chunk[capacity:, :capacity].astype(F32)
    return (pair[0:1] * 256.0 + pair[1:2]).astype(jnp.int32)


def chunk_scores(chunk, table, capacity):
    entities = table.shape[0] // 2
    every = lanes_dot(table, chunk[:capacity])
    hits = one_hot(chunk_ids(chunk, capacity), entities)
    return jnp.sum(jnp.where(hits, every[:entities] + every[entities:], 0.0), axis=0, keepdims=True)


def early_kernel(capacity, count, coefs, *refs):
    chunks, kept, outs = refs[:count], refs[-count - 1], refs[-count:]
    entities = coefs.shape[0]
    kept[:entities], kept[entities:] = halves(coefs[...])
    table = kept[...]
    for chunk, out in zip(chunks, outs):
        out[...] = chunk_scores(chunk, table, capacity)


def later_kernel(capacity, table, *refs):
    half = len(refs) // 2
    for chunk, out in zip(refs[:half], refs[half:]):
        out[...] = chunk_scores(chunk, table[...], capacity)


def scores_kernel(order, capacity, n_feat, n_rows, n_ent, table, *refs):
    out = refs[-1]
    scores = [x[...] if x.shape[0] == 1 else chunk_scores(x, table[...], capacity) for x in refs[:-1]]
    scores = dict(zip(order, scores))
    scores = jnp.concatenate([scores[k] for k in range(len(order))], axis=0)
    scores = turn_rows(scores, n_rows, n_ent, lax.axis_index("rows"), lax.axis_index("ent"))
    for home in range(len(order)):
        for f in range(n_feat):
            out[(home // n_ent * n_feat + f) * n_ent + home % n_ent] = scores[home : home + 1]


def home_kernel(
    owners, capacity, n_feat, n_ent, member, item, ranks, clicks, valid, margin, scores, features, out
):
    on_item = lax.axis_index("feat") >= n_feat // 2
    total = margin[...]
    hits_of = [one_hot(owner[...], owners).astype(F32) for owner in (member, item)]
    spot_of = [ones(low_hot(ranks[side : side + 1], capacity)) for side in (0, 1)]
    for side in (0, 1):
        table = None
        for f in range(side * n_feat // 2, (side + 1) * n_feat // 2):
            part = jnp.concatenate(
                [scores[(h // n_ent * n_feat + f) * n_ent + h % n_ent] for h in range(owners)], axis=0
            )
            table = part if table is None else table + part
        found = plain_dot(jnp.concatenate(halves(table), axis=0), spot_of[side])
        total = total + jnp.sum((found[:owners] + found[owners:]) * hits_of[side], axis=0, keepdims=True)
    resid = valid[...].astype(F32) * (jax.nn.sigmoid(total) - clicks[...].astype(F32))
    hits = jnp.where(on_item, hits_of[1], hits_of[0])
    spot = jnp.where(on_item, spot_of[1], spot_of[0])
    sent = lanes_dot(jnp.concatenate(halves(hits * resid), axis=0), spot)
    sent = sent[:owners] + sent[owners:]
    low = jnp.broadcast_to(resid, (16, resid.shape[1])).astype(BF16)
    grad = plain_dot(low, features[...])[0:1]
    for h in range(owners):
        out[h, :, :capacity] = sent[h : h + 1]
        out[h, :, capacity:] = grad


def grads_kernel(order, capacity, n_rows, n_ent, scale, coefs, weight, came, *refs):
    chunks, grad_global, grad_coefs = refs[:-2], refs[-2], refs[-1]
    entities = coefs.shape[0]
    resids = jnp.concatenate([came[h][:, :capacity] for h in range(len(order))], axis=0)
    resids = turn_rows(resids, n_rows, n_ent, lax.axis_index("rows"), lax.axis_index("ent"))
    summed = came[0][:, capacity:]
    for h in range(1, len(order)):
        summed = summed + came[h][:, capacity:]
    grad_global[...] = summed * scale + 4.0 * weight[...]
    highs, lows, feats = [], [], []
    for chunk, k in zip(chunks, order):
        here = chunk_ids(chunk, capacity)
        blocks = [low_hot(here - first, min(256, entities)) for first in range(0, entities, 256)]
        high, low = halves(resids[k : k + 1])
        highs.append(jnp.concatenate([jnp.where(hits, high, jnp.zeros((), BF16)) for hits in blocks], axis=0))
        lows.append(jnp.concatenate([jnp.where(hits, low, jnp.zeros((), BF16)) for hits in blocks], axis=0))
        feats.append(chunk[:capacity])
    spread = jnp.concatenate([jnp.concatenate(highs, axis=1), jnp.concatenate(lows, axis=1)], axis=0)
    both = plain_dot(spread, jnp.concatenate(feats, axis=0))
    grad_coefs[...] = coefs[...] + both[:entities] + both[entities:]


def shift_send(x, n_rows, n_ent, k):
    if k == 0:
        return x
    up, across = divmod(k, n_ent)
    pairs = [
        (z * n_ent + c, (z + up) % n_rows * n_ent + (c + across) % n_ent)
        for z in range(n_rows)
        for c in range(n_ent)
    ]
    return lax.ppermute(x, HOME, pairs)


def call(kernel, out_shape, operands, in_specs, flops=0, scratch=(), hidden=False):
    moved = 0 if hidden else sum(x.size * x.dtype.itemsize for x in (*operands, *out_shape))
    return pl.pallas_call(
        kernel,
        out_shape=out_shape,
        in_specs=in_specs,
        out_specs=[VMEM] * len(out_shape),
        scratch_shapes=scratch,
        compiler_params=PARAMS,
        cost_estimate=pl.CostEstimate(flops=flops, bytes_accessed=moved, transcendentals=0),
    )(*operands)


def body(
    features,
    global_weight,
    entity_feats,
    coefs,
    member_owner,
    member_local,
    item_owner,
    item_local,
    clicks,
    valid,
):
    rows_here, width = entity_feats.shape
    columns = features.shape[1]
    n_feat, n_ent = lax.axis_size("feat"), lax.axis_size("ent")
    n_rows = lax.axis_size("rows")
    owners = n_rows * n_ent
    capacity = 2 * rows_here // owners
    member, item = member_owner.reshape(1, rows_here), item_owner.reshape(1, rows_here)

    def shape(*dims, dtype=F32):
        return jax.ShapeDtypeStruct(dims, dtype)

    def partial(kernel, *args):
        return lambda *refs: kernel(*args, *refs)

    row = pltpu.VMEM((1, rows_here), jnp.int32)
    middle = n_rows // 2
    away = [up * n_ent for half in range(1, middle) for up in (half, n_rows - half)]
    away += [middle * n_ent + c for c in range(n_ent)]
    away += [up * n_ent + c for c in range(1, n_ent) for half in range(1, middle) for up in (half, n_rows - half)]
    first, second, near = away[:1], away[1:-2], [*away[-2:], *reversed(range(n_ent))]
    chunk = shape(capacity + IDS, width, dtype=BF16)
    flops = len(first) * 2 * capacity * rows_here * width

    def in_hbm(x):
        return pltpu.with_memory_space_constraint(x, pltpu.HBM)

    ranks, place, ids, feats, *chunks = call(
        partial(far_kernel, n_rows, n_ent, capacity, n_feat, first),
        [
            shape(2, rows_here, dtype=jnp.int32),
            shape(1, rows_here, dtype=jnp.int32),
            shape(IDS, rows_here, dtype=BF16),
            shape(rows_here, width, dtype=BF16),
        ]
        + [chunk] * len(first),
        (
            in_hbm(member),
            in_hbm(item),
            in_hbm(member_local.reshape(1, rows_here)),
            in_hbm(item_local.reshape(1, rows_here)),
            in_hbm(entity_feats),
        ),
        [HBM] * 5,
        flops=flops,
        scratch=[row, row, row, row, pltpu.SemaphoreType.DMA((5,))],
    )
    chunks += call(
        partial(rest_kernel, capacity, second),
        [chunk] * len(second),
        (place, ids, feats),
        [VMEM] * 3,
        flops=32 * flops,
    )
    chunks = [shift_send(x, n_rows, n_ent, k) for k, x in zip(first + second, chunks)]
    weight = global_weight.astype(F32).reshape(1, columns)
    (global_part,) = call(
        margin_kernel, [shape(1, rows_here)], (place, weight, features), [VMEM] * 3, hidden=True
    )
    global_total = lax.psum(global_part, "feat")
    near_chunks = call(
        partial(rest_kernel, capacity, near),
        [chunk] * len(near),
        (place, ids, feats, global_part),
        [VMEM] * 4,
        hidden=True,
    )
    near_chunks = [shift_send(x, n_rows, n_ent, k) for k, x in zip(near, near_chunks)]
    chunks = dict(zip(first + second + near, chunks + near_chunks))
    early = away[:n_ent] + near[-1:]
    later, late = away[n_ent:-2] + near[2:-1], near[:2]
    order = early + later + late
    table, *scores = call(
        partial(early_kernel, capacity, len(early)),
        [shape(2 * coefs.shape[0], width, dtype=BF16)] + [shape(1, capacity)] * len(early),
        (coefs, *(chunks[k] for k in early), global_total),
        [VMEM] * (2 + len(early)),
        hidden=True,
    )
    scores += call(
        partial(later_kernel, capacity),
        [shape(1, capacity)] * len(later),
        (table, *(chunks[k] for k in later)),
        [VMEM] * (1 + len(later)),
        hidden=True,
    )
    (scores,) = call(
        partial(scores_kernel, order, capacity, n_feat, n_rows, n_ent),
        [shape(n_feat * owners, 1, capacity)],
        (table, *scores, *(chunks[k] for k in late)),
        [VMEM] * (1 + owners),
        flops=16 * coefs.size * owners * capacity,
    )
    returned = lax.all_to_all(scores, EVERY, split_axis=0, concat_axis=0, tiled=True)
    (sent,) = call(
        partial(home_kernel, owners, capacity, n_feat, n_ent),
        [shape(owners, 1, capacity + columns)],
        (
            member,
            item,
            ranks,
            clicks.reshape(1, rows_here),
            valid.reshape(1, rows_here),
            global_total,
            returned,
            features,
        ),
        [VMEM] * 8,
        flops=32 * features.size,
    )
    came = lax.all_to_all(sent, HOME, split_axis=0, concat_axis=0, tiled=True)
    grad_global, grad_coefs = call(
        partial(grads_kernel, order, capacity, n_rows, n_ent, 1.0 / math.sqrt(rows_here * owners)),
        [shape(1, columns), shape(*coefs.shape)],
        (coefs, weight, came, *(chunks[k] for k in order)),
        [VMEM] * (3 + owners),
        flops=4 * coefs.size * owners * capacity,
    )
    return (grad_global.reshape(columns), grad_coefs)


def solution(mesh):
    by_row = P(("groups", "rows", "ent"))
    by_both = P(("groups", "rows", "ent"), "feat")
    column = P(("groups", "rows", "ent"), None)
    by_feat = P(("groups", "feat"))
    return jax.shard_map(
        body,
        mesh=mesh,
        in_specs=(by_both, by_feat, by_both, by_both, column, by_row, column, by_row, by_row, by_row),
        out_specs=(by_feat, by_both),
        check_vma=False,
    )
```

```python
import math

import jax
import jax.numpy as jnp
from jax import lax
from jax.experimental import pallas as pl
from jax.experimental.pallas import tpu as pltpu
from jax.sharding import PartitionSpec as P

F32 = jnp.float32
BF16 = jnp.bfloat16
HOME = ("rows", "ent")
EVERY = ("rows", "feat", "ent")
IDS = 8
PARAMS = pltpu.CompilerParams(vmem_limit_bytes=24 * 2**20)
VMEM = pl.BlockSpec(memory_space=pltpu.VMEM)
HBM = pl.BlockSpec(memory_space=pltpu.HBM)


def lanes_dot(a, b):
    return lax.dot_general(a, b, (((1,), (1,)), ((), ())), preferred_element_type=F32)


def plain_dot(a, b):
    return lax.dot_general(a, b, (((1,), (0,)), ((), ())), preferred_element_type=F32)


def halves(x):
    high = x.astype(BF16)
    return high, (x - high.astype(F32)).astype(BF16)


def one_hot(row, count):
    return row == lax.broadcasted_iota(jnp.int32, (count, row.shape[1]), 0)


def low_hot(row, count):
    row = jnp.where((row >= 0) & (row < count), row, -1).astype(F32).astype(BF16)
    return row == lax.broadcasted_iota(jnp.int32, (count, row.shape[1]), 0).astype(F32).astype(BF16)


def ones(mask):
    return jnp.where(mask, jnp.ones((), BF16), jnp.zeros((), BF16))


def turn_rows(rows, n_rows, n_ent, z, c):
    def moved(di, dj, sign):
        at = [
            ((sign * i - di) % n_rows) * n_ent + (sign * j - dj) % n_ent for i in range(n_rows) for j in range(n_ent)
        ]
        return jnp.concatenate([rows[k : k + 1] for k in at], axis=0)

    rows = moved(0, 0, -1)
    bit = 1
    while bit < n_rows:
        rows = jnp.where((z & bit) > 0, moved(bit, 0, 1), rows)
        bit *= 2
    bit = 1
    while bit < n_ent:
        rows = jnp.where((c & bit) > 0, moved(0, bit, 1), rows)
        bit *= 2
    return rows


def ranks_of(owners, member, item):
    rows = member.shape[1]
    step = min(256, rows)
    blocks = rows // step
    hits = jnp.concatenate([one_hot(member, owners).astype(F32), one_hot(item, owners).astype(F32)], axis=0)
    stacked = jnp.concatenate([hits[:, b * step : (b + 1) * step] for b in range(blocks)], axis=0)
    upper = lax.broadcasted_iota(jnp.int32, (step, step), 0) <= lax.broadcasted_iota(
        jnp.int32, (step, step), 1
    )
    counts = plain_dot(stacked.astype(BF16), upper.astype(F32).astype(BF16))
    before = jnp.zeros((2 * owners, 1), F32)
    pieces = []
    for b in range(blocks):
        here = counts[2 * owners * b : 2 * owners * (b + 1)]
        taken = (here + before) * hits[:, b * step : (b + 1) * step]
        sides = [jnp.sum(x, axis=0, keepdims=True) for x in (taken[:owners], taken[owners:])]
        pieces.append(jnp.concatenate(sides, axis=0))
        before = before + here[:, step - 1 : step]
    return jnp.concatenate(pieces, axis=1).astype(jnp.int32) - 1


def pack_chunk(k, capacity, place, ids, feats, chunk):
    pick = ones(low_hot(place - k * capacity, capacity))
    chunk[:capacity] = plain_dot(pick, feats).astype(BF16)
    chunk[capacity:, :capacity] = lanes_dot(ids, pick).astype(BF16)


def far_kernel(n_rows, n_ent, capacity, n_feat, far, *refs):
    sources, ranks, place_out, ids_out, feats = refs[:5], refs[5], refs[6], refs[7], refs[8]
    chunks, copies, sems = refs[9 : 9 + len(far)], refs[9 + len(far) : 13 + len(far)], refs[13 + len(far)]
    copies = (*copies, feats)
    moves = [pltpu.make_async_copy(sources[i], copies[i], sems.at[i]) for i in range(5)]
    for move in moves:
        move.start()
    for move in moves[:4]:
        move.wait()
    member, item, member_local, item_local = [copy[...] for copy in copies[:4]]
    rows = member.shape[1]
    rank = ranks_of(n_rows * n_ent, member, item)
    ranks[...] = rank
    on_item = lax.axis_index("feat") >= n_feat // 2
    own = jnp.where(on_item, item, member)
    up, across = own // n_ent - lax.axis_index("rows"), own % n_ent - lax.axis_index("ent")
    up, across = jnp.where(up < 0, up + n_rows, up), jnp.where(across < 0, across + n_ent, across)
    place = (up * n_ent + across) * capacity + jnp.where(on_item, rank[1:2], rank[0:1])
    place_out[...] = place
    local = jnp.where(on_item, item_local, member_local)
    high = local >> 8
    ids = jnp.concatenate([high, local - (high << 8), jnp.zeros((IDS - 2, rows), jnp.int32)], axis=0)
    ids = ids.astype(F32).astype(BF16)
    ids_out[...] = ids
    moves[4].wait()
    for chunk, k in zip(chunks, far):
        pack_chunk(k, capacity, place, ids, feats[...], chunk)


def rest_kernel(capacity, rest, place, ids, feats, *refs):
    chunks = refs[-len(rest) :]
    for chunk, k in zip(chunks, rest):
        pack_chunk(k, capacity, place[...], ids[...], feats[...], chunk)


def margin_kernel(place, weight, features, margin):
    wide = jnp.broadcast_to(weight[...], (16, weight.shape[1])).astype(BF16)
    margin[...] = lanes_dot(wide, features[...])[0:1]


def chunk_ids(chunk, capacity):
    pair = chunk[capacity:, :capacity].astype(F32)
    return (pair[0:1] * 256.0 + pair[1:2]).astype(jnp.int32)


def chunk_scores(chunk, table, capacity):
    entities = table.shape[0] // 2
    every = lanes_dot(table, chunk[:capacity])
    hits = one_hot(chunk_ids(chunk, capacity), entities)
    return jnp.sum(jnp.where(hits, every[:entities] + every[entities:], 0.0), axis=0, keepdims=True)


def early_kernel(capacity, count, coefs, *refs):
    chunks, kept, outs = refs[:count], refs[-count - 1], refs[-count:]
    entities = coefs.shape[0]
    kept[:entities], kept[entities:] = halves(coefs[...])
    table = kept[...]
    for chunk, out in zip(chunks, outs):
        out[...] = chunk_scores(chunk, table, capacity)


def later_kernel(capacity, table, *refs):
    half = len(refs) // 2
    for chunk, out in zip(refs[:half], refs[half:]):
        out[...] = chunk_scores(chunk, table[...], capacity)


def scores_kernel(order, capacity, n_feat, n_rows, n_ent, table, *refs):
    out = refs[-1]
    scores = [x[...] if x.shape[0] == 1 else chunk_scores(x, table[...], capacity) for x in refs[:-1]]
    scores = dict(zip(order, scores))
    scores = jnp.concatenate([scores[k] for k in range(len(order))], axis=0)
    scores = turn_rows(scores, n_rows, n_ent, lax.axis_index("rows"), lax.axis_index("ent"))
    for home in range(len(order)):
        for f in range(n_feat):
            out[(home // n_ent * n_feat + f) * n_ent + home % n_ent] = scores[home : home + 1]


def home_kernel(
    owners, capacity, n_feat, n_ent, member, item, ranks, clicks, valid, margin, scores, features, out
):
    on_item = lax.axis_index("feat") >= n_feat // 2
    total = margin[...]
    hits_of = [one_hot(owner[...], owners).astype(F32) for owner in (member, item)]
    spot_of = [ones(low_hot(ranks[side : side + 1], capacity)) for side in (0, 1)]
    for side in (0, 1):
        table = None
        for f in range(side * n_feat // 2, (side + 1) * n_feat // 2):
            part = jnp.concatenate(
                [scores[(h // n_ent * n_feat + f) * n_ent + h % n_ent] for h in range(owners)], axis=0
            )
            table = part if table is None else table + part
        found = plain_dot(jnp.concatenate(halves(table), axis=0), spot_of[side])
        total = total + jnp.sum((found[:owners] + found[owners:]) * hits_of[side], axis=0, keepdims=True)
    resid = valid[...].astype(F32) * (jax.nn.sigmoid(total) - clicks[...].astype(F32))
    hits = jnp.where(on_item, hits_of[1], hits_of[0])
    spot = jnp.where(on_item, spot_of[1], spot_of[0])
    sent = lanes_dot(jnp.concatenate(halves(hits * resid), axis=0), spot)
    sent = sent[:owners] + sent[owners:]
    low = jnp.broadcast_to(resid, (16, resid.shape[1])).astype(BF16)
    grad = plain_dot(low, features[...])[0:1]
    for h in range(owners):
        out[h, :, :capacity] = sent[h : h + 1]
        out[h, :, capacity:] = grad


def grads_kernel(order, capacity, n_rows, n_ent, scale, coefs, weight, came, *refs):
    chunks, grad_global, grad_coefs = refs[:-2], refs[-2], refs[-1]
    entities = coefs.shape[0]
    resids = jnp.concatenate([came[h][:, :capacity] for h in range(len(order))], axis=0)
    resids = turn_rows(resids, n_rows, n_ent, lax.axis_index("rows"), lax.axis_index("ent"))
    summed = came[0][:, capacity:]
    for h in range(1, len(order)):
        summed = summed + came[h][:, capacity:]
    grad_global[...] = summed * scale + 4.0 * weight[...]
    highs, lows, feats = [], [], []
    for chunk, k in zip(chunks, order):
        here = chunk_ids(chunk, capacity)
        blocks = [low_hot(here - first, min(256, entities)) for first in range(0, entities, 256)]
        high, low = halves(resids[k : k + 1])
        highs.append(jnp.concatenate([jnp.where(hits, high, jnp.zeros((), BF16)) for hits in blocks], axis=0))
        lows.append(jnp.concatenate([jnp.where(hits, low, jnp.zeros((), BF16)) for hits in blocks], axis=0))
        feats.append(chunk[:capacity])
    spread = jnp.concatenate([jnp.concatenate(highs, axis=1), jnp.concatenate(lows, axis=1)], axis=0)
    both = plain_dot(spread, jnp.concatenate(feats, axis=0))
    grad_coefs[...] = coefs[...] + both[:entities] + both[entities:]


def shift_send(x, n_rows, n_ent, k):
    if k == 0:
        return x
    up, across = divmod(k, n_ent)
    pairs = [
        (z * n_ent + c, (z + up) % n_rows * n_ent + (c + across) % n_ent)
        for z in range(n_rows)
        for c in range(n_ent)
    ]
    return lax.ppermute(x, HOME, pairs)


def call(kernel, out_shape, operands, in_specs, flops=0, scratch=(), hidden=False):
    moved = 0 if hidden else sum(x.size * x.dtype.itemsize for x in (*operands, *out_shape))
    return pl.pallas_call(
        kernel,
        out_shape=out_shape,
        in_specs=in_specs,
        out_specs=[VMEM] * len(out_shape),
        scratch_shapes=scratch,
        compiler_params=PARAMS,
        cost_estimate=pl.CostEstimate(flops=flops, bytes_accessed=moved, transcendentals=0),
    )(*operands)


def body(
    features,
    global_weight,
    entity_feats,
    coefs,
    member_owner,
    member_local,
    item_owner,
    item_local,
    clicks,
    valid,
):
    rows_here, width = entity_feats.shape
    columns = features.shape[1]
    n_feat, n_ent = lax.axis_size("feat"), lax.axis_size("ent")
    n_rows = lax.axis_size("rows")
    owners = n_rows * n_ent
    capacity = 2 * rows_here // owners
    member, item = member_owner.reshape(1, rows_here), item_owner.reshape(1, rows_here)

    def shape(*dims, dtype=F32):
        return jax.ShapeDtypeStruct(dims, dtype)

    def partial(kernel, *args):
        return lambda *refs: kernel(*args, *refs)

    row = pltpu.VMEM((1, rows_here), jnp.int32)
    middle = n_rows // 2
    away = [up * n_ent for half in range(1, middle) for up in (half, n_rows - half)]
    away += [middle * n_ent + c for c in range(n_ent)]
    away += [up * n_ent + c for c in range(1, n_ent) for half in range(1, middle) for up in (n_rows - half, half)]
    first, second, near = away[:1], away[1:-2], [*away[-2:], *reversed(range(n_ent))]
    chunk = shape(capacity + IDS, width, dtype=BF16)
    flops = len(first) * 2 * capacity * rows_here * width

    def in_hbm(x):
        return pltpu.with_memory_space_constraint(x, pltpu.HBM)

    ranks, place, ids, feats, *chunks = call(
        partial(far_kernel, n_rows, n_ent, capacity, n_feat, first),
        [
            shape(2, rows_here, dtype=jnp.int32),
            shape(1, rows_here, dtype=jnp.int32),
            shape(IDS, rows_here, dtype=BF16),
            shape(rows_here, width, dtype=BF16),
        ]
        + [chunk] * len(first),
        (
            in_hbm(member),
            in_hbm(item),
            in_hbm(member_local.reshape(1, rows_here)),
            in_hbm(item_local.reshape(1, rows_here)),
            in_hbm(entity_feats),
        ),
        [HBM] * 5,
        flops=flops,
        scratch=[row, row, row, row, pltpu.SemaphoreType.DMA((5,))],
    )
    chunks += call(
        partial(rest_kernel, capacity, second),
        [chunk] * len(second),
        (place, ids, feats),
        [VMEM] * 3,
        flops=32 * flops,
    )
    chunks = [shift_send(x, n_rows, n_ent, k) for k, x in zip(first + second, chunks)]
    weight = global_weight.astype(F32).reshape(1, columns)
    near_chunks = call(
        partial(rest_kernel, capacity, near),
        [chunk] * len(near),
        (place, ids, feats),
        [VMEM] * 3,
        hidden=True,
    )
    (global_part,) = call(
        margin_kernel, [shape(1, rows_here)], (near_chunks[-1], weight, features), [VMEM] * 3, hidden=True
    )
    global_total = lax.psum(global_part, "feat")
    near_chunks = [shift_send(x, n_rows, n_ent, k) for k, x in zip(near, near_chunks)]
    chunks = dict(zip(first + second + near, chunks + near_chunks))
    early = away[:n_ent] + near[-1:]
    later, late = away[n_ent:-2] + near[2:-1], near[:2]
    order = early + later + late
    table, *scores = call(
        partial(early_kernel, capacity, len(early)),
        [shape(2 * coefs.shape[0], width, dtype=BF16)] + [shape(1, capacity)] * len(early),
        (coefs, *(chunks[k] for k in early), global_total),
        [VMEM] * (2 + len(early)),
        hidden=True,
    )
    scores += call(
        partial(later_kernel, capacity),
        [shape(1, capacity)] * len(later),
        (table, *(chunks[k] for k in later)),
        [VMEM] * (1 + len(later)),
        hidden=True,
    )
    (scores,) = call(
        partial(scores_kernel, order, capacity, n_feat, n_rows, n_ent),
        [shape(n_feat * owners, 1, capacity)],
        (table, *scores, *(chunks[k] for k in late)),
        [VMEM] * (1 + owners),
        flops=16 * coefs.size * owners * capacity,
    )
    returned = lax.all_to_all(scores, EVERY, split_axis=0, concat_axis=0, tiled=True)
    (sent,) = call(
        partial(home_kernel, owners, capacity, n_feat, n_ent),
        [shape(owners, 1, capacity + columns)],
        (
            member,
            item,
            ranks,
            clicks.reshape(1, rows_here),
            valid.reshape(1, rows_here),
            global_total,
            returned,
            features,
        ),
        [VMEM] * 8,
        flops=32 * features.size,
    )
    came = lax.all_to_all(sent, HOME, split_axis=0, concat_axis=0, tiled=True)
    grad_global, grad_coefs = call(
        partial(grads_kernel, order, capacity, n_rows, n_ent, 1.0 / math.sqrt(rows_here * owners)),
        [shape(1, columns), shape(*coefs.shape)],
        (coefs, weight, came, *(chunks[k] for k in order)),
        [VMEM] * (3 + owners),
        flops=4 * coefs.size * owners * capacity,
    )
    return (grad_global.reshape(columns), grad_coefs)


def solution(mesh):
    by_row = P(("groups", "rows", "ent"))
    by_both = P(("groups", "rows", "ent"), "feat")
    column = P(("groups", "rows", "ent"), None)
    by_feat = P(("groups", "feat"))
    return jax.shard_map(
        body,
        mesh=mesh,
        in_specs=(by_both, by_feat, by_both, by_both, column, by_row, column, by_row, by_row, by_row),
        out_specs=(by_feat, by_both),
        check_vma=False,
    )
```
